32 devices in a mesh: row: 8 (over y, x, core), col: 4 (over z).
Axes of the slice: x: 2, y: 2, z: 4, core: 2. Of those that a mesh axis runs over, the one named last changes fastest.
Arguments:
- grad_out: float32 [16384, 256], P(('row', 'col')), may hold values from -6 to 6
- relu_mask: int32 [16384, 256], P(('row', 'col')), may hold values 0 or 1
- basis_zero: float32 [16384, 256], P(('row', 'col')), may hold values from -6 to 6
- basis_one: float32 [16384, 256], P(('row', 'col')), may hold values from -6 to 6
- basis_two: float32 [16384, 256], P(('row', 'col')), may hold values from -6 to 6
- cheb_weight: float32 [3, 256, 256], replicated, may hold values from -0.375 to 0.375
- tile_values: float32 [32, 128, 128, 128], P(('row', 'col')), may hold values from -0.125 to 0.125
- tile_rows: int32 [32, 128], P(('row', 'col')), may hold values from 0 to 15
- tile_slots: int32 [32, 128], P(('row', 'col')), may hold values from 0 to 7, as said below
- send_blocks: int32 [32, 8, 1], P(('row', 'col')), may hold values from 0 to 3
- live_tiles: int32 [32], P(('row', 'col')), may hold values from 8 to 128, as said below
Outputs:
- grad_features: float32 [16384, 256], P(('row', 'col'))
- weight_grad: float32 [3, 256, 256], replicated
The draws below stay inside these ranges and needn't reach their ends.
Inputs may be any that keep to these rules, and one draw needn't show every extreme that they name: `tile_slots`: slot q of device (r, c) is the node block send_blocks[q * 4 + c, r, 0] of device q * 4 + c. On every device each of the 8 slots is the column of at least one used operator block. `send_blocks`: indices of the device's own node blocks. `live_tiles`: some device uses all 128 slots.
All inputs are finite; a program needn't handle non-finite values. No bound on the sum of `relu_mask` on one device may be relied on, other than what follows from the above.
Results may differ from the reference program's by a relative error of at most 0.0001.
Values sent between devices are 32-bit elements; how exact they have to be, the bound alone decides.
No kernel may reach another device: no remote copies, remote signals or barrier semaphores. Data moves between devices by JAX's collectives and lax.ppermute only.
A program may use at most 128 MiB of HBM per device.

```python
import jax
import jax.numpy as jnp
from jax import lax

F = 256
TB = 128
CAP = 1
CHB = 4
TILES_DEV = 128
RB = 16
SLOTS = 8
NODES = 16384
N_ROW = 8
N_COL = 4
DEVICES = 32


def draw_tile_slots(key, part):
    first_key, rest_key = jax.random.split(jax.random.fold_in(key, 11))
    scores = jax.random.randint(first_key, (DEVICES, SLOTS), 0, 65536) * SLOTS + jnp.arange(SLOTS, dtype=jnp.int32)[None, :]
    leading = jnp.argsort(scores, axis=1).astype(jnp.int32)
    others = jax.random.randint(rest_key, (DEVICES, TILES_DEV - SLOTS), 0, SLOTS).astype(jnp.int32)
    return jnp.concatenate([leading, others], axis=1).astype(jnp.int32)


def draw_live_tiles(key, part):
    first_key, second_key, pick_key = jax.random.split(jax.random.fold_in(key, 23), 3)
    spread = max(TILES_DEV - SLOTS, 1)
    first = jax.random.randint(first_key, (DEVICES,), 0, spread + 1)
    second = jax.random.randint(second_key, (DEVICES,), 0, spread + 1)
    counts = SLOTS + first * second // spread
    counts = jnp.minimum(counts, TILES_DEV).astype(jnp.int32)
    busiest = jax.random.randint(pick_key, (), 0, DEVICES)
    counts = jnp.where(jnp.arange(DEVICES, dtype=jnp.int32) == busiest, TILES_DEV, counts)
    return counts.astype(jnp.int32)


def place_ends(values, stream_key, low, largest):
    dims = values.shape
    place = [jax.random.randint(jax.random.fold_in(stream_key, axis), (), 0, dims[axis]) for axis in range(len(dims))]
    values = values.at[tuple(place)].set(low)
    longest = dims.index(max(dims))
    place[longest] = (place[longest] + 1) % dims[longest]
    return values.at[tuple(place)].set(largest)


def level_of(stream_key, extent, cuts, low, top_value):
    gain, own = 1.0, jax.random.fold_in(stream_key, 6)
    for position, blocks in cuts:
        draws = jnp.exp(jax.random.uniform(jax.random.fold_in(own, position), (blocks,), jnp.float32, low / len(cuts), top_value / len(cuts)))
        gain = gain * jnp.repeat(draws, extent[position] // blocks).reshape([-1 if axis == position else 1 for axis in range(len(extent))])
    return gain


def gaussian(rng, shape, deviation, bound, pieces=(), kind=jnp.bfloat16):
    values = deviation * jax.random.normal(rng, shape, jnp.float32)
    if pieces:
        values = values * level_of(rng, shape, pieces, -0.22, 0.18)
    return jnp.clip(values, -bound, bound).astype(kind)


def setup_inputs(seed: int = 0) -> dict:
    splits = jax.random.split(jax.random.key(seed), 12)
    return {
        "grad_out": gaussian(splits[0], (NODES, F), 1.0, 6.0, ((0, 32),), jnp.float32),
        "relu_mask": place_ends((jax.random.randint(splits[1], (NODES, F), 0, 2) < 1).astype(jnp.int32), jax.random.fold_in(splits[1], 1), 0, 1),
        "basis_zero": gaussian(splits[2], (NODES, F), 1.0, 6.0, ((0, 32),), jnp.float32),
        "basis_one": gaussian(splits[3], (NODES, F), 1.0, 6.0, ((0, 32),), jnp.float32),
        "basis_two": gaussian(splits[4], (NODES, F), 1.0, 6.0, ((0, 32),), jnp.float32),
        "cheb_weight": gaussian(splits[5], (3, F, F), F ** -0.5, 0.375, (), jnp.float32),
        "tile_values": gaussian(splits[6], (DEVICES, TILES_DEV, TB, TB), (TB * TILES_DEV // (2 * CHB)) ** -0.5, 0.125, ((0, 32),), jnp.float32),
        "tile_rows": place_ends(jax.random.randint(splits[7], (DEVICES, TILES_DEV), 0, RB), jax.random.fold_in(splits[7], 1), 0, RB - 1).astype(jnp.int32),
        "tile_slots": draw_tile_slots(jax.random.fold_in(splits[11], 71), 0),
        "send_blocks": place_ends(jax.random.randint(splits[9], (DEVICES, N_ROW, CAP), 0, CHB), jax.random.fold_in(splits[9], 1), 0, CHB - 1).astype(jnp.int32),
        "live_tiles": draw_live_tiles(jax.random.fold_in(splits[11], 71), 0),
    }


def reference(grad_out, relu_mask, basis_zero, basis_one, basis_two, cheb_weight, tile_values, tile_rows, tile_slots, send_blocks, live_tiles):
    highest = lax.Precision.HIGHEST
    masked = jnp.where(relu_mask > 0, grad_out, jnp.zeros_like(grad_out))
    bases = jnp.stack([basis_zero, basis_one, basis_two])
    weight_grad = jnp.einsum('knf,ng->kfg', bases, masked, precision=highest)
    terms = jnp.einsum('ng,kfg->knf', masked, cheb_weight, precision=highest)
    devices_all = N_ROW * N_COL
    blocks_all = CHB * devices_all
    device_ids = jnp.arange(devices_all, dtype=jnp.int32)
    row_ids = device_ids // N_COL
    col_ids = device_ids % N_COL
    glob_rows = (row_ids[:, None] * RB + tile_rows).astype(jnp.int32)
    senders = ((tile_slots // CAP) * N_COL + col_ids[:, None]).astype(jnp.int32)
    picks = send_blocks[senders, jnp.broadcast_to(row_ids[:, None], senders.shape), tile_slots % CAP]
    glob_cols = (senders * CHB + picks).astype(jnp.int32)
    keep = (jnp.arange(TILES_DEV, dtype=jnp.int32)[None, :] < live_tiles[:, None]).astype(tile_values.dtype)

    def transposed(field):
        blocks = field.reshape(blocks_all, TB, F)

        def one_device(acc, items):
            values, rows, cols, used = items
            gathered = blocks[rows]
            contrib = jnp.einsum('tab,taf->tbf', values, gathered, precision=highest) * used[:, None, None]
            return acc.at[cols].add(contrib), None

        start = jnp.zeros((blocks_all, TB, F), dtype=field.dtype)
        total, _ = lax.scan(one_device, start, (tile_values, glob_rows, glob_cols, keep))
        return total.reshape(blocks_all * TB, F)

    carried = terms[1] + 2.0 * transposed(terms[2])
    grad_features = terms[0] - terms[2] + transposed(carried)
    return grad_features, weight_grad
```

```python
import functools

import jax
import jax.numpy as jnp
from jax import lax
from jax.experimental import pallas as pl
from jax.experimental.pallas import tpu as pltpu
from jax.sharding import PartitionSpec as P

F = 256
H = 128
TB = 128
CHB = 4
NODES_DEV = CHB * TB
TILES_DEV = 128
GROUPS = 8
MIB = 1 << 20
BF16 = jnp.bfloat16
F32 = jnp.float32

SMEM = pl.BlockSpec(memory_space=pltpu.SMEM)
VMEM = pl.BlockSpec(memory_space=pltpu.VMEM)
ANY = pl.BlockSpec(memory_space=pl.ANY)


def params(mib):
    return pltpu.CompilerParams(vmem_limit_bytes=mib * MIB)


def cost(flops, bytes_accessed):
    return pl.CostEstimate(flops=flops, bytes_accessed=bytes_accessed, transcendentals=0)


def split(x):
    high = x.astype(BF16)
    low = (x - high.astype(F32)).astype(BF16)
    return high, low


def dot3(a, b, dims):
    ah, al = a
    bh, bl = b

    def one(x, y):
        return lax.dot_general(x, y, (dims, ((), ())), preferred_element_type=F32)

    return one(ah, bh) + (one(ah, bl) + one(al, bh))


def masked_of(grad_ref, mask_ref):
    grad = grad_ref[...]
    return jnp.where(mask_ref[...] > 0, grad, jnp.zeros_like(grad))


def term_two_kernel(grad_ref, mask_ref, weight_ref, left_ref, right_ref):
    term = dot3(split(masked_of(grad_ref, mask_ref)), split(weight_ref[0]), ((1,), (1,)))
    left_ref[...] = term[:, :H]
    right_ref[...] = term[:, H:]


def term_two(grad_out, relu_mask, cheb_weight):
    full = pl.BlockSpec((NODES_DEV, F), lambda i: (0, 0))
    half = pl.BlockSpec((NODES_DEV, H), lambda i: (0, 0))
    out = jax.ShapeDtypeStruct((NODES_DEV, H), F32)
    return pl.pallas_call(
        term_two_kernel,
        grid=(1,),
        in_specs=[full, full, pl.BlockSpec((1, F, F), lambda i: (2, 0, 0))],
        out_specs=[half, half],
        out_shape=[out, out],
        compiler_params=params(16),
        cost_estimate=cost(6 * NODES_DEV * F * F, 4 * NODES_DEV * F * 3 + 4 * F * F),
        name="term_two",
    )(grad_out, relu_mask, cheb_weight)


def local_kernel(n_row, ids_ref, grad_ref, mask_ref, b0, b1, b2, weight_ref, *rest):
    left_ref, right_ref, diff_ref = rest[:3]
    pieces = rest[3 : 3 + n_row]
    total = rest[3 + n_row]
    masked = split(masked_of(grad_ref, mask_ref))
    term = dot3(masked, split(weight_ref[1]), ((1,), (1,)))
    left_ref[...] = term[:, :H]
    right_ref[...] = term[:, H:]
    diff_ref[...] = dot3(masked, split(weight_ref[0] - weight_ref[2]), ((1,), (1,)))
    for k, basis in enumerate((b0, b1, b2)):
        total[k * F : (k + 1) * F, :] = dot3(split(basis[...]), masked, ((0,), (0,)))
    rows = 3 * F // n_row
    for j, piece in enumerate(pieces):
        begin = pl.multiple_of((ids_ref[0] ^ j) * rows, 8)
        piece[...] = total[pl.ds(begin, rows), :]


def local_terms(n_row, ids, grad_out, relu_mask, b0, b1, b2, cheb_weight):
    half = jax.ShapeDtypeStruct((NODES_DEV, H), F32)
    piece = jax.ShapeDtypeStruct((3 * F // n_row, F), F32)
    outs = pl.pallas_call(
        functools.partial(local_kernel, n_row),
        in_specs=[SMEM] + [VMEM] * 6,
        out_specs=[VMEM] * (3 + n_row),
        out_shape=[half, half, jax.ShapeDtypeStruct((NODES_DEV, F), F32)] + [piece] * n_row,
        scratch_shapes=[pltpu.VMEM((3 * F, F), F32)],
        compiler_params=params(32),
        cost_estimate=cost(30 * NODES_DEV * F * F, 4 * NODES_DEV * F * 8),
        name="local_terms",
    )(ids, grad_out, relu_mask, b0, b1, b2, cheb_weight)
    return outs[0], outs[1], outs[2], outs[3:]


def operator_kernel(n_row, n_col, ids_ref, live_ref, rows_ref, slots_ref, values_ref, out_ref, tiles, acc, lists, counts, sems):
    origin = pl.program_id(0)
    size = TILES_DEV // GROUPS

    def copy(g):
        part = pl.ds(g * size, size)
        return pltpu.make_async_copy(values_ref.at[part], tiles.at[part], sems.at[g])

    @pl.when(origin == 0)
    def _():
        for g in range(GROUPS):
            copy(g).start()
        for s in range(n_col):
            counts[s] = 0

        def place(t, carry):
            row = rows_ref[t]
            s = lax.rem(row // CHB - ids_ref[1] + n_col, n_col)
            position = (slots_ref[t] ^ ids_ref[0]) * CHB + lax.rem(row, CHB)
            n = counts[s]
            lists[s, n] = position * TILES_DEV + t
            counts[s] = n + 1
            return carry

        lax.fori_loop(0, live_ref[0], place, 0)
        for g in range(GROUPS):
            copy(g).wait()

    acc[...] = jnp.zeros_like(acc)

    def add(n, carry):
        entry = lists[origin, n]
        position = entry // TILES_DEV
        acc[position] += tiles[lax.rem(entry, TILES_DEV)]
        return carry

    lax.fori_loop(0, counts[origin], add, 0)

    def store(slot, carry):
        here = pl.ds(pl.multiple_of(slot * TB, TB), TB)
        for i in range(CHB):
            high, low = split(acc[slot * CHB + i].T)
            out_ref[0, here, i * TB : (i + 1) * TB] = high
            out_ref[0, here, NODES_DEV + i * TB : NODES_DEV + (i + 1) * TB] = low
        return carry

    lax.fori_loop(0, n_row, store, 0)


def build_operator(n_row, n_col, ids, live, rows, slots, values):
    wide = (n_row * TB, 2 * NODES_DEV)
    return pl.pallas_call(
        functools.partial(operator_kernel, n_row, n_col),
        grid=(n_col,),
        in_specs=[SMEM] * 4 + [ANY],
        out_specs=pl.BlockSpec((1,) + wide, lambda s: (s, 0, 0)),
        out_shape=jax.ShapeDtypeStruct((n_col,) + wide, BF16),
        scratch_shapes=[
            pltpu.VMEM((TILES_DEV, TB, TB), F32),
            pltpu.VMEM((n_row * CHB, TB, TB), F32),
            pltpu.SMEM((n_col, TILES_DEV), jnp.int32),
            pltpu.SMEM((n_col,), jnp.int32),
            pltpu.SemaphoreType.DMA((GROUPS,)),
        ],
        compiler_params=params(48),
        cost_estimate=cost(0, 4 * TILES_DEV * TB * TB * 5),
        name="operator",
    )(ids, live, rows, slots, values)


def product_kernel(n_row, origins, has_prev, last, *refs):
    n = len(origins)
    op_ref, fields = refs[0], refs[1 : 1 + n]
    prev = refs[1 + n] if has_prev else None
    outs = refs[1 + n + has_prev : -2]
    buf, sems = refs[-2:]
    pairs = n_row // 2
    wide = 2 * TB

    def copy(k, p):
        source = op_ref.at[origins[k], pl.ds(p * wide, wide)]
        return pltpu.make_async_copy(source, buf.at[k, pl.ds(p * wide, wide)], sems.at[k, p])

    for p in range(pairs):
        for k in range(n):
            copy(k, p).start()
    right = []
    for field in fields:
        high, low = split(field[...])
        both = jnp.concatenate([high, low], axis=1)
        right.append(jnp.concatenate([both, both], axis=0))
    for p in range(pairs):
        total = None
        for k in range(n):
            copy(k, p).wait()
            here = jnp.dot(buf[k, p * wide : (p + 1) * wide, :], right[k], preferred_element_type=F32)
            total = here if total is None else total + here
        summed = total[:, :H] + total[:, H:]
        if has_prev:
            summed = summed + prev[p * wide : (p + 1) * wide, :]
        if last:
            outs[2 * p][...] = summed[:TB]
            outs[2 * p + 1][...] = summed[TB:]
        else:
            outs[0][p * wide : (p + 1) * wide, :] = summed


def product(n_row, origins, operator, fields, prev, last):
    rows = n_row * TB
    n = len(origins)
    has_prev = prev is not None
    if last:
        out_shape = [jax.ShapeDtypeStruct((TB, H), F32)] * n_row
    else:
        out_shape = [jax.ShapeDtypeStruct((rows, H), F32)]
    out = pl.pallas_call(
        functools.partial(product_kernel, n_row, origins, has_prev, last),
        in_specs=[ANY] + [VMEM] * (n + has_prev),
        out_specs=[VMEM] * len(out_shape),
        out_shape=out_shape,
        scratch_shapes=[
            pltpu.VMEM((n, rows, 2 * NODES_DEV), BF16),
            pltpu.SemaphoreType.DMA((n, n_row // 2)),
        ],
        compiler_params=params(40),
        cost_estimate=cost(
            2 * n * rows * 2 * NODES_DEV * F, n * rows * NODES_DEV * 4 + 4 * n * NODES_DEV * H + 8 * rows * H
        ),
        name="product",
    )(operator, *fields, *((prev,) if has_prev else ()))
    return out if last else out[0]


def collect_kernel(n_row, scale, halves, ids_ref, owners_ref, base_ref, *refs):
    out_ref = refs[-1]
    out_ref[...] = base_ref[...]
    for h in range(halves):
        for j in range(n_row):
            owner = owners_ref[ids_ref[0] ^ j]
            here = pl.ds(pl.multiple_of(owner * TB, TB), TB)
            came = refs[h * n_row + j][...]
            out_ref[here, h * H : (h + 1) * H] += came if scale == 1.0 else scale * came


def collect(n_row, scale, ids, owners, base, received):
    halves = len(received) // n_row
    return pl.pallas_call(
        functools.partial(collect_kernel, n_row, scale, halves),
        in_specs=[SMEM, SMEM] + [VMEM] * (1 + len(received)),
        out_specs=VMEM,
        out_shape=jax.ShapeDtypeStruct(base.shape, F32),
        compiler_params=params(24),
        cost_estimate=cost(0, 4 * (2 * base.size + len(received) * TB * H)),
        name="collect",
    )(ids, owners, base, *received)


def assemble_kernel(n_row, ids_ref, *refs):
    out_ref = refs[-1]
    rows = 3 * F // n_row
    for j in range(n_row):
        begin = pl.multiple_of((ids_ref[0] ^ j) * rows, 8)
        out_ref[pl.ds(begin, rows), :] = refs[j][...]


def assemble(n_row, ids, pieces):
    return pl.pallas_call(
        functools.partial(assemble_kernel, n_row),
        in_specs=[SMEM] + [VMEM] * n_row,
        out_specs=VMEM,
        out_shape=jax.ShapeDtypeStruct((3 * F, F), F32),
        compiler_params=params(16),
        cost_estimate=cost(0, 8 * 3 * F * F),
        name="assemble",
    )(ids, *pieces)


def exchange(n_row, pieces):
    moved = [pieces[0]]
    for j in range(1, n_row):
        moved.append(lax.ppermute(pieces[j], "row", [(r, r ^ j) for r in range(n_row)]))
    return moved


def shift(n_col, x, step):
    return lax.ppermute(x, "col", [(c, (c + step) % n_col) for c in range(n_col)])


def reduce_weights(n_row, n_col, ids, pieces):
    mine = functools.reduce(jnp.add, exchange(n_row, pieces))
    step = 1
    while step < n_col:
        mine = mine + lax.ppermute(mine, "col", [(c, c ^ step) for c in range(n_col)])
        step *= 2
    return assemble(n_row, ids, exchange(n_row, [mine] * n_row)).reshape(3, F, F)


def transposed(n_row, n_col, operator, field, side):
    long = n_col // 2
    short = n_col - 1 - long
    total = product(n_row, (0,), operator, [field], None, n_col == 1)
    ahead, behind = field, field
    for s in range(1, long + 1):
        fields, origins = [], []
        ahead = shift(n_col, ahead, side)
        fields.append(ahead)
        origins.append((-side * s) % n_col)
        if s <= short:
            behind = shift(n_col, behind, -side)
            fields.append(behind)
            origins.append((side * s) % n_col)
        total = product(n_row, tuple(origins), operator, fields, total, s == long)
    return exchange(n_row, total)


def per_device(
    grad_out,
    relu_mask,
    basis_zero,
    basis_one,
    basis_two,
    cheb_weight,
    tile_values,
    tile_rows,
    tile_slots,
    send_blocks,
    live_tiles,
):
    n_row = lax.axis_size("row")
    n_col = lax.axis_size("col")
    ids = jnp.stack([lax.axis_index("row"), lax.axis_index("col")]).astype(jnp.int32)
    owners = send_blocks.reshape(n_row)
    two = term_two(grad_out, relu_mask, cheb_weight)
    operator = build_operator(
        n_row, n_col, ids, live_tiles, tile_rows.reshape(TILES_DEV), tile_slots.reshape(TILES_DEV), tile_values[0]
    )
    one_left, one_right, diff, pieces = local_terms(
        n_row, ids, grad_out, relu_mask, basis_zero, basis_one, basis_two, cheb_weight
    )
    received = []
    for side, field, one in ((1, two[0], one_left), (-1, two[1], one_right)):
        first = transposed(n_row, n_col, operator, field, side)
        carried = collect(n_row, 2.0, ids, owners, one, first)
        received += transposed(n_row, n_col, operator, carried, side)
    weight_grad = reduce_weights(n_row, n_col, ids, pieces)
    grad_features = collect(n_row, 1.0, ids, owners, diff, received)
    return grad_features, weight_grad


def solution(mesh):
    placed = (
        P(("row", "col"), None),
        P(("row", "col"), None),
        P(("row", "col"), None),
        P(("row", "col"), None),
        P(("row", "col"), None),
        P(),
        P(("row", "col"), None, None, None),
        P(("row", "col"), None),
        P(("row", "col"), None),
        P(("row", "col"), None, None),
        P(("row", "col")),
    )
    return jax.shard_map(
        per_device,
        mesh=mesh,
        in_specs=placed,
        out_specs=(P(("row", "col"), None), P()),
        check_vma=False,
    )
```

```python
import functools

import jax
import jax.numpy as jnp
from jax import lax
from jax.experimental import pallas as pl
from jax.experimental.pallas import tpu as pltpu
from jax.sharding import PartitionSpec as P

F = 256
H = 128
TB = 128
CHB = 4
NODES_DEV = CHB * TB
TILES_DEV = 128
GROUPS = 8
MIB = 1 << 20
BF16 = jnp.bfloat16
F32 = jnp.float32

SMEM = pl.BlockSpec(memory_space=pltpu.SMEM)
VMEM = pl.BlockSpec(memory_space=pltpu.VMEM)
HBM = pl.BlockSpec(memory_space=pltpu.HBM)
RESIDENT_BYTES = 16 * MIB


def params(mib):
    return pltpu.CompilerParams(vmem_limit_bytes=mib * MIB)


def in_hbm(*arrays):
    return [pltpu.with_memory_space_constraint(x, pltpu.HBM) for x in arrays]


def cost(flops, bytes_accessed):
    return pl.CostEstimate(flops=flops, bytes_accessed=bytes_accessed, transcendentals=0)


def split(x):
    high = x.astype(BF16)
    low = (x - high.astype(F32)).astype(BF16)
    return high, low


def dot3(a, b, dims):
    ah, al = a
    bh, bl = b

    def one(x, y):
        return lax.dot_general(x, y, (dims, ((), ())), preferred_element_type=F32)

    return one(ah, bh) + (one(ah, bl) + one(al, bh))


def fetch(sources, targets, sems):
    copies = [pltpu.make_async_copy(a, b, sems.at[i]) for i, (a, b) in enumerate(zip(sources, targets))]
    for copy in copies:
        copy.start()
    return copies


def masked_of(grad, mask):
    return jnp.where(mask > 0, grad, jnp.zeros_like(grad))


def term_two_kernel(grad_hbm, mask_hbm, weight_hbm, left_ref, right_ref, grad, mask, weight, sems):
    for copy in fetch((grad_hbm, mask_hbm, weight_hbm.at[2]), (grad, mask, weight), sems):
        copy.wait()
    term = dot3(split(masked_of(grad[...], mask[...])), split(weight[...]), ((1,), (1,)))
    left_ref[...] = term[:, :H]
    right_ref[...] = term[:, H:]


def term_two(grad_out, relu_mask, cheb_weight):
    out = jax.ShapeDtypeStruct((NODES_DEV, H), F32)
    return pl.pallas_call(
        term_two_kernel,
        in_specs=[HBM] * 3,
        out_specs=[VMEM, VMEM],
        out_shape=[out, out],
        scratch_shapes=[
            pltpu.VMEM((NODES_DEV, F), F32),
            pltpu.VMEM((NODES_DEV, F), jnp.int32),
            pltpu.VMEM((F, F), F32),
            pltpu.SemaphoreType.DMA((3,)),
        ],
        compiler_params=params(16),
        cost_estimate=cost(6 * NODES_DEV * F * F, 4 * NODES_DEV * F * 3 + 4 * F * F),
        name="term_two",
    )(*in_hbm(grad_out, relu_mask, cheb_weight))


def local_kernel(
    grad_hbm, mask_hbm, weight_hbm, h0, h1, h2, left_ref, right_ref, diff_ref, total_ref, grad, mask, weight, bases, sems
):
    sources = (grad_hbm, mask_hbm, weight_hbm, h0, h1, h2)
    copies = fetch(sources, (grad, mask, weight, bases.at[0], bases.at[1], bases.at[2]), sems)
    for copy in copies[:3]:
        copy.wait()
    masked = split(masked_of(grad[...], mask[...]))
    term = dot3(masked, split(weight[1]), ((1,), (1,)))
    left_ref[...] = term[:, :H]
    right_ref[...] = term[:, H:]
    diff_ref[...] = dot3(masked, split(weight[0] - weight[2]), ((1,), (1,)))
    for k in range(3):
        copies[3 + k].wait()
        total_ref[k] = dot3(split(bases[k]), masked, ((0,), (0,)))


def local_terms(grad_out, relu_mask, cheb_weight, b0, b1, b2):
    half = jax.ShapeDtypeStruct((NODES_DEV, H), F32)
    return pl.pallas_call(
        local_kernel,
        in_specs=[HBM] * 6,
        out_specs=[VMEM] * 4,
        out_shape=[half, half, jax.ShapeDtypeStruct((NODES_DEV, F), F32), jax.ShapeDtypeStruct((3, F, F), F32)],
        scratch_shapes=[
            pltpu.VMEM((NODES_DEV, F), F32),
            pltpu.VMEM((NODES_DEV, F), jnp.int32),
            pltpu.VMEM((3, F, F), F32),
            pltpu.VMEM((3, NODES_DEV, F), F32),
            pltpu.SemaphoreType.DMA((6,)),
        ],
        compiler_params=params(32),
        cost_estimate=cost(30 * NODES_DEV * F * F, 4 * NODES_DEV * F * 8),
        name="local_terms",
    )(*in_hbm(grad_out, relu_mask, cheb_weight, b0, b1, b2))


def operator_kernel(
    n_row, n_col, resident, ids_ref, live_ref, rows_hbm, slots_hbm, values_ref, out_ref,
    tiles, acc, lists, counts, rows, slots, sems, small_sems,
):
    size = TILES_DEV // GROUPS

    def copy(g):
        part = pl.ds(g * size, size)
        return pltpu.make_async_copy(values_ref.at[0, part], tiles.at[part], sems.at[g])

    def begin():
        small = fetch((rows_hbm, slots_hbm), (rows, slots), small_sems)
        for g in range(GROUPS):
            copy(g).start()
        for s in range(n_col):
            counts[s] = 0
        for item in small:
            item.wait()

        def place(t, carry):
            row = rows[0, t]
            s = lax.rem(row // CHB - ids_ref[0] + n_col, n_col)
            position = slots[0, t] * CHB + lax.rem(row, CHB)
            n = counts[s]
            lists[s, n] = position * TILES_DEV + t
            counts[s] = n + 1
            return carry

        lax.fori_loop(0, live_ref[0], place, 0)
        for g in range(GROUPS):
            copy(g).wait()

    def one(origin, to):
        acc[...] = jnp.zeros_like(acc)

        def add(n, carry):
            entry = lists[origin, n]
            position = entry // TILES_DEV
            acc[position] += tiles[lax.rem(entry, TILES_DEV)]
            return carry

        lax.fori_loop(0, counts[origin], add, 0)

        def store(slot, carry):
            here = pl.ds(pl.multiple_of(slot * TB, TB), TB)
            for i in range(CHB):
                high, low = split(acc[slot * CHB + i].T)
                out_ref[to, here, i * TB : (i + 1) * TB] = high
                out_ref[to, here, NODES_DEV + i * TB : NODES_DEV + (i + 1) * TB] = low
            return carry

        lax.fori_loop(0, n_row, store, 0)

    if resident:
        begin()

        def each(origin, carry):
            one(origin, origin)
            return carry

        lax.fori_loop(0, n_col, each, 0)
    else:
        pl.when(pl.program_id(0) == 0)(begin)
        one(pl.program_id(0), 0)


def fits(n_row, n_col):
    return 4 * n_col * n_row * TB * NODES_DEV <= RESIDENT_BYTES


def build_operator(n_row, n_col, ids, live, rows, slots, values):
    wide = (n_row * TB, 2 * NODES_DEV)
    resident = fits(n_row, n_col)
    grid = {} if resident else {"grid": (n_col,)}
    return pl.pallas_call(
        functools.partial(operator_kernel, n_row, n_col, resident),
        in_specs=[SMEM] * 2 + [HBM] * 3,
        out_specs=VMEM if resident else pl.BlockSpec((1,) + wide, lambda s: (s, 0, 0)),
        out_shape=jax.ShapeDtypeStruct((n_col,) + wide, BF16),
        scratch_shapes=[
            pltpu.VMEM((TILES_DEV, TB, TB), F32),
            pltpu.VMEM((n_row * CHB, TB, TB), F32),
            pltpu.SMEM((n_col, TILES_DEV), jnp.int32),
            pltpu.SMEM((n_col,), jnp.int32),
            pltpu.SMEM((1, TILES_DEV), jnp.int32),
            pltpu.SMEM((1, TILES_DEV), jnp.int32),
            pltpu.SemaphoreType.DMA((GROUPS,)),
            pltpu.SemaphoreType.DMA((2,)),
        ],
        compiler_params=params(40),
        cost_estimate=cost(0, 4 * TILES_DEV * TB * TB * 5),
        name="operator",
        **grid,
    )(ids, live, *in_hbm(rows, slots, values))


def product_kernel(n_row, origins, has_prev, resident, *refs):
    n = len(origins)
    op_ref, fields = refs[0], refs[1 : 1 + n]
    prev = refs[1 + n] if has_prev else None
    out_ref = refs[1 + n + has_prev]
    pairs = n_row // 2
    wide = 2 * TB
    if not resident:
        buf, sems = refs[-2:]

        def copy(k, p):
            source = op_ref.at[origins[k], pl.ds(p * wide, wide)]
            return pltpu.make_async_copy(source, buf.at[k, pl.ds(p * wide, wide)], sems.at[k, p])

        for p in range(pairs):
            for k in range(n):
                copy(k, p).start()
    right = []
    for field in fields:
        high, low = split(field[...])
        both = jnp.concatenate([high, low], axis=1)
        right.append(jnp.concatenate([both, both], axis=0))
    for p in range(pairs):
        here = slice(p * wide, (p + 1) * wide)
        total = None
        for k in range(n):
            if resident:
                left = op_ref[origins[k], here, :]
            else:
                copy(k, p).wait()
                left = buf[k, here, :]
            part = jnp.dot(left, right[k], preferred_element_type=F32)
            total = part if total is None else total + part
        summed = total[:, :H] + total[:, H:]
        out_ref[here, :] = summed + prev[here, :] if has_prev else summed


def product(n_row, n_col, origins, operator, fields, prev):
    rows = n_row * TB
    n = len(origins)
    has_prev = prev is not None
    resident = fits(n_row, n_col)
    scratch = [
        pltpu.VMEM((n, rows, 2 * NODES_DEV), BF16),
        pltpu.SemaphoreType.DMA((n, n_row // 2)),
    ]
    return pl.pallas_call(
        functools.partial(product_kernel, n_row, origins, has_prev, resident),
        in_specs=[VMEM if resident else HBM] + [VMEM] * (n + has_prev),
        out_specs=VMEM,
        out_shape=jax.ShapeDtypeStruct((rows, H), F32),
        scratch_shapes=[] if resident else scratch,
        compiler_params=params(24 if resident else 40),
        cost_estimate=cost(
            2 * n * rows * 2 * NODES_DEV * F, n * rows * NODES_DEV * 4 + 4 * n * NODES_DEV * H + 8 * rows * H
        ),
        name="product",
    )(operator, *fields, *((prev,) if has_prev else ()))


def collect_kernel(n_row, scale, owners_ref, base_ref, *refs):
    out_ref = refs[-1]
    out_ref[...] = base_ref[...]
    for h, came in enumerate(refs[:-1]):
        for q in range(n_row):
            here = pl.ds(pl.multiple_of(owners_ref[q] * TB, TB), TB)
            out_ref[here, h * H : (h + 1) * H] += came[q] if scale == 1.0 else scale * came[q]


def collect(n_row, scale, owners, base, received):
    return pl.pallas_call(
        functools.partial(collect_kernel, n_row, scale),
        in_specs=[SMEM] + [VMEM] * (1 + len(received)),
        out_specs=VMEM,
        out_shape=jax.ShapeDtypeStruct(base.shape, F32),
        compiler_params=params(24),
        cost_estimate=cost(0, 4 * (2 * base.size + len(received) * n_row * TB * H)),
        name="collect",
    )(owners, base, *received)


def shift(n_col, x, step):
    return lax.ppermute(x, "col", [(c, (c + step) % n_col) for c in range(n_col)])


def exchange(pieces):
    return lax.all_to_all(pieces, "row", split_axis=0, concat_axis=0, tiled=True)


def reduce_weights(n_row, local):
    mine = jnp.sum(exchange(local.reshape(n_row, 3 * F // n_row, F)), axis=0)
    mine = jnp.sum(lax.all_gather(mine, "col", axis=0), axis=0)
    return lax.all_gather(mine, "row", axis=0, tiled=True).reshape(3, F, F)


def transposed(n_row, n_col, operator, field, side):
    long = n_col // 2
    short = n_col - 1 - long
    total = product(n_row, n_col, (0,), operator, [field], None)
    ahead, behind = field, field
    for s in range(1, long + 1):
        fields, origins = [], []
        ahead = shift(n_col, ahead, side)
        fields.append(ahead)
        origins.append((-side * s) % n_col)
        if s <= short:
            behind = shift(n_col, behind, -side)
            fields.append(behind)
            origins.append((side * s) % n_col)
        total = product(n_row, n_col, tuple(origins), operator, fields, total)
    return exchange(total.reshape(n_row, TB, H))


def per_device(
    grad_out,
    relu_mask,
    basis_zero,
    basis_one,
    basis_two,
    cheb_weight,
    tile_values,
    tile_rows,
    tile_slots,
    send_blocks,
    live_tiles,
):
    n_row = lax.axis_size("row")
    n_col = lax.axis_size("col")
    ids = lax.axis_index("col").astype(jnp.int32).reshape(1)
    owners = send_blocks.reshape(n_row)
    two = term_two(grad_out, relu_mask, cheb_weight)
    operator = build_operator(n_row, n_col, ids, live_tiles, tile_rows, tile_slots, tile_values)
    one_left, one_right, diff, local = local_terms(
        grad_out, relu_mask, cheb_weight, basis_zero, basis_one, basis_two
    )
    received = []
    for side, field, one in ((1, two[0], one_left), (-1, two[1], one_right)):
        first = transposed(n_row, n_col, operator, field, side)
        carried = collect(n_row, 2.0, owners, one, [first])
        received.append(transposed(n_row, n_col, operator, carried, side))
    weight_grad = reduce_weights(n_row, local)
    grad_features = collect(n_row, 1.0, owners, diff, received)
    return grad_features, weight_grad


def solution(mesh):
    placed = (
        P(("row", "col"), None),
        P(("row", "col"), None),
        P(("row", "col"), None),
        P(("row", "col"), None),
        P(("row", "col"), None),
        P(),
        P(("row", "col"), None, None, None),
        P(("row", "col"), None),
        P(("row", "col"), None),
        P(("row", "col"), None, None),
        P(("row", "col")),
    )
    return jax.shard_map(
        per_device,
        mesh=mesh,
        in_specs=placed,
        out_specs=(P(("row", "col"), None), P()),
        check_vma=False,
    )
```

```python
import functools

import jax
import jax.numpy as jnp
from jax import lax
from jax.experimental import pallas as pl
from jax.experimental.pallas import tpu as pltpu
from jax.sharding import PartitionSpec as P

F = 256
H = 128
TB = 128
CHB = 4
NODES_DEV = CHB * TB
TILES_DEV = 128
GROUPS = 8
MIB = 1 << 20
BF16 = jnp.bfloat16
F32 = jnp.float32

SMEM = pl.BlockSpec(memory_space=pltpu.SMEM)
VMEM = pl.BlockSpec(memory_space=pltpu.VMEM)
HBM = pl.BlockSpec(memory_space=pltpu.HBM)
RESIDENT_BYTES = 16 * MIB


def params(mib):
    return pltpu.CompilerParams(vmem_limit_bytes=mib * MIB)


def in_hbm(*arrays):
    return [pltpu.with_memory_space_constraint(x, pltpu.HBM) for x in arrays]


def cost(flops, bytes_accessed):
    return pl.CostEstimate(flops=flops, bytes_accessed=bytes_accessed, transcendentals=0)


def split(x):
    high = x.astype(BF16)
    low = (x - high.astype(F32)).astype(BF16)
    return high, low


def dot3(a, b, dims):
    ah, al = a
    bh, bl = b

    def one(x, y):
        return lax.dot_general(x, y, (dims, ((), ())), preferred_element_type=F32)

    return one(ah, bh) + (one(ah, bl) + one(al, bh))


def fetch(sources, targets, sems):
    copies = [pltpu.make_async_copy(a, b, sems.at[i]) for i, (a, b) in enumerate(zip(sources, targets))]
    for copy in copies:
        copy.start()
    return copies


def masked_of(grad, mask):
    return jnp.where(mask > 0, grad, jnp.zeros_like(grad))


def term_two_kernel(grad_hbm, mask_hbm, weight_hbm, left_ref, right_ref, grad, mask, weight, sems):
    for copy in fetch((grad_hbm, mask_hbm, weight_hbm.at[2]), (grad, mask, weight), sems):
        copy.wait()
    term = dot3(split(masked_of(grad[...], mask[...])), split(weight[...]), ((1,), (1,)))
    left_ref[...] = term[:, :H]
    right_ref[...] = term[:, H:]


def term_two(grad_out, relu_mask, cheb_weight):
    out = jax.ShapeDtypeStruct((NODES_DEV, H), F32)
    return pl.pallas_call(
        term_two_kernel,
        in_specs=[HBM] * 3,
        out_specs=[VMEM, VMEM],
        out_shape=[out, out],
        scratch_shapes=[
            pltpu.VMEM((NODES_DEV, F), F32),
            pltpu.VMEM((NODES_DEV, F), jnp.int32),
            pltpu.VMEM((F, F), F32),
            pltpu.SemaphoreType.DMA((3,)),
        ],
        compiler_params=params(16),
        cost_estimate=cost(6 * NODES_DEV * F * F, 4 * NODES_DEV * F * 3 + 4 * F * F),
        name="term_two",
    )(*in_hbm(grad_out, relu_mask, cheb_weight))


def local_kernel(
    grad_hbm, mask_hbm, weight_hbm, h0, h1, h2, left_ref, right_ref, diff_ref, total_ref, grad, mask, weight, bases, sems
):
    sources = (grad_hbm, mask_hbm, weight_hbm, h0, h1, h2)
    copies = fetch(sources, (grad, mask, weight, bases.at[0], bases.at[1], bases.at[2]), sems)
    for copy in copies[:3]:
        copy.wait()
    masked = split(masked_of(grad[...], mask[...]))
    term = dot3(masked, split(weight[1]), ((1,), (1,)))
    left_ref[...] = term[:, :H]
    right_ref[...] = term[:, H:]
    diff_ref[...] = dot3(masked, split(weight[0] - weight[2]), ((1,), (1,)))
    for k in range(3):
        copies[3 + k].wait()
        total_ref[k] = dot3(split(bases[k]), masked, ((0,), (0,)))


def local_terms(grad_out, relu_mask, cheb_weight, b0, b1, b2):
    half = jax.ShapeDtypeStruct((NODES_DEV, H), F32)
    return pl.pallas_call(
        local_kernel,
        in_specs=[HBM] * 6,
        out_specs=[VMEM] * 4,
        out_shape=[half, half, jax.ShapeDtypeStruct((NODES_DEV, F), F32), jax.ShapeDtypeStruct((3, F, F), F32)],
        scratch_shapes=[
            pltpu.VMEM((NODES_DEV, F), F32),
            pltpu.VMEM((NODES_DEV, F), jnp.int32),
            pltpu.VMEM((3, F, F), F32),
            pltpu.VMEM((3, NODES_DEV, F), F32),
            pltpu.SemaphoreType.DMA((6,)),
        ],
        compiler_params=params(32),
        cost_estimate=cost(30 * NODES_DEV * F * F, 4 * NODES_DEV * F * 8),
        name="local_terms",
    )(*in_hbm(grad_out, relu_mask, cheb_weight, b0, b1, b2))


def operator_kernel(
    n_row, n_col, resident, ids_ref, live_ref, rows_hbm, slots_hbm, values_ref, out_ref,
    tiles, acc, lists, counts, rows, slots, sems, small_sems,
):
    size = TILES_DEV // GROUPS

    def copy(g):
        part = pl.ds(g * size, size)
        return pltpu.make_async_copy(values_ref.at[0, part], tiles.at[part], sems.at[g])

    def begin():
        small = fetch((rows_hbm, slots_hbm), (rows, slots), small_sems)
        for g in range(GROUPS):
            copy(g).start()
        for s in range(n_col):
            counts[s] = 0
        for item in small:
            item.wait()

        def place(t, carry):
            row = rows[0, t]
            s = lax.rem(row // CHB - ids_ref[0] + n_col, n_col)
            position = slots[0, t] * CHB + lax.rem(row, CHB)
            n = counts[s]
            lists[s, n] = position * TILES_DEV + t
            counts[s] = n + 1
            return carry

        lax.fori_loop(0, live_ref[0], place, 0)
        for g in range(GROUPS):
            copy(g).wait()

    def one(origin, to):
        acc[...] = jnp.zeros_like(acc)

        def add(n, carry):
            entry = lists[origin, n]
            position = entry // TILES_DEV
            acc[position] += tiles[lax.rem(entry, TILES_DEV)]
            return carry

        lax.fori_loop(0, counts[origin], add, 0)

        def store(slot, carry):
            here = pl.ds(pl.multiple_of(slot * TB, TB), TB)
            for i in range(CHB):
                high, low = split(acc[slot * CHB + i].T)
                out_ref[to, here, i * TB : (i + 1) * TB] = high
                out_ref[to, here, NODES_DEV + i * TB : NODES_DEV + (i + 1) * TB] = low
            return carry

        lax.fori_loop(0, n_row, store, 0)

    if resident:
        begin()

        def each(origin, carry):
            one(origin, origin)
            return carry

        lax.fori_loop(0, n_col, each, 0)
    else:
        pl.when(pl.program_id(0) == 0)(begin)
        one(pl.program_id(0), 0)


def fits(n_row, n_col):
    return 4 * n_col * n_row * TB * NODES_DEV <= RESIDENT_BYTES


def build_operator(n_row, n_col, ids, live, rows, slots, values):
    wide = (n_row * TB, 2 * NODES_DEV)
    resident = fits(n_row, n_col)
    grid = {} if resident else {"grid": (n_col,)}
    return pl.pallas_call(
        functools.partial(operator_kernel, n_row, n_col, resident),
        in_specs=[SMEM] * 2 + [HBM] * 3,
        out_specs=VMEM if resident else pl.BlockSpec((1,) + wide, lambda s: (s, 0, 0)),
        out_shape=(pltpu.VMEM if resident else jax.ShapeDtypeStruct)((n_col,) + wide, BF16),
        scratch_shapes=[
            pltpu.VMEM((TILES_DEV, TB, TB), F32),
            pltpu.VMEM((n_row * CHB, TB, TB), F32),
            pltpu.SMEM((n_col, TILES_DEV), jnp.int32),
            pltpu.SMEM((n_col,), jnp.int32),
            pltpu.SMEM((1, TILES_DEV), jnp.int32),
            pltpu.SMEM((1, TILES_DEV), jnp.int32),
            pltpu.SemaphoreType.DMA((GROUPS,)),
            pltpu.SemaphoreType.DMA((2,)),
        ],
        compiler_params=params(40),
        cost_estimate=cost(0, 4 * TILES_DEV * TB * TB * 5),
        name="operator",
        **grid,
    )(ids, live, *in_hbm(rows, slots, values))


def product_kernel(n_row, origins, has_prev, resident, *refs):
    n = len(origins)
    op_ref, fields = refs[0], refs[1 : 1 + n]
    prev = refs[1 + n] if has_prev else None
    out_ref = refs[1 + n + has_prev]
    pairs = n_row // 2
    wide = 2 * TB
    if not resident:
        buf, sems = refs[-2:]

        def copy(k, p):
            source = op_ref.at[origins[k], pl.ds(p * wide, wide)]
            return pltpu.make_async_copy(source, buf.at[k, pl.ds(p * wide, wide)], sems.at[k, p])

        for p in range(pairs):
            for k in range(n):
                copy(k, p).start()
    right = []
    for field in fields:
        high, low = split(field[...])
        both = jnp.concatenate([high, low], axis=1)
        right.append(jnp.concatenate([both, both], axis=0))
    for p in range(pairs):
        here = slice(p * wide, (p + 1) * wide)
        total = None
        for k in range(n):
            if resident:
                left = op_ref[origins[k], here, :]
            else:
                copy(k, p).wait()
                left = buf[k, here, :]
            part = jnp.dot(left, right[k], preferred_element_type=F32)
            total = part if total is None else total + part
        summed = total[:, :H] + total[:, H:]
        out_ref[here, :] = summed + prev[here, :] if has_prev else summed


def product(n_row, n_col, origins, operator, fields, prev):
    rows = n_row * TB
    n = len(origins)
    has_prev = prev is not None
    resident = fits(n_row, n_col)
    scratch = [
        pltpu.VMEM((n, rows, 2 * NODES_DEV), BF16),
        pltpu.SemaphoreType.DMA((n, n_row // 2)),
    ]
    return pl.pallas_call(
        functools.partial(product_kernel, n_row, origins, has_prev, resident),
        in_specs=[VMEM if resident else HBM] + [VMEM] * (n + has_prev),
        out_specs=VMEM,
        out_shape=jax.ShapeDtypeStruct((rows, H), F32),
        scratch_shapes=[] if resident else scratch,
        compiler_params=params(24 if resident else 40),
        cost_estimate=cost(
            2 * n * rows * 2 * NODES_DEV * F, n * rows * NODES_DEV * 4 + 4 * n * NODES_DEV * H + 8 * rows * H
        ),
        name="product",
    )(
        pltpu.with_memory_space_constraint(operator, pltpu.VMEM) if resident else operator,
        *fields,
        *((prev,) if has_prev else ()),
    )


def collect_kernel(n_row, scale, owners_ref, base_ref, *refs):
    out_ref = refs[-1]
    out_ref[...] = base_ref[...]
    for h, came in enumerate(refs[:-1]):
        for q in range(n_row):
            here = pl.ds(pl.multiple_of(owners_ref[q] * TB, TB), TB)
            out_ref[here, h * H : (h + 1) * H] += came[q] if scale == 1.0 else scale * came[q]


def collect(n_row, scale, owners, base, received):
    return pl.pallas_call(
        functools.partial(collect_kernel, n_row, scale),
        in_specs=[SMEM] + [VMEM] * (1 + len(received)),
        out_specs=VMEM,
        out_shape=jax.ShapeDtypeStruct(base.shape, F32),
        compiler_params=params(24),
        cost_estimate=cost(0, 4 * (2 * base.size + len(received) * n_row * TB * H)),
        name="collect",
    )(owners, base, *received)


def shift(n_col, x, step):
    return lax.ppermute(x, "col", [(c, (c + step) % n_col) for c in range(n_col)])


def exchange(pieces):
    return lax.all_to_all(pieces, "row", split_axis=0, concat_axis=0, tiled=True)


def after(x, *others):
    return lax.optimization_barrier((x, *others))[0]


def gather(n_col, field, side):
    long = n_col // 2
    short = n_col - 1 - long
    ahead, behind = field, field
    steps = []
    for s in range(1, long + 1):
        ahead = shift(n_col, ahead, side)
        step = [((-side * s) % n_col, ahead)]
        if s <= short:
            behind = shift(n_col, behind, -side)
            step.append(((side * s) % n_col, behind))
        steps.append(step)
    return steps


def transposed(n_row, n_col, operator, field, steps):
    total = product(n_row, n_col, (0,), operator, [field], None)
    for step in steps:
        total = product(n_row, n_col, tuple(o for o, _ in step), operator, [x for _, x in step], total)
    return exchange(total.reshape(n_row, TB, H))


def per_device(
    grad_out,
    relu_mask,
    basis_zero,
    basis_one,
    basis_two,
    cheb_weight,
    tile_values,
    tile_rows,
    tile_slots,
    send_blocks,
    live_tiles,
):
    n_row = lax.axis_size("row")
    n_col = lax.axis_size("col")
    ids = lax.axis_index("col").astype(jnp.int32).reshape(1)
    owners = send_blocks.reshape(n_row)
    left, right = term_two(grad_out, relu_mask, cheb_weight)
    left_steps = gather(n_col, left, 1)
    one_left, one_right, diff, local = local_terms(
        grad_out, relu_mask, cheb_weight, basis_zero, basis_one, basis_two
    )
    pieces = exchange(local.reshape(n_row, 3 * F // n_row, F))
    ids = after(ids, local)
    operator = build_operator(n_row, n_col, ids, live_tiles, tile_rows, tile_slots, tile_values)
    right_steps = gather(n_col, after(right, left_steps[0][0][1]), -1)
    left_first = transposed(n_row, n_col, operator, after(left, pieces), left_steps)
    shares = lax.all_gather(jnp.sum(pieces, axis=0), "col", axis=0)

    left_carried = collect(n_row, 2.0, owners, one_left, [left_first])
    left_steps = gather(n_col, left_carried, 1)
    right_first = transposed(n_row, n_col, operator, right, right_steps)
    right_carried = collect(n_row, 2.0, owners, one_right, [after(right_first, shares)])
    weight_grad = lax.all_gather(jnp.sum(shares, axis=0), "row", axis=0, tiled=True)
    right_steps = gather(n_col, right_carried, -1)
    left_second = transposed(n_row, n_col, operator, left_carried, left_steps)
    right_second = transposed(n_row, n_col, operator, right_carried, right_steps)
    grad_features = collect(n_row, 1.0, owners, diff, [left_second, right_second])
    return grad_features, weight_grad.reshape(3, F, F)


def solution(mesh):
    placed = (
        P(("row", "col"), None),
        P(("row", "col"), None),
        P(("row", "col"), None),
        P(("row", "col"), None),
        P(("row", "col"), None),
        P(),
        P(("row", "col"), None, None, None),
        P(("row", "col"), None),
        P(("row", "col"), None),
        P(("row", "col"), None, None),
        P(("row", "col")),
    )
    return jax.shard_map(
        per_device,
        mesh=mesh,
        in_specs=placed,
        out_specs=(P(("row", "col"), None), P()),
        check_vma=False,
    )
```

```python
import functools

import jax
import jax.numpy as jnp
from jax import lax
from jax.experimental import pallas as pl
from jax.experimental.pallas import tpu as pltpu
from jax.sharding import PartitionSpec as P

F = 256
H = 128
TB = 128
CHB = 4
NODES_DEV = CHB * TB
TILES_DEV = 128
GROUPS = 8
MIB = 1 << 20
LIGHT = pl.CostEstimate(flops=1024, bytes_accessed=1024, transcendentals=0)
BF16 = jnp.bfloat16
F32 = jnp.float32

SMEM = pl.BlockSpec(memory_space=pltpu.SMEM)
VMEM = pl.BlockSpec(memory_space=pltpu.VMEM)
HBM = pl.BlockSpec(memory_space=pltpu.HBM)


def params(mib):
    return pltpu.CompilerParams(vmem_limit_bytes=mib * MIB)


def in_hbm(*arrays):
    return [pltpu.with_memory_space_constraint(x, pltpu.HBM) for x in arrays]


def split(x):
    high = x.astype(BF16)
    low = (x - high.astype(F32)).astype(BF16)
    return high, low


def dot3(a, b, dims):
    ah, al = a
    bh, bl = b

    def one(x, y):
        return lax.dot_general(x, y, (dims, ((), ())), preferred_element_type=F32)

    return one(ah, bh) + (one(ah, bl) + one(al, bh))


def fetch(sources, targets, sems):
    copies = [pltpu.make_async_copy(a, b, sems.at[i]) for i, (a, b) in enumerate(zip(sources, targets))]
    for copy in copies:
        copy.start()
    return copies


def masked_of(grad, mask):
    return jnp.where(mask > 0, grad, jnp.zeros_like(grad))


def term_two_kernel(grad_hbm, mask_hbm, weight_hbm, left_ref, right_ref, grad, mask, weight, sems):
    for copy in fetch((grad_hbm, mask_hbm, weight_hbm.at[2]), (grad, mask, weight), sems):
        copy.wait()
    term = dot3(split(masked_of(grad[...], mask[...])), split(weight[...]), ((1,), (1,)))
    left_ref[...] = term[:, :H]
    right_ref[...] = term[:, H:]


def term_two(grad_out, relu_mask, cheb_weight):
    out = jax.ShapeDtypeStruct((NODES_DEV, H), F32)
    return pl.pallas_call(
        term_two_kernel,
        in_specs=[HBM] * 3,
        out_specs=[VMEM, VMEM],
        out_shape=[out, out],
        scratch_shapes=[
            pltpu.VMEM((NODES_DEV, F), F32),
            pltpu.VMEM((NODES_DEV, F), jnp.int32),
            pltpu.VMEM((F, F), F32),
            pltpu.SemaphoreType.DMA((3,)),
        ],
        compiler_params=params(16),
        cost_estimate=LIGHT,
        name="term_two",
    )(*in_hbm(grad_out, relu_mask, cheb_weight))


def local_kernel(
    first_ref, grad_hbm, mask_hbm, weight_hbm, h0, h1, h2, left_ref, right_ref, diff_ref, total_ref, grad, mask, weight, bases, sems
):
    sources = (grad_hbm, mask_hbm, weight_hbm, h0, h1, h2)
    copies = fetch(sources, (grad, mask, weight, bases.at[0], bases.at[1], bases.at[2]), sems)
    for copy in copies[:3]:
        copy.wait()
    masked = split(masked_of(grad[...], mask[...]))
    term = dot3(masked, split(weight[1]), ((1,), (1,)))
    left_ref[...] = term[:, :H]
    right_ref[...] = term[:, H:]
    diff_ref[...] = dot3(masked, split(weight[0] - weight[2]), ((1,), (1,)))
    for k in range(3):
        copies[3 + k].wait()
        total_ref[k] = dot3(split(bases[k]), masked, ((0,), (0,)))


def local_terms(first, grad_out, relu_mask, cheb_weight, b0, b1, b2):
    half = jax.ShapeDtypeStruct((NODES_DEV, H), F32)
    return pl.pallas_call(
        local_kernel,
        in_specs=[pl.BlockSpec(memory_space=pl.ANY)] + [HBM] * 6,
        out_specs=[VMEM] * 4,
        out_shape=[half, half, jax.ShapeDtypeStruct((NODES_DEV, F), F32), jax.ShapeDtypeStruct((3, F, F), F32)],
        scratch_shapes=[
            pltpu.VMEM((NODES_DEV, F), F32),
            pltpu.VMEM((NODES_DEV, F), jnp.int32),
            pltpu.VMEM((3, F, F), F32),
            pltpu.VMEM((3, NODES_DEV, F), F32),
            pltpu.SemaphoreType.DMA((6,)),
        ],
        compiler_params=params(32),
        cost_estimate=LIGHT,
        name="local_terms",
    )(first, *in_hbm(grad_out, relu_mask, cheb_weight, b0, b1, b2))


def operator_kernel(
    n_row, n_col, ids_ref, live_ref, rows_hbm, slots_hbm, values_ref, out_ref,
    tiles, acc, lists, counts, rows, slots, sems, small_sems,
):
    origin = pl.program_id(0)
    size = TILES_DEV // GROUPS

    def copy(g):
        part = pl.ds(g * size, size)
        return pltpu.make_async_copy(values_ref.at[0, part], tiles.at[part], sems.at[g])

    @pl.when(origin == 0)
    def _():
        small = fetch((rows_hbm, slots_hbm), (rows, slots), small_sems)
        for g in range(GROUPS):
            copy(g).start()
        for s in range(n_col):
            counts[s] = 0
        for item in small:
            item.wait()

        def place(t, carry):
            row = rows[0, t]
            s = lax.rem(row // CHB - ids_ref[0] + n_col, n_col)
            position = slots[0, t] * CHB + lax.rem(row, CHB)
            n = counts[s]
            lists[s, n] = position * TILES_DEV + t
            counts[s] = n + 1
            return carry

        lax.fori_loop(0, live_ref[0], place, 0)
        for g in range(GROUPS):
            copy(g).wait()

    acc[...] = jnp.zeros_like(acc)

    def add(n, carry):
        entry = lists[origin, n]
        acc[entry // TILES_DEV] += tiles[lax.rem(entry, TILES_DEV)]
        return carry

    lax.fori_loop(0, counts[origin], add, 0)

    def store(slot, carry):
        here = pl.ds(pl.multiple_of(slot * TB, TB), TB)
        for i in range(CHB):
            high, low = split(acc[slot * CHB + i].T)
            out_ref[0, here, i * TB : (i + 1) * TB] = high
            out_ref[0, here, NODES_DEV + i * TB : NODES_DEV + (i + 1) * TB] = low
        return carry

    lax.fori_loop(0, n_row, store, 0)


def build_operator(n_row, n_col, ids, live, rows, slots, values):
    wide = (n_row * TB, 2 * NODES_DEV)
    return pl.pallas_call(
        functools.partial(operator_kernel, n_row, n_col),
        grid=(n_col,),
        in_specs=[SMEM] * 2 + [HBM] * 3,
        out_specs=pl.BlockSpec((1,) + wide, lambda s: (s, 0, 0)),
        out_shape=pltpu.HBM((n_col,) + wide, BF16),
        scratch_shapes=[
            pltpu.VMEM((TILES_DEV, TB, TB), F32),
            pltpu.VMEM((n_row * CHB, TB, TB), F32),
            pltpu.SMEM((n_col, TILES_DEV), jnp.int32),
            pltpu.SMEM((n_col,), jnp.int32),
            pltpu.SMEM((1, TILES_DEV), jnp.int32),
            pltpu.SMEM((1, TILES_DEV), jnp.int32),
            pltpu.SemaphoreType.DMA((GROUPS,)),
            pltpu.SemaphoreType.DMA((2,)),
        ],
        compiler_params=params(40),
        cost_estimate=LIGHT,
        name="operator",
    )(ids, live, *in_hbm(rows, slots, values))


def product_kernel(n_row, n_col, origins, has_prev, extra, *refs):
    n = len(origins)
    ids_ref, op_ref, refs = refs[0], refs[1], refs[2:]
    fields, refs = refs[:n], refs[n:]
    if has_prev:
        prev, refs = refs[0], refs[1:]
    if extra:
        carriers, refs = refs[:n_col], refs[n_col:]
        out_ref, buf, sems, ordered = refs
    else:
        out_ref, buf, sems = refs
    pairs = n_row // 2
    wide = 2 * TB

    def copy(k, p):
        source = op_ref.at[origins[k], pl.ds(p * wide, wide)]
        return pltpu.make_async_copy(source, buf.at[k, pl.ds(p * wide, wide)], sems.at[k, p])

    for p in range(pairs):
        for k in range(n):
            copy(k, p).start()
    right = []
    for field in fields:
        high, low = split(field[:NODES_DEV, :])
        both = jnp.concatenate([high, low], axis=1)
        right.append(jnp.concatenate([both, both], axis=0))
    if extra:
        for k in range(n_col):
            ordered[lax.rem(ids_ref[0] + k, n_col)] = carriers[k][NODES_DEV:, :]
        share = ordered[0]
        for k in range(1, n_col):
            share = share + ordered[k]
        for q in range(n_row):
            out_ref[q, TB:, :] = share
    for p in range(pairs):
        here = slice(p * wide, (p + 1) * wide)
        total = None
        for k in range(n):
            copy(k, p).wait()
            part = jnp.dot(buf[k, here, :], right[k], preferred_element_type=F32)
            total = part if total is None else total + part
        summed = total[:, :H] + total[:, H:]
        if has_prev:
            summed = summed + prev[here, :]
        if extra:
            out_ref[2 * p, :TB, :] = summed[:TB]
            out_ref[2 * p + 1, :TB, :] = summed[TB:]
        else:
            out_ref[here, :] = summed


def product(n_row, n_col, ids, origins, operator, fields, prev, carriers=()):
    rows = n_row * TB
    n = len(origins)
    has_prev = prev is not None
    extra = carriers[0].shape[0] - NODES_DEV if carriers else 0
    shape = (n_row, TB + extra, H) if extra else (rows, H)
    scratch = [
        pltpu.VMEM((n, rows, 2 * NODES_DEV), BF16),
        pltpu.SemaphoreType.DMA((n, n_row // 2)),
    ]
    if extra:
        scratch.append(pltpu.VMEM((n_col, extra, H), F32))
    return pl.pallas_call(
        functools.partial(product_kernel, n_row, n_col, origins, has_prev, extra),
        in_specs=[SMEM, HBM] + [VMEM] * (n + has_prev + len(carriers)),
        out_specs=VMEM,
        out_shape=jax.ShapeDtypeStruct(shape, F32),
        scratch_shapes=scratch,
        compiler_params=params(40),
        cost_estimate=LIGHT,
        name="product",
    )(ids, *in_hbm(operator), *fields, *((prev,) if has_prev else ()), *carriers)


def collect_kernel(n_row, scale, halves, owners_ref, base_ref, *refs):
    came, refs = refs[:halves], refs[halves:]
    out_ref = refs[-1]
    out_ref[:NODES_DEV, :] = base_ref[...]
    for h in range(halves):
        for q in range(n_row):
            here = pl.ds(pl.multiple_of(owners_ref[q] * TB, TB), TB)
            block = came[h][q, :TB, :]
            out_ref[here, h * H : (h + 1) * H] += block if scale == 1.0 else scale * block
    if len(refs) > 1:
        half = refs[0].shape[0]
        out_ref[NODES_DEV : NODES_DEV + half, :] = refs[0][:, :H]
        out_ref[NODES_DEV + half :, :] = refs[0][:, H:]


def collect(n_row, scale, owners, base, received, share=None):
    shares = () if share is None else (share,)
    under = 2 * share.shape[0] if shares else 0
    return pl.pallas_call(
        functools.partial(collect_kernel, n_row, scale, len(received)),
        in_specs=[SMEM] + [VMEM] * (1 + len(received) + len(shares)),
        out_specs=VMEM,
        out_shape=jax.ShapeDtypeStruct((NODES_DEV + under, base.shape[1]), F32),
        compiler_params=params(24),
        cost_estimate=LIGHT,
        name="collect",
    )(owners, base, *received, *shares)


def assemble_kernel(n_row, came_ref, out_ref):
    rows = 3 * F // n_row
    for q in range(n_row):
        out_ref[q * rows : (q + 1) * rows, :H] = came_ref[q, TB : TB + rows, :]
        out_ref[q * rows : (q + 1) * rows, H:] = came_ref[q, TB + rows :, :]


def assemble(n_row, came):
    return pl.pallas_call(
        functools.partial(assemble_kernel, n_row),
        in_specs=[VMEM],
        out_specs=VMEM,
        out_shape=jax.ShapeDtypeStruct((3 * F, F), F32),
        compiler_params=params(16),
        cost_estimate=LIGHT,
        name="assemble",
    )(came).reshape(3, F, F)


def shift(n_col, x, step):
    return lax.ppermute(x, "col", [(c, (c + step) % n_col) for c in range(n_col)])


def exchange(pieces):
    return lax.all_to_all(pieces, "row", split_axis=0, concat_axis=0, tiled=True)


def after(x, *others):
    return lax.optimization_barrier((x, *others))[0]


def gather(n_col, field, side):
    long = n_col // 2
    short = n_col - 1 - long
    ahead, behind = field, field
    steps = []
    for s in range(1, long + 1):
        ahead = shift(n_col, ahead, side)
        step = [((-side * s) % n_col, ahead)]
        if s <= short:
            behind = shift(n_col, behind, -side)
            step.append(((side * s) % n_col, behind))
        steps.append(step)
    return steps


def transposed(n_row, n_col, ids, operator, field, steps, carrying=False):
    total = product(n_row, n_col, ids, (0,), operator, [field], None)
    carriers = [None] * n_col
    carriers[0] = field
    for step in steps:
        for origin, x in step:
            carriers[origin] = x
        last = carrying and step is steps[-1]
        origins, fields = zip(*step)
        total = product(n_row, n_col, ids, origins, operator, fields, total, carriers if last else ())
    return exchange(total.reshape(n_row, -1, H))


def per_device(
    grad_out,
    relu_mask,
    basis_zero,
    basis_one,
    basis_two,
    cheb_weight,
    tile_values,
    tile_rows,
    tile_slots,
    send_blocks,
    live_tiles,
):
    n_row = lax.axis_size("row")
    n_col = lax.axis_size("col")
    ids = lax.axis_index("col").astype(jnp.int32).reshape(1)
    owners = send_blocks.reshape(n_row)
    left, right = term_two(grad_out, relu_mask, cheb_weight)
    left_steps = gather(n_col, left, 1)
    one_left, one_right, diff, local = local_terms(
        left, grad_out, relu_mask, cheb_weight, basis_zero, basis_one, basis_two
    )
    pieces = exchange(local.reshape(n_row, 3 * F // n_row, F))
    operator = build_operator(n_row, n_col, after(ids, local), live_tiles, tile_rows, tile_slots, tile_values)
    right_steps = gather(n_col, after(right, left_steps[0][0][1]), -1)
    left_first = transposed(n_row, n_col, ids, operator, left, left_steps)
    share = jnp.sum(pieces, axis=0)

    left_carried = collect(n_row, 2.0, owners, one_left, [left_first], share)
    left_steps = gather(n_col, left_carried, 1)
    right_first = transposed(n_row, n_col, ids, operator, right, right_steps)
    right_carried = collect(n_row, 2.0, owners, one_right, [right_first])
    right_steps = gather(n_col, right_carried, -1)
    left_second = transposed(n_row, n_col, ids, operator, left_carried, left_steps, True)
    weight_grad = assemble(n_row, left_second)
    right_second = transposed(n_row, n_col, ids, operator, right_carried, right_steps)
    grad_features = collect(n_row, 1.0, owners, diff, [left_second, right_second])
    return grad_features, weight_grad


def solution(mesh):
    placed = (
        P(("row", "col"), None),
        P(("row", "col"), None),
        P(("row", "col"), None),
        P(("row", "col"), None),
        P(("row", "col"), None),
        P(),
        P(("row", "col"), None, None, None),
        P(("row", "col"), None),
        P(("row", "col"), None),
        P(("row", "col"), None, None),
        P(("row", "col")),
    )
    return jax.shard_map(
        per_device,
        mesh=mesh,
        in_specs=placed,
        out_specs=(P(("row", "col"), None), P()),
        check_vma=False,
    )
```

```python
import functools

import jax
import jax.numpy as jnp
from jax import lax
from jax.experimental import pallas as pl
from jax.experimental.pallas import tpu as pltpu
from jax.sharding import PartitionSpec as P

F = 256
H = 128
TB = 128
CHB = 4
WIDE = 2 * TB
LANES = 128
NODES_DEV = CHB * TB
TILES_DEV = 128
GROUPS = 8
MIB = 1 << 20
LIGHT = pl.CostEstimate(flops=1024, bytes_accessed=1024, transcendentals=0)
BF16 = jnp.bfloat16
F32 = jnp.float32

SMEM = pl.BlockSpec(memory_space=pltpu.SMEM)
VMEM = pl.BlockSpec(memory_space=pltpu.VMEM)
HBM = pl.BlockSpec(memory_space=pltpu.HBM)


def params(mib):
    return pltpu.CompilerParams(vmem_limit_bytes=mib * MIB)


def in_hbm(*arrays):
    return [pltpu.with_memory_space_constraint(x, pltpu.HBM) for x in arrays]


def split(x):
    high = x.astype(BF16)
    low = (x - high.astype(F32)).astype(BF16)
    return high, low


def dot3(a, b, dims):
    ah, al = a
    bh, bl = b

    def one(x, y):
        return lax.dot_general(x, y, (dims, ((), ())), preferred_element_type=F32)

    return one(ah, bh) + (one(ah, bl) + one(al, bh))


def fetch(sources, targets, sems):
    copies = [pltpu.make_async_copy(a, b, sems.at[i]) for i, (a, b) in enumerate(zip(sources, targets))]
    for copy in copies:
        copy.start()
    return copies


def masked_of(grad, mask):
    return jnp.where(mask > 0, grad, jnp.zeros_like(grad))


def term_two_kernel(grad_hbm, mask_hbm, weight_hbm, left_ref, right_ref, grad, mask, weight, sems):
    for copy in fetch((grad_hbm, mask_hbm, weight_hbm.at[2]), (grad, mask, weight), sems):
        copy.wait()
    term = dot3(split(weight[...]), split(masked_of(grad[...], mask[...])), ((1,), (1,)))
    left_ref[...] = term[:H]
    right_ref[...] = term[H:]


def term_two(grad_out, relu_mask, cheb_weight):
    out = jax.ShapeDtypeStruct((H, NODES_DEV), F32)
    return pl.pallas_call(
        term_two_kernel,
        in_specs=[HBM] * 3,
        out_specs=[VMEM, VMEM],
        out_shape=[out, out],
        scratch_shapes=[
            pltpu.VMEM((NODES_DEV, F), F32),
            pltpu.VMEM((NODES_DEV, F), jnp.int32),
            pltpu.VMEM((F, F), F32),
            pltpu.SemaphoreType.DMA((3,)),
        ],
        compiler_params=params(16),
        cost_estimate=LIGHT,
        name="term_two",
    )(*in_hbm(grad_out, relu_mask, cheb_weight))


def local_kernel(
    n_row, first_ref, grad_hbm, mask_hbm, weight_hbm, h0, h1, h2, left_ref, right_ref, diff_ref, pieces_ref,
    grad, mask, weight, bases, sems,
):
    sources = (grad_hbm, mask_hbm, weight_hbm, h0, h1, h2)
    copies = fetch(sources, (grad, mask, weight, bases.at[0], bases.at[1], bases.at[2]), sems)
    for copy in copies[:3]:
        copy.wait()
    values = masked_of(grad[...], mask[...])
    masked = split(values)
    term = dot3(split(weight[1]), masked, ((1,), (1,)))
    left_ref[...] = term[:H]
    right_ref[...] = term[H:]
    diff_ref[...] = dot3(split(weight[0] - weight[2]), masked, ((1,), (1,)))
    turned = split(values.T)
    rows = F // n_row
    for k in range(3):
        copies[3 + k].wait()
        part = dot3(turned, split(bases[k]), ((1,), (0,)))
        for j in range(F // LANES):
            here = (k * (F // LANES) + j) * rows
            for q in range(n_row):
                pieces_ref[q, here : here + rows, :] = part[q * rows : (q + 1) * rows, j * LANES : (j + 1) * LANES]


def local_terms(n_row, first, grad_out, relu_mask, cheb_weight, b0, b1, b2):
    half = jax.ShapeDtypeStruct((H, NODES_DEV), F32)
    share = 3 * F * F // n_row // LANES
    return pl.pallas_call(
        functools.partial(local_kernel, n_row),
        in_specs=[pl.BlockSpec(memory_space=pl.ANY)] + [HBM] * 6,
        out_specs=[VMEM] * 4,
        out_shape=[
            half,
            half,
            jax.ShapeDtypeStruct((F, NODES_DEV), F32),
            jax.ShapeDtypeStruct((n_row, share, LANES), F32),
        ],
        scratch_shapes=[
            pltpu.VMEM((NODES_DEV, F), F32),
            pltpu.VMEM((NODES_DEV, F), jnp.int32),
            pltpu.VMEM((3, F, F), F32),
            pltpu.VMEM((3, NODES_DEV, F), F32),
            pltpu.SemaphoreType.DMA((6,)),
        ],
        compiler_params=params(32),
        cost_estimate=LIGHT,
        name="local_terms",
    )(first, *in_hbm(grad_out, relu_mask, cheb_weight, b0, b1, b2))


def operator_kernel(
    n_col, ids_ref, live_ref, rows_hbm, slots_hbm, values_ref, out_ref,
    tiles, acc, lists, counts, rows, slots, sems, small_sems,
):
    origin = pl.program_id(0)
    size = TILES_DEV // GROUPS

    def copy(g):
        part = pl.ds(g * size, size)
        return pltpu.make_async_copy(values_ref.at[0, part], tiles.at[part], sems.at[g])

    @pl.when(origin == 0)
    def _():
        small = fetch((rows_hbm, slots_hbm), (rows, slots), small_sems)
        for g in range(GROUPS):
            copy(g).start()
        for s in range(n_col):
            counts[s] = 0
        for item in small:
            item.wait()

        def place(t, carry):
            row = rows[0, t]
            s = lax.rem(row // CHB - ids_ref[0] + n_col, n_col)
            position = slots[0, t] * CHB + lax.rem(row, CHB)
            n = counts[s]
            lists[s, n] = position * TILES_DEV + t
            counts[s] = n + 1
            return carry

        lax.fori_loop(0, live_ref[0], place, 0)

    acc[...] = jnp.zeros_like(acc)

    @pl.when(origin == 0)
    def _():
        for g in range(GROUPS):
            copy(g).wait()

    def add(n, carry):
        entry = lists[origin, n]
        position = entry // TILES_DEV
        slot = position // CHB
        at_row = pl.ds(pl.multiple_of(lax.rem(position, CHB) * TB, TB), TB)
        at_lane = pl.ds(pl.multiple_of(lax.rem(slot, 2) * TB, TB), TB)
        acc[slot // 2, at_row, at_lane] += tiles[lax.rem(entry, TILES_DEV)]
        return carry

    lax.fori_loop(0, counts[origin], add, 0)
    for p in range(acc.shape[0]):
        high, low = split(acc[p])
        out_ref[0, p, :NODES_DEV, :] = high
        out_ref[0, p, NODES_DEV:, :] = low


def build_operator(n_row, n_col, ids, live, rows, slots, values):
    part = (n_row // 2, 2 * NODES_DEV, WIDE)
    return pl.pallas_call(
        functools.partial(operator_kernel, n_col),
        grid=(n_col,),
        in_specs=[SMEM] * 2 + [HBM] * 3,
        out_specs=pl.BlockSpec((1,) + part, lambda s: (s, 0, 0, 0)),
        out_shape=pltpu.HBM((n_col,) + part, BF16),
        scratch_shapes=[
            pltpu.VMEM((TILES_DEV, TB, TB), F32),
            pltpu.VMEM((n_row // 2, NODES_DEV, WIDE), F32),
            pltpu.SMEM((n_col, TILES_DEV), jnp.int32),
            pltpu.SMEM((n_col,), jnp.int32),
            pltpu.SMEM((1, TILES_DEV), jnp.int32),
            pltpu.SMEM((1, TILES_DEV), jnp.int32),
            pltpu.SemaphoreType.DMA((GROUPS,)),
            pltpu.SemaphoreType.DMA((2,)),
        ],
        compiler_params=params(40),
        cost_estimate=LIGHT,
        name="operator",
    )(ids, live, *in_hbm(rows, slots, values))


def product_kernel(n_row, n_col, origins, has_prev, last, has_under, n_carriers, *refs):
    n = len(origins)
    ids_ref, op_ref, refs = refs[0], refs[1], refs[2:]
    fields, refs = refs[:n], refs[n:]
    if has_prev:
        prev, refs = refs[0], refs[1:]
    if has_under:
        under, refs = refs[0], refs[1:]
    carriers, refs = refs[:n_carriers], refs[n_carriers:]
    out_ref, buf, sems = refs[:3]

    def copy(k, p):
        return pltpu.make_async_copy(op_ref.at[origins[k], p], buf.at[k, p], sems.at[k, p])

    for p in range(n_row // 2):
        for k in range(n):
            copy(k, p).start()
    left = []
    for field in fields:
        high, low = split(field[:H, :])
        left.append(jnp.concatenate([jnp.concatenate([x, x], axis=1) for x in (high, low)], axis=0))
    if has_under:
        out_ref[:, H:, :] = under[...]
    if n_carriers:
        ordered = refs[3]
        for k in range(n_col):
            ordered[lax.rem(ids_ref[0] + k, n_col)] = carriers[k][H:, :]
        share = ordered[0]
        for k in range(1, n_col):
            share = share + ordered[k]
        rows = share.shape[0]
        for j in range(NODES_DEV // LANES):
            for q in range(n_row):
                out_ref[q, H + j * rows : H + (j + 1) * rows, :] = share[:, j * LANES : (j + 1) * LANES]
    for p in range(n_row // 2):
        here = slice(p * WIDE, (p + 1) * WIDE)
        total = None
        for k in range(n):
            copy(k, p).wait()
            part = jnp.dot(left[k], buf[k, p], preferred_element_type=F32)
            total = part if total is None else total + part
        summed = total[:H] + total[H:]
        if has_prev:
            summed = summed + prev[:, here]
        if last:
            out_ref[2 * p, :H, :] = summed[:, :TB]
            out_ref[2 * p + 1, :H, :] = summed[:, TB:]
        else:
            out_ref[:, here] = summed


def product(n_row, n_col, ids, origins, operator, fields, prev, last, under=None, carriers=()):
    n = len(origins)
    has_prev = prev is not None
    has_under = under is not None
    share = under.shape[1] if has_under else 0
    scratch = [
        pltpu.VMEM((n, n_row // 2, 2 * NODES_DEV, WIDE), BF16),
        pltpu.SemaphoreType.DMA((n, n_row // 2)),
    ]
    if carriers:
        rows = carriers[0].shape[0] - H
        share = rows * NODES_DEV // LANES
        scratch.append(pltpu.VMEM((n_col, rows, NODES_DEV), F32))
    shape = (n_row, H + share, TB) if last else (H, n_row * TB)
    count = n + has_prev + has_under + len(carriers)
    return pl.pallas_call(
        functools.partial(product_kernel, n_row, n_col, origins, has_prev, last, has_under, len(carriers)),
        in_specs=[SMEM, HBM] + [VMEM] * count,
        out_specs=VMEM,
        out_shape=jax.ShapeDtypeStruct(shape, F32),
        scratch_shapes=scratch,
        compiler_params=params(48),
        cost_estimate=LIGHT,
        name="product",
    )(
        ids,
        *in_hbm(operator),
        *fields,
        *((prev,) if has_prev else ()),
        *((under,) if has_under else ()),
        *carriers,
    )


def carry_kernel(n_row, rows, owners_ref, base_ref, came_ref, out_ref):
    out_ref[:H, :] = base_ref[...]
    for q in range(n_row):
        here = pl.ds(pl.multiple_of(owners_ref[q] * TB, TB), TB)
        out_ref[:H, here] += 2.0 * came_ref[q, :H, :]
    if rows:
        share = came_ref[0, H:, :]
        for q in range(1, n_row):
            share = share + came_ref[q, H:, :]
        for j in range(NODES_DEV // LANES):
            out_ref[H:, j * LANES : (j + 1) * LANES] = share[j * rows : (j + 1) * rows, :]


def carry(n_row, owners, base, came):
    rows = (came.shape[1] - H) * LANES // NODES_DEV
    return pl.pallas_call(
        functools.partial(carry_kernel, n_row, rows),
        in_specs=[SMEM, VMEM, VMEM],
        out_specs=VMEM,
        out_shape=jax.ShapeDtypeStruct((H + rows, NODES_DEV), F32),
        compiler_params=params(24),
        cost_estimate=LIGHT,
        name="carry",
    )(owners, base, came)


def finish_kernel(n_row, owners_ref, base_ref, left_ref, right_ref, out_ref, total):
    total[...] = base_ref[...]
    for h, came in enumerate((left_ref, right_ref)):
        for q in range(n_row):
            here = pl.ds(pl.multiple_of(owners_ref[q] * TB, TB), TB)
            total[h * H : (h + 1) * H, here] += came[q, :H, :]
    out_ref[...] = total[...].T


def finish(n_row, owners, base, left, right):
    return pl.pallas_call(
        functools.partial(finish_kernel, n_row),
        in_specs=[SMEM] + [VMEM] * 3,
        out_specs=VMEM,
        out_shape=jax.ShapeDtypeStruct((NODES_DEV, F), F32),
        scratch_shapes=[pltpu.VMEM((F, NODES_DEV), F32)],
        compiler_params=params(24),
        cost_estimate=LIGHT,
        name="finish",
    )(owners, base, left, right)


def assemble_kernel(n_row, came_ref, out_ref, turned):
    rows = F // n_row
    per = F // LANES
    for q in range(n_row):
        for j in range(3 * per):
            here = slice(H + j * rows, H + (j + 1) * rows)
            turned[q * rows : (q + 1) * rows, j * LANES : (j + 1) * LANES] = came_ref[q, here, :]
    for k in range(3):
        out_ref[k] = turned[:, k * F : (k + 1) * F].T


def assemble(n_row, came):
    return pl.pallas_call(
        functools.partial(assemble_kernel, n_row),
        in_specs=[VMEM],
        out_specs=VMEM,
        out_shape=jax.ShapeDtypeStruct((3, F, F), F32),
        scratch_shapes=[pltpu.VMEM((F, 3 * F), F32)],
        compiler_params=params(16),
        cost_estimate=LIGHT,
        name="assemble",
    )(came)


def shift(n_col, x, step):
    return lax.ppermute(x, "col", [(c, (c + step) % n_col) for c in range(n_col)])


def exchange(pieces):
    return lax.all_to_all(pieces, "row", split_axis=0, concat_axis=0, tiled=True)


def after(x, *others):
    return lax.optimization_barrier((x, *others))[0]


def gather(n_col, field, side, *done):
    long = n_col // 2
    short = n_col - 1 - long
    ahead, behind = field, field
    steps = [[(0, field)]]
    for s in range(1, long + 1):
        if s == 2:
            ahead = after(ahead, behind, *done)
        ahead = shift(n_col, ahead, side)
        step = [((-side * s) % n_col, ahead)]
        if s <= short:
            behind = shift(n_col, behind, -side)
            step.append(((side * s) % n_col, behind))
        steps.append(step)
    return steps


def early(n_row, n_col, ids, operator, steps):
    pairs = [pair for step in steps[:-1] for pair in step]
    total = None
    for begin in range(0, len(pairs), 3):
        origins, fields = zip(*pairs[begin : begin + 3])
        total = product(n_row, n_col, ids, origins, operator, fields, total, False)
    return total


def final(n_row, n_col, ids, operator, steps, total, under=None, carrying=False):
    origins, fields = zip(*steps[-1])
    carriers = [x for _, x in sorted((p for step in steps for p in step), key=lambda p: p[0])] if carrying else ()
    return product(n_row, n_col, ids, origins, operator, fields, total, True, under, carriers)


def per_device(
    grad_out,
    relu_mask,
    basis_zero,
    basis_one,
    basis_two,
    cheb_weight,
    tile_values,
    tile_rows,
    tile_slots,
    send_blocks,
    live_tiles,
):
    n_row = lax.axis_size("row")
    n_col = lax.axis_size("col")
    ids = lax.axis_index("col").astype(jnp.int32).reshape(1)
    owners = send_blocks.reshape(n_row)
    left, right = term_two(grad_out, relu_mask, cheb_weight)
    one_left, one_right, diff, pieces = local_terms(
        n_row, left, grad_out, relu_mask, cheb_weight, basis_zero, basis_one, basis_two
    )
    operator = build_operator(n_row, n_col, ids, live_tiles, tile_rows, tile_slots, tile_values)
    common = (n_row, n_col, ids, operator)

    steps = gather(n_col, left, 1, operator, pieces)
    left_early = early(*common, steps)
    right_steps = gather(n_col, after(right, left_early, steps[-1][0][1]), -1)
    left_came = exchange(final(*common, steps, left_early, under=pieces))
    right_early = early(*common, right_steps)

    left_carried = carry(n_row, owners, after(one_left, right_early, right_steps[-1][0][1]), left_came)
    steps = gather(n_col, left_carried, 1)
    right_came = exchange(final(*common, right_steps, right_early))
    left_early = early(*common, steps)

    right_carried = carry(n_row, owners, after(one_right, left_early, steps[-1][0][1]), right_came)
    right_steps = gather(n_col, right_carried, -1)
    left_came = exchange(final(*common, steps, left_early, carrying=True))
    right_early = early(*common, right_steps)

    right_came = exchange(final(*common, right_steps, right_early))
    weight_grad = assemble(n_row, left_came)
    return finish(n_row, owners, diff, left_came, right_came), weight_grad


def solution(mesh):
    placed = (
        P(("row", "col"), None),
        P(("row", "col"), None),
        P(("row", "col"), None),
        P(("row", "col"), None),
        P(("row", "col"), None),
        P(),
        P(("row", "col"), None, None, None),
        P(("row", "col"), None),
        P(("row", "col"), None),
        P(("row", "col"), None, None),
        P(("row", "col")),
    )
    return jax.shard_map(
        per_device,
        mesh=mesh,
        in_specs=placed,
        out_specs=(P(("row", "col"), None), P()),
        check_vma=False,
    )
```

```python
import functools

import jax
import jax.numpy as jnp
from jax import lax
from jax.experimental import pallas as pl
from jax.experimental.pallas import tpu as pltpu
from jax.sharding import PartitionSpec as P

F = 256
H = 128
TB = 128
CHB = 4
WIDE = 2 * TB
LANES = 128
NODES_DEV = CHB * TB
TILES_DEV = 128
GROUPS = 8
MIB = 1 << 20
HEAVY = pl.CostEstimate(flops=1 << 34, bytes_accessed=64 * MIB, transcendentals=0)
LIGHT = pl.CostEstimate(flops=1024, bytes_accessed=1024, transcendentals=0)
BF16 = jnp.bfloat16
F32 = jnp.float32

SMEM = pl.BlockSpec(memory_space=pltpu.SMEM)
VMEM = pl.BlockSpec(memory_space=pltpu.VMEM)
HBM = pl.BlockSpec(memory_space=pltpu.HBM)


def params(mib):
    return pltpu.CompilerParams(vmem_limit_bytes=mib * MIB)


def in_hbm(*arrays):
    return [pltpu.with_memory_space_constraint(x, pltpu.HBM) for x in arrays]


def split(x):
    high = x.astype(BF16)
    low = (x - high.astype(F32)).astype(BF16)
    return high, low


def dot3(a, b, dims):
    ah, al = a
    bh, bl = b

    def one(x, y):
        return lax.dot_general(x, y, (dims, ((), ())), preferred_element_type=F32)

    return one(ah, bh) + (one(ah, bl) + one(al, bh))


def fetch(sources, targets, sems):
    copies = [pltpu.make_async_copy(a, b, sems.at[i]) for i, (a, b) in enumerate(zip(sources, targets))]
    for copy in copies:
        copy.start()
    return copies


def masked_of(grad, mask):
    return jnp.where(mask > 0, grad, jnp.zeros_like(grad))


def term_two_kernel(grad_hbm, mask_hbm, weight_hbm, left_ref, right_ref, grad, mask, weight, sems):
    for copy in fetch((grad_hbm, mask_hbm, weight_hbm.at[2]), (grad, mask, weight), sems):
        copy.wait()
    term = dot3(split(weight[...]), split(masked_of(grad[...], mask[...])), ((1,), (1,)))
    left_ref[...] = term[:H]
    right_ref[...] = term[H:]


def term_two(grad_out, relu_mask, cheb_weight):
    out = jax.ShapeDtypeStruct((H, NODES_DEV), F32)
    return pl.pallas_call(
        term_two_kernel,
        in_specs=[HBM] * 3,
        out_specs=[VMEM, VMEM],
        out_shape=[out, out],
        scratch_shapes=[
            pltpu.VMEM((NODES_DEV, F), F32),
            pltpu.VMEM((NODES_DEV, F), jnp.int32),
            pltpu.VMEM((F, F), F32),
            pltpu.SemaphoreType.DMA((3,)),
        ],
        compiler_params=params(16),
        cost_estimate=LIGHT,
        name="term_two",
    )(*in_hbm(grad_out, relu_mask, cheb_weight))


def local_kernel(
    n_row, first_ref, grad_hbm, mask_hbm, weight_hbm, h0, h1, h2, left_ref, right_ref, diff_ref, pieces_ref,
    grad, mask, weight, bases, sems,
):
    sources = (grad_hbm, mask_hbm, weight_hbm, h0, h1, h2)
    copies = fetch(sources, (grad, mask, weight, bases.at[0], bases.at[1], bases.at[2]), sems)
    for copy in copies[:3]:
        copy.wait()
    values = masked_of(grad[...], mask[...])
    masked = split(values)
    term = dot3(split(weight[1]), masked, ((1,), (1,)))
    left_ref[...] = term[:H]
    right_ref[...] = term[H:]
    diff_ref[...] = dot3(split(weight[0] - weight[2]), masked, ((1,), (1,)))
    turned = split(values.T)
    rows = F // n_row
    for k in range(3):
        copies[3 + k].wait()
        part = dot3(turned, split(bases[k]), ((1,), (0,)))
        for j in range(F // LANES):
            here = (k * (F // LANES) + j) * rows
            for q in range(n_row):
                pieces_ref[q, here : here + rows, :] = part[q * rows : (q + 1) * rows, j * LANES : (j + 1) * LANES]


def local_terms(n_row, first, grad_out, relu_mask, cheb_weight, b0, b1, b2):
    half = jax.ShapeDtypeStruct((H, NODES_DEV), F32)
    share = 3 * F * F // n_row // LANES
    return pl.pallas_call(
        functools.partial(local_kernel, n_row),
        in_specs=[pl.BlockSpec(memory_space=pl.ANY)] + [HBM] * 6,
        out_specs=[VMEM] * 4,
        out_shape=[
            half,
            half,
            jax.ShapeDtypeStruct((F, NODES_DEV), F32),
            jax.ShapeDtypeStruct((n_row, share, LANES), F32),
        ],
        scratch_shapes=[
            pltpu.VMEM((NODES_DEV, F), F32),
            pltpu.VMEM((NODES_DEV, F), jnp.int32),
            pltpu.VMEM((3, F, F), F32),
            pltpu.VMEM((3, NODES_DEV, F), F32),
            pltpu.SemaphoreType.DMA((6,)),
        ],
        compiler_params=params(32),
        cost_estimate=LIGHT,
        name="local_terms",
    )(first, *in_hbm(grad_out, relu_mask, cheb_weight, b0, b1, b2))


def operator_kernel(
    n_col, ids_ref, live_ref, rows_hbm, slots_hbm, values_ref, out_ref,
    tiles, acc, lists, counts, rows, slots, sems, small_sems,
):
    origin = pl.program_id(0)
    size = TILES_DEV // GROUPS

    def copy(g):
        part = pl.ds(g * size, size)
        return pltpu.make_async_copy(values_ref.at[0, part], tiles.at[part], sems.at[g])

    @pl.when(origin == 0)
    def _():
        small = fetch((rows_hbm, slots_hbm), (rows, slots), small_sems)
        for g in range(GROUPS):
            copy(g).start()
        for s in range(n_col):
            counts[s] = 0
        for item in small:
            item.wait()

        def place(t, carry):
            row = rows[0, t]
            s = lax.rem(row // CHB - ids_ref[0] + n_col, n_col)
            position = slots[0, t] * CHB + lax.rem(row, CHB)
            n = counts[s]
            lists[s, n] = position * TILES_DEV + t
            counts[s] = n + 1
            return carry

        lax.fori_loop(0, live_ref[0], place, 0)

    acc[...] = jnp.zeros_like(acc)

    @pl.when(origin == 0)
    def _():
        for g in range(GROUPS):
            copy(g).wait()

    def add(n, carry):
        entry = lists[origin, n]
        position = entry // TILES_DEV
        slot = position // CHB
        at_row = pl.ds(pl.multiple_of(lax.rem(position, CHB) * TB, TB), TB)
        at_lane = pl.ds(pl.multiple_of(lax.rem(slot, 2) * TB, TB), TB)
        acc[slot // 2, at_row, at_lane] += tiles[lax.rem(entry, TILES_DEV)]
        return carry

    lax.fori_loop(0, counts[origin], add, 0)
    for p in range(acc.shape[0]):
        high, low = split(acc[p])
        out_ref[0, p, :NODES_DEV, :] = high
        out_ref[0, p, NODES_DEV:, :] = low


def build_operator(n_row, n_col, ids, live, rows, slots, values):
    part = (n_row // 2, 2 * NODES_DEV, WIDE)
    return pl.pallas_call(
        functools.partial(operator_kernel, n_col),
        grid=(n_col,),
        in_specs=[SMEM] * 2 + [HBM] * 3,
        out_specs=pl.BlockSpec((1,) + part, lambda s: (s, 0, 0, 0)),
        out_shape=pltpu.HBM((n_col,) + part, BF16),
        scratch_shapes=[
            pltpu.VMEM((TILES_DEV, TB, TB), F32),
            pltpu.VMEM((n_row // 2, NODES_DEV, WIDE), F32),
            pltpu.SMEM((n_col, TILES_DEV), jnp.int32),
            pltpu.SMEM((n_col,), jnp.int32),
            pltpu.SMEM((1, TILES_DEV), jnp.int32),
            pltpu.SMEM((1, TILES_DEV), jnp.int32),
            pltpu.SemaphoreType.DMA((GROUPS,)),
            pltpu.SemaphoreType.DMA((2,)),
        ],
        compiler_params=params(40),
        cost_estimate=LIGHT,
        name="operator",
    )(ids, live, *in_hbm(rows, slots, values))


def product_kernel(n_row, n_col, origins, has_prev, last, has_under, n_carriers, *refs):
    n = len(origins)
    ids_ref, op_ref, refs = refs[0], refs[1], refs[2:]
    fields, refs = refs[:n], refs[n:]
    if has_prev:
        prev, refs = refs[0], refs[1:]
    if has_under:
        under, refs = refs[0], refs[1:]
    carriers, refs = refs[:n_carriers], refs[n_carriers:]
    out_ref, buf, sems = refs[:3]

    def copy(k, p):
        return pltpu.make_async_copy(op_ref.at[origins[k], p], buf.at[k, p], sems.at[k, p])

    for p in range(n_row // 2):
        for k in range(n):
            copy(k, p).start()
    left = []
    for field in fields:
        high, low = split(field[:H, :])
        left.append(jnp.concatenate([jnp.concatenate([x, x], axis=1) for x in (high, low)], axis=0))
    if has_under:
        out_ref[:, H:, :] = under[...]
    if n_carriers:
        ordered = refs[3]
        for k in range(n_col):
            ordered[lax.rem(ids_ref[0] + k, n_col)] = carriers[k][H:, :]
        share = ordered[0]
        for k in range(1, n_col):
            share = share + ordered[k]
        rows = share.shape[0]
        for j in range(NODES_DEV // LANES):
            for q in range(n_row):
                out_ref[q, H + j * rows : H + (j + 1) * rows, :] = share[:, j * LANES : (j + 1) * LANES]
    for p in range(n_row // 2):
        here = slice(p * WIDE, (p + 1) * WIDE)
        total = None
        for k in range(n):
            copy(k, p).wait()
            part = jnp.dot(left[k], buf[k, p], preferred_element_type=F32)
            total = part if total is None else total + part
        summed = total[:H] + total[H:]
        if has_prev:
            summed = summed + prev[:, here]
        if last:
            out_ref[2 * p, :H, :] = summed[:, :TB]
            out_ref[2 * p + 1, :H, :] = summed[:, TB:]
        else:
            out_ref[:, here] = summed


def product(n_row, n_col, ids, origins, operator, fields, prev, last, under=None, carriers=()):
    n = len(origins)
    has_prev = prev is not None
    has_under = under is not None
    share = under.shape[1] if has_under else 0
    scratch = [
        pltpu.VMEM((n, n_row // 2, 2 * NODES_DEV, WIDE), BF16),
        pltpu.SemaphoreType.DMA((n, n_row // 2)),
    ]
    if carriers:
        rows = carriers[0].shape[0] - H
        share = rows * NODES_DEV // LANES
        scratch.append(pltpu.VMEM((n_col, rows, NODES_DEV), F32))
    shape = (n_row, H + share, TB) if last else (H, n_row * TB)
    count = n + has_prev + has_under + len(carriers)
    return pl.pallas_call(
        functools.partial(product_kernel, n_row, n_col, origins, has_prev, last, has_under, len(carriers)),
        in_specs=[SMEM, HBM] + [VMEM] * count,
        out_specs=VMEM,
        out_shape=jax.ShapeDtypeStruct(shape, F32),
        scratch_shapes=scratch,
        compiler_params=params(48),
        cost_estimate=LIGHT if last else HEAVY,
        name="product",
    )(
        ids,
        *in_hbm(operator),
        *fields,
        *((prev,) if has_prev else ()),
        *((under,) if has_under else ()),
        *carriers,
    )


def carry_kernel(n_row, rows, owners_ref, base_ref, came_ref, out_ref):
    out_ref[:H, :] = base_ref[...]
    for q in range(n_row):
        here = pl.ds(pl.multiple_of(owners_ref[q] * TB, TB), TB)
        out_ref[:H, here] += 2.0 * came_ref[q, :H, :]
    if rows:
        share = came_ref[0, H:, :]
        for q in range(1, n_row):
            share = share + came_ref[q, H:, :]
        for j in range(NODES_DEV // LANES):
            out_ref[H:, j * LANES : (j + 1) * LANES] = share[j * rows : (j + 1) * rows, :]


def carry(n_row, owners, base, came):
    rows = (came.shape[1] - H) * LANES // NODES_DEV
    return pl.pallas_call(
        functools.partial(carry_kernel, n_row, rows),
        in_specs=[SMEM, VMEM, VMEM],
        out_specs=VMEM,
        out_shape=jax.ShapeDtypeStruct((H + rows, NODES_DEV), F32),
        compiler_params=params(24),
        cost_estimate=LIGHT,
        name="carry",
    )(owners, base, came)


def finish_kernel(n_row, owners_ref, base_ref, left_ref, right_ref, out_ref, total):
    total[...] = base_ref[...]
    for h, came in enumerate((left_ref, right_ref)):
        for q in range(n_row):
            here = pl.ds(pl.multiple_of(owners_ref[q] * TB, TB), TB)
            total[h * H : (h + 1) * H, here] += came[q, :H, :]
    out_ref[...] = total[...].T


def finish(n_row, owners, base, left, right):
    return pl.pallas_call(
        functools.partial(finish_kernel, n_row),
        in_specs=[SMEM] + [VMEM] * 3,
        out_specs=VMEM,
        out_shape=jax.ShapeDtypeStruct((NODES_DEV, F), F32),
        scratch_shapes=[pltpu.VMEM((F, NODES_DEV), F32)],
        compiler_params=params(24),
        cost_estimate=LIGHT,
        name="finish",
    )(owners, base, left, right)


def assemble_kernel(n_row, came_ref, out_ref, turned):
    rows = F // n_row
    per = F // LANES
    for q in range(n_row):
        for j in range(3 * per):
            here = slice(H + j * rows, H + (j + 1) * rows)
            turned[q * rows : (q + 1) * rows, j * LANES : (j + 1) * LANES] = came_ref[q, here, :]
    for k in range(3):
        out_ref[k] = turned[:, k * F : (k + 1) * F].T


def assemble(n_row, came):
    return pl.pallas_call(
        functools.partial(assemble_kernel, n_row),
        in_specs=[VMEM],
        out_specs=VMEM,
        out_shape=jax.ShapeDtypeStruct((3, F, F), F32),
        scratch_shapes=[pltpu.VMEM((F, 3 * F), F32)],
        compiler_params=params(16),
        cost_estimate=LIGHT,
        name="assemble",
    )(came)


def shift(n_col, x, step):
    return lax.ppermute(x, "col", [(c, (c + step) % n_col) for c in range(n_col)])


def exchange(pieces):
    return lax.all_to_all(pieces, "row", split_axis=0, concat_axis=0, tiled=True)


def after(x, *others):
    return lax.optimization_barrier((x, *others))[0]


def gather(n_col, field, side, *done):
    long = n_col // 2
    short = n_col - 1 - long
    ahead, behind = field, field
    steps = [[(0, field)]]
    for s in range(1, long + 1):
        if s == 2:
            ahead = after(ahead, behind, *done)
        ahead = shift(n_col, ahead, side)
        step = [((-side * s) % n_col, ahead)]
        if s <= short:
            behind = shift(n_col, behind, -side)
            step.append(((side * s) % n_col, behind))
        steps.append(step)
    return steps


def early(n_row, n_col, ids, operator, steps):
    pairs = [pair for step in steps[:-1] for pair in step]
    total = None
    for begin in range(0, len(pairs), 3):
        origins, fields = zip(*pairs[begin : begin + 3])
        total = product(n_row, n_col, ids, origins, operator, fields, total, False)
    return total


def final(n_row, n_col, ids, operator, steps, total, under=None, carrying=False):
    origins, fields = zip(*steps[-1])
    carriers = [x for _, x in sorted((p for step in steps for p in step), key=lambda p: p[0])] if carrying else ()
    return product(n_row, n_col, ids, origins, operator, fields, total, True, under, carriers)


def per_device(
    grad_out,
    relu_mask,
    basis_zero,
    basis_one,
    basis_two,
    cheb_weight,
    tile_values,
    tile_rows,
    tile_slots,
    send_blocks,
    live_tiles,
):
    n_row = lax.axis_size("row")
    n_col = lax.axis_size("col")
    ids = lax.axis_index("col").astype(jnp.int32).reshape(1)
    owners = send_blocks.reshape(n_row)
    left, right = term_two(grad_out, relu_mask, cheb_weight)
    one_left, one_right, diff, pieces = local_terms(
        n_row, left, grad_out, relu_mask, cheb_weight, basis_zero, basis_one, basis_two
    )
    operator = build_operator(n_row, n_col, ids, live_tiles, tile_rows, tile_slots, tile_values)
    common = (n_row, n_col, ids, operator)

    steps = gather(n_col, left, 1, operator, pieces)
    left_early = early(*common, steps)
    right_steps = gather(n_col, after(right, left_early, steps[-1][0][1]), -1)
    left_came = exchange(final(*common, steps, left_early, under=pieces))
    right_early = early(*common, right_steps)

    left_carried = carry(n_row, owners, after(one_left, right_early, right_steps[-1][0][1]), left_came)
    steps = gather(n_col, left_carried, 1)
    right_came = exchange(final(*common, right_steps, right_early))
    left_early = early(*common, steps)

    right_carried = carry(n_row, owners, after(one_right, left_early, steps[-1][0][1]), right_came)
    right_steps = gather(n_col, right_carried, -1)
    left_came = exchange(final(*common, steps, left_early, carrying=True))
    right_early = early(*common, right_steps)

    right_came = exchange(final(*common, right_steps, right_early))
    weight_grad = assemble(n_row, left_came)
    return finish(n_row, owners, diff, left_came, right_came), weight_grad


def solution(mesh):
    placed = (
        P(("row", "col"), None),
        P(("row", "col"), None),
        P(("row", "col"), None),
        P(("row", "col"), None),
        P(("row", "col"), None),
        P(),
        P(("row", "col"), None, None, None),
        P(("row", "col"), None),
        P(("row", "col"), None),
        P(("row", "col"), None, None),
        P(("row", "col")),
    )
    return jax.shard_map(
        per_device,
        mesh=mesh,
        in_specs=placed,
        out_specs=(P(("row", "col"), None), P()),
        check_vma=False,
    )
```

```python
import functools

import jax
import jax.numpy as jnp
from jax import lax
from jax.experimental import pallas as pl
from jax.experimental.pallas import tpu as pltpu
from jax.sharding import PartitionSpec as P

F = 256
H = 128
TB = 128
CHB = 4
WIDE = 2 * TB
LANES = 128
NODES_DEV = CHB * TB
TILES_DEV = 128
GROUPS = 8
MIB = 1 << 20
HEAVY = pl.CostEstimate(flops=1 << 34, bytes_accessed=64 * MIB, transcendentals=0)
LIGHT = pl.CostEstimate(flops=1024, bytes_accessed=1024, transcendentals=0)
BF16 = jnp.bfloat16
F32 = jnp.float32

SMEM = pl.BlockSpec(memory_space=pltpu.SMEM)
VMEM = pl.BlockSpec(memory_space=pltpu.VMEM)
HBM = pl.BlockSpec(memory_space=pltpu.HBM)


def params(mib):
    return pltpu.CompilerParams(vmem_limit_bytes=mib * MIB)


def in_hbm(*arrays):
    return [pltpu.with_memory_space_constraint(x, pltpu.HBM) for x in arrays]


def split(x):
    high = x.astype(BF16)
    low = (x - high.astype(F32)).astype(BF16)
    return high, low


def dot3(a, b, dims):
    ah, al = a
    bh, bl = b

    def one(x, y):
        return lax.dot_general(x, y, (dims, ((), ())), preferred_element_type=F32)

    return one(ah, bh) + (one(ah, bl) + one(al, bh))


def fetch(sources, targets, sems):
    copies = [pltpu.make_async_copy(a, b, sems.at[i]) for i, (a, b) in enumerate(zip(sources, targets))]
    for copy in copies:
        copy.start()
    return copies


def masked_of(grad, mask):
    return jnp.where(mask > 0, grad, jnp.zeros_like(grad))


def term_two_kernel(grad_hbm, mask_hbm, weight_hbm, left_ref, right_ref, grad, mask, weight, sems):
    for copy in fetch((grad_hbm, mask_hbm, weight_hbm.at[2]), (grad, mask, weight), sems):
        copy.wait()
    term = dot3(split(weight[...]), split(masked_of(grad[...], mask[...])), ((1,), (1,)))
    left_ref[...] = term[:H]
    right_ref[...] = term[H:]


def term_two(grad_out, relu_mask, cheb_weight):
    out = jax.ShapeDtypeStruct((H, NODES_DEV), F32)
    return pl.pallas_call(
        term_two_kernel,
        in_specs=[HBM] * 3,
        out_specs=[VMEM, VMEM],
        out_shape=[out, out],
        scratch_shapes=[
            pltpu.VMEM((NODES_DEV, F), F32),
            pltpu.VMEM((NODES_DEV, F), jnp.int32),
            pltpu.VMEM((F, F), F32),
            pltpu.SemaphoreType.DMA((3,)),
        ],
        compiler_params=params(16),
        cost_estimate=LIGHT,
        name="term_two",
    )(*in_hbm(grad_out, relu_mask, cheb_weight))


def local_kernel(
    n_row, first_ref, grad_hbm, mask_hbm, weight_hbm, h0, h1, h2, left_ref, right_ref, diff_ref, pieces_ref,
    grad, mask, weight, bases, sems,
):
    sources = (grad_hbm, mask_hbm, weight_hbm, h0, h1, h2)
    copies = fetch(sources, (grad, mask, weight, bases.at[0], bases.at[1], bases.at[2]), sems)
    for copy in copies[:3]:
        copy.wait()
    values = masked_of(grad[...], mask[...])
    masked = split(values)
    term = dot3(split(weight[1]), masked, ((1,), (1,)))
    left_ref[...] = term[:H]
    right_ref[...] = term[H:]
    diff_ref[...] = dot3(split(weight[0] - weight[2]), masked, ((1,), (1,)))
    turned = split(values.T)
    rows = F // n_row
    for k in range(3):
        copies[3 + k].wait()
        part = dot3(turned, split(bases[k]), ((1,), (0,)))
        for j in range(F // LANES):
            here = (k * (F // LANES) + j) * rows
            for q in range(n_row):
                pieces_ref[q, here : here + rows, :] = part[q * rows : (q + 1) * rows, j * LANES : (j + 1) * LANES]


def local_terms(n_row, first, grad_out, relu_mask, cheb_weight, b0, b1, b2):
    half = jax.ShapeDtypeStruct((H, NODES_DEV), F32)
    share = 3 * F * F // n_row // LANES
    return pl.pallas_call(
        functools.partial(local_kernel, n_row),
        in_specs=[pl.BlockSpec(memory_space=pl.ANY)] + [HBM] * 6,
        out_specs=[VMEM] * 4,
        out_shape=[
            half,
            half,
            jax.ShapeDtypeStruct((F, NODES_DEV), F32),
            jax.ShapeDtypeStruct((n_row, share, LANES), F32),
        ],
        scratch_shapes=[
            pltpu.VMEM((NODES_DEV, F), F32),
            pltpu.VMEM((NODES_DEV, F), jnp.int32),
            pltpu.VMEM((3, F, F), F32),
            pltpu.VMEM((3, NODES_DEV, F), F32),
            pltpu.SemaphoreType.DMA((6,)),
        ],
        compiler_params=params(32),
        cost_estimate=LIGHT,
        name="local_terms",
    )(first, *in_hbm(grad_out, relu_mask, cheb_weight, b0, b1, b2))


def operator_kernel(
    n_col, ids_ref, live_ref, rows_hbm, slots_hbm, values_ref, out_ref,
    tiles, acc, lists, counts, rows, slots, sems, small_sems,
):
    origin = pl.program_id(0)
    size = TILES_DEV // GROUPS

    def copy(g):
        part = pl.ds(g * size, size)
        return pltpu.make_async_copy(values_ref.at[0, part], tiles.at[part], sems.at[g])

    @pl.when(origin == 0)
    def _():
        small = fetch((rows_hbm, slots_hbm), (rows, slots), small_sems)
        for g in range(GROUPS):
            copy(g).start()
        for s in range(n_col):
            counts[s] = 0
        for item in small:
            item.wait()

        def place(t, carry):
            row = rows[0, t]
            s = lax.rem(row // CHB - ids_ref[0] + n_col, n_col)
            position = slots[0, t] * CHB + lax.rem(row, CHB)
            n = counts[s]
            lists[s, n] = position * TILES_DEV + t
            counts[s] = n + 1
            return carry

        lax.fori_loop(0, live_ref[0], place, 0)

    acc[...] = jnp.zeros_like(acc)

    @pl.when(origin == 0)
    def _():
        for g in range(GROUPS):
            copy(g).wait()

    def add(n, carry):
        entry = lists[origin, n]
        position = entry // TILES_DEV
        slot = position // CHB
        at_row = pl.ds(pl.multiple_of(lax.rem(position, CHB) * TB, TB), TB)
        at_lane = pl.ds(pl.multiple_of(lax.rem(slot, 2) * TB, TB), TB)
        acc[slot // 2, at_row, at_lane] += tiles[lax.rem(entry, TILES_DEV)]
        return carry

    lax.fori_loop(0, counts[origin], add, 0)
    for p in range(acc.shape[0]):
        high, low = split(acc[p])
        out_ref[0, p, :NODES_DEV, :] = high
        out_ref[0, p, NODES_DEV:, :] = low


def build_operator(n_row, n_col, ids, live, rows, slots, values):
    part = (n_row // 2, 2 * NODES_DEV, WIDE)
    return pl.pallas_call(
        functools.partial(operator_kernel, n_col),
        grid=(n_col,),
        in_specs=[SMEM] * 2 + [HBM] * 3,
        out_specs=pl.BlockSpec((1,) + part, lambda s: (s, 0, 0, 0)),
        out_shape=pltpu.HBM((n_col,) + part, BF16),
        scratch_shapes=[
            pltpu.VMEM((TILES_DEV, TB, TB), F32),
            pltpu.VMEM((n_row // 2, NODES_DEV, WIDE), F32),
            pltpu.SMEM((n_col, TILES_DEV), jnp.int32),
            pltpu.SMEM((n_col,), jnp.int32),
            pltpu.SMEM((1, TILES_DEV), jnp.int32),
            pltpu.SMEM((1, TILES_DEV), jnp.int32),
            pltpu.SemaphoreType.DMA((GROUPS,)),
            pltpu.SemaphoreType.DMA((2,)),
        ],
        compiler_params=params(40),
        cost_estimate=LIGHT,
        name="operator",
    )(ids, live, *in_hbm(rows, slots, values))


def product_kernel(n_row, n_col, origins, has_prev, last, n_carriers, *refs):
    n = len(origins)
    ids_ref, op_ref, refs = refs[0], refs[1], refs[2:]
    fields, refs = refs[:n], refs[n:]
    if has_prev:
        prev, refs = refs[0], refs[1:]
    carriers, refs = refs[:n_carriers], refs[n_carriers:]
    out_ref, buf, sems = refs[:3]

    def copy(k, p):
        return pltpu.make_async_copy(op_ref.at[origins[k], p], buf.at[k, p], sems.at[k, p])

    for p in range(n_row // 2):
        for k in range(n):
            copy(k, p).start()
    left = []
    for field in fields:
        high, low = split(field[:H, :])
        left.append(jnp.concatenate([jnp.concatenate([x, x], axis=1) for x in (high, low)], axis=0))
    if n_carriers:
        ordered = refs[3]
        for k in range(n_col):
            ordered[lax.rem(ids_ref[0] + k, n_col)] = carriers[k][H:, :]
        share = ordered[0]
        for k in range(1, n_col):
            share = share + ordered[k]
        rows = share.shape[0]
        for j in range(NODES_DEV // LANES):
            for q in range(n_row):
                out_ref[q, H + j * rows : H + (j + 1) * rows, :] = share[:, j * LANES : (j + 1) * LANES]
    for p in range(n_row // 2):
        here = slice(p * WIDE, (p + 1) * WIDE)
        total = None
        for k in range(n):
            copy(k, p).wait()
            part = jnp.dot(left[k], buf[k, p], preferred_element_type=F32)
            total = part if total is None else total + part
        summed = total[:H] + total[H:]
        if has_prev:
            summed = summed + prev[:, here]
        if last:
            out_ref[2 * p, :H, :] = summed[:, :TB]
            out_ref[2 * p + 1, :H, :] = summed[:, TB:]
        else:
            out_ref[:, here] = summed


def product(n_row, n_col, ids, origins, operator, fields, prev, last, carriers=()):
    n = len(origins)
    has_prev = prev is not None
    share = 0
    scratch = [
        pltpu.VMEM((n, n_row // 2, 2 * NODES_DEV, WIDE), BF16),
        pltpu.SemaphoreType.DMA((n, n_row // 2)),
    ]
    if carriers:
        rows = carriers[0].shape[0] - H
        share = rows * NODES_DEV // LANES
        scratch.append(pltpu.VMEM((n_col, rows, NODES_DEV), F32))
    shape = (n_row, H + share, TB) if last else (H, n_row * TB)
    count = n + has_prev + len(carriers)
    return pl.pallas_call(
        functools.partial(product_kernel, n_row, n_col, origins, has_prev, last, len(carriers)),
        in_specs=[SMEM, HBM] + [VMEM] * count,
        out_specs=VMEM,
        out_shape=jax.ShapeDtypeStruct(shape, F32),
        scratch_shapes=scratch,
        compiler_params=params(48),
        cost_estimate=LIGHT if last else HEAVY,
        name="product",
    )(
        ids,
        *in_hbm(operator),
        *fields,
        *((prev,) if has_prev else ()),
        *carriers,
    )


def carry_kernel(n_row, rows, owners_ref, base_ref, came_ref, *refs):
    out_ref = refs[-1]
    out_ref[:H, :] = base_ref[...]
    for q in range(n_row):
        here = pl.ds(pl.multiple_of(owners_ref[q] * TB, TB), TB)
        out_ref[:H, here] += 2.0 * came_ref[q]
    if rows:
        pieces_ref = refs[0]
        share = pieces_ref[0]
        for q in range(1, n_row):
            share = share + pieces_ref[q]
        for j in range(NODES_DEV // LANES):
            out_ref[H:, j * LANES : (j + 1) * LANES] = share[j * rows : (j + 1) * rows, :]


def carry(n_row, owners, base, came, *pieces):
    rows = pieces[0].shape[1] * LANES // NODES_DEV if pieces else 0
    return pl.pallas_call(
        functools.partial(carry_kernel, n_row, rows),
        in_specs=[SMEM] + [VMEM] * (2 + len(pieces)),
        out_specs=VMEM,
        out_shape=jax.ShapeDtypeStruct((H + rows, NODES_DEV), F32),
        compiler_params=params(24),
        cost_estimate=LIGHT,
        name="carry",
    )(owners, base, came, *pieces)


def finish_kernel(n_row, owners_ref, base_ref, left_ref, right_ref, out_ref, total):
    total[...] = base_ref[...]
    for h, came in enumerate((left_ref, right_ref)):
        for q in range(n_row):
            here = pl.ds(pl.multiple_of(owners_ref[q] * TB, TB), TB)
            total[h * H : (h + 1) * H, here] += came[q, :H, :]
    out_ref[...] = total[...].T


def finish(n_row, owners, base, left, right):
    return pl.pallas_call(
        functools.partial(finish_kernel, n_row),
        in_specs=[SMEM] + [VMEM] * 3,
        out_specs=VMEM,
        out_shape=jax.ShapeDtypeStruct((NODES_DEV, F), F32),
        scratch_shapes=[pltpu.VMEM((F, NODES_DEV), F32)],
        compiler_params=params(24),
        cost_estimate=LIGHT,
        name="finish",
    )(owners, base, left, right)


def assemble_kernel(n_row, came_ref, out_ref, turned):
    rows = F // n_row
    per = F // LANES
    for q in range(n_row):
        for j in range(3 * per):
            here = slice(H + j * rows, H + (j + 1) * rows)
            turned[q * rows : (q + 1) * rows, j * LANES : (j + 1) * LANES] = came_ref[q, here, :]
    for k in range(3):
        out_ref[k] = turned[:, k * F : (k + 1) * F].T


def assemble(n_row, came):
    return pl.pallas_call(
        functools.partial(assemble_kernel, n_row),
        in_specs=[VMEM],
        out_specs=VMEM,
        out_shape=jax.ShapeDtypeStruct((3, F, F), F32),
        scratch_shapes=[pltpu.VMEM((F, 3 * F), F32)],
        compiler_params=params(16),
        cost_estimate=LIGHT,
        name="assemble",
    )(came)


def shift(n_col, x, step):
    return lax.ppermute(x, "col", [(c, (c + step) % n_col) for c in range(n_col)])


def exchange(pieces):
    return lax.all_to_all(pieces, "row", split_axis=0, concat_axis=0, tiled=True)


def after(x, *others):
    return lax.optimization_barrier((x, *others))[0]


def opposite(field, below, above):
    col = lax.axis_index("col")
    sent = jnp.where(col == 1, above, jnp.where(col == 2, below, field))
    return lax.ppermute(sent, "col", [(1, 0), (2, 3), (3, 1), (0, 2)])


def gather(n_col, field, side, *done):
    long = n_col // 2
    short = n_col - 1 - long
    ahead, behind = field, field
    steps = [[(0, field)]]
    for s in range(1, long + 1):
        if s == 2:
            ahead = after(ahead, behind, *done)
        if s == 2 and n_col == 4:
            ahead = opposite(field, ahead, behind) if side > 0 else opposite(field, behind, ahead)
        else:
            ahead = shift(n_col, ahead, side)
        step = [((-side * s) % n_col, ahead)]
        if s <= short:
            behind = shift(n_col, behind, -side)
            step.append(((side * s) % n_col, behind))
        steps.append(step)
    return steps


def early(n_row, n_col, ids, operator, steps):
    pairs = [pair for step in steps[:-1] for pair in step]
    total = None
    for begin in range(0, len(pairs), 3):
        origins, fields = zip(*pairs[begin : begin + 3])
        total = product(n_row, n_col, ids, origins, operator, fields, total, False)
    return total


def final(n_row, n_col, ids, operator, steps, total, carrying=False):
    origins, fields = zip(*steps[-1])
    carriers = [x for _, x in sorted((p for step in steps for p in step), key=lambda p: p[0])] if carrying else ()
    return product(n_row, n_col, ids, origins, operator, fields, total, True, carriers)


def per_device(
    grad_out,
    relu_mask,
    basis_zero,
    basis_one,
    basis_two,
    cheb_weight,
    tile_values,
    tile_rows,
    tile_slots,
    send_blocks,
    live_tiles,
):
    n_row = lax.axis_size("row")
    n_col = lax.axis_size("col")
    ids = lax.axis_index("col").astype(jnp.int32).reshape(1)
    owners = send_blocks.reshape(n_row)
    left, right = term_two(grad_out, relu_mask, cheb_weight)
    one_left, one_right, diff, pieces = local_terms(
        n_row, left, grad_out, relu_mask, cheb_weight, basis_zero, basis_one, basis_two
    )
    operator = build_operator(n_row, n_col, ids, live_tiles, tile_rows, tile_slots, tile_values)
    common = (n_row, n_col, ids, operator)

    steps = gather(n_col, left, 1, operator, pieces)
    pieces = exchange(after(pieces, steps[1][0][1]))
    left_early = early(*common, steps)
    right_steps = gather(n_col, after(right, left_early, steps[-1][0][1]), -1)
    left_came = exchange(final(*common, steps, left_early))
    right_early = early(*common, right_steps)

    left_carried = carry(n_row, owners, after(one_left, right_early, right_steps[-1][0][1]), left_came, pieces)
    steps = gather(n_col, left_carried, 1)
    right_came = exchange(final(*common, right_steps, right_early))
    left_early = early(*common, steps)

    right_carried = carry(n_row, owners, after(one_right, left_early, steps[-1][0][1]), right_came)
    right_steps = gather(n_col, right_carried, -1)
    left_came = exchange(final(*common, steps, left_early, carrying=True))
    right_early = early(*common, right_steps)

    right_came = exchange(final(*common, right_steps, right_early))
    weight_grad = assemble(n_row, left_came)
    return finish(n_row, owners, diff, left_came, right_came), weight_grad


def solution(mesh):
    placed = (
        P(("row", "col"), None),
        P(("row", "col"), None),
        P(("row", "col"), None),
        P(("row", "col"), None),
        P(("row", "col"), None),
        P(),
        P(("row", "col"), None, None, None),
        P(("row", "col"), None),
        P(("row", "col"), None),
        P(("row", "col"), None, None),
        P(("row", "col")),
    )
    return jax.shard_map(
        per_device,
        mesh=mesh,
        in_specs=placed,
        out_specs=(P(("row", "col"), None), P()),
        check_vma=False,
    )
```

```python
import functools

import jax
import jax.numpy as jnp
from jax import lax
from jax.experimental import pallas as pl
from jax.experimental.pallas import tpu as pltpu
from jax.sharding import PartitionSpec as P

F = 256
H = 128
TB = 128
CHB = 4
WIDE = 2 * TB
LANES = 128
NODES_DEV = CHB * TB
TILES_DEV = 128
GROUPS = 8
MIB = 1 << 20
HEAVY = pl.CostEstimate(flops=1 << 34, bytes_accessed=64 * MIB, transcendentals=0)
LIGHT = pl.CostEstimate(flops=1024, bytes_accessed=1024, transcendentals=0)
BF16 = jnp.bfloat16
F32 = jnp.float32

SMEM = pl.BlockSpec(memory_space=pltpu.SMEM)
VMEM = pl.BlockSpec(memory_space=pltpu.VMEM)
HBM = pl.BlockSpec(memory_space=pltpu.HBM)


def params(mib):
    return pltpu.CompilerParams(vmem_limit_bytes=mib * MIB)


def in_hbm(*arrays):
    return [pltpu.with_memory_space_constraint(x, pltpu.HBM) for x in arrays]


def split(x):
    high = x.astype(BF16)
    low = (x - high.astype(F32)).astype(BF16)
    return high, low


def dot3(a, b, dims):
    ah, al = a
    bh, bl = b

    def one(x, y):
        return lax.dot_general(x, y, (dims, ((), ())), preferred_element_type=F32)

    return one(ah, bh) + (one(ah, bl) + one(al, bh))


def fetch(sources, targets, sems):
    copies = [pltpu.make_async_copy(a, b, sems.at[i]) for i, (a, b) in enumerate(zip(sources, targets))]
    for copy in copies:
        copy.start()
    return copies


def masked_of(grad, mask):
    return jnp.where(mask > 0, grad, jnp.zeros_like(grad))


def term_two_kernel(grad_hbm, mask_hbm, weight_hbm, left_ref, right_ref, grad, mask, weight, sems):
    for copy in fetch((grad_hbm, mask_hbm, weight_hbm.at[2]), (grad, mask, weight), sems):
        copy.wait()
    term = dot3(split(weight[...]), split(masked_of(grad[...], mask[...])), ((1,), (1,)))
    left_ref[...] = term[:H]
    right_ref[...] = term[H:]


def term_two(grad_out, relu_mask, cheb_weight):
    out = jax.ShapeDtypeStruct((H, NODES_DEV), F32)
    return pl.pallas_call(
        term_two_kernel,
        in_specs=[HBM] * 3,
        out_specs=[VMEM, VMEM],
        out_shape=[out, out],
        scratch_shapes=[
            pltpu.VMEM((NODES_DEV, F), F32),
            pltpu.VMEM((NODES_DEV, F), jnp.int32),
            pltpu.VMEM((F, F), F32),
            pltpu.SemaphoreType.DMA((3,)),
        ],
        compiler_params=params(16),
        cost_estimate=LIGHT,
        name="term_two",
    )(*in_hbm(grad_out, relu_mask, cheb_weight))


def local_kernel(
    n_row, first_ref, grad_hbm, mask_hbm, weight_hbm, h0, h1, h2, left_ref, right_ref, diff_ref, pieces_ref,
    grad, mask, weight, bases, sems,
):
    sources = (grad_hbm, mask_hbm, weight_hbm, h0, h1, h2)
    copies = fetch(sources, (grad, mask, weight, bases.at[0], bases.at[1], bases.at[2]), sems)
    for copy in copies[:3]:
        copy.wait()
    values = masked_of(grad[...], mask[...])
    masked = split(values)
    term = dot3(split(weight[1]), masked, ((1,), (1,)))
    left_ref[...] = term[:H]
    right_ref[...] = term[H:]
    diff_ref[...] = dot3(split(weight[0] - weight[2]), masked, ((1,), (1,)))
    turned = split(values.T)
    rows = F // n_row
    for k in range(3):
        copies[3 + k].wait()
        part = dot3(turned, split(bases[k]), ((1,), (0,)))
        for j in range(F // LANES):
            here = (k * (F // LANES) + j) * rows
            for q in range(n_row):
                pieces_ref[q, here : here + rows, :] = part[q * rows : (q + 1) * rows, j * LANES : (j + 1) * LANES]


def local_terms(n_row, first, grad_out, relu_mask, cheb_weight, b0, b1, b2):
    half = jax.ShapeDtypeStruct((H, NODES_DEV), F32)
    share = 3 * F * F // n_row // LANES
    return pl.pallas_call(
        functools.partial(local_kernel, n_row),
        in_specs=[pl.BlockSpec(memory_space=pl.ANY)] + [HBM] * 6,
        out_specs=[VMEM] * 4,
        out_shape=[
            half,
            half,
            jax.ShapeDtypeStruct((F, NODES_DEV), F32),
            jax.ShapeDtypeStruct((n_row, share, LANES), F32),
        ],
        scratch_shapes=[
            pltpu.VMEM((NODES_DEV, F), F32),
            pltpu.VMEM((NODES_DEV, F), jnp.int32),
            pltpu.VMEM((3, F, F), F32),
            pltpu.VMEM((3, NODES_DEV, F), F32),
            pltpu.SemaphoreType.DMA((6,)),
        ],
        compiler_params=params(32),
        cost_estimate=LIGHT,
        name="local_terms",
    )(first, *in_hbm(grad_out, relu_mask, cheb_weight, b0, b1, b2))


def stacked(field):
    high, low = split(field)
    return jnp.concatenate([jnp.concatenate([x, x], axis=1) for x in (high, low)], axis=0)


def operator_kernel(n_col, origins, ids_ref, live_ref, rows_hbm, slots_hbm, values_ref, *refs):
    fields, refs = refs[: len(origins)], refs[len(origins) :]
    out_ref, total_ref, tiles, acc, lists, counts, rows, slots, sems, small_sems = refs
    origin = pl.program_id(0)
    size = TILES_DEV // GROUPS

    def copy(g):
        part = pl.ds(g * size, size)
        return pltpu.make_async_copy(values_ref.at[0, part], tiles.at[part], sems.at[g])

    @pl.when(origin == 0)
    def _():
        small = fetch((rows_hbm, slots_hbm), (rows, slots), small_sems)
        for g in range(GROUPS):
            copy(g).start()
        for s in range(n_col):
            counts[s] = 0
        for item in small:
            item.wait()

        def place(t, carry):
            row = rows[0, t]
            s = lax.rem(row // CHB - ids_ref[0] + n_col, n_col)
            position = slots[0, t] * CHB + lax.rem(row, CHB)
            n = counts[s]
            lists[s, n] = position * TILES_DEV + t
            counts[s] = n + 1
            return carry

        lax.fori_loop(0, live_ref[0], place, 0)

    acc[...] = jnp.zeros_like(acc)

    @pl.when(origin == 0)
    def _():
        for g in range(GROUPS):
            copy(g).wait()

    def add(n, carry):
        entry = lists[origin, n]
        position = entry // TILES_DEV
        slot = position // CHB
        at_row = pl.ds(pl.multiple_of(lax.rem(position, CHB) * TB, TB), TB)
        at_lane = pl.ds(pl.multiple_of(lax.rem(slot, 2) * TB, TB), TB)
        acc[slot // 2, at_row, at_lane] += tiles[lax.rem(entry, TILES_DEV)]
        return carry

    lax.fori_loop(0, counts[origin], add, 0)
    pairs = acc.shape[0]
    for p in range(pairs):
        high, low = split(acc[p])
        out_ref[0, p, :NODES_DEV, :] = high
        out_ref[0, p, NODES_DEV:, :] = low

    for k, field in zip(origins, fields):

        @pl.when(origin == k)
        def _():
            left = stacked(field[...])
            for p in range(pairs):
                part = jnp.dot(left, out_ref[0, p], preferred_element_type=F32)
                summed = part[:H] + part[H:]
                here = slice(p * WIDE, (p + 1) * WIDE)
                total_ref[:, here] = summed if k == 0 else total_ref[:, here] + summed


def build_operator(n_row, n_col, ids, live, rows, slots, values, pairs):
    part = (n_row // 2, 2 * NODES_DEV, WIDE)
    origins, fields = zip(*pairs)
    return pl.pallas_call(
        functools.partial(operator_kernel, n_col, origins),
        grid=(n_col,),
        in_specs=[SMEM] * 2 + [HBM] * 3 + [pl.BlockSpec((H, NODES_DEV), lambda s: (0, 0))] * len(fields),
        out_specs=[
            pl.BlockSpec((1,) + part, lambda s: (s, 0, 0, 0)),
            pl.BlockSpec((H, n_row * TB), lambda s: (0, 0)),
        ],
        out_shape=[pltpu.HBM((n_col,) + part, BF16), jax.ShapeDtypeStruct((H, n_row * TB), F32)],
        scratch_shapes=[
            pltpu.VMEM((TILES_DEV, TB, TB), F32),
            pltpu.VMEM((n_row // 2, NODES_DEV, WIDE), F32),
            pltpu.SMEM((n_col, TILES_DEV), jnp.int32),
            pltpu.SMEM((n_col,), jnp.int32),
            pltpu.SMEM((1, TILES_DEV), jnp.int32),
            pltpu.SMEM((1, TILES_DEV), jnp.int32),
            pltpu.SemaphoreType.DMA((GROUPS,)),
            pltpu.SemaphoreType.DMA((2,)),
        ],
        compiler_params=params(40),
        cost_estimate=HEAVY,
        name="operator",
    )(ids, live, *in_hbm(rows, slots, values), *fields)


def product_kernel(n_row, n_col, origins, has_prev, last, n_carriers, *refs):
    n = len(origins)
    ids_ref, op_ref, refs = refs[0], refs[1], refs[2:]
    fields, refs = refs[:n], refs[n:]
    if has_prev:
        prev, refs = refs[0], refs[1:]
    carriers, refs = refs[:n_carriers], refs[n_carriers:]
    out_ref, buf, sems = refs[:3]

    def copy(k, p):
        return pltpu.make_async_copy(op_ref.at[origins[k], p], buf.at[k, p], sems.at[k, p])

    for p in range(n_row // 2):
        for k in range(n):
            copy(k, p).start()
    left = [stacked(field[:H, :]) for field in fields]
    if n_carriers:
        ordered = refs[3]
        for k in range(n_col):
            ordered[lax.rem(ids_ref[0] + k, n_col)] = carriers[k][H:, :]
        share = ordered[0]
        for k in range(1, n_col):
            share = share + ordered[k]
        rows = share.shape[0]
        for j in range(NODES_DEV // LANES):
            for q in range(n_row):
                out_ref[q, H + j * rows : H + (j + 1) * rows, :] = share[:, j * LANES : (j + 1) * LANES]
    for p in range(n_row // 2):
        here = slice(p * WIDE, (p + 1) * WIDE)
        total = None
        for k in range(n):
            copy(k, p).wait()
            part = jnp.dot(left[k], buf[k, p], preferred_element_type=F32)
            total = part if total is None else total + part
        summed = total[:H] + total[H:]
        if has_prev:
            summed = summed + prev[:, here]
        if last:
            out_ref[2 * p, :H, :] = summed[:, :TB]
            out_ref[2 * p + 1, :H, :] = summed[:, TB:]
        else:
            out_ref[:, here] = summed


def product(n_row, n_col, ids, origins, operator, fields, prev, last, carriers=()):
    n = len(origins)
    has_prev = prev is not None
    share = 0
    scratch = [
        pltpu.VMEM((n, n_row // 2, 2 * NODES_DEV, WIDE), BF16),
        pltpu.SemaphoreType.DMA((n, n_row // 2)),
    ]
    if carriers:
        rows = carriers[0].shape[0] - H
        share = rows * NODES_DEV // LANES
        scratch.append(pltpu.VMEM((n_col, rows, NODES_DEV), F32))
    shape = (n_row, H + share, TB) if last else (H, n_row * TB)
    count = n + has_prev + len(carriers)
    return pl.pallas_call(
        functools.partial(product_kernel, n_row, n_col, origins, has_prev, last, len(carriers)),
        in_specs=[SMEM, HBM] + [VMEM] * count,
        out_specs=VMEM,
        out_shape=jax.ShapeDtypeStruct(shape, F32),
        scratch_shapes=scratch,
        compiler_params=params(48),
        cost_estimate=LIGHT if last else HEAVY,
        name="product",
    )(
        ids,
        *in_hbm(operator),
        *fields,
        *((prev,) if has_prev else ()),
        *carriers,
    )


def carry_kernel(n_row, rows, owners_ref, base_ref, came_ref, *refs):
    out_ref = refs[-1]
    out_ref[:H, :] = base_ref[...]
    for q in range(n_row):
        here = pl.ds(pl.multiple_of(owners_ref[q] * TB, TB), TB)
        out_ref[:H, here] += 2.0 * came_ref[q]
    if rows:
        pieces_ref = refs[0]
        share = pieces_ref[0]
        for q in range(1, n_row):
            share = share + pieces_ref[q]
        for j in range(NODES_DEV // LANES):
            out_ref[H:, j * LANES : (j + 1) * LANES] = share[j * rows : (j + 1) * rows, :]


def carry(n_row, owners, base, came, *pieces):
    rows = pieces[0].shape[1] * LANES // NODES_DEV if pieces else 0
    return pl.pallas_call(
        functools.partial(carry_kernel, n_row, rows),
        in_specs=[SMEM] + [VMEM] * (2 + len(pieces)),
        out_specs=VMEM,
        out_shape=jax.ShapeDtypeStruct((H + rows, NODES_DEV), F32),
        compiler_params=params(24),
        cost_estimate=LIGHT,
        name="carry",
    )(owners, base, came, *pieces)


def finish_kernel(n_row, owners_ref, base_ref, left_ref, right_ref, out_ref, total):
    total[...] = base_ref[...]
    for h, came in enumerate((left_ref, right_ref)):
        for q in range(n_row):
            here = pl.ds(pl.multiple_of(owners_ref[q] * TB, TB), TB)
            total[h * H : (h + 1) * H, here] += came[q, :H, :]
    out_ref[...] = total[...].T


def finish(n_row, owners, base, left, right):
    return pl.pallas_call(
        functools.partial(finish_kernel, n_row),
        in_specs=[SMEM] + [VMEM] * 3,
        out_specs=VMEM,
        out_shape=jax.ShapeDtypeStruct((NODES_DEV, F), F32),
        scratch_shapes=[pltpu.VMEM((F, NODES_DEV), F32)],
        compiler_params=params(24),
        cost_estimate=LIGHT,
        name="finish",
    )(owners, base, left, right)


def assemble_kernel(n_row, came_ref, out_ref, turned):
    rows = F // n_row
    per = F // LANES
    for q in range(n_row):
        for j in range(3 * per):
            here = slice(H + j * rows, H + (j + 1) * rows)
            turned[q * rows : (q + 1) * rows, j * LANES : (j + 1) * LANES] = came_ref[q, here, :]
    for k in range(3):
        out_ref[k] = turned[:, k * F : (k + 1) * F].T


def assemble(n_row, came):
    return pl.pallas_call(
        functools.partial(assemble_kernel, n_row),
        in_specs=[VMEM],
        out_specs=VMEM,
        out_shape=jax.ShapeDtypeStruct((3, F, F), F32),
        scratch_shapes=[pltpu.VMEM((F, 3 * F), F32)],
        compiler_params=params(16),
        cost_estimate=LIGHT,
        name="assemble",
    )(came)


def shift(n_col, x, step):
    return lax.ppermute(x, "col", [(c, (c + step) % n_col) for c in range(n_col)])


def exchange(pieces):
    return lax.all_to_all(pieces, "row", split_axis=0, concat_axis=0, tiled=True)


def after(x, *others):
    return lax.optimization_barrier((x, *others))[0]


def opposite(field, below, above):
    col = lax.axis_index("col")
    sent = jnp.where(col == 1, above, jnp.where(col == 2, below, field))
    return lax.ppermute(sent, "col", [(1, 0), (2, 3), (3, 1), (0, 2)])


def gather(n_col, field, side):
    long = n_col // 2
    short = n_col - 1 - long
    ahead, behind = field, field
    steps = [[(0, field)]]
    for s in range(1, long + 1):
        if s == 2:
            ahead = after(ahead, behind)
        if s == 2 and n_col == 4:
            ahead = opposite(field, ahead, behind) if side > 0 else opposite(field, behind, ahead)
        else:
            ahead = shift(n_col, ahead, side)
        step = [((-side * s) % n_col, ahead)]
        if s <= short:
            behind = shift(n_col, behind, -side)
            step.append(((side * s) % n_col, behind))
        steps.append(step)
    return steps


def early(n_row, n_col, ids, operator, steps, total=None, done=0):
    pairs = [pair for step in steps[:-1] for pair in step][done:]
    for begin in range(0, len(pairs), 3):
        origins, fields = zip(*pairs[begin : begin + 3])
        total = product(n_row, n_col, ids, origins, operator, fields, total, False)
    return total


def final(n_row, n_col, ids, operator, steps, total, carrying=False):
    origins, fields = zip(*steps[-1])
    carriers = [x for _, x in sorted((p for step in steps for p in step), key=lambda p: p[0])] if carrying else ()
    return product(n_row, n_col, ids, origins, operator, fields, total, True, carriers)


def per_device(
    grad_out,
    relu_mask,
    basis_zero,
    basis_one,
    basis_two,
    cheb_weight,
    tile_values,
    tile_rows,
    tile_slots,
    send_blocks,
    live_tiles,
):
    n_row = lax.axis_size("row")
    n_col = lax.axis_size("col")
    ids = lax.axis_index("col").astype(jnp.int32).reshape(1)
    owners = send_blocks.reshape(n_row)
    left, right = term_two(grad_out, relu_mask, cheb_weight)
    one_left, one_right, diff, pieces = local_terms(
        n_row, left, grad_out, relu_mask, cheb_weight, basis_zero, basis_one, basis_two
    )
    steps = gather(n_col, left, 1)
    first = steps[0] + steps[1] if len(steps) > 2 else steps[0]
    operator, left_early = build_operator(
        n_row, n_col, ids, live_tiles, tile_rows, tile_slots, tile_values, first
    )
    pieces = exchange(pieces)
    common = (n_row, n_col, ids, operator)

    left_early = early(*common, steps, left_early, len(first))
    right_steps = gather(n_col, after(right, left_early, steps[-1][0][1]), -1)
    left_came = exchange(final(*common, steps, after(left_early, pieces)))
    right_early = early(*common, right_steps)

    left_carried = carry(n_row, owners, after(one_left, right_early, right_steps[-1][0][1]), left_came, pieces)
    steps = gather(n_col, left_carried, 1)
    right_came = exchange(final(*common, right_steps, right_early))
    left_early = early(*common, steps)

    right_carried = carry(n_row, owners, after(one_right, left_early, steps[-1][0][1]), right_came)
    right_steps = gather(n_col, right_carried, -1)
    left_came = exchange(final(*common, steps, left_early, carrying=True))
    right_early = early(*common, right_steps)

    right_came = exchange(final(*common, right_steps, right_early))
    weight_grad = assemble(n_row, left_came)
    return finish(n_row, owners, diff, left_came, right_came), weight_grad


def solution(mesh):
    placed = (
        P(("row", "col"), None),
        P(("row", "col"), None),
        P(("row", "col"), None),
        P(("row", "col"), None),
        P(("row", "col"), None),
        P(),
        P(("row", "col"), None, None, None),
        P(("row", "col"), None),
        P(("row", "col"), None),
        P(("row", "col"), None, None),
        P(("row", "col")),
    )
    return jax.shard_map(
        per_device,
        mesh=mesh,
        in_specs=placed,
        out_specs=(P(("row", "col"), None), P()),
        check_vma=False,
    )
```

```python
import functools

import jax
import jax.numpy as jnp
from jax import lax
from jax.experimental import pallas as pl
from jax.experimental.pallas import tpu as pltpu
from jax.sharding import PartitionSpec as P

F = 256
H = 128
TB = 128
CHB = 4
WIDE = 2 * TB
LANES = 128
NODES_DEV = CHB * TB
TILES_DEV = 128
GROUPS = 8
MIB = 1 << 20
HEAVY = pl.CostEstimate(flops=1 << 34, bytes_accessed=64 * MIB, transcendentals=0)
LIGHT = pl.CostEstimate(flops=1024, bytes_accessed=1024, transcendentals=0)
BF16 = jnp.bfloat16
F32 = jnp.float32

SMEM = pl.BlockSpec(memory_space=pltpu.SMEM)
VMEM = pl.BlockSpec(memory_space=pltpu.VMEM)
HBM = pl.BlockSpec(memory_space=pltpu.HBM)


def params(mib):
    return pltpu.CompilerParams(vmem_limit_bytes=mib * MIB)


def in_hbm(*arrays):
    return [pltpu.with_memory_space_constraint(x, pltpu.HBM) for x in arrays]


def split(x):
    high = x.astype(BF16)
    low = (x - high.astype(F32)).astype(BF16)
    return high, low


def dot3(a, b, dims):
    ah, al = a
    bh, bl = b

    def one(x, y):
        return lax.dot_general(x, y, (dims, ((), ())), preferred_element_type=F32)

    return one(ah, bh) + (one(ah, bl) + one(al, bh))


def fetch(sources, targets, sems):
    copies = [pltpu.make_async_copy(a, b, sems.at[i]) for i, (a, b) in enumerate(zip(sources, targets))]
    for copy in copies:
        copy.start()
    return copies


def masked_of(grad, mask):
    return jnp.where(mask > 0, grad, jnp.zeros_like(grad))


def term_two_kernel(grad_hbm, mask_hbm, weight_hbm, left_ref, right_ref, grad, mask, weight, sems):
    for copy in fetch((grad_hbm, mask_hbm, weight_hbm.at[2]), (grad, mask, weight), sems):
        copy.wait()
    term = dot3(split(weight[...]), split(masked_of(grad[...], mask[...])), ((1,), (1,)))
    left_ref[...] = term[:H]
    right_ref[...] = term[H:]


def term_two(grad_out, relu_mask, cheb_weight):
    out = jax.ShapeDtypeStruct((H, NODES_DEV), F32)
    return pl.pallas_call(
        term_two_kernel,
        in_specs=[HBM] * 3,
        out_specs=[VMEM, VMEM],
        out_shape=[out, out],
        scratch_shapes=[
            pltpu.VMEM((NODES_DEV, F), F32),
            pltpu.VMEM((NODES_DEV, F), jnp.int32),
            pltpu.VMEM((F, F), F32),
            pltpu.SemaphoreType.DMA((3,)),
        ],
        compiler_params=params(16),
        cost_estimate=LIGHT,
        name="term_two",
    )(*in_hbm(grad_out, relu_mask, cheb_weight))


def local_kernel(
    n_row, first_ref, grad_hbm, mask_hbm, weight_hbm, h0, h1, h2, left_ref, right_ref, diff_ref, pieces_ref,
    grad, mask, weight, bases, sems,
):
    sources = (grad_hbm, mask_hbm, weight_hbm, h0, h1, h2)
    copies = fetch(sources, (grad, mask, weight, bases.at[0], bases.at[1], bases.at[2]), sems)
    for copy in copies[:3]:
        copy.wait()
    values = masked_of(grad[...], mask[...])
    masked = split(values)
    term = dot3(split(weight[1]), masked, ((1,), (1,)))
    left_ref[...] = term[:H]
    right_ref[...] = term[H:]
    diff_ref[...] = dot3(split(weight[0] - weight[2]), masked, ((1,), (1,)))
    turned = split(values.T)
    rows = F // n_row
    for k in range(3):
        copies[3 + k].wait()
        part = dot3(turned, split(bases[k]), ((1,), (0,)))
        for j in range(F // LANES):
            here = (k * (F // LANES) + j) * rows
            for q in range(n_row):
                pieces_ref[q, here : here + rows, :] = part[q * rows : (q + 1) * rows, j * LANES : (j + 1) * LANES]


def local_terms(n_row, first, grad_out, relu_mask, cheb_weight, b0, b1, b2):
    half = jax.ShapeDtypeStruct((H, NODES_DEV), F32)
    share = 3 * F * F // n_row // LANES
    return pl.pallas_call(
        functools.partial(local_kernel, n_row),
        in_specs=[pl.BlockSpec(memory_space=pl.ANY)] + [HBM] * 6,
        out_specs=[VMEM] * 4,
        out_shape=[
            half,
            half,
            jax.ShapeDtypeStruct((F, NODES_DEV), F32),
            jax.ShapeDtypeStruct((n_row, share, LANES), F32),
        ],
        scratch_shapes=[
            pltpu.VMEM((NODES_DEV, F), F32),
            pltpu.VMEM((NODES_DEV, F), jnp.int32),
            pltpu.VMEM((3, F, F), F32),
            pltpu.VMEM((3, NODES_DEV, F), F32),
            pltpu.SemaphoreType.DMA((6,)),
        ],
        compiler_params=params(32),
        cost_estimate=LIGHT,
        name="local_terms",
    )(first, *in_hbm(grad_out, relu_mask, cheb_weight, b0, b1, b2))


def stacked(field):
    high, low = split(field)
    return jnp.concatenate([jnp.concatenate([x, x], axis=1) for x in (high, low)], axis=0)


def operator_kernel(n_col, origins, ids_ref, live_ref, rows_hbm, slots_hbm, values_ref, *refs):
    fields, refs = refs[: len(origins)], refs[len(origins) :]
    out_ref, total_ref, tiles, acc, lists, counts, rows, slots, sems, small_sems = refs
    origin = pl.program_id(0)
    size = TILES_DEV // GROUPS

    def copy(g):
        part = pl.ds(g * size, size)
        return pltpu.make_async_copy(values_ref.at[0, part], tiles.at[part], sems.at[g])

    @pl.when(origin == 0)
    def _():
        small = fetch((rows_hbm, slots_hbm), (rows, slots), small_sems)
        for g in range(GROUPS):
            copy(g).start()
        for s in range(n_col):
            counts[s] = 0
        for item in small:
            item.wait()

        def place(t, carry):
            row = rows[0, t]
            s = lax.rem(row // CHB - ids_ref[0] + n_col, n_col)
            position = slots[0, t] * CHB + lax.rem(row, CHB)
            n = counts[s]
            lists[s, n] = position * TILES_DEV + t
            counts[s] = n + 1
            return carry

        lax.fori_loop(0, live_ref[0], place, 0)

    acc[...] = jnp.zeros_like(acc)

    @pl.when(origin == 0)
    def _():
        for g in range(GROUPS):
            copy(g).wait()

    def add(n, carry):
        entry = lists[origin, n]
        position = entry // TILES_DEV
        slot = position // CHB
        at_row = pl.ds(pl.multiple_of(lax.rem(position, CHB) * TB, TB), TB)
        at_lane = pl.ds(pl.multiple_of(lax.rem(slot, 2) * TB, TB), TB)
        acc[slot // 2, at_row, at_lane] += tiles[lax.rem(entry, TILES_DEV)]
        return carry

    lax.fori_loop(0, counts[origin], add, 0)
    pairs = acc.shape[0]
    for p in range(pairs):
        high, low = split(acc[p])
        out_ref[0, p, :NODES_DEV, :] = high
        out_ref[0, p, NODES_DEV:, :] = low

    for k, field in zip(origins, fields):

        @pl.when(origin == k)
        def _():
            left = stacked(field[...])
            for p in range(pairs):
                part = jnp.dot(left, out_ref[0, p], preferred_element_type=F32)
                summed = part[:H] + part[H:]
                here = slice(p * WIDE, (p + 1) * WIDE)
                total_ref[:, here] = summed if k == 0 else total_ref[:, here] + summed


def build_operator(n_row, n_col, ids, live, rows, slots, values, pairs):
    part = (n_row // 2, 2 * NODES_DEV, WIDE)
    origins, fields = zip(*pairs)
    return pl.pallas_call(
        functools.partial(operator_kernel, n_col, origins),
        grid=(n_col,),
        in_specs=[SMEM] * 2 + [HBM] * 3 + [pl.BlockSpec((H, NODES_DEV), lambda s: (0, 0))] * len(fields),
        out_specs=[
            pl.BlockSpec((1,) + part, lambda s: (s, 0, 0, 0)),
            pl.BlockSpec((H, n_row * TB), lambda s: (0, 0)),
        ],
        out_shape=[pltpu.HBM((n_col,) + part, BF16), jax.ShapeDtypeStruct((H, n_row * TB), F32)],
        scratch_shapes=[
            pltpu.VMEM((TILES_DEV, TB, TB), F32),
            pltpu.VMEM((n_row // 2, NODES_DEV, WIDE), F32),
            pltpu.SMEM((n_col, TILES_DEV), jnp.int32),
            pltpu.SMEM((n_col,), jnp.int32),
            pltpu.SMEM((1, TILES_DEV), jnp.int32),
            pltpu.SMEM((1, TILES_DEV), jnp.int32),
            pltpu.SemaphoreType.DMA((GROUPS,)),
            pltpu.SemaphoreType.DMA((2,)),
        ],
        compiler_params=params(40),
        cost_estimate=HEAVY,
        name="operator",
    )(ids, live, *in_hbm(rows, slots, values), *fields)


def product_kernel(n_row, n_col, origins, has_prev, last, n_carriers, *refs):
    n = len(origins)
    ids_ref, op_ref, refs = refs[0], refs[1], refs[2:]
    fields, refs = refs[:n], refs[n:]
    if has_prev:
        prev, refs = refs[0], refs[1:]
    carriers, refs = refs[:n_carriers], refs[n_carriers:]
    out_ref, buf, sems = refs[:3]

    def copy(k, p):
        return pltpu.make_async_copy(op_ref.at[origins[k], p], buf.at[k, p], sems.at[k, p])

    for p in range(n_row // 2):
        for k in range(n):
            copy(k, p).start()
    left = [stacked(field[:H, :]) for field in fields]
    if n_carriers:
        ordered = refs[3]
        for k in range(n_col):
            ordered[lax.rem(ids_ref[0] + k, n_col)] = carriers[k][H:, :]
        share = ordered[0]
        for k in range(1, n_col):
            share = share + ordered[k]
        rows = share.shape[0]
        for j in range(NODES_DEV // LANES):
            for q in range(n_row):
                out_ref[q, H + j * rows : H + (j + 1) * rows, :] = share[:, j * LANES : (j + 1) * LANES]
    for p in range(n_row // 2):
        here = slice(p * WIDE, (p + 1) * WIDE)
        total = None
        for k in range(n):
            copy(k, p).wait()
            part = jnp.dot(left[k], buf[k, p], preferred_element_type=F32)
            total = part if total is None else total + part
        summed = total[:H] + total[H:]
        if has_prev:
            summed = summed + prev[:, here]
        if last:
            out_ref[2 * p, :H, :] = summed[:, :TB]
            out_ref[2 * p + 1, :H, :] = summed[:, TB:]
        else:
            out_ref[:, here] = summed


def product(n_row, n_col, ids, origins, operator, fields, prev, last, carriers=(), weight=LIGHT):
    n = len(origins)
    has_prev = prev is not None
    share = 0
    scratch = [
        pltpu.VMEM((n, n_row // 2, 2 * NODES_DEV, WIDE), BF16),
        pltpu.SemaphoreType.DMA((n, n_row // 2)),
    ]
    if carriers:
        rows = carriers[0].shape[0] - H
        share = rows * NODES_DEV // LANES
        scratch.append(pltpu.VMEM((n_col, rows, NODES_DEV), F32))
    shape = (n_row, H + share, TB) if last else (H, n_row * TB)
    count = n + has_prev + len(carriers)
    return pl.pallas_call(
        functools.partial(product_kernel, n_row, n_col, origins, has_prev, last, len(carriers)),
        in_specs=[SMEM, HBM] + [VMEM] * count,
        out_specs=VMEM,
        out_shape=jax.ShapeDtypeStruct(shape, F32),
        scratch_shapes=scratch,
        compiler_params=params(48),
        cost_estimate=weight,
        name="product",
    )(
        ids,
        *in_hbm(operator),
        *fields,
        *((prev,) if has_prev else ()),
        *carriers,
    )


def carry_kernel(n_row, rows, owners_ref, base_ref, came_ref, *refs):
    out_ref = refs[-1]
    out_ref[:H, :] = base_ref[...]
    for q in range(n_row):
        here = pl.ds(pl.multiple_of(owners_ref[q] * TB, TB), TB)
        out_ref[:H, here] += 2.0 * came_ref[q]
    if rows:
        pieces_ref = refs[0]
        share = pieces_ref[0]
        for q in range(1, n_row):
            share = share + pieces_ref[q]
        for j in range(NODES_DEV // LANES):
            out_ref[H:, j * LANES : (j + 1) * LANES] = share[j * rows : (j + 1) * rows, :]


def carry(n_row, owners, base, came, *pieces, weight=LIGHT):
    rows = pieces[0].shape[1] * LANES // NODES_DEV if pieces else 0
    return pl.pallas_call(
        functools.partial(carry_kernel, n_row, rows),
        in_specs=[SMEM] + [VMEM] * (2 + len(pieces)),
        out_specs=VMEM,
        out_shape=jax.ShapeDtypeStruct((H + rows, NODES_DEV), F32),
        compiler_params=params(24),
        cost_estimate=weight,
        name="carry",
    )(owners, base, came, *pieces)


def finish_kernel(n_row, owners_ref, base_ref, left_ref, right_ref, out_ref, total):
    total[...] = base_ref[...]
    for h, came in enumerate((left_ref, right_ref)):
        for q in range(n_row):
            here = pl.ds(pl.multiple_of(owners_ref[q] * TB, TB), TB)
            total[h * H : (h + 1) * H, here] += came[q, :H, :]
    out_ref[...] = total[...].T


def finish(n_row, owners, base, left, right):
    return pl.pallas_call(
        functools.partial(finish_kernel, n_row),
        in_specs=[SMEM] + [VMEM] * 3,
        out_specs=VMEM,
        out_shape=jax.ShapeDtypeStruct((NODES_DEV, F), F32),
        scratch_shapes=[pltpu.VMEM((F, NODES_DEV), F32)],
        compiler_params=params(24),
        cost_estimate=LIGHT,
        name="finish",
    )(owners, base, left, right)


def assemble_kernel(n_row, came_ref, out_ref, turned):
    rows = F // n_row
    per = F // LANES
    for q in range(n_row):
        for j in range(3 * per):
            here = slice(H + j * rows, H + (j + 1) * rows)
            turned[q * rows : (q + 1) * rows, j * LANES : (j + 1) * LANES] = came_ref[q, here, :]
    for k in range(3):
        out_ref[k] = turned[:, k * F : (k + 1) * F].T


def assemble(n_row, came):
    return pl.pallas_call(
        functools.partial(assemble_kernel, n_row),
        in_specs=[VMEM],
        out_specs=VMEM,
        out_shape=jax.ShapeDtypeStruct((3, F, F), F32),
        scratch_shapes=[pltpu.VMEM((F, 3 * F), F32)],
        compiler_params=params(16),
        cost_estimate=LIGHT,
        name="assemble",
    )(came)


def shift(n_col, x, step):
    return lax.ppermute(x, "col", [(c, (c + step) % n_col) for c in range(n_col)])


def exchange(pieces):
    return lax.all_to_all(pieces, "row", split_axis=0, concat_axis=0, tiled=True)


def after(x, *others):
    return lax.optimization_barrier((x, *others))[0]


def for_opposite(field, below, above):
    col = lax.axis_index("col")
    return jnp.where(col == 1, above, jnp.where(col == 2, below, field))


def opposite(sent):
    return lax.ppermute(sent, "col", [(1, 0), (2, 3), (3, 1), (0, 2)])


def begin(n_col, field, side):
    return shift(n_col, field, side), shift(n_col, field, -side) if n_col > 2 else field


def then_sent(n_col, field, side, begun, *done):
    ahead, behind = begun
    ahead = after(ahead, behind, *done)
    if n_col != 4:
        return ahead
    return for_opposite(field, ahead, behind) if side > 0 else for_opposite(field, behind, ahead)


def gather(n_col, field, side, begun, sent):
    long = n_col // 2
    short = n_col - 1 - long
    ahead, behind = begun
    steps = [[(0, field)]]
    for s in range(1, long + 1):
        if s == 2 and n_col == 4:
            ahead = opposite(sent)
        elif s > 1:
            ahead = shift(n_col, sent if s == 2 else ahead, side)
        step = [((-side * s) % n_col, ahead)]
        if s <= short:
            behind = shift(n_col, behind, -side) if s > 1 else behind
            step.append(((side * s) % n_col, behind))
        steps.append(step)
    return steps


def early(n_row, n_col, ids, operator, steps, total=None, done=0, weight=HEAVY):
    pairs = [pair for step in steps[:-1] for pair in step][done:]
    for begin in range(0, len(pairs), 3):
        origins, fields = zip(*pairs[begin : begin + 3])
        total = product(n_row, n_col, ids, origins, operator, fields, total, False, weight=weight)
    return total


def final(n_row, n_col, ids, operator, steps, total, carrying=False):
    origins, fields = zip(*steps[-1])
    carriers = [x for _, x in sorted((p for step in steps for p in step), key=lambda p: p[0])] if carrying else ()
    return product(n_row, n_col, ids, origins, operator, fields, total, True, carriers)


def per_device(
    grad_out,
    relu_mask,
    basis_zero,
    basis_one,
    basis_two,
    cheb_weight,
    tile_values,
    tile_rows,
    tile_slots,
    send_blocks,
    live_tiles,
):
    n_row = lax.axis_size("row")
    n_col = lax.axis_size("col")
    ids = lax.axis_index("col").astype(jnp.int32).reshape(1)
    owners = send_blocks.reshape(n_row)
    left, right = term_two(grad_out, relu_mask, cheb_weight)
    one_left, one_right, diff, pieces = local_terms(
        n_row, left, grad_out, relu_mask, cheb_weight, basis_zero, basis_one, basis_two
    )
    begun = begin(n_col, left, 1)
    sent = then_sent(n_col, left, 1, begun)
    steps = gather(n_col, left, 1, begun, sent)
    first = steps[0] + steps[1] if len(steps) > 2 else steps[0]
    operator, left_early = build_operator(
        n_row, n_col, ids, live_tiles, tile_rows, tile_slots, tile_values, first
    )
    pieces = exchange(pieces)
    common = (n_row, n_col, ids, operator)

    right_begun = begin(n_col, after(right, sent), -1)
    left_early = early(*common, steps, left_early, len(first))
    left_last = final(*common, steps, after(left_early, pieces))
    left_came = exchange(left_last)
    sent = then_sent(n_col, right, -1, right_begun, left_last)
    right_steps = gather(n_col, after(right, left_last), -1, right_begun, sent)
    right_last = final(*common, right_steps, early(*common, right_steps))

    left_carried = carry(n_row, owners, after(one_left, right_last), left_came, pieces)
    begun = begin(n_col, left_carried, 1)
    steps = gather(n_col, left_carried, 1, begun, then_sent(n_col, left_carried, 1, begun))
    right_came = exchange(right_last)

    right_carried = carry(n_row, owners, after(one_right, *begun), right_came, weight=HEAVY)
    right_begun = begin(n_col, right_carried, -1)
    steps[0] = [(0, after(left_carried, right_carried))]
    left_last = final(*common, steps, early(*common, steps, weight=LIGHT), carrying=True)
    left_came = exchange(left_last)
    sent = then_sent(n_col, right_carried, -1, right_begun, left_last)
    right_steps = gather(n_col, right_carried, -1, right_begun, sent)

    right_came = exchange(final(*common, right_steps, early(*common, right_steps)))
    weight_grad = assemble(n_row, left_came)
    return finish(n_row, owners, diff, left_came, right_came), weight_grad


def solution(mesh):
    placed = (
        P(("row", "col"), None),
        P(("row", "col"), None),
        P(("row", "col"), None),
        P(("row", "col"), None),
        P(("row", "col"), None),
        P(),
        P(("row", "col"), None, None, None),
        P(("row", "col"), None),
        P(("row", "col"), None),
        P(("row", "col"), None, None),
        P(("row", "col")),
    )
    return jax.shard_map(
        per_device,
        mesh=mesh,
        in_specs=placed,
        out_specs=(P(("row", "col"), None), P()),
        check_vma=False,
    )
```

```python
import functools

import jax
import jax.numpy as jnp
from jax import lax
from jax.experimental import pallas as pl
from jax.experimental.pallas import tpu as pltpu
from jax.sharding import PartitionSpec as P

F = 256
H = 128
TB = 128
CHB = 4
WIDE = 2 * TB
LANES = 128
NODES_DEV = CHB * TB
TILES_DEV = 128
GROUPS = 8
MIB = 1 << 20
HEAVY = pl.CostEstimate(flops=1 << 34, bytes_accessed=64 * MIB, transcendentals=0)
LIGHT = pl.CostEstimate(flops=1024, bytes_accessed=1024, transcendentals=0)
BF16 = jnp.bfloat16
F32 = jnp.float32

SMEM = pl.BlockSpec(memory_space=pltpu.SMEM)
VMEM = pl.BlockSpec(memory_space=pltpu.VMEM)
HBM = pl.BlockSpec(memory_space=pltpu.HBM)


def params(mib):
    return pltpu.CompilerParams(vmem_limit_bytes=mib * MIB)


def in_hbm(*arrays):
    return [pltpu.with_memory_space_constraint(x, pltpu.HBM) for x in arrays]


def split(x):
    high = x.astype(BF16)
    low = (x - high.astype(F32)).astype(BF16)
    return high, low


def dot3(a, b, dims):
    ah, al = a
    bh, bl = b

    def one(x, y):
        return lax.dot_general(x, y, (dims, ((), ())), preferred_element_type=F32)

    return one(ah, bh) + (one(ah, bl) + one(al, bh))


def fetch(sources, targets, sems):
    copies = [pltpu.make_async_copy(a, b, sems.at[i]) for i, (a, b) in enumerate(zip(sources, targets))]
    for copy in copies:
        copy.start()
    return copies


def masked_of(grad, mask):
    return jnp.where(mask > 0, grad, jnp.zeros_like(grad))


def term_two_kernel(grad_hbm, mask_hbm, weight_hbm, left_ref, right_ref, grad, mask, weight, sems):
    for copy in fetch((grad_hbm, mask_hbm, weight_hbm.at[2]), (grad, mask, weight), sems):
        copy.wait()
    term = dot3(split(weight[...]), split(masked_of(grad[...], mask[...])), ((1,), (1,)))
    left_ref[...] = term[:H]
    right_ref[...] = term[H:]


def term_two(grad_out, relu_mask, cheb_weight):
    out = jax.ShapeDtypeStruct((H, NODES_DEV), F32)
    return pl.pallas_call(
        term_two_kernel,
        in_specs=[HBM] * 3,
        out_specs=[VMEM, VMEM],
        out_shape=[out, out],
        scratch_shapes=[
            pltpu.VMEM((NODES_DEV, F), F32),
            pltpu.VMEM((NODES_DEV, F), jnp.int32),
            pltpu.VMEM((F, F), F32),
            pltpu.SemaphoreType.DMA((3,)),
        ],
        compiler_params=params(16),
        cost_estimate=LIGHT,
        name="term_two",
    )(*in_hbm(grad_out, relu_mask, cheb_weight))


def local_kernel(
    first_ref, grad_hbm, mask_hbm, weight_hbm, h0, h1, h2, left_ref, right_ref, diff_ref, upper_ref, lower_ref,
    grad, mask, weight, bases, sems,
):
    sources = (grad_hbm, mask_hbm, weight_hbm, h0, h1, h2)
    copies = fetch(sources, (grad, mask, weight, bases.at[0], bases.at[1], bases.at[2]), sems)
    for copy in copies[:3]:
        copy.wait()
    masked = split(masked_of(grad[...], mask[...]))
    term = dot3(split(weight[1]), masked, ((1,), (1,)))
    left_ref[...] = term[:H]
    right_ref[...] = term[H:]
    diff_ref[...] = dot3(split(weight[0] - weight[2]), masked, ((1,), (1,)))
    for k in range(3):
        copies[3 + k].wait()
        part = dot3(split(bases[k]), masked, ((0,), (0,)))
        for j in range(2):
            place = k * F + j * H
            target = upper_ref if place < 3 * H else lower_ref
            target[place % (3 * H) : place % (3 * H) + H, :] = part[j * H : (j + 1) * H]


def local_terms(first, grad_out, relu_mask, cheb_weight, b0, b1, b2):
    half = jax.ShapeDtypeStruct((H, NODES_DEV), F32)
    part = jax.ShapeDtypeStruct((3 * H, F), F32)
    return pl.pallas_call(
        local_kernel,
        in_specs=[pl.BlockSpec(memory_space=pl.ANY)] + [HBM] * 6,
        out_specs=[VMEM] * 5,
        out_shape=[half, half, jax.ShapeDtypeStruct((F, NODES_DEV), F32), part, part],
        scratch_shapes=[
            pltpu.VMEM((NODES_DEV, F), F32),
            pltpu.VMEM((NODES_DEV, F), jnp.int32),
            pltpu.VMEM((3, F, F), F32),
            pltpu.VMEM((3, NODES_DEV, F), F32),
            pltpu.SemaphoreType.DMA((6,)),
        ],
        compiler_params=params(32),
        cost_estimate=LIGHT,
        name="local_terms",
    )(first, *in_hbm(grad_out, relu_mask, cheb_weight, b0, b1, b2))


def stacked(field):
    high, low = split(field)
    return jnp.concatenate([jnp.concatenate([x, x], axis=1) for x in (high, low)], axis=0)


def operator_kernel(n_col, origins, ids_ref, live_ref, rows_hbm, slots_hbm, values_ref, *refs):
    fields, refs = refs[: len(origins)], refs[len(origins) :]
    out_ref, total_ref, tiles, acc, lists, counts, rows, slots, sems, small_sems = refs
    origin = pl.program_id(0)
    size = TILES_DEV // GROUPS

    def copy(g):
        part = pl.ds(g * size, size)
        return pltpu.make_async_copy(values_ref.at[0, part], tiles.at[part], sems.at[g])

    @pl.when(origin == 0)
    def _():
        small = fetch((rows_hbm, slots_hbm), (rows, slots), small_sems)
        for g in range(GROUPS):
            copy(g).start()
        for s in range(n_col):
            counts[s] = 0
        for item in small:
            item.wait()

        def place(t, carry):
            row = rows[0, t]
            s = lax.rem(row // CHB - ids_ref[0] + n_col, n_col)
            position = slots[0, t] * CHB + lax.rem(row, CHB)
            n = counts[s]
            lists[s, n] = position * TILES_DEV + t
            counts[s] = n + 1
            return carry

        lax.fori_loop(0, live_ref[0], place, 0)

    acc[...] = jnp.zeros_like(acc)

    @pl.when(origin == 0)
    def _():
        for g in range(GROUPS):
            copy(g).wait()

    def add(n, carry):
        entry = lists[origin, n]
        position = entry // TILES_DEV
        slot = position // CHB
        at_row = pl.ds(pl.multiple_of(lax.rem(position, CHB) * TB, TB), TB)
        at_lane = pl.ds(pl.multiple_of(lax.rem(slot, 2) * TB, TB), TB)
        acc[slot // 2, at_row, at_lane] += tiles[lax.rem(entry, TILES_DEV)]
        return carry

    lax.fori_loop(0, counts[origin], add, 0)
    pairs = acc.shape[0]
    for p in range(pairs):
        high, low = split(acc[p])
        out_ref[0, p, :NODES_DEV, :] = high
        out_ref[0, p, NODES_DEV:, :] = low

    for k, field in zip(origins, fields):

        @pl.when(origin == k)
        def _():
            left = stacked(field[...])
            for p in range(pairs):
                part = jnp.dot(left, out_ref[0, p], preferred_element_type=F32)
                summed = part[:H] + part[H:]
                here = slice(p * WIDE, (p + 1) * WIDE)
                total_ref[:, here] = summed if k == 0 else total_ref[:, here] + summed


def build_operator(n_row, n_col, ids, live, rows, slots, values, pairs):
    part = (n_row // 2, 2 * NODES_DEV, WIDE)
    origins, fields = zip(*pairs)
    return pl.pallas_call(
        functools.partial(operator_kernel, n_col, origins),
        grid=(n_col,),
        in_specs=[SMEM] * 2 + [HBM] * 3 + [pl.BlockSpec((H, NODES_DEV), lambda s: (0, 0))] * len(fields),
        out_specs=[
            pl.BlockSpec((1,) + part, lambda s: (s, 0, 0, 0)),
            pl.BlockSpec((H, n_row * TB), lambda s: (0, 0)),
        ],
        out_shape=[pltpu.HBM((n_col,) + part, BF16), jax.ShapeDtypeStruct((H, n_row * TB), F32)],
        scratch_shapes=[
            pltpu.VMEM((TILES_DEV, TB, TB), F32),
            pltpu.VMEM((n_row // 2, NODES_DEV, WIDE), F32),
            pltpu.SMEM((n_col, TILES_DEV), jnp.int32),
            pltpu.SMEM((n_col,), jnp.int32),
            pltpu.SMEM((1, TILES_DEV), jnp.int32),
            pltpu.SMEM((1, TILES_DEV), jnp.int32),
            pltpu.SemaphoreType.DMA((GROUPS,)),
            pltpu.SemaphoreType.DMA((2,)),
        ],
        compiler_params=params(40),
        cost_estimate=HEAVY,
        name="operator",
    )(ids, live, *in_hbm(rows, slots, values), *fields)


def product_kernel(n_row, origins, has_prev, last, *refs):
    n = len(origins)
    op_ref, fields, refs = refs[0], refs[1 : 1 + n], refs[1 + n :]
    if has_prev:
        prev, refs = refs[0], refs[1:]
    out_ref, buf, sems = refs

    def copy(k, p):
        return pltpu.make_async_copy(op_ref.at[origins[k], p], buf.at[k, p], sems.at[k, p])

    for p in range(n_row // 2):
        for k in range(n):
            copy(k, p).start()
    left = [stacked(field[...]) for field in fields]
    for p in range(n_row // 2):
        here = slice(p * WIDE, (p + 1) * WIDE)
        total = None
        for k in range(n):
            copy(k, p).wait()
            part = jnp.dot(left[k], buf[k, p], preferred_element_type=F32)
            total = part if total is None else total + part
        summed = total[:H] + total[H:]
        if has_prev:
            summed = summed + prev[:, here]
        if last:
            out_ref[2 * p] = summed[:, :TB]
            out_ref[2 * p + 1] = summed[:, TB:]
        else:
            out_ref[:, here] = summed


def product(n_row, origins, operator, fields, prev, last):
    n = len(origins)
    has_prev = prev is not None
    return pl.pallas_call(
        functools.partial(product_kernel, n_row, origins, has_prev, last),
        in_specs=[HBM] + [VMEM] * (n + has_prev),
        out_specs=VMEM,
        out_shape=jax.ShapeDtypeStruct((n_row, H, TB) if last else (H, n_row * TB), F32),
        scratch_shapes=[
            pltpu.VMEM((n, n_row // 2, 2 * NODES_DEV, WIDE), BF16),
            pltpu.SemaphoreType.DMA((n, n_row // 2)),
        ],
        compiler_params=params(48),
        cost_estimate=LIGHT if last else HEAVY,
        name="product",
    )(*in_hbm(operator), *fields, *((prev,) if has_prev else ()))


def carry_kernel(n_row, owners_ref, base_ref, came_ref, out_ref):
    out_ref[...] = base_ref[...]
    for q in range(n_row):
        here = pl.ds(pl.multiple_of(owners_ref[q] * TB, TB), TB)
        out_ref[:, here] += 2.0 * came_ref[q]


def carry(n_row, owners, base, came):
    return pl.pallas_call(
        functools.partial(carry_kernel, n_row),
        in_specs=[SMEM, VMEM, VMEM],
        out_specs=VMEM,
        out_shape=jax.ShapeDtypeStruct((H, NODES_DEV), F32),
        compiler_params=params(24),
        cost_estimate=LIGHT,
        name="carry",
    )(owners, base, came)


def finish_kernel(n_row, owners_ref, base_ref, left_ref, right_ref, out_ref, total):
    total[...] = base_ref[...]
    for h, came in enumerate((left_ref, right_ref)):
        for q in range(n_row):
            here = pl.ds(pl.multiple_of(owners_ref[q] * TB, TB), TB)
            total[h * H : (h + 1) * H, here] += came[q]
    out_ref[...] = total[...].T


def finish(n_row, owners, base, left, right):
    return pl.pallas_call(
        functools.partial(finish_kernel, n_row),
        in_specs=[SMEM] + [VMEM] * 3,
        out_specs=VMEM,
        out_shape=jax.ShapeDtypeStruct((NODES_DEV, F), F32),
        scratch_shapes=[pltpu.VMEM((F, NODES_DEV), F32)],
        compiler_params=params(24),
        cost_estimate=LIGHT,
        name="finish",
    )(owners, base, left, right)


def shift(n_col, x, step):
    return lax.ppermute(x, "col", [(c, (c + step) % n_col) for c in range(n_col)])


def exchange(pieces):
    return lax.all_to_all(pieces, "row", split_axis=0, concat_axis=0, tiled=True)


def after(x, *others):
    return lax.optimization_barrier((x, *others))[0]


def opposite(field, below, above):
    col = lax.axis_index("col")
    sent = jnp.where(col == 1, above, jnp.where(col == 2, below, field))
    return lax.ppermute(sent, "col", [(1, 0), (2, 3), (3, 1), (0, 2)])


def gather(n_col, field, side):
    long = n_col // 2
    short = n_col - 1 - long
    ahead, behind = field, field
    steps = [[(0, field)]]
    for s in range(1, long + 1):
        if s == 2:
            ahead = after(ahead, behind)
        if s == 2 and n_col == 4:
            ahead = opposite(field, ahead, behind) if side > 0 else opposite(field, behind, ahead)
        else:
            ahead = shift(n_col, ahead, side)
        step = [((-side * s) % n_col, ahead)]
        if s <= short:
            behind = shift(n_col, behind, -side)
            step.append(((side * s) % n_col, behind))
        steps.append(step)
    return steps


def early(n_row, operator, steps, total=None, done=0):
    pairs = [pair for step in steps[:-1] for pair in step][done:]
    for begin in range(0, len(pairs), 3):
        origins, fields = zip(*pairs[begin : begin + 3])
        total = product(n_row, origins, operator, fields, total, False)
    return total


def final(n_row, operator, steps, total):
    origins, fields = zip(*steps[-1])
    return product(n_row, origins, operator, fields, total, True)


def per_device(
    grad_out,
    relu_mask,
    basis_zero,
    basis_one,
    basis_two,
    cheb_weight,
    tile_values,
    tile_rows,
    tile_slots,
    send_blocks,
    live_tiles,
):
    n_row = lax.axis_size("row")
    n_col = lax.axis_size("col")
    ids = lax.axis_index("col").astype(jnp.int32).reshape(1)
    owners = send_blocks.reshape(n_row)
    left, right = term_two(grad_out, relu_mask, cheb_weight)
    one_left, one_right, diff, upper, lower = local_terms(
        left, grad_out, relu_mask, cheb_weight, basis_zero, basis_one, basis_two
    )
    upper_sum, lower_sum = lax.psum(upper, ("row", "col")), lax.psum(lower, ("col", "row"))
    steps = gather(n_col, left, 1)
    first = steps[0] + steps[1] if len(steps) > 2 else steps[0]
    operator, left_early = build_operator(
        n_row, n_col, after(ids, upper), live_tiles, tile_rows, tile_slots, tile_values, first
    )
    common = (n_row, operator)

    left_early = early(*common, steps, left_early, len(first))
    right_steps = gather(n_col, after(right, left_early, steps[-1][0][1]), -1)
    left_came = exchange(final(*common, steps, left_early))
    right_early = early(*common, right_steps)

    left_carried = carry(n_row, owners, after(one_left, right_early, right_steps[-1][0][1]), left_came)
    steps = gather(n_col, left_carried, 1)
    right_came = exchange(final(*common, right_steps, right_early))
    left_early = early(*common, steps)

    right_carried = carry(n_row, owners, after(one_right, left_early, steps[-1][0][1]), right_came)
    right_steps = gather(n_col, right_carried, -1)
    left_came = exchange(final(*common, steps, left_early))
    right_early = early(*common, right_steps)

    right_last = final(*common, right_steps, right_early)
    right_came = exchange(right_last)
    weight_grad = jnp.concatenate([after(upper_sum, right_last), after(lower_sum, right_last)])
    return finish(n_row, owners, diff, left_came, right_came), weight_grad.reshape(3, F, F)


def solution(mesh):
    placed = (
        P(("row", "col"), None),
        P(("row", "col"), None),
        P(("row", "col"), None),
        P(("row", "col"), None),
        P(("row", "col"), None),
        P(),
        P(("row", "col"), None, None, None),
        P(("row", "col"), None),
        P(("row", "col"), None),
        P(("row", "col"), None, None),
        P(("row", "col")),
    )
    return jax.shard_map(
        per_device,
        mesh=mesh,
        in_specs=placed,
        out_specs=(P(("row", "col"), None), P()),
        check_vma=False,
    )
```

```python
import functools

import jax
import jax.numpy as jnp
from jax import lax
from jax.experimental import pallas as pl
from jax.experimental.pallas import tpu as pltpu
from jax.sharding import PartitionSpec as P

F = 256
H = 128
TB = 128
CHB = 4
WIDE = 2 * TB
LANES = 128
NODES_DEV = CHB * TB
TILES_DEV = 128
GROUPS = 8
MIB = 1 << 20
HEAVY = pl.CostEstimate(flops=1 << 34, bytes_accessed=64 * MIB, transcendentals=0)
LIGHT = pl.CostEstimate(flops=1024, bytes_accessed=1024, transcendentals=0)
BF16 = jnp.bfloat16
F32 = jnp.float32

SMEM = pl.BlockSpec(memory_space=pltpu.SMEM)
VMEM = pl.BlockSpec(memory_space=pltpu.VMEM)
HBM = pl.BlockSpec(memory_space=pltpu.HBM)


def params(mib):
    return pltpu.CompilerParams(vmem_limit_bytes=mib * MIB)


def in_hbm(*arrays):
    return [pltpu.with_memory_space_constraint(x, pltpu.HBM) for x in arrays]


def split(x):
    high = x.astype(BF16)
    low = (x - high.astype(F32)).astype(BF16)
    return high, low


def dot3(a, b, dims):
    ah, al = a
    bh, bl = b

    def one(x, y):
        return lax.dot_general(x, y, (dims, ((), ())), preferred_element_type=F32)

    return one(ah, bh) + (one(ah, bl) + one(al, bh))


def fetch(sources, targets, sems):
    copies = [pltpu.make_async_copy(a, b, sems.at[i]) for i, (a, b) in enumerate(zip(sources, targets))]
    for copy in copies:
        copy.start()
    return copies


def masked_of(grad, mask):
    return jnp.where(mask > 0, grad, jnp.zeros_like(grad))


def term_two_kernel(grad_hbm, mask_hbm, weight_hbm, left_ref, right_ref, grad, mask, weight, sems):
    for copy in fetch((grad_hbm, mask_hbm, weight_hbm.at[2]), (grad, mask, weight), sems):
        copy.wait()
    term = dot3(split(weight[...]), split(masked_of(grad[...], mask[...])), ((1,), (1,)))
    left_ref[...] = term[:H]
    right_ref[...] = term[H:]


def term_two(grad_out, relu_mask, cheb_weight):
    out = jax.ShapeDtypeStruct((H, NODES_DEV), F32)
    return pl.pallas_call(
        term_two_kernel,
        in_specs=[HBM] * 3,
        out_specs=[VMEM, VMEM],
        out_shape=[out, out],
        scratch_shapes=[
            pltpu.VMEM((NODES_DEV, F), F32),
            pltpu.VMEM((NODES_DEV, F), jnp.int32),
            pltpu.VMEM((F, F), F32),
            pltpu.SemaphoreType.DMA((3,)),
        ],
        compiler_params=params(16),
        cost_estimate=LIGHT,
        name="term_two",
    )(*in_hbm(grad_out, relu_mask, cheb_weight))


def local_kernel(
    n_row, first_ref, grad_hbm, mask_hbm, weight_hbm, h0, h1, h2, left_ref, right_ref, diff_ref, pieces_ref,
    grad, mask, weight, bases, sems,
):
    sources = (grad_hbm, mask_hbm, weight_hbm, h0, h1, h2)
    copies = fetch(sources, (grad, mask, weight, bases.at[0], bases.at[1], bases.at[2]), sems)
    for copy in copies[:3]:
        copy.wait()
    values = masked_of(grad[...], mask[...])
    masked = split(values)
    term = dot3(split(weight[1]), masked, ((1,), (1,)))
    left_ref[...] = term[:H]
    right_ref[...] = term[H:]
    diff_ref[...] = dot3(split(weight[0] - weight[2]), masked, ((1,), (1,)))
    turned = split(values.T)
    rows = F // n_row
    for k in range(3):
        copies[3 + k].wait()
        part = dot3(turned, split(bases[k]), ((1,), (0,)))
        for j in range(F // LANES):
            here = (k * (F // LANES) + j) * rows
            for q in range(n_row):
                pieces_ref[q, here : here + rows, :] = part[q * rows : (q + 1) * rows, j * LANES : (j + 1) * LANES]


def local_terms(n_row, first, grad_out, relu_mask, cheb_weight, b0, b1, b2):
    half = jax.ShapeDtypeStruct((H, NODES_DEV), F32)
    share = 3 * F * F // n_row // LANES
    return pl.pallas_call(
        functools.partial(local_kernel, n_row),
        in_specs=[pl.BlockSpec(memory_space=pl.ANY)] + [HBM] * 6,
        out_specs=[VMEM] * 4,
        out_shape=[
            half,
            half,
            jax.ShapeDtypeStruct((F, NODES_DEV), F32),
            jax.ShapeDtypeStruct((n_row, share, LANES), F32),
        ],
        scratch_shapes=[
            pltpu.VMEM((NODES_DEV, F), F32),
            pltpu.VMEM((NODES_DEV, F), jnp.int32),
            pltpu.VMEM((3, F, F), F32),
            pltpu.VMEM((3, NODES_DEV, F), F32),
            pltpu.SemaphoreType.DMA((6,)),
        ],
        compiler_params=params(32),
        cost_estimate=LIGHT,
        name="local_terms",
    )(first, *in_hbm(grad_out, relu_mask, cheb_weight, b0, b1, b2))


def stacked(field):
    high, low = split(field)
    return jnp.concatenate([jnp.concatenate([x, x], axis=1) for x in (high, low)], axis=0)


def operator_kernel(n_col, origins, ids_ref, live_ref, rows_hbm, slots_hbm, values_ref, *refs):
    fields, refs = refs[: len(origins)], refs[len(origins) :]
    out_ref, total_ref, tiles, acc, lists, counts, rows, slots, sems, small_sems = refs
    origin = pl.program_id(0)
    size = TILES_DEV // GROUPS

    def copy(g):
        part = pl.ds(g * size, size)
        return pltpu.make_async_copy(values_ref.at[0, part], tiles.at[part], sems.at[g])

    @pl.when(origin == 0)
    def _():
        small = fetch((rows_hbm, slots_hbm), (rows, slots), small_sems)
        for g in range(GROUPS):
            copy(g).start()
        for s in range(n_col):
            counts[s] = 0
        for item in small:
            item.wait()

        def place(t, carry):
            row = rows[0, t]
            s = lax.rem(row // CHB - ids_ref[0] + n_col, n_col)
            position = slots[0, t] * CHB + lax.rem(row, CHB)
            n = counts[s]
            lists[s, n] = position * TILES_DEV + t
            counts[s] = n + 1
            return carry

        lax.fori_loop(0, live_ref[0], place, 0)

    acc[...] = jnp.zeros_like(acc)

    @pl.when(origin == 0)
    def _():
        for g in range(GROUPS):
            copy(g).wait()

    def add(n, carry):
        entry = lists[origin, n]
        position = entry // TILES_DEV
        slot = position // CHB
        at_row = pl.ds(pl.multiple_of(lax.rem(position, CHB) * TB, TB), TB)
        at_lane = pl.ds(pl.multiple_of(lax.rem(slot, 2) * TB, TB), TB)
        acc[slot // 2, at_row, at_lane] += tiles[lax.rem(entry, TILES_DEV)]
        return carry

    lax.fori_loop(0, counts[origin], add, 0)
    pairs = acc.shape[0]
    for p in range(pairs):
        high, low = split(acc[p])
        out_ref[0, p, :NODES_DEV, :] = high
        out_ref[0, p, NODES_DEV:, :] = low

    for k, field in zip(origins, fields):

        @pl.when(origin == k)
        def _():
            left = stacked(field[...])
            for p in range(pairs):
                part = jnp.dot(left, out_ref[0, p], preferred_element_type=F32)
                summed = part[:H] + part[H:]
                here = slice(p * WIDE, (p + 1) * WIDE)
                total_ref[:, here] = summed if k == 0 else total_ref[:, here] + summed


def build_operator(n_row, n_col, ids, live, rows, slots, values, pairs):
    part = (n_row // 2, 2 * NODES_DEV, WIDE)
    origins, fields = zip(*pairs)
    return pl.pallas_call(
        functools.partial(operator_kernel, n_col, origins),
        grid=(n_col,),
        in_specs=[SMEM] * 2 + [HBM] * 3 + [pl.BlockSpec((H, NODES_DEV), lambda s: (0, 0))] * len(fields),
        out_specs=[
            pl.BlockSpec((1,) + part, lambda s: (s, 0, 0, 0)),
            pl.BlockSpec((H, n_row * TB), lambda s: (0, 0)),
        ],
        out_shape=[pltpu.HBM((n_col,) + part, BF16), jax.ShapeDtypeStruct((H, n_row * TB), F32)],
        scratch_shapes=[
            pltpu.VMEM((TILES_DEV, TB, TB), F32),
            pltpu.VMEM((n_row // 2, NODES_DEV, WIDE), F32),
            pltpu.SMEM((n_col, TILES_DEV), jnp.int32),
            pltpu.SMEM((n_col,), jnp.int32),
            pltpu.SMEM((1, TILES_DEV), jnp.int32),
            pltpu.SMEM((1, TILES_DEV), jnp.int32),
            pltpu.SemaphoreType.DMA((GROUPS,)),
            pltpu.SemaphoreType.DMA((2,)),
        ],
        compiler_params=params(40),
        cost_estimate=HEAVY,
        name="operator",
    )(ids, live, *in_hbm(rows, slots, values), *fields)


def product_kernel(n_row, n_col, origins, has_prev, last, n_carriers, *refs):
    n = len(origins)
    ids_ref, op_ref, refs = refs[0], refs[1], refs[2:]
    fields, refs = refs[:n], refs[n:]
    if has_prev:
        prev, refs = refs[0], refs[1:]
    carriers, refs = refs[:n_carriers], refs[n_carriers:]
    out_ref, buf, sems = refs[:3]

    def copy(k, p):
        return pltpu.make_async_copy(op_ref.at[origins[k], p], buf.at[k, p], sems.at[k, p])

    for p in range(n_row // 2):
        for k in range(n):
            copy(k, p).start()
    left = [stacked(field[:H, :]) for field in fields]
    if n_carriers:
        ordered = refs[3]
        for k in range(n_col):
            ordered[lax.rem(ids_ref[0] + k, n_col)] = carriers[k][H:, :]
        share = ordered[0]
        for k in range(1, n_col):
            share = share + ordered[k]
        rows = share.shape[0]
        groups = NODES_DEV // LANES // 2
        for j in range(groups):
            for q in range(n_row):
                from_lane = (q % 2 * groups + j) * LANES
                out_ref[q, H + j * rows : H + (j + 1) * rows, :] = share[:, from_lane : from_lane + LANES]
    for p in range(n_row // 2):
        here = slice(p * WIDE, (p + 1) * WIDE)
        total = None
        for k in range(n):
            copy(k, p).wait()
            part = jnp.dot(left[k], buf[k, p], preferred_element_type=F32)
            total = part if total is None else total + part
        summed = total[:H] + total[H:]
        if has_prev:
            summed = summed + prev[:, here]
        if last:
            out_ref[2 * p, :H, :] = summed[:, :TB]
            out_ref[2 * p + 1, :H, :] = summed[:, TB:]
        else:
            out_ref[:, here] = summed


def product(n_row, n_col, ids, origins, operator, fields, prev, last, carriers=()):
    n = len(origins)
    has_prev = prev is not None
    share = 0
    scratch = [
        pltpu.VMEM((n, n_row // 2, 2 * NODES_DEV, WIDE), BF16),
        pltpu.SemaphoreType.DMA((n, n_row // 2)),
    ]
    if carriers:
        rows = carriers[0].shape[0] - H
        share = rows * NODES_DEV // LANES // 2
        scratch.append(pltpu.VMEM((n_col, rows, NODES_DEV), F32))
    shape = (n_row, H + share, TB) if last else (H, n_row * TB)
    count = n + has_prev + len(carriers)
    return pl.pallas_call(
        functools.partial(product_kernel, n_row, n_col, origins, has_prev, last, len(carriers)),
        in_specs=[SMEM, HBM] + [VMEM] * count,
        out_specs=VMEM,
        out_shape=jax.ShapeDtypeStruct(shape, F32),
        scratch_shapes=scratch,
        compiler_params=params(48),
        cost_estimate=LIGHT if last else HEAVY,
        name="product",
    )(
        ids,
        *in_hbm(operator),
        *fields,
        *((prev,) if has_prev else ()),
        *carriers,
    )


def carry_kernel(n_row, rows, owners_ref, base_ref, came_ref, *refs):
    out_ref = refs[-1]
    out_ref[:H, :] = base_ref[...]
    for q in range(n_row):
        here = pl.ds(pl.multiple_of(owners_ref[q] * TB, TB), TB)
        out_ref[:H, here] += 2.0 * came_ref[q]
    if rows:
        pieces_ref = refs[0]
        share = pieces_ref[0]
        for q in range(1, n_row):
            share = share + pieces_ref[q]
        for j in range(NODES_DEV // LANES):
            out_ref[H:, j * LANES : (j + 1) * LANES] = share[j * rows : (j + 1) * rows, :]


def carry(n_row, owners, base, came, *pieces):
    rows = pieces[0].shape[1] * LANES // NODES_DEV if pieces else 0
    return pl.pallas_call(
        functools.partial(carry_kernel, n_row, rows),
        in_specs=[SMEM] + [VMEM] * (2 + len(pieces)),
        out_specs=VMEM,
        out_shape=jax.ShapeDtypeStruct((H + rows, NODES_DEV), F32),
        compiler_params=params(24),
        cost_estimate=LIGHT,
        name="carry",
    )(owners, base, came, *pieces)


def finish_kernel(n_row, owners_ref, base_ref, left_ref, right_ref, out_ref, total):
    total[...] = base_ref[...]
    for h, came in enumerate((left_ref, right_ref)):
        for q in range(n_row):
            here = pl.ds(pl.multiple_of(owners_ref[q] * TB, TB), TB)
            total[h * H : (h + 1) * H, here] += came[q, :H, :]
    out_ref[...] = total[...].T


def finish(n_row, owners, base, left, right):
    return pl.pallas_call(
        functools.partial(finish_kernel, n_row),
        in_specs=[SMEM] + [VMEM] * 3,
        out_specs=VMEM,
        out_shape=jax.ShapeDtypeStruct((NODES_DEV, F), F32),
        scratch_shapes=[pltpu.VMEM((F, NODES_DEV), F32)],
        compiler_params=params(24),
        cost_estimate=LIGHT,
        name="finish",
    )(owners, base, left, right)


def assemble_kernel(n_row, row_ref, own_ref, other_ref, out_ref, halves, turned):
    rows = F // n_row
    half = lax.rem(row_ref[0], 2)
    halves[half] = own_ref[:, H:, :]
    halves[1 - half] = other_ref[:, H:, :]
    groups = 3 * F // LANES // 2
    for q in range(n_row):
        for j in range(2 * groups):
            here = slice(j % groups * rows, (j % groups + 1) * rows)
            turned[q * rows : (q + 1) * rows, j * LANES : (j + 1) * LANES] = halves[j // groups, q, here, :]
    for k in range(3):
        out_ref[k] = turned[:, k * F : (k + 1) * F].T


def assemble(n_row, row, own, other):
    return pl.pallas_call(
        functools.partial(assemble_kernel, n_row),
        in_specs=[SMEM, VMEM, VMEM],
        out_specs=VMEM,
        out_shape=jax.ShapeDtypeStruct((3, F, F), F32),
        scratch_shapes=[
            pltpu.VMEM((2, n_row, own.shape[1] - H, LANES), F32),
            pltpu.VMEM((F, 3 * F), F32),
        ],
        compiler_params=params(16),
        cost_estimate=LIGHT,
        name="assemble",
    )(row, own, other)


def shift(n_col, x, step):
    return lax.ppermute(x, "col", [(c, (c + step) % n_col) for c in range(n_col)])


def exchange(pieces):
    return lax.all_to_all(pieces, "row", split_axis=0, concat_axis=0, tiled=True)


def after(x, *others):
    return lax.optimization_barrier((x, *others))[0]


def opposite(field, below, above):
    col = lax.axis_index("col")
    sent = jnp.where(col == 1, above, jnp.where(col == 2, below, field))
    return lax.ppermute(sent, "col", [(1, 0), (2, 3), (3, 1), (0, 2)])


def gather(n_col, field, side):
    long = n_col // 2
    short = n_col - 1 - long
    ahead, behind = field, field
    steps = [[(0, field)]]
    for s in range(1, long + 1):
        if s == 2:
            ahead = after(ahead, behind)
        if s == 2 and n_col == 4:
            ahead = opposite(field, ahead, behind) if side > 0 else opposite(field, behind, ahead)
        else:
            ahead = shift(n_col, ahead, side)
        step = [((-side * s) % n_col, ahead)]
        if s <= short:
            behind = shift(n_col, behind, -side)
            step.append(((side * s) % n_col, behind))
        steps.append(step)
    return steps


def early(n_row, n_col, ids, operator, steps, total=None, done=0):
    pairs = [pair for step in steps[:-1] for pair in step][done:]
    for begin in range(0, len(pairs), 3):
        origins, fields = zip(*pairs[begin : begin + 3])
        total = product(n_row, n_col, ids, origins, operator, fields, total, False)
    return total


def final(n_row, n_col, ids, operator, steps, total, carrying=False):
    origins, fields = zip(*steps[-1])
    carriers = [x for _, x in sorted((p for step in steps for p in step), key=lambda p: p[0])] if carrying else ()
    return product(n_row, n_col, ids, origins, operator, fields, total, True, carriers)


def per_device(
    grad_out,
    relu_mask,
    basis_zero,
    basis_one,
    basis_two,
    cheb_weight,
    tile_values,
    tile_rows,
    tile_slots,
    send_blocks,
    live_tiles,
):
    n_row = lax.axis_size("row")
    n_col = lax.axis_size("col")
    ids = lax.axis_index("col").astype(jnp.int32).reshape(1)
    owners = send_blocks.reshape(n_row)
    left, right = term_two(grad_out, relu_mask, cheb_weight)
    one_left, one_right, diff, pieces = local_terms(
        n_row, left, grad_out, relu_mask, cheb_weight, basis_zero, basis_one, basis_two
    )
    steps = gather(n_col, left, 1)
    first = steps[0] + steps[1] if len(steps) > 2 else steps[0]
    operator, left_early = build_operator(
        n_row, n_col, ids, live_tiles, tile_rows, tile_slots, tile_values, first
    )
    pieces = exchange(pieces)
    common = (n_row, n_col, ids, operator)

    left_early = early(*common, steps, left_early, len(first))
    right_steps = gather(n_col, after(right, left_early, steps[-1][0][1]), -1)
    left_came = exchange(final(*common, steps, after(left_early, pieces)))
    right_early = early(*common, right_steps)

    left_carried = carry(n_row, owners, after(one_left, right_early, right_steps[-1][0][1]), left_came, pieces)
    steps = gather(n_col, left_carried, 1)
    right_came = exchange(final(*common, right_steps, right_early))
    left_early = early(*common, steps)

    right_carried = carry(n_row, owners, after(one_right, left_early, steps[-1][0][1]), right_came)
    right_steps = gather(n_col, right_carried, -1)
    left_came = exchange(final(*common, steps, left_early, carrying=True))
    right_early = early(*common, right_steps)

    right_came = exchange(final(*common, right_steps, right_early))
    other = lax.ppermute(left_came, "row", [(r, r ^ 1) for r in range(n_row)])
    row = lax.axis_index("row").astype(jnp.int32).reshape(1)
    weight_grad = assemble(n_row, row, left_came, other)
    return finish(n_row, owners, after(diff, weight_grad), left_came, right_came), weight_grad


def solution(mesh):
    placed = (
        P(("row", "col"), None),
        P(("row", "col"), None),
        P(("row", "col"), None),
        P(("row", "col"), None),
        P(("row", "col"), None),
        P(),
        P(("row", "col"), None, None, None),
        P(("row", "col"), None),
        P(("row", "col"), None),
        P(("row", "col"), None, None),
        P(("row", "col")),
    )
    return jax.shard_map(
        per_device,
        mesh=mesh,
        in_specs=placed,
        out_specs=(P(("row", "col"), None), P()),
        check_vma=False,
    )
```

```python
import functools

import jax
import jax.numpy as jnp
from jax import lax
from jax.experimental import pallas as pl
from jax.experimental.pallas import tpu as pltpu
from jax.sharding import PartitionSpec as P

F = 256
H = 128
TB = 128
CHB = 4
WIDE = 2 * TB
LANES = 128
NODES_DEV = CHB * TB
TILES_DEV = 128
GROUPS = 8
MIB = 1 << 20
HEAVY = pl.CostEstimate(flops=1 << 34, bytes_accessed=64 * MIB, transcendentals=0)
LIGHT = pl.CostEstimate(flops=1024, bytes_accessed=1024, transcendentals=0)
BF16 = jnp.bfloat16
F32 = jnp.float32

SMEM = pl.BlockSpec(memory_space=pltpu.SMEM)
VMEM = pl.BlockSpec(memory_space=pltpu.VMEM)
HBM = pl.BlockSpec(memory_space=pltpu.HBM)
ANY = pl.BlockSpec(memory_space=pl.ANY)


def params(mib):
    return pltpu.CompilerParams(vmem_limit_bytes=mib * MIB)


def in_hbm(*arrays):
    return [pltpu.with_memory_space_constraint(x, pltpu.HBM) for x in arrays]


def split(x):
    high = x.astype(BF16)
    low = (x - high.astype(F32)).astype(BF16)
    return high, low


def dot3(a, b, dims):
    ah, al = a
    bh, bl = b

    def one(x, y):
        return lax.dot_general(x, y, (dims, ((), ())), preferred_element_type=F32)

    return one(ah, bh) + (one(ah, bl) + one(al, bh))


def fetch(sources, targets, sems):
    copies = [pltpu.make_async_copy(a, b, sems.at[i]) for i, (a, b) in enumerate(zip(sources, targets))]
    for copy in copies:
        copy.start()
    return copies


def masked_of(grad, mask):
    return jnp.where(mask > 0, grad, jnp.zeros_like(grad))


def term_two_kernel(grad_hbm, mask_hbm, weight_hbm, left_ref, right_ref, grad, mask, weight, sems):
    for copy in fetch((grad_hbm, mask_hbm, weight_hbm.at[2]), (grad, mask, weight), sems):
        copy.wait()
    term = dot3(split(weight[...]), split(masked_of(grad[...], mask[...])), ((1,), (1,)))
    left_ref[...] = term[:H]
    right_ref[...] = term[H:]


def term_two(grad_out, relu_mask, cheb_weight):
    out = jax.ShapeDtypeStruct((H, NODES_DEV), F32)
    return pl.pallas_call(
        term_two_kernel,
        in_specs=[HBM] * 3,
        out_specs=[VMEM, VMEM],
        out_shape=[out, out],
        scratch_shapes=[
            pltpu.VMEM((NODES_DEV, F), F32),
            pltpu.VMEM((NODES_DEV, F), jnp.int32),
            pltpu.VMEM((F, F), F32),
            pltpu.SemaphoreType.DMA((3,)),
        ],
        compiler_params=params(16),
        cost_estimate=LIGHT,
        name="term_two",
    )(*in_hbm(grad_out, relu_mask, cheb_weight))


def local_kernel(
    n_row, first_ref, grad_hbm, mask_hbm, weight_hbm, h0, h1, h2, left_hbm, right_hbm, diff_ref, pieces_ref,
    grad, mask, weight, bases, one, sems, one_sems,
):
    sources = (grad_hbm, mask_hbm, weight_hbm, h0, h1, h2)
    copies = fetch(sources, (grad, mask, weight, bases.at[0], bases.at[1], bases.at[2]), sems)
    for copy in copies[:3]:
        copy.wait()
    values = masked_of(grad[...], mask[...])
    masked = split(values)
    term = dot3(split(weight[1]), masked, ((1,), (1,)))
    one[...] = term
    one_copies = fetch((one.at[pl.ds(0, H)], one.at[pl.ds(H, H)]), (left_hbm, right_hbm), one_sems)
    diff_ref[...] = dot3(split(weight[0] - weight[2]), masked, ((1,), (1,)))
    turned = split(values.T)
    rows = F // n_row
    for k in range(3):
        copies[3 + k].wait()
        part = dot3(turned, split(bases[k]), ((1,), (0,)))
        for j in range(F // LANES):
            here = (k * (F // LANES) + j) * rows
            for q in range(n_row):
                pieces_ref[q, here : here + rows, :] = part[q * rows : (q + 1) * rows, j * LANES : (j + 1) * LANES]
    for copy in one_copies:
        copy.wait()


def local_terms(n_row, first, grad_out, relu_mask, cheb_weight, b0, b1, b2):
    half = pltpu.HBM((H, NODES_DEV), F32)
    share = 3 * F * F // n_row // LANES
    return pl.pallas_call(
        functools.partial(local_kernel, n_row),
        in_specs=[ANY] + [HBM] * 6,
        out_specs=[HBM, HBM, VMEM, VMEM],
        out_shape=[
            half,
            half,
            jax.ShapeDtypeStruct((F, NODES_DEV), F32),
            jax.ShapeDtypeStruct((n_row, share, LANES), F32),
        ],
        scratch_shapes=[
            pltpu.VMEM((NODES_DEV, F), F32),
            pltpu.VMEM((NODES_DEV, F), jnp.int32),
            pltpu.VMEM((3, F, F), F32),
            pltpu.VMEM((3, NODES_DEV, F), F32),
            pltpu.VMEM((F, NODES_DEV), F32),
            pltpu.SemaphoreType.DMA((6,)),
            pltpu.SemaphoreType.DMA((2,)),
        ],
        compiler_params=params(32),
        cost_estimate=LIGHT,
        name="local_terms",
    )(first, *in_hbm(grad_out, relu_mask, cheb_weight, b0, b1, b2))


def stacked(field):
    high, low = split(field)
    return jnp.concatenate([jnp.concatenate([x, x], axis=1) for x in (high, low)], axis=0)


def operator_kernel(n_col, origins, ids_ref, live_ref, rows_hbm, slots_hbm, values_ref, *refs):
    fields, refs = refs[: len(origins)], refs[len(origins) :]
    out_ref, total_ref, tiles, acc, lists, counts, rows, slots, sems, small_sems = refs
    origin = pl.program_id(0)
    size = TILES_DEV // GROUPS

    def copy(g):
        part = pl.ds(g * size, size)
        return pltpu.make_async_copy(values_ref.at[0, part], tiles.at[part], sems.at[g])

    @pl.when(origin == 0)
    def _():
        small = fetch((rows_hbm, slots_hbm), (rows, slots), small_sems)
        for g in range(GROUPS):
            copy(g).start()
        for s in range(n_col):
            counts[s] = 0
        for item in small:
            item.wait()

        def place(t, carry):
            row = rows[0, t]
            s = lax.rem(row // CHB - ids_ref[0] + n_col, n_col)
            position = slots[0, t] * CHB + lax.rem(row, CHB)
            n = counts[s]
            lists[s, n] = position * TILES_DEV + t
            counts[s] = n + 1
            return carry

        lax.fori_loop(0, live_ref[0], place, 0)

    acc[...] = jnp.zeros_like(acc)

    @pl.when(origin == 0)
    def _():
        for g in range(GROUPS):
            copy(g).wait()

    def add(n, carry):
        entry = lists[origin, n]
        position = entry // TILES_DEV
        slot = position // CHB
        at_row = pl.ds(pl.multiple_of(lax.rem(position, CHB) * TB, TB), TB)
        at_lane = pl.ds(pl.multiple_of(lax.rem(slot, 2) * TB, TB), TB)
        acc[slot // 2, at_row, at_lane] += tiles[lax.rem(entry, TILES_DEV)]
        return carry

    lax.fori_loop(0, counts[origin], add, 0)
    pairs = acc.shape[0]
    for p in range(pairs):
        high, low = split(acc[p])
        out_ref[0, p, :NODES_DEV, :] = high
        out_ref[0, p, NODES_DEV:, :] = low

    for k, field in zip(origins, fields):

        @pl.when(origin == k)
        def _():
            left = stacked(field[...])
            for p in range(pairs):
                part = jnp.dot(left, out_ref[0, p], preferred_element_type=F32)
                summed = part[:H] + part[H:]
                here = slice(p * WIDE, (p + 1) * WIDE)
                total_ref[:, here] = summed if k == 0 else total_ref[:, here] + summed


def build_operator(n_row, n_col, ids, live, rows, slots, values, pairs):
    part = (n_row // 2, 2 * NODES_DEV, WIDE)
    origins, fields = zip(*pairs)
    return pl.pallas_call(
        functools.partial(operator_kernel, n_col, origins),
        grid=(n_col,),
        in_specs=[SMEM] * 2 + [HBM] * 3 + [pl.BlockSpec((H, NODES_DEV), lambda s: (0, 0))] * len(fields),
        out_specs=[
            pl.BlockSpec((1,) + part, lambda s: (s, 0, 0, 0)),
            pl.BlockSpec((H, n_row * TB), lambda s: (0, 0)),
        ],
        out_shape=[pltpu.HBM((n_col,) + part, BF16), jax.ShapeDtypeStruct((H, n_row * TB), F32)],
        scratch_shapes=[
            pltpu.VMEM((TILES_DEV, TB, TB), F32),
            pltpu.VMEM((n_row // 2, NODES_DEV, WIDE), F32),
            pltpu.SMEM((n_col, TILES_DEV), jnp.int32),
            pltpu.SMEM((n_col,), jnp.int32),
            pltpu.SMEM((1, TILES_DEV), jnp.int32),
            pltpu.SMEM((1, TILES_DEV), jnp.int32),
            pltpu.SemaphoreType.DMA((GROUPS,)),
            pltpu.SemaphoreType.DMA((2,)),
        ],
        compiler_params=params(40),
        cost_estimate=HEAVY,
        name="operator",
    )(ids, live, *in_hbm(rows, slots, values), *fields)


def product_kernel(n_row, n_col, origins, has_prev, last, n_carriers, *refs):
    n = len(origins)
    ids_ref, op_ref, refs = refs[0], refs[1], refs[2:]
    fields, refs = refs[:n], refs[n:]
    if has_prev:
        prev, refs = refs[0], refs[1:]
    carriers, refs = refs[:n_carriers], refs[n_carriers:]
    out_ref, held, buf, field_sems, sems = refs[:5]

    def copy(k, p):
        return pltpu.make_async_copy(op_ref.at[origins[k], p], buf.at[k, p], sems.at[k, p])

    field_copies = fetch([x.at[pl.ds(0, H)] for x in fields], [held.at[k] for k in range(n)], field_sems)
    for p in range(n_row // 2):
        for k in range(n):
            copy(k, p).start()
    left = []
    for k in range(n):
        field_copies[k].wait()
        left.append(stacked(held[k]))
    if n_carriers:
        ordered = refs[5]
        for k in range(n_col):
            ordered[lax.rem(ids_ref[0] + k, n_col)] = carriers[k][H:, :]
        share = ordered[0]
        for k in range(1, n_col):
            share = share + ordered[k]
        rows = share.shape[0]
        groups = NODES_DEV // LANES // 2
        for j in range(groups):
            for q in range(n_row):
                from_lane = (q % 2 * groups + j) * LANES
                out_ref[q, H + j * rows : H + (j + 1) * rows, :] = share[:, from_lane : from_lane + LANES]
    for p in range(n_row // 2):
        here = slice(p * WIDE, (p + 1) * WIDE)
        total = None
        for k in range(n):
            copy(k, p).wait()
            part = jnp.dot(left[k], buf[k, p], preferred_element_type=F32)
            total = part if total is None else total + part
        summed = total[:H] + total[H:]
        if has_prev:
            summed = summed + prev[:, here]
        if last:
            out_ref[2 * p, :H, :] = summed[:, :TB]
            out_ref[2 * p + 1, :H, :] = summed[:, TB:]
        else:
            out_ref[:, here] = summed


def product(n_row, n_col, ids, origins, operator, fields, prev, last, carriers=()):
    n = len(origins)
    has_prev = prev is not None
    share = 0
    scratch = [
        pltpu.VMEM((n, H, NODES_DEV), F32),
        pltpu.VMEM((n, n_row // 2, 2 * NODES_DEV, WIDE), BF16),
        pltpu.SemaphoreType.DMA((n,)),
        pltpu.SemaphoreType.DMA((n, n_row // 2)),
    ]
    if carriers:
        rows = carriers[0].shape[0] - H
        share = rows * NODES_DEV // LANES // 2
        scratch.append(pltpu.VMEM((n_col, rows, NODES_DEV), F32))
    shape = (n_row, H + share, TB) if last else (H, n_row * TB)
    count = has_prev + len(carriers)
    return pl.pallas_call(
        functools.partial(product_kernel, n_row, n_col, origins, has_prev, last, len(carriers)),
        in_specs=[SMEM, HBM] + [ANY] * n + [VMEM] * count,
        out_specs=VMEM,
        out_shape=jax.ShapeDtypeStruct(shape, F32),
        scratch_shapes=scratch,
        compiler_params=params(48),
        cost_estimate=LIGHT if last else HEAVY,
        name="product",
    )(
        ids,
        *in_hbm(operator),
        *fields,
        *((prev,) if has_prev else ()),
        *carriers,
    )


def carry_kernel(n_row, rows, owners_ref, base_hbm, came_ref, *refs):
    out_ref, base, sems = refs[-3:]
    (base_copy,) = fetch([base_hbm], [base], sems)
    out_ref[:H, :] = jnp.zeros((H, NODES_DEV), F32)
    for q in range(n_row):
        here = pl.ds(pl.multiple_of(owners_ref[q] * TB, TB), TB)
        out_ref[:H, here] += came_ref[q]
    if rows:
        pieces_ref = refs[0]
        share = pieces_ref[0]
        for q in range(1, n_row):
            share = share + pieces_ref[q]
        for j in range(NODES_DEV // LANES):
            out_ref[H:, j * LANES : (j + 1) * LANES] = share[j * rows : (j + 1) * rows, :]
    base_copy.wait()
    out_ref[:H, :] = base[...] + 2.0 * out_ref[:H, :]


def carry(n_row, owners, base, came, *pieces):
    rows = pieces[0].shape[1] * LANES // NODES_DEV if pieces else 0
    return pl.pallas_call(
        functools.partial(carry_kernel, n_row, rows),
        in_specs=[SMEM, HBM] + [VMEM] * (1 + len(pieces)),
        out_specs=VMEM,
        out_shape=jax.ShapeDtypeStruct((H + rows, NODES_DEV), F32),
        scratch_shapes=[pltpu.VMEM((H, NODES_DEV), F32), pltpu.SemaphoreType.DMA((1,))],
        compiler_params=params(24),
        cost_estimate=LIGHT,
        name="carry",
    )(owners, *in_hbm(base), came, *pieces)


def finish_kernel(n_row, owners_ref, base_ref, left_ref, right_ref, out_ref, total):
    total[...] = base_ref[...]
    for h, came in enumerate((left_ref, right_ref)):
        for q in range(n_row):
            here = pl.ds(pl.multiple_of(owners_ref[q] * TB, TB), TB)
            total[h * H : (h + 1) * H, here] += came[q, :H, :]
    out_ref[...] = total[...].T


def finish(n_row, owners, base, left, right):
    return pl.pallas_call(
        functools.partial(finish_kernel, n_row),
        in_specs=[SMEM] + [VMEM] * 3,
        out_specs=VMEM,
        out_shape=jax.ShapeDtypeStruct((NODES_DEV, F), F32),
        scratch_shapes=[pltpu.VMEM((F, NODES_DEV), F32)],
        compiler_params=params(24),
        cost_estimate=LIGHT,
        name="finish",
    )(owners, base, left, right)


def assemble_kernel(n_row, row_ref, own_ref, other_ref, out_ref, halves, turned):
    rows = F // n_row
    half = lax.rem(row_ref[0], 2)
    halves[half] = own_ref[:, H:, :]
    halves[1 - half] = other_ref[:, H:, :]
    groups = 3 * F // LANES // 2
    for q in range(n_row):
        for j in range(2 * groups):
            here = slice(j % groups * rows, (j % groups + 1) * rows)
            turned[q * rows : (q + 1) * rows, j * LANES : (j + 1) * LANES] = halves[j // groups, q, here, :]
    for k in range(3):
        out_ref[k] = turned[:, k * F : (k + 1) * F].T


def assemble(n_row, row, own, other):
    return pl.pallas_call(
        functools.partial(assemble_kernel, n_row),
        in_specs=[SMEM, VMEM, VMEM],
        out_specs=VMEM,
        out_shape=jax.ShapeDtypeStruct((3, F, F), F32),
        scratch_shapes=[
            pltpu.VMEM((2, n_row, own.shape[1] - H, LANES), F32),
            pltpu.VMEM((F, 3 * F), F32),
        ],
        compiler_params=params(16),
        cost_estimate=LIGHT,
        name="assemble",
    )(row, own, other)


def shift(n_col, x, step):
    return lax.ppermute(x, "col", [(c, (c + step) % n_col) for c in range(n_col)])


def exchange(pieces):
    return lax.all_to_all(pieces, "row", split_axis=0, concat_axis=0, tiled=True)


def after(x, *others):
    return lax.optimization_barrier((x, *others))[0]


def opposite(field, below, above):
    col = lax.axis_index("col")
    sent = jnp.where(col == 1, above, jnp.where(col == 2, below, field))
    return lax.ppermute(sent, "col", [(1, 0), (2, 3), (3, 1), (0, 2)])


def gather(n_col, field, side):
    long = n_col // 2
    short = n_col - 1 - long
    ahead, behind = field, field
    steps = [[(0, field)]]
    for s in range(1, long + 1):
        if s == 2:
            ahead = after(ahead, behind)
        if s == 2 and n_col == 4:
            ahead = opposite(field, ahead, behind) if side > 0 else opposite(field, behind, ahead)
        else:
            ahead = shift(n_col, ahead, side)
        step = [((-side * s) % n_col, ahead)]
        if s <= short:
            behind = shift(n_col, behind, -side)
            step.append(((side * s) % n_col, behind))
        steps.append(step)
    return steps


def early(n_row, n_col, ids, operator, steps, total=None, done=0):
    pairs = [pair for step in steps[:-1] for pair in step][done:]
    for begin in range(0, len(pairs), 3):
        origins, fields = zip(*pairs[begin : begin + 3])
        total = product(n_row, n_col, ids, origins, operator, fields, total, False)
    return total


def final(n_row, n_col, ids, operator, steps, total, carrying=False):
    origins, fields = zip(*steps[-1])
    carriers = [x for _, x in sorted((p for step in steps for p in step), key=lambda p: p[0])] if carrying else ()
    return product(n_row, n_col, ids, origins, operator, fields, total, True, carriers)


def per_device(
    grad_out,
    relu_mask,
    basis_zero,
    basis_one,
    basis_two,
    cheb_weight,
    tile_values,
    tile_rows,
    tile_slots,
    send_blocks,
    live_tiles,
):
    n_row = lax.axis_size("row")
    n_col = lax.axis_size("col")
    ids = lax.axis_index("col").astype(jnp.int32).reshape(1)
    owners = send_blocks.reshape(n_row)
    left, right = term_two(grad_out, relu_mask, cheb_weight)
    one_left, one_right, diff, pieces = local_terms(
        n_row, left, grad_out, relu_mask, cheb_weight, basis_zero, basis_one, basis_two
    )
    steps = gather(n_col, left, 1)
    first = steps[0] + steps[1] if len(steps) > 2 else steps[0]
    operator, left_early = build_operator(
        n_row, n_col, ids, live_tiles, tile_rows, tile_slots, tile_values, first
    )
    pieces = exchange(pieces)
    common = (n_row, n_col, ids, operator)

    left_early = early(*common, steps, left_early, len(first))
    right_steps = gather(n_col, after(right, left_early, steps[-1][0][1]), -1)
    left_came = exchange(final(*common, steps, after(left_early, pieces)))
    right_early = early(*common, right_steps)

    left_carried = carry(n_row, owners, after(one_left, right_early, right_steps[-1][0][1]), left_came, pieces)
    steps = gather(n_col, left_carried, 1)
    right_came = exchange(final(*common, right_steps, right_early))
    left_early = early(*common, steps)

    right_carried = carry(n_row, owners, after(one_right, left_early, steps[-1][0][1]), right_came)
    right_steps = gather(n_col, right_carried, -1)
    left_came = exchange(final(*common, steps, left_early, carrying=True))
    right_early = early(*common, right_steps)

    right_last = final(*common, right_steps, right_early)
    right_came = exchange(right_last)
    other = lax.ppermute(after(left_came, right_last), "row", [(r, r ^ 1) for r in range(n_row)])
    row = lax.axis_index("row").astype(jnp.int32).reshape(1)
    weight_grad = assemble(n_row, row, left_came, other)
    return finish(n_row, owners, after(diff, weight_grad), left_came, right_came), weight_grad


def solution(mesh):
    placed = (
        P(("row", "col"), None),
        P(("row", "col"), None),
        P(("row", "col"), None),
        P(("row", "col"), None),
        P(("row", "col"), None),
        P(),
        P(("row", "col"), None, None, None),
        P(("row", "col"), None),
        P(("row", "col"), None),
        P(("row", "col"), None, None),
        P(("row", "col")),
    )
    return jax.shard_map(
        per_device,
        mesh=mesh,
        in_specs=placed,
        out_specs=(P(("row", "col"), None), P()),
        check_vma=False,
    )
```

```python
import functools

import jax
import jax.numpy as jnp
from jax import lax
from jax.experimental import pallas as pl
from jax.experimental.pallas import tpu as pltpu
from jax.sharding import PartitionSpec as P

F = 256
H = 128
TB = 128
CHB = 4
WIDE = 2 * TB
LANES = 128
NODES_DEV = CHB * TB
TILES_DEV = 128
GROUPS = 8
MIB = 1 << 20
HEAVY = pl.CostEstimate(flops=1 << 34, bytes_accessed=64 * MIB, transcendentals=0)
LIGHT = pl.CostEstimate(flops=1024, bytes_accessed=1024, transcendentals=0)
BF16 = jnp.bfloat16
F32 = jnp.float32

SMEM = pl.BlockSpec(memory_space=pltpu.SMEM)
VMEM = pl.BlockSpec(memory_space=pltpu.VMEM)
HBM = pl.BlockSpec(memory_space=pltpu.HBM)
ANY = pl.BlockSpec(memory_space=pl.ANY)


def params(mib):
    return pltpu.CompilerParams(vmem_limit_bytes=mib * MIB)


def in_hbm(*arrays):
    return [pltpu.with_memory_space_constraint(x, pltpu.HBM) for x in arrays]


def split(x):
    high = x.astype(BF16)
    low = (x - high.astype(F32)).astype(BF16)
    return high, low


def dot3(a, b, dims):
    ah, al = a
    bh, bl = b

    def one(x, y):
        return lax.dot_general(x, y, (dims, ((), ())), preferred_element_type=F32)

    return one(ah, bh) + (one(ah, bl) + one(al, bh))


def fetch(sources, targets, sems):
    copies = [pltpu.make_async_copy(a, b, sems.at[i]) for i, (a, b) in enumerate(zip(sources, targets))]
    for copy in copies:
        copy.start()
    return copies


def masked_of(grad, mask):
    return jnp.where(mask > 0, grad, jnp.zeros_like(grad))


def term_two_kernel(grad_hbm, mask_hbm, weight_hbm, left_ref, right_ref, grad, mask, weight, sems):
    for copy in fetch((grad_hbm, mask_hbm, weight_hbm.at[2]), (grad, mask, weight), sems):
        copy.wait()
    term = dot3(split(weight[...]), split(masked_of(grad[...], mask[...])), ((1,), (1,)))
    left_ref[...] = term[:H]
    right_ref[...] = term[H:]


def term_two(grad_out, relu_mask, cheb_weight):
    out = jax.ShapeDtypeStruct((H, NODES_DEV), F32)
    return pl.pallas_call(
        term_two_kernel,
        in_specs=[HBM] * 3,
        out_specs=[VMEM, VMEM],
        out_shape=[out, out],
        scratch_shapes=[
            pltpu.VMEM((NODES_DEV, F), F32),
            pltpu.VMEM((NODES_DEV, F), jnp.int32),
            pltpu.VMEM((F, F), F32),
            pltpu.SemaphoreType.DMA((3,)),
        ],
        compiler_params=params(16),
        cost_estimate=LIGHT,
        name="term_two",
    )(*in_hbm(grad_out, relu_mask, cheb_weight))


def local_kernel(
    n_row, first_ref, grad_hbm, mask_hbm, weight_hbm, h0, h1, h2, left_hbm, right_hbm, diff_ref, pieces_ref,
    grad, mask, weight, bases, one, sems, one_sems,
):
    sources = (grad_hbm, mask_hbm, weight_hbm, h0, h1, h2)
    copies = fetch(sources, (grad, mask, weight, bases.at[0], bases.at[1], bases.at[2]), sems)
    for copy in copies[:3]:
        copy.wait()
    values = masked_of(grad[...], mask[...])
    masked = split(values)
    term = dot3(split(weight[1]), masked, ((1,), (1,)))
    one[...] = term
    one_copies = fetch((one.at[pl.ds(0, H)], one.at[pl.ds(H, H)]), (left_hbm, right_hbm), one_sems)
    diff_ref[...] = dot3(split(weight[0] - weight[2]), masked, ((1,), (1,)))
    turned = split(values.T)
    rows = F // n_row
    for k in range(3):
        copies[3 + k].wait()
        part = dot3(turned, split(bases[k]), ((1,), (0,)))
        for j in range(F // LANES):
            here = (k * (F // LANES) + j) * rows
            for q in range(n_row):
                pieces_ref[q, here : here + rows, :] = part[q * rows : (q + 1) * rows, j * LANES : (j + 1) * LANES]
    for copy in one_copies:
        copy.wait()


def local_terms(n_row, first, grad_out, relu_mask, cheb_weight, b0, b1, b2):
    half = pltpu.HBM((H, NODES_DEV), F32)
    share = 3 * F * F // n_row // LANES
    return pl.pallas_call(
        functools.partial(local_kernel, n_row),
        in_specs=[ANY] + [HBM] * 6,
        out_specs=[HBM, HBM, VMEM, VMEM],
        out_shape=[
            half,
            half,
            jax.ShapeDtypeStruct((F, NODES_DEV), F32),
            jax.ShapeDtypeStruct((n_row, share, LANES), F32),
        ],
        scratch_shapes=[
            pltpu.VMEM((NODES_DEV, F), F32),
            pltpu.VMEM((NODES_DEV, F), jnp.int32),
            pltpu.VMEM((3, F, F), F32),
            pltpu.VMEM((3, NODES_DEV, F), F32),
            pltpu.VMEM((F, NODES_DEV), F32),
            pltpu.SemaphoreType.DMA((6,)),
            pltpu.SemaphoreType.DMA((2,)),
        ],
        compiler_params=params(32),
        cost_estimate=LIGHT,
        name="local_terms",
    )(first, *in_hbm(grad_out, relu_mask, cheb_weight, b0, b1, b2))


def stacked(field):
    high, low = split(field)
    return jnp.concatenate([jnp.concatenate([x, x], axis=1) for x in (high, low)], axis=0)


def add_block(acc, entry, block):
    position = entry // TILES_DEV
    slot = position // CHB
    at_row = pl.ds(pl.multiple_of(lax.rem(position, CHB) * TB, TB), TB)
    at_lane = pl.ds(pl.multiple_of(lax.rem(slot, 2) * TB, TB), TB)
    acc[slot // 2, at_row, at_lane] += block


def operator_kernel(n_col, origins, ids_ref, live_ref, rows_hbm, slots_hbm, values_ref, *refs):
    fields, refs = refs[: len(origins)], refs[len(origins) :]
    out_ref, total_ref, lists, counts, tiles, acc, rows, slots, sems, small_sems = refs
    step = pl.program_id(0)
    origin = jnp.where(step < n_col // 2, step, step + 1)
    size = TILES_DEV // GROUPS

    def copy(g):
        part = pl.ds(g * size, size)
        return pltpu.make_async_copy(values_ref.at[0, part], tiles.at[part], sems.at[g])

    @pl.when(step == 0)
    def _():
        small = fetch((rows_hbm, slots_hbm), (rows, slots), small_sems)
        for g in range(GROUPS):
            copy(g).start()
        for s in range(n_col):
            counts[s] = 0
        for item in small:
            item.wait()

        def place(t, carry):
            row = rows[0, t]
            s = lax.rem(row // CHB - ids_ref[0] + n_col, n_col)
            position = slots[0, t] * CHB + lax.rem(row, CHB)
            n = counts[s]
            lists[s, n] = position * TILES_DEV + t
            counts[s] = n + 1
            return carry

        lax.fori_loop(0, live_ref[0], place, 0)

    acc[...] = jnp.zeros_like(acc)

    @pl.when(step == 0)
    def _():
        for g in range(GROUPS):
            copy(g).wait()

    def add(n, carry):
        entry = lists[origin, n]
        add_block(acc, entry, tiles[lax.rem(entry, TILES_DEV)])
        return carry

    lax.fori_loop(0, counts[origin], add, 0)
    pairs = acc.shape[0]
    for p in range(pairs):
        high, low = split(acc[p])
        out_ref[0, p, :NODES_DEV, :] = high
        out_ref[0, p, NODES_DEV:, :] = low

    for k, field in zip(origins, fields):

        @pl.when(origin == k)
        def _():
            left = stacked(field[...])
            for p in range(pairs):
                part = jnp.dot(left, out_ref[0, p], preferred_element_type=F32)
                summed = part[:H] + part[H:]
                here = slice(p * WIDE, (p + 1) * WIDE)
                total_ref[:, here] = summed if k == 0 else total_ref[:, here] + summed


def build_operator(n_row, n_col, ids, live, rows, slots, values, pairs):
    part = (n_row // 2, 2 * NODES_DEV, WIDE)
    origins, fields = zip(*pairs)
    return pl.pallas_call(
        functools.partial(operator_kernel, n_col, origins),
        grid=(n_col - 1,),
        in_specs=[SMEM] * 2 + [HBM] * 3 + [pl.BlockSpec((H, NODES_DEV), lambda s: (0, 0))] * len(fields),
        out_specs=[
            pl.BlockSpec((1,) + part, lambda s: (s, 0, 0, 0)),
            pl.BlockSpec((H, n_row * TB), lambda s: (0, 0)),
            SMEM,
            SMEM,
        ],
        out_shape=[
            pltpu.HBM((n_col - 1,) + part, BF16),
            jax.ShapeDtypeStruct((H, n_row * TB), F32),
            jax.ShapeDtypeStruct((n_col, TILES_DEV), jnp.int32),
            jax.ShapeDtypeStruct((n_col,), jnp.int32),
        ],
        scratch_shapes=[
            pltpu.VMEM((TILES_DEV, TB, TB), F32),
            pltpu.VMEM((n_row // 2, NODES_DEV, WIDE), F32),
            pltpu.SMEM((1, TILES_DEV), jnp.int32),
            pltpu.SMEM((1, TILES_DEV), jnp.int32),
            pltpu.SemaphoreType.DMA((GROUPS,)),
            pltpu.SemaphoreType.DMA((2,)),
        ],
        compiler_params=params(40),
        cost_estimate=HEAVY,
        name="operator",
    )(ids, live, *in_hbm(rows, slots, values), *fields)


def opposite_kernel(n_row, origin, lists, counts, values_ref, field_ref, prev, op_ref, out_ref, tiles, acc, held, buf, *sems):
    tile_sems, field_sems, out_sems = sems

    def copy(n):
        t = lax.rem(lists[origin, n], TILES_DEV)
        return pltpu.make_async_copy(values_ref.at[0, t], tiles.at[n], tile_sems.at[n])

    def begin(n, carry):
        copy(n).start()
        return carry

    (field_copy,) = fetch([field_ref], [held], field_sems)
    lax.fori_loop(0, counts[origin], begin, 0)
    acc[...] = jnp.zeros_like(acc)
    field_copy.wait()
    left = stacked(held[...])

    def add(n, carry):
        copy(n).wait()
        add_block(acc, lists[origin, n], tiles[n])
        return carry

    lax.fori_loop(0, counts[origin], add, 0)
    copies = []
    for p in range(n_row // 2):
        here = slice(p * WIDE, (p + 1) * WIDE)
        high, low = split(acc[p])
        buf[p, :NODES_DEV, :] = high
        buf[p, NODES_DEV:, :] = low
        copies.append(pltpu.make_async_copy(buf.at[p], op_ref.at[0, p], out_sems.at[p]))
        copies[-1].start()
        part = jnp.dot(left, buf[p], preferred_element_type=F32)
        summed = part[:H] + part[H:] + prev[:, here]
        out_ref[2 * p] = summed[:, :TB]
        out_ref[2 * p + 1] = summed[:, TB:]
    for item in copies:
        item.wait()


def build_opposite(n_row, n_col, lists, counts, values, field, prev):
    part = (n_row // 2, 2 * NODES_DEV, WIDE)
    return pl.pallas_call(
        functools.partial(opposite_kernel, n_row, n_col // 2),
        in_specs=[SMEM, SMEM, HBM, ANY, VMEM],
        out_specs=[HBM, VMEM],
        out_shape=[pltpu.HBM((1,) + part, BF16), jax.ShapeDtypeStruct((n_row, H, TB), F32)],
        scratch_shapes=[
            pltpu.VMEM((TILES_DEV, TB, TB), F32),
            pltpu.VMEM((n_row // 2, NODES_DEV, WIDE), F32),
            pltpu.VMEM((H, NODES_DEV), F32),
            pltpu.VMEM(part, BF16),
            pltpu.SemaphoreType.DMA((TILES_DEV,)),
            pltpu.SemaphoreType.DMA((1,)),
            pltpu.SemaphoreType.DMA((n_row // 2,)),
        ],
        compiler_params=params(48),
        cost_estimate=LIGHT,
        name="opposite",
    )(lists, counts, *in_hbm(values), field, prev)


def product_kernel(n_row, n_col, origins, has_prev, last, n_carriers, has_base, *refs):
    n = len(origins)
    ids_ref, op_ref, refs = refs[0], refs[1], refs[2:]
    fields, refs = refs[:n], refs[n:]
    if has_prev:
        prev, refs = refs[0], refs[1:]
    carriers, refs = refs[:n_carriers], refs[n_carriers:]
    if has_base:
        base_hbm, out_ref, base_ref, refs = refs[0], refs[1], refs[2], refs[3:]
    else:
        out_ref, refs = refs[0], refs[1:]
    held, buf, field_sems, sems = refs[:4]

    def copy(k, p):
        return pltpu.make_async_copy(op_ref.at[origins[k], p], buf.at[k, p], sems.at[k, p])

    field_copies = fetch([x.at[pl.ds(0, H)] for x in fields], [held.at[k] for k in range(n)], field_sems)
    for p in range(n_row // 2):
        for k in range(n):
            copy(k, p).start()
    if has_base:
        (base_copy,) = fetch([base_hbm], [base_ref], refs[4])
    left = []
    for k in range(n):
        field_copies[k].wait()
        left.append(stacked(held[k]))
    if n_carriers:
        ordered = refs[4]
        for k in range(n_col):
            ordered[lax.rem(ids_ref[0] + k, n_col)] = carriers[k][H:, :]
        share = ordered[0]
        for k in range(1, n_col):
            share = share + ordered[k]
        rows = share.shape[0]
        groups = NODES_DEV // LANES // 2
        for j in range(groups):
            for q in range(n_row):
                from_lane = (q % 2 * groups + j) * LANES
                out_ref[q, H + j * rows : H + (j + 1) * rows, :] = share[:, from_lane : from_lane + LANES]
    for p in range(n_row // 2):
        here = slice(p * WIDE, (p + 1) * WIDE)
        total = None
        for k in range(n):
            copy(k, p).wait()
            part = jnp.dot(left[k], buf[k, p], preferred_element_type=F32)
            total = part if total is None else total + part
        summed = total[:H] + total[H:]
        if has_prev:
            summed = summed + prev[:, here]
        if last:
            out_ref[2 * p, :H, :] = summed[:, :TB]
            out_ref[2 * p + 1, :H, :] = summed[:, TB:]
        else:
            out_ref[:, here] = summed
    if has_base:
        base_copy.wait()


def product(n_row, n_col, ids, origins, operator, fields, prev, last, carriers=(), base=None):
    n = len(origins)
    has_prev = prev is not None
    has_base = base is not None
    share = 0
    scratch = [
        pltpu.VMEM((n, H, NODES_DEV), F32),
        pltpu.VMEM((n, n_row // 2, 2 * NODES_DEV, WIDE), BF16),
        pltpu.SemaphoreType.DMA((n,)),
        pltpu.SemaphoreType.DMA((n, n_row // 2)),
    ]
    if carriers:
        rows = carriers[0].shape[0] - H
        share = rows * NODES_DEV // LANES // 2
        scratch.append(pltpu.VMEM((n_col, rows, NODES_DEV), F32))
    if has_base:
        scratch.append(pltpu.SemaphoreType.DMA((1,)))
    out = jax.ShapeDtypeStruct((n_row, H + share, TB) if last else (H, n_row * TB), F32)
    count = has_prev + len(carriers)
    return pl.pallas_call(
        functools.partial(product_kernel, n_row, n_col, origins, has_prev, last, len(carriers), has_base),
        in_specs=[SMEM, HBM] + [ANY] * n + [VMEM] * count + [HBM] * has_base,
        out_specs=[VMEM, VMEM] if has_base else VMEM,
        out_shape=[out, jax.ShapeDtypeStruct(base.shape, F32)] if has_base else out,
        scratch_shapes=scratch,
        compiler_params=params(48),
        cost_estimate=LIGHT if last else HEAVY,
        name="product",
    )(
        ids,
        *in_hbm(operator),
        *fields,
        *((prev,) if has_prev else ()),
        *carriers,
        *(in_hbm(base) if has_base else ()),
    )


def carry_kernel(n_row, rows, owners_ref, base_ref, came_ref, *refs):
    out_ref = refs[-1]
    out_ref[:H, :] = base_ref[...]
    for q in range(n_row):
        here = pl.ds(pl.multiple_of(owners_ref[q] * TB, TB), TB)
        out_ref[:H, here] += 2.0 * came_ref[q]
    if rows:
        pieces_ref = refs[0]
        share = pieces_ref[0]
        for q in range(1, n_row):
            share = share + pieces_ref[q]
        for j in range(NODES_DEV // LANES):
            out_ref[H:, j * LANES : (j + 1) * LANES] = share[j * rows : (j + 1) * rows, :]


def carry(n_row, owners, base, came, *pieces):
    rows = pieces[0].shape[1] * LANES // NODES_DEV if pieces else 0
    return pl.pallas_call(
        functools.partial(carry_kernel, n_row, rows),
        in_specs=[SMEM] + [VMEM] * (2 + len(pieces)),
        out_specs=VMEM,
        out_shape=jax.ShapeDtypeStruct((H + rows, NODES_DEV), F32),
        compiler_params=params(24),
        cost_estimate=LIGHT,
        name="carry",
    )(owners, base, came, *pieces)


def finish_kernel(n_row, owners_ref, base_ref, left_ref, right_ref, out_ref, total):
    total[...] = base_ref[...]
    for h, came in enumerate((left_ref, right_ref)):
        for q in range(n_row):
            here = pl.ds(pl.multiple_of(owners_ref[q] * TB, TB), TB)
            total[h * H : (h + 1) * H, here] += came[q, :H, :]
    out_ref[...] = total[...].T


def finish(n_row, owners, base, left, right):
    return pl.pallas_call(
        functools.partial(finish_kernel, n_row),
        in_specs=[SMEM] + [VMEM] * 3,
        out_specs=VMEM,
        out_shape=jax.ShapeDtypeStruct((NODES_DEV, F), F32),
        scratch_shapes=[pltpu.VMEM((F, NODES_DEV), F32)],
        compiler_params=params(24),
        cost_estimate=LIGHT,
        name="finish",
    )(owners, base, left, right)


def assemble_kernel(n_row, row_ref, own_ref, other_ref, out_ref, halves, turned):
    rows = F // n_row
    half = lax.rem(row_ref[0], 2)
    halves[half] = own_ref[:, H:, :]
    halves[1 - half] = other_ref[:, H:, :]
    groups = 3 * F // LANES // 2
    for q in range(n_row):
        for j in range(2 * groups):
            here = slice(j % groups * rows, (j % groups + 1) * rows)
            turned[q * rows : (q + 1) * rows, j * LANES : (j + 1) * LANES] = halves[j // groups, q, here, :]
    for k in range(3):
        out_ref[k] = turned[:, k * F : (k + 1) * F].T


def assemble(n_row, row, own, other):
    return pl.pallas_call(
        functools.partial(assemble_kernel, n_row),
        in_specs=[SMEM, VMEM, VMEM],
        out_specs=VMEM,
        out_shape=jax.ShapeDtypeStruct((3, F, F), F32),
        scratch_shapes=[
            pltpu.VMEM((2, n_row, own.shape[1] - H, LANES), F32),
            pltpu.VMEM((F, 3 * F), F32),
        ],
        compiler_params=params(16),
        cost_estimate=LIGHT,
        name="assemble",
    )(row, own, other)


def shift(n_col, x, step):
    return lax.ppermute(x, "col", [(c, (c + step) % n_col) for c in range(n_col)])


def exchange(pieces):
    return lax.all_to_all(pieces, "row", split_axis=0, concat_axis=0, tiled=True)


def after(x, *others):
    return lax.optimization_barrier((x, *others))[0]


def opposite(field, below, above):
    col = lax.axis_index("col")
    sent = jnp.where(col == 1, above, jnp.where(col == 2, below, field))
    return lax.ppermute(sent, "col", [(1, 0), (2, 3), (3, 1), (0, 2)])


def gather(n_col, field, side):
    long = n_col // 2
    short = n_col - 1 - long
    ahead, behind = field, field
    steps = [[(0, field)]]
    for s in range(1, long + 1):
        if s == 2:
            ahead = after(ahead, behind)
        if s == 2 and n_col == 4:
            ahead = opposite(field, ahead, behind) if side > 0 else opposite(field, behind, ahead)
        else:
            ahead = shift(n_col, ahead, side)
        step = [((-side * s) % n_col, ahead)]
        if s <= short:
            behind = shift(n_col, behind, -side)
            step.append(((side * s) % n_col, behind))
        steps.append(step)
    return steps


def early(n_row, n_col, ids, operators, steps, total=None, done=0, base=None):
    pairs = [pair for step in steps[:-1] for pair in step][done:]
    for begin in range(0, len(pairs), 3):
        origins, fields = zip(*pairs[begin : begin + 3])
        origins = tuple(o if o < n_col // 2 else o - 1 for o in origins)
        brought = base if begin + 3 >= len(pairs) else None
        total = product(n_row, n_col, ids, origins, operators[0], fields, total, False, base=brought)
    return total


def final(n_row, n_col, ids, operators, steps, total, carrying=False):
    ((_, field),) = steps[-1]
    carriers = [x for _, x in sorted((p for step in steps for p in step), key=lambda p: p[0])] if carrying else ()
    return product(n_row, n_col, ids, (0,), operators[1], [field], total, True, carriers)


def per_device(
    grad_out,
    relu_mask,
    basis_zero,
    basis_one,
    basis_two,
    cheb_weight,
    tile_values,
    tile_rows,
    tile_slots,
    send_blocks,
    live_tiles,
):
    n_row = lax.axis_size("row")
    n_col = lax.axis_size("col")
    ids = lax.axis_index("col").astype(jnp.int32).reshape(1)
    owners = send_blocks.reshape(n_row)
    left, right = term_two(grad_out, relu_mask, cheb_weight)
    one_left, one_right, diff, pieces = local_terms(
        n_row, left, grad_out, relu_mask, cheb_weight, basis_zero, basis_one, basis_two
    )
    steps = gather(n_col, left, 1)
    first = steps[0] + steps[1] if len(steps) > 2 else steps[0]
    operator, left_early, lists, counts = build_operator(
        n_row, n_col, ids, live_tiles, tile_rows, tile_slots, tile_values, first
    )
    pieces = exchange(pieces)

    left_early = early(n_row, n_col, ids, (operator,), steps, left_early, len(first))
    right_steps = gather(n_col, after(right, left_early, steps[-1][0][1]), -1)
    opposite_part, left_last = build_opposite(
        n_row, n_col, lists, counts, tile_values, steps[-1][0][1], after(left_early, pieces)
    )
    left_came = exchange(left_last)
    common = (n_row, n_col, ids, (operator, opposite_part))
    right_early, one_left = early(*common, right_steps, base=one_left)

    left_carried = carry(n_row, owners, after(one_left, right_early, right_steps[-1][0][1]), left_came, pieces)
    steps = gather(n_col, left_carried, 1)
    right_came = exchange(final(*common, right_steps, right_early))
    left_early, one_right = early(*common, steps, base=one_right)

    right_carried = carry(n_row, owners, after(one_right, left_early, steps[-1][0][1]), right_came)
    right_steps = gather(n_col, right_carried, -1)
    left_came = exchange(final(*common, steps, left_early, carrying=True))
    right_early = early(*common, right_steps)

    right_last = final(*common, right_steps, right_early)
    right_came = exchange(right_last)
    other = lax.ppermute(after(left_came, right_last), "row", [(r, r ^ 1) for r in range(n_row)])
    row = lax.axis_index("row").astype(jnp.int32).reshape(1)
    weight_grad = assemble(n_row, row, left_came, other)
    return finish(n_row, owners, after(diff, weight_grad), left_came, right_came), weight_grad


def solution(mesh):
    placed = (
        P(("row", "col"), None),
        P(("row", "col"), None),
        P(("row", "col"), None),
        P(("row", "col"), None),
        P(("row", "col"), None),
        P(),
        P(("row", "col"), None, None, None),
        P(("row", "col"), None),
        P(("row", "col"), None),
        P(("row", "col"), None, None),
        P(("row", "col")),
    )
    return jax.shard_map(
        per_device,
        mesh=mesh,
        in_specs=placed,
        out_specs=(P(("row", "col"), None), P()),
        check_vma=False,
    )
```

```python
import functools

import jax
import jax.numpy as jnp
from jax import lax
from jax.experimental import pallas as pl
from jax.experimental.pallas import tpu as pltpu
from jax.sharding import PartitionSpec as P

F = 256
H = 128
TB = 128
CHB = 4
WIDE = 2 * TB
LANES = 128
NODES_DEV = CHB * TB
TILES_DEV = 128
GROUPS = 8
MIB = 1 << 20
HEAVY = pl.CostEstimate(flops=1 << 34, bytes_accessed=64 * MIB, transcendentals=0)
LIGHT = pl.CostEstimate(flops=1024, bytes_accessed=1024, transcendentals=0)
BF16 = jnp.bfloat16
F32 = jnp.float32

SMEM = pl.BlockSpec(memory_space=pltpu.SMEM)
VMEM = pl.BlockSpec(memory_space=pltpu.VMEM)
HBM = pl.BlockSpec(memory_space=pltpu.HBM)
ANY = pl.BlockSpec(memory_space=pl.ANY)


def params(mib):
    return pltpu.CompilerParams(vmem_limit_bytes=mib * MIB)


def in_hbm(*arrays):
    return [pltpu.with_memory_space_constraint(x, pltpu.HBM) for x in arrays]


def split(x):
    high = x.astype(BF16)
    low = (x - high.astype(F32)).astype(BF16)
    return high, low


def dot3(a, b, dims):
    ah, al = a
    bh, bl = b

    def one(x, y):
        return lax.dot_general(x, y, (dims, ((), ())), preferred_element_type=F32)

    return one(ah, bh) + (one(ah, bl) + one(al, bh))


def fetch(sources, targets, sems):
    copies = [pltpu.make_async_copy(a, b, sems.at[i]) for i, (a, b) in enumerate(zip(sources, targets))]
    for copy in copies:
        copy.start()
    return copies


def masked_of(grad, mask):
    return jnp.where(mask > 0, grad, jnp.zeros_like(grad))


def term_two_kernel(grad_hbm, mask_hbm, weight_hbm, left_ref, right_ref, grad, mask, weight, sems):
    for copy in fetch((grad_hbm, mask_hbm, weight_hbm.at[2]), (grad, mask, weight), sems):
        copy.wait()
    term = dot3(split(weight[...]), split(masked_of(grad[...], mask[...])), ((1,), (1,)))
    left_ref[...] = term[:H]
    right_ref[...] = term[H:]


def term_two(grad_out, relu_mask, cheb_weight):
    out = jax.ShapeDtypeStruct((H, NODES_DEV), F32)
    return pl.pallas_call(
        term_two_kernel,
        in_specs=[HBM] * 3,
        out_specs=[VMEM, VMEM],
        out_shape=[out, out],
        scratch_shapes=[
            pltpu.VMEM((NODES_DEV, F), F32),
            pltpu.VMEM((NODES_DEV, F), jnp.int32),
            pltpu.VMEM((F, F), F32),
            pltpu.SemaphoreType.DMA((3,)),
        ],
        compiler_params=params(16),
        cost_estimate=LIGHT,
        name="term_two",
    )(*in_hbm(grad_out, relu_mask, cheb_weight))


def local_kernel(
    n_row, first_ref, grad_hbm, mask_hbm, weight_hbm, h0, h1, h2, left_hbm, right_hbm, diff_ref, pieces_ref,
    grad, mask, weight, bases, one, sems, one_sems,
):
    sources = (grad_hbm, mask_hbm, weight_hbm, h0, h1, h2)
    copies = fetch(sources, (grad, mask, weight, bases.at[0], bases.at[1], bases.at[2]), sems)
    for copy in copies[:3]:
        copy.wait()
    values = masked_of(grad[...], mask[...])
    masked = split(values)
    term = dot3(split(weight[1]), masked, ((1,), (1,)))
    one[...] = term
    one_copies = fetch((one.at[pl.ds(0, H)], one.at[pl.ds(H, H)]), (left_hbm, right_hbm), one_sems)
    diff_ref[...] = dot3(split(weight[0] - weight[2]), masked, ((1,), (1,)))
    turned = split(values.T)
    rows = F // n_row
    for k in range(3):
        copies[3 + k].wait()
        part = dot3(turned, split(bases[k]), ((1,), (0,)))
        for j in range(F // LANES):
            here = (k * (F // LANES) + j) * rows
            for q in range(n_row):
                pieces_ref[q, here : here + rows, :] = part[q * rows : (q + 1) * rows, j * LANES : (j + 1) * LANES]
    for copy in one_copies:
        copy.wait()


def local_terms(n_row, first, grad_out, relu_mask, cheb_weight, b0, b1, b2):
    half = pltpu.HBM((H, NODES_DEV), F32)
    share = 3 * F * F // n_row // LANES
    return pl.pallas_call(
        functools.partial(local_kernel, n_row),
        in_specs=[ANY] + [HBM] * 6,
        out_specs=[HBM, HBM, VMEM, VMEM],
        out_shape=[
            half,
            half,
            jax.ShapeDtypeStruct((F, NODES_DEV), F32),
            jax.ShapeDtypeStruct((n_row, share, LANES), F32),
        ],
        scratch_shapes=[
            pltpu.VMEM((NODES_DEV, F), F32),
            pltpu.VMEM((NODES_DEV, F), jnp.int32),
            pltpu.VMEM((3, F, F), F32),
            pltpu.VMEM((3, NODES_DEV, F), F32),
            pltpu.VMEM((F, NODES_DEV), F32),
            pltpu.SemaphoreType.DMA((6,)),
            pltpu.SemaphoreType.DMA((2,)),
        ],
        compiler_params=params(32),
        cost_estimate=LIGHT,
        name="local_terms",
    )(first, *in_hbm(grad_out, relu_mask, cheb_weight, b0, b1, b2))


def stacked(field):
    high, low = split(field)
    return jnp.concatenate([jnp.concatenate([x, x], axis=1) for x in (high, low)], axis=0)


def operator_kernel(n_row, n_col, origins, ids_ref, live_ref, rows_hbm, slots_hbm, values_ref, *refs):
    fields, refs = refs[: len(origins)], refs[len(origins) :]
    out_hbm, total_ref, tiles, acc, buf, held, lists, counts, rows, slots, sems, small_sems, field_sems, out_sems = refs
    size = TILES_DEV // GROUPS
    pairs = n_row // 2
    small = fetch((rows_hbm, slots_hbm), (rows, slots), small_sems)
    parts = [pl.ds(g * size, size) for g in range(GROUPS)]
    tile_copies = fetch([values_ref.at[0, part] for part in parts], [tiles.at[part] for part in parts], sems)
    field_copies = fetch(fields, [held.at[k] for k in range(len(fields))], field_sems)
    for item in small:
        item.wait()

    def place(t, counted):
        row = rows[0, t]
        s = lax.rem(row // CHB - ids_ref[0] + n_col, n_col)
        if n_col & (n_col - 1) == 0:
            s = (lax.shift_right_logical(row, CHB.bit_length() - 1) - ids_ref[0]) & (n_col - 1)
        position = slots[0, t] * CHB + (row & (CHB - 1))
        n = counted[0]
        for k in range(1, n_col):
            n = jnp.where(s == k, counted[k], n)
        lists[s, n] = position * TILES_DEV + t
        return tuple(c + (s == k).astype(jnp.int32) for k, c in enumerate(counted))

    counted = lax.fori_loop(0, live_ref[0], place, (jnp.int32(0),) * n_col)
    for s in range(n_col):
        counts[s] = counted[s]

    def out_copy(origin, p):
        return pltpu.make_async_copy(buf.at[origin % 2, p], out_hbm.at[origin, p], out_sems.at[origin % 2, p])

    for origin in range(n_col):
        acc[...] = jnp.zeros_like(acc)
        if origin == 0:
            for item in tile_copies:
                item.wait()

        def add(n, carry):
            entry = lists[origin, n]
            tile = entry & (TILES_DEV - 1)
            position = lax.shift_right_logical(entry, TILES_DEV.bit_length() - 1)
            slot = lax.shift_right_logical(position, CHB.bit_length() - 1)
            at_row = pl.ds(pl.multiple_of((position & (CHB - 1)) * TB, TB), TB)
            at_lane = pl.ds(pl.multiple_of((slot & 1) * TB, TB), TB)
            acc[lax.shift_right_logical(slot, 1), at_row, at_lane] += tiles[tile]
            return carry

        lax.fori_loop(0, counts[origin], add, 0)
        for p in range(pairs):
            if origin >= 2:
                out_copy(origin - 2, p).wait()
            high, low = split(acc[p])
            buf[origin % 2, p, :NODES_DEV, :] = high
            buf[origin % 2, p, NODES_DEV:, :] = low
            out_copy(origin, p).start()
        if origin in origins:
            k = origins.index(origin)
            field_copies[k].wait()
            left = stacked(held[k])
            for p in range(pairs):
                part = jnp.dot(left, buf[origin % 2, p], preferred_element_type=F32)
                summed = part[:H] + part[H:]
                here = slice(p * WIDE, (p + 1) * WIDE)
                total_ref[:, here] = summed if origin == 0 else total_ref[:, here] + summed
    for origin in range(n_col - 2, n_col):
        for p in range(pairs):
            out_copy(origin, p).wait()


def build_operator(n_row, n_col, ids, live, rows, slots, values, pairs):
    part = (n_row // 2, 2 * NODES_DEV, WIDE)
    origins, fields = zip(*pairs)
    return pl.pallas_call(
        functools.partial(operator_kernel, n_row, n_col, origins),
        in_specs=[SMEM] * 2 + [HBM] * 3 + [ANY] * len(fields),
        out_specs=[HBM, VMEM],
        out_shape=[pltpu.HBM((n_col,) + part, BF16), jax.ShapeDtypeStruct((H, n_row * TB), F32)],
        scratch_shapes=[
            pltpu.VMEM((TILES_DEV, TB, TB), F32),
            pltpu.VMEM((n_row // 2, NODES_DEV, WIDE), F32),
            pltpu.VMEM((2,) + part, BF16),
            pltpu.VMEM((len(fields), H, NODES_DEV), F32),
            pltpu.SMEM((n_col, TILES_DEV), jnp.int32),
            pltpu.SMEM((n_col,), jnp.int32),
            pltpu.SMEM((1, TILES_DEV), jnp.int32),
            pltpu.SMEM((1, TILES_DEV), jnp.int32),
            pltpu.SemaphoreType.DMA((GROUPS,)),
            pltpu.SemaphoreType.DMA((2,)),
            pltpu.SemaphoreType.DMA((len(fields),)),
            pltpu.SemaphoreType.DMA((2, n_row // 2)),
        ],
        compiler_params=params(48),
        cost_estimate=HEAVY,
        name="operator",
    )(ids, live, *in_hbm(rows, slots, values), *fields)


def product_kernel(n_row, n_col, origins, has_prev, last, n_carriers, *refs):
    n = len(origins)
    ids_ref, op_ref, refs = refs[0], refs[1], refs[2:]
    fields, refs = refs[:n], refs[n:]
    if has_prev:
        prev, refs = refs[0], refs[1:]
    carriers, refs = refs[:n_carriers], refs[n_carriers:]
    out_ref, held, buf, field_sems, sems = refs[:5]

    def copy(k, p):
        return pltpu.make_async_copy(op_ref.at[origins[k], p], buf.at[k, p], sems.at[k, p])

    field_copies = fetch([x.at[pl.ds(0, H)] for x in fields], [held.at[k] for k in range(n)], field_sems)
    for p in range(n_row // 2):
        for k in range(n):
            copy(k, p).start()
    left = []
    for k in range(n):
        field_copies[k].wait()
        left.append(stacked(held[k]))
    if n_carriers:
        ordered = refs[5]
        for k in range(n_col):
            ordered[lax.rem(ids_ref[0] + k, n_col)] = carriers[k][H:, :]
        share = ordered[0]
        for k in range(1, n_col):
            share = share + ordered[k]
        rows = share.shape[0]
        groups = NODES_DEV // LANES // 2
        for j in range(groups):
            for q in range(n_row):
                from_lane = (q % 2 * groups + j) * LANES
                out_ref[q, H + j * rows : H + (j + 1) * rows, :] = share[:, from_lane : from_lane + LANES]
    for p in range(n_row // 2):
        here = slice(p * WIDE, (p + 1) * WIDE)
        total = None
        for k in range(n):
            copy(k, p).wait()
            part = jnp.dot(left[k], buf[k, p], preferred_element_type=F32)
            total = part if total is None else total + part
        summed = total[:H] + total[H:]
        if has_prev:
            summed = summed + prev[:, here]
        if last:
            out_ref[2 * p, :H, :] = summed[:, :TB]
            out_ref[2 * p + 1, :H, :] = summed[:, TB:]
        else:
            out_ref[:, here] = summed


def product(n_row, n_col, ids, origins, operator, fields, prev, last, carriers=()):
    n = len(origins)
    has_prev = prev is not None
    share = 0
    scratch = [
        pltpu.VMEM((n, H, NODES_DEV), F32),
        pltpu.VMEM((n, n_row // 2, 2 * NODES_DEV, WIDE), BF16),
        pltpu.SemaphoreType.DMA((n,)),
        pltpu.SemaphoreType.DMA((n, n_row // 2)),
    ]
    if carriers:
        rows = carriers[0].shape[0] - H
        share = rows * NODES_DEV // LANES // 2
        scratch.append(pltpu.VMEM((n_col, rows, NODES_DEV), F32))
    shape = (n_row, H + share, TB) if last else (H, n_row * TB)
    count = has_prev + len(carriers)
    return pl.pallas_call(
        functools.partial(product_kernel, n_row, n_col, origins, has_prev, last, len(carriers)),
        in_specs=[SMEM, HBM] + [ANY] * n + [VMEM] * count,
        out_specs=VMEM,
        out_shape=jax.ShapeDtypeStruct(shape, F32),
        scratch_shapes=scratch,
        compiler_params=params(48),
        cost_estimate=LIGHT if last else HEAVY,
        name="product",
    )(
        ids,
        *in_hbm(operator),
        *fields,
        *((prev,) if has_prev else ()),
        *carriers,
    )


def carry_kernel(n_row, rows, owners_ref, base_hbm, came_ref, *refs):
    out_ref, base, sems = refs[-3:]
    (base_copy,) = fetch([base_hbm], [base], sems)
    out_ref[:H, :] = jnp.zeros((H, NODES_DEV), F32)
    for q in range(n_row):
        here = pl.ds(pl.multiple_of(owners_ref[q] * TB, TB), TB)
        out_ref[:H, here] += came_ref[q]
    if rows:
        pieces_ref = refs[0]
        share = pieces_ref[0]
        for q in range(1, n_row):
            share = share + pieces_ref[q]
        for j in range(NODES_DEV // LANES):
            out_ref[H:, j * LANES : (j + 1) * LANES] = share[j * rows : (j + 1) * rows, :]
    base_copy.wait()
    out_ref[:H, :] = base[...] + 2.0 * out_ref[:H, :]


def carry(n_row, owners, base, came, *pieces):
    rows = pieces[0].shape[1] * LANES // NODES_DEV if pieces else 0
    return pl.pallas_call(
        functools.partial(carry_kernel, n_row, rows),
        in_specs=[SMEM, HBM] + [VMEM] * (1 + len(pieces)),
        out_specs=VMEM,
        out_shape=jax.ShapeDtypeStruct((H + rows, NODES_DEV), F32),
        scratch_shapes=[pltpu.VMEM((H, NODES_DEV), F32), pltpu.SemaphoreType.DMA((1,))],
        compiler_params=params(24),
        cost_estimate=LIGHT,
        name="carry",
    )(owners, *in_hbm(base), came, *pieces)


def finish_kernel(n_row, owners_ref, base_ref, left_ref, right_ref, out_ref, total):
    total[...] = base_ref[...]
    for h, came in enumerate((left_ref, right_ref)):
        for q in range(n_row):
            here = pl.ds(pl.multiple_of(owners_ref[q] * TB, TB), TB)
            total[h * H : (h + 1) * H, here] += came[q, :H, :]
    out_ref[...] = total[...].T


def finish(n_row, owners, base, left, right):
    return pl.pallas_call(
        functools.partial(finish_kernel, n_row),
        in_specs=[SMEM] + [VMEM] * 3,
        out_specs=VMEM,
        out_shape=jax.ShapeDtypeStruct((NODES_DEV, F), F32),
        scratch_shapes=[pltpu.VMEM((F, NODES_DEV), F32)],
        compiler_params=params(24),
        cost_estimate=LIGHT,
        name="finish",
    )(owners, base, left, right)


def assemble_kernel(n_row, row_ref, own_ref, other_ref, out_ref, halves, turned):
    rows = F // n_row
    half = lax.rem(row_ref[0], 2)
    halves[half] = own_ref[:, H:, :]
    halves[1 - half] = other_ref[:, H:, :]
    groups = 3 * F // LANES // 2
    for q in range(n_row):
        for j in range(2 * groups):
            here = slice(j % groups * rows, (j % groups + 1) * rows)
            turned[q * rows : (q + 1) * rows, j * LANES : (j + 1) * LANES] = halves[j // groups, q, here, :]
    for k in range(3):
        out_ref[k] = turned[:, k * F : (k + 1) * F].T


def assemble(n_row, row, own, other):
    return pl.pallas_call(
        functools.partial(assemble_kernel, n_row),
        in_specs=[SMEM, VMEM, VMEM],
        out_specs=VMEM,
        out_shape=jax.ShapeDtypeStruct((3, F, F), F32),
        scratch_shapes=[
            pltpu.VMEM((2, n_row, own.shape[1] - H, LANES), F32),
            pltpu.VMEM((F, 3 * F), F32),
        ],
        compiler_params=params(16),
        cost_estimate=LIGHT,
        name="assemble",
    )(row, own, other)


def shift(n_col, x, step):
    return lax.ppermute(x, "col", [(c, (c + step) % n_col) for c in range(n_col)])


def exchange(pieces):
    return lax.all_to_all(pieces, "row", split_axis=0, concat_axis=0, tiled=True)


def after(x, *others):
    return lax.optimization_barrier((x, *others))[0]


def opposite(field, below, above):
    col = lax.axis_index("col")
    sent = jnp.where(col == 1, above, jnp.where(col == 2, below, field))
    return lax.ppermute(sent, "col", [(1, 0), (2, 3), (3, 1), (0, 2)])


def gather(n_col, field, side):
    long = n_col // 2
    short = n_col - 1 - long
    ahead, behind = field, field
    steps = [[(0, field)]]
    for s in range(1, long + 1):
        if s == 2:
            ahead = after(ahead, behind)
        if s == 2 and n_col == 4:
            ahead = opposite(field, ahead, behind) if side > 0 else opposite(field, behind, ahead)
        else:
            ahead = shift(n_col, ahead, side)
        step = [((-side * s) % n_col, ahead)]
        if s <= short:
            behind = shift(n_col, behind, -side)
            step.append(((side * s) % n_col, behind))
        steps.append(step)
    return steps


def early(n_row, n_col, ids, operator, steps, total=None, done=0):
    pairs = [pair for step in steps[:-1] for pair in step][done:]
    for begin in range(0, len(pairs), 3):
        origins, fields = zip(*pairs[begin : begin + 3])
        total = product(n_row, n_col, ids, origins, operator, fields, total, False)
    return total


def final(n_row, n_col, ids, operator, steps, total, carrying=False):
    origins, fields = zip(*steps[-1])
    carriers = [x for _, x in sorted((p for step in steps for p in step), key=lambda p: p[0])] if carrying else ()
    return product(n_row, n_col, ids, origins, operator, fields, total, True, carriers)


def per_device(
    grad_out,
    relu_mask,
    basis_zero,
    basis_one,
    basis_two,
    cheb_weight,
    tile_values,
    tile_rows,
    tile_slots,
    send_blocks,
    live_tiles,
):
    n_row = lax.axis_size("row")
    n_col = lax.axis_size("col")
    ids = lax.axis_index("col").astype(jnp.int32).reshape(1)
    owners = send_blocks.reshape(n_row)
    left, right = term_two(grad_out, relu_mask, cheb_weight)
    one_left, one_right, diff, pieces = local_terms(
        n_row, left, grad_out, relu_mask, cheb_weight, basis_zero, basis_one, basis_two
    )
    steps = gather(n_col, left, 1)
    first = steps[0] + steps[1] if len(steps) > 2 else steps[0]
    operator, left_early = build_operator(
        n_row, n_col, ids, live_tiles, tile_rows, tile_slots, tile_values, first
    )
    pieces = exchange(pieces)
    common = (n_row, n_col, ids, operator)

    left_early = early(*common, steps, left_early, len(first))
    right_steps = gather(n_col, after(right, left_early, steps[-1][0][1]), -1)
    left_came = exchange(final(*common, steps, after(left_early, pieces)))
    right_early = early(*common, right_steps)

    left_carried = carry(n_row, owners, after(one_left, right_early, right_steps[-1][0][1]), left_came, pieces)
    steps = gather(n_col, left_carried, 1)
    right_came = exchange(final(*common, right_steps, right_early))
    left_early = early(*common, steps)

    right_carried = carry(n_row, owners, after(one_right, left_early, steps[-1][0][1]), right_came)
    right_steps = gather(n_col, right_carried, -1)
    left_came = exchange(final(*common, steps, left_early, carrying=True))
    right_early = early(*common, right_steps)

    right_last = final(*common, right_steps, right_early)
    right_came = exchange(right_last)
    other = lax.ppermute(after(left_came, right_last), "row", [(r, r ^ 1) for r in range(n_row)])
    row = lax.axis_index("row").astype(jnp.int32).reshape(1)
    weight_grad = assemble(n_row, row, left_came, other)
    return finish(n_row, owners, after(diff, weight_grad), left_came, right_came), weight_grad


def solution(mesh):
    placed = (
        P(("row", "col"), None),
        P(("row", "col"), None),
        P(("row", "col"), None),
        P(("row", "col"), None),
        P(("row", "col"), None),
        P(),
        P(("row", "col"), None, None, None),
        P(("row", "col"), None),
        P(("row", "col"), None),
        P(("row", "col"), None, None),
        P(("row", "col")),
    )
    return jax.shard_map(
        per_device,
        mesh=mesh,
        in_specs=placed,
        out_specs=(P(("row", "col"), None), P()),
        check_vma=False,
    )
```

```python
import functools

import jax
import jax.numpy as jnp
from jax import lax
from jax.experimental import pallas as pl
from jax.experimental.pallas import tpu as pltpu
from jax.sharding import PartitionSpec as P

F = 256
H = 128
TB = 128
CHB = 4
WIDE = 2 * TB
LANES = 128
NODES_DEV = CHB * TB
TILES_DEV = 128
GROUPS = 8
MIB = 1 << 20
WHOLE_BYTES = 12 * MIB
DEPTH = 4
HEAVY = pl.CostEstimate(flops=1 << 34, bytes_accessed=64 * MIB, transcendentals=0)
LIGHT = pl.CostEstimate(flops=1024, bytes_accessed=1024, transcendentals=0)
BF16 = jnp.bfloat16
F32 = jnp.float32

SMEM = pl.BlockSpec(memory_space=pltpu.SMEM)
VMEM = pl.BlockSpec(memory_space=pltpu.VMEM)
HBM = pl.BlockSpec(memory_space=pltpu.HBM)
ANY = pl.BlockSpec(memory_space=pl.ANY)


def params(mib):
    return pltpu.CompilerParams(vmem_limit_bytes=mib * MIB)


def in_hbm(*arrays):
    return [pltpu.with_memory_space_constraint(x, pltpu.HBM) for x in arrays]


def split(x):
    high = x.astype(BF16)
    low = (x - high.astype(F32)).astype(BF16)
    return high, low


def dot3(a, b, dims):
    ah, al = a
    bh, bl = b

    def one(x, y):
        return lax.dot_general(x, y, (dims, ((), ())), preferred_element_type=F32)

    return one(ah, bh) + (one(ah, bl) + one(al, bh))


def fetch(sources, targets, sems):
    copies = [pltpu.make_async_copy(a, b, sems.at[i]) for i, (a, b) in enumerate(zip(sources, targets))]
    for copy in copies:
        copy.start()
    return copies


def masked_of(grad, mask):
    return jnp.where(mask > 0, grad, jnp.zeros_like(grad))


def term_two_kernel(grad_hbm, mask_hbm, weight_hbm, left_ref, right_ref, grad, mask, weight, sems):
    for copy in fetch((grad_hbm, mask_hbm, weight_hbm.at[2]), (grad, mask, weight), sems):
        copy.wait()
    term = dot3(split(weight[...]), split(masked_of(grad[...], mask[...])), ((1,), (1,)))
    left_ref[...] = term[:H]
    right_ref[...] = term[H:]


def term_two(grad_out, relu_mask, cheb_weight):
    out = jax.ShapeDtypeStruct((H, NODES_DEV), F32)
    return pl.pallas_call(
        term_two_kernel,
        in_specs=[HBM] * 3,
        out_specs=[VMEM, VMEM],
        out_shape=[out, out],
        scratch_shapes=[
            pltpu.VMEM((NODES_DEV, F), F32),
            pltpu.VMEM((NODES_DEV, F), jnp.int32),
            pltpu.VMEM((F, F), F32),
            pltpu.SemaphoreType.DMA((3,)),
        ],
        compiler_params=params(16),
        cost_estimate=LIGHT,
        name="term_two",
    )(*in_hbm(grad_out, relu_mask, cheb_weight))


def local_kernel(
    n_row, first_ref, grad_hbm, mask_hbm, weight_hbm, h0, h1, h2, left_hbm, right_hbm, diff_ref, pieces_ref,
    grad, mask, weight, bases, one, sems, one_sems,
):
    sources = (grad_hbm, mask_hbm, weight_hbm, h0, h1, h2)
    copies = fetch(sources, (grad, mask, weight, bases.at[0], bases.at[1], bases.at[2]), sems)
    for copy in copies[:3]:
        copy.wait()
    values = masked_of(grad[...], mask[...])
    masked = split(values)
    term = dot3(split(weight[1]), masked, ((1,), (1,)))
    one[...] = term
    one_copies = fetch((one.at[pl.ds(0, H)], one.at[pl.ds(H, H)]), (left_hbm, right_hbm), one_sems)
    diff_ref[...] = dot3(split(weight[0] - weight[2]), masked, ((1,), (1,)))
    turned = split(values.T)
    rows = F // n_row
    for k in range(3):
        copies[3 + k].wait()
        part = dot3(turned, split(bases[k]), ((1,), (0,)))
        for j in range(F // LANES):
            here = (k * (F // LANES) + j) * rows
            for q in range(n_row):
                pieces_ref[q, here : here + rows, :] = part[q * rows : (q + 1) * rows, j * LANES : (j + 1) * LANES]
    for copy in one_copies:
        copy.wait()


def local_terms(n_row, first, grad_out, relu_mask, cheb_weight, b0, b1, b2):
    half = pltpu.HBM((H, NODES_DEV), F32)
    share = 3 * F * F // n_row // LANES
    return pl.pallas_call(
        functools.partial(local_kernel, n_row),
        in_specs=[ANY] + [HBM] * 6,
        out_specs=[HBM, HBM, VMEM, VMEM],
        out_shape=[
            half,
            half,
            jax.ShapeDtypeStruct((F, NODES_DEV), F32),
            jax.ShapeDtypeStruct((n_row, share, LANES), F32),
        ],
        scratch_shapes=[
            pltpu.VMEM((NODES_DEV, F), F32),
            pltpu.VMEM((NODES_DEV, F), jnp.int32),
            pltpu.VMEM((3, F, F), F32),
            pltpu.VMEM((3, NODES_DEV, F), F32),
            pltpu.VMEM((F, NODES_DEV), F32),
            pltpu.SemaphoreType.DMA((6,)),
            pltpu.SemaphoreType.DMA((2,)),
        ],
        compiler_params=params(32),
        cost_estimate=LIGHT,
        name="local_terms",
    )(first, *in_hbm(grad_out, relu_mask, cheb_weight, b0, b1, b2))


def stacked(field):
    high, low = split(field)
    return jnp.concatenate([jnp.concatenate([x, x], axis=1) for x in (high, low)], axis=0)


def operator_kernel(n_row, n_col, origins, ids_ref, live_ref, rows_hbm, slots_hbm, values_ref, *refs):
    fields, refs = refs[: len(origins)], refs[len(origins) :]
    out_hbm, total_ref, tiles, acc, buf, held, lists, counts, rows, slots, sems, small_sems, field_sems, out_sems = refs
    size = TILES_DEV // GROUPS
    pairs = n_row // 2
    whole = acc.shape[0] == n_col
    small = fetch((rows_hbm, slots_hbm), (rows, slots), small_sems)
    parts = [pl.ds(g * size, size) for g in range(GROUPS)]
    tile_copies = fetch([values_ref.at[0, part] for part in parts], [tiles.at[part] for part in parts], sems)
    field_copies = fetch(fields, [held.at[k] for k in range(len(fields))], field_sems)
    for item in small:
        item.wait()

    def place_of(t):
        row = rows[0, t]
        if n_col & (n_col - 1) == 0:
            s = (lax.shift_right_logical(row, CHB.bit_length() - 1) - ids_ref[0]) & (n_col - 1)
        else:
            s = lax.rem(row // CHB - ids_ref[0] + n_col, n_col)
        return s, slots[0, t] * CHB + (row & (CHB - 1))

    def add_block(into, position, tile):
        slot = lax.shift_right_logical(position, CHB.bit_length() - 1)
        at_row = pl.ds(pl.multiple_of((position & (CHB - 1)) * TB, TB), TB)
        at_lane = pl.ds(pl.multiple_of((slot & 1) * TB, TB), TB)
        acc[into, lax.shift_right_logical(slot, 1), at_row, at_lane] += tiles[tile]

    if whole:

        def add_now(t, carry):
            s, position = place_of(t)
            add_block(s, position, t)
            return carry

        acc[...] = jnp.zeros_like(acc)
        for g, item in enumerate(tile_copies):
            item.wait()
            end = (g + 1) * size

            @pl.when(live_ref[0] >= end)
            def _():
                lax.fori_loop(end - size, end, add_now, 0, unroll=4)

            @pl.when(live_ref[0] < end)
            def _():
                lax.fori_loop(end - size, live_ref[0], add_now, 0)

    else:

        def place(t, counted):
            s, position = place_of(t)
            n = counted[0]
            for k in range(1, n_col):
                n = jnp.where(s == k, counted[k], n)
            lists[s, n] = position * TILES_DEV + t
            return tuple(c + (s == k).astype(jnp.int32) for k, c in enumerate(counted))

        counted = lax.fori_loop(0, live_ref[0], place, (jnp.int32(0),) * n_col)
        for s in range(n_col):
            counts[s] = counted[s]
        for item in tile_copies:
            item.wait()

    def out_copy(origin, p):
        return pltpu.make_async_copy(buf.at[origin % 2, p], out_hbm.at[origin, p], out_sems.at[origin % 2, p])

    for origin in range(n_col):
        if not whole:

            def add(n, carry):
                entry = lists[origin, n]
                add_block(0, lax.shift_right_logical(entry, TILES_DEV.bit_length() - 1), entry & (TILES_DEV - 1))
                return carry

            acc[...] = jnp.zeros_like(acc)
            lax.fori_loop(0, counts[origin], add, 0)
        summed_blocks = acc.at[origin if whole else 0]
        for p in range(pairs):
            if origin >= 2:
                out_copy(origin - 2, p).wait()
            high, low = split(summed_blocks[p])
            buf[origin % 2, p, :NODES_DEV, :] = high
            buf[origin % 2, p, NODES_DEV:, :] = low
            out_copy(origin, p).start()
        if origin in origins:
            k = origins.index(origin)
            field_copies[k].wait()
            left = stacked(held[k])
            for p in range(pairs):
                part = jnp.dot(left, buf[origin % 2, p], preferred_element_type=F32)
                summed = part[:H] + part[H:]
                here = slice(p * WIDE, (p + 1) * WIDE)
                total_ref[:, here] = summed if origin == 0 else total_ref[:, here] + summed
    for origin in range(n_col - 2, n_col):
        for p in range(pairs):
            out_copy(origin, p).wait()


def build_operator(n_row, n_col, ids, live, rows, slots, values, pairs):
    part = (n_row // 2, 2 * NODES_DEV, WIDE)
    sums = (n_row // 2, NODES_DEV, WIDE)
    held_origins = n_col if 4 * n_col * n_row * TB * NODES_DEV <= WHOLE_BYTES else 1
    origins, fields = zip(*pairs)
    return pl.pallas_call(
        functools.partial(operator_kernel, n_row, n_col, origins),
        in_specs=[SMEM] * 2 + [HBM] * 3 + [ANY] * len(fields),
        out_specs=[HBM, VMEM],
        out_shape=[pltpu.HBM((n_col,) + part, BF16), jax.ShapeDtypeStruct((H, n_row * TB), F32)],
        scratch_shapes=[
            pltpu.VMEM((TILES_DEV, TB, TB), F32),
            pltpu.VMEM((held_origins,) + sums, F32),
            pltpu.VMEM((2,) + part, BF16),
            pltpu.VMEM((len(fields), H, NODES_DEV), F32),
            pltpu.SMEM((n_col, TILES_DEV), jnp.int32),
            pltpu.SMEM((n_col,), jnp.int32),
            pltpu.SMEM((1, TILES_DEV), jnp.int32),
            pltpu.SMEM((1, TILES_DEV), jnp.int32),
            pltpu.SemaphoreType.DMA((GROUPS,)),
            pltpu.SemaphoreType.DMA((2,)),
            pltpu.SemaphoreType.DMA((len(fields),)),
            pltpu.SemaphoreType.DMA((2, n_row // 2)),
        ],
        compiler_params=params(48),
        cost_estimate=HEAVY,
        name="operator",
    )(ids, live, *in_hbm(rows, slots, values), *fields)


def product_kernel(n_row, n_col, origins, has_prev, last, n_carriers, *refs):
    n = len(origins)
    ids_ref, op_ref, refs = refs[0], refs[1], refs[2:]
    fields, refs = refs[:n], refs[n:]
    if has_prev:
        prev, refs = refs[0], refs[1:]
    carriers, refs = refs[:n_carriers], refs[n_carriers:]
    out_ref, held, buf, field_sems, sems, out, out_sems = refs[:7]
    order = [(k, p) for p in range(n_row // 2) for k in range(n)]

    def copy(k, p):
        return pltpu.make_async_copy(op_ref.at[origins[k], p], buf.at[k, p], sems.at[k, p])

    field_copies = fetch([x.at[pl.ds(0, H)] for x in fields], [held.at[k] for k in range(n)], field_sems)
    for k, p in order[:DEPTH]:
        copy(k, p).start()
    left = []
    for k in range(n):
        field_copies[k].wait()
        left.append(stacked(held[k]))
    if n_carriers:
        ordered = refs[7]
        for k in range(n_col):
            ordered[lax.rem(ids_ref[0] + k, n_col)] = carriers[k][H:, :]
        share = ordered[0]
        for k in range(1, n_col):
            share = share + ordered[k]
        rows = share.shape[0]
        groups = NODES_DEV // LANES // 2
        for j in range(groups):
            for q in range(n_row):
                from_lane = (q % 2 * groups + j) * LANES
                out[q, H + j * rows : H + (j + 1) * rows, :] = share[:, from_lane : from_lane + LANES]
    sent = []
    for p in range(n_row // 2):
        here = slice(p * WIDE, (p + 1) * WIDE)
        total = None
        for k in range(n):
            copy(k, p).wait()
            ahead = p * n + k + DEPTH
            if ahead < len(order):
                copy(*order[ahead]).start()
            part = jnp.dot(left[k], buf[k, p], preferred_element_type=F32)
            total = part if total is None else total + part
        summed = total[:H] + total[H:]
        if has_prev:
            summed = summed + prev[:, here]
        if last:
            out[2 * p, :H, :] = summed[:, :TB]
            out[2 * p + 1, :H, :] = summed[:, TB:]
            both = pl.ds(2 * p, 2)
            sent.append(pltpu.make_async_copy(out.at[both], out_ref.at[both], out_sems.at[p]))
            sent[-1].start()
        else:
            out_ref[:, here] = summed
    for item in sent:
        item.wait()


def product(n_row, n_col, ids, origins, operator, fields, prev, last, carriers=()):
    n = len(origins)
    has_prev = prev is not None
    share = 0
    scratch = [
        pltpu.VMEM((n, H, NODES_DEV), F32),
        pltpu.VMEM((n, n_row // 2, 2 * NODES_DEV, WIDE), BF16),
        pltpu.SemaphoreType.DMA((n,)),
        pltpu.SemaphoreType.DMA((n, n_row // 2)),
    ]
    if carriers:
        rows = carriers[0].shape[0] - H
        share = rows * NODES_DEV // LANES // 2
    scratch += [pltpu.VMEM((n_row, H + share, TB) if last else (8, LANES), F32), pltpu.SemaphoreType.DMA((n_row // 2,))]
    if carriers:
        scratch.append(pltpu.VMEM((n_col, rows, NODES_DEV), F32))
    shape = (n_row, H + share, TB) if last else (H, n_row * TB)
    count = has_prev + len(carriers)
    return pl.pallas_call(
        functools.partial(product_kernel, n_row, n_col, origins, has_prev, last, len(carriers)),
        in_specs=[SMEM, HBM] + [ANY] * n + [VMEM] * count,
        out_specs=HBM if last else VMEM,
        out_shape=(pltpu.HBM if last else jax.ShapeDtypeStruct)(shape, F32),
        scratch_shapes=scratch,
        compiler_params=params(48),
        cost_estimate=LIGHT if last else HEAVY,
        name="product",
    )(
        ids,
        *in_hbm(operator),
        *fields,
        *((prev,) if has_prev else ()),
        *carriers,
    )


def carry_kernel(n_row, rows, owners_ref, base_hbm, came_ref, *refs):
    out_ref, base, sems = refs[-3:]
    (base_copy,) = fetch([base_hbm], [base], sems)
    out_ref[:H, :] = jnp.zeros((H, NODES_DEV), F32)
    for q in range(n_row):
        here = pl.ds(pl.multiple_of(owners_ref[q] * TB, TB), TB)
        out_ref[:H, here] += came_ref[q]
    if rows:
        pieces_ref = refs[0]
        share = pieces_ref[0]
        for q in range(1, n_row):
            share = share + pieces_ref[q]
        for j in range(NODES_DEV // LANES):
            out_ref[H:, j * LANES : (j + 1) * LANES] = share[j * rows : (j + 1) * rows, :]
    base_copy.wait()
    out_ref[:H, :] = base[...] + 2.0 * out_ref[:H, :]


def carry(n_row, owners, base, came, *pieces):
    rows = pieces[0].shape[1] * LANES // NODES_DEV if pieces else 0
    return pl.pallas_call(
        functools.partial(carry_kernel, n_row, rows),
        in_specs=[SMEM, HBM] + [VMEM] * (1 + len(pieces)),
        out_specs=VMEM,
        out_shape=jax.ShapeDtypeStruct((H + rows, NODES_DEV), F32),
        scratch_shapes=[pltpu.VMEM((H, NODES_DEV), F32), pltpu.SemaphoreType.DMA((1,))],
        compiler_params=params(24),
        cost_estimate=LIGHT,
        name="carry",
    )(owners, *in_hbm(base), came, *pieces)


def finish_kernel(n_row, owners_ref, base_ref, left_ref, right_ref, out_ref, total):
    total[...] = base_ref[...]
    for h, came in enumerate((left_ref, right_ref)):
        for q in range(n_row):
            here = pl.ds(pl.multiple_of(owners_ref[q] * TB, TB), TB)
            total[h * H : (h + 1) * H, here] += came[q, :H, :]
    out_ref[...] = total[...].T


def finish(n_row, owners, base, left, right):
    return pl.pallas_call(
        functools.partial(finish_kernel, n_row),
        in_specs=[SMEM] + [VMEM] * 3,
        out_specs=VMEM,
        out_shape=jax.ShapeDtypeStruct((NODES_DEV, F), F32),
        scratch_shapes=[pltpu.VMEM((F, NODES_DEV), F32)],
        compiler_params=params(24),
        cost_estimate=LIGHT,
        name="finish",
    )(owners, base, left, right)


def assemble_kernel(n_row, row_ref, own_ref, other_ref, out_ref, halves, turned):
    rows = F // n_row
    half = lax.rem(row_ref[0], 2)
    halves[half] = own_ref[:, H:, :]
    halves[1 - half] = other_ref[:, H:, :]
    groups = 3 * F // LANES // 2
    for q in range(n_row):
        for j in range(2 * groups):
            here = slice(j % groups * rows, (j % groups + 1) * rows)
            turned[q * rows : (q + 1) * rows, j * LANES : (j + 1) * LANES] = halves[j // groups, q, here, :]
    for k in range(3):
        out_ref[k] = turned[:, k * F : (k + 1) * F].T


def assemble(n_row, row, own, other):
    return pl.pallas_call(
        functools.partial(assemble_kernel, n_row),
        in_specs=[SMEM, VMEM, VMEM],
        out_specs=VMEM,
        out_shape=jax.ShapeDtypeStruct((3, F, F), F32),
        scratch_shapes=[
            pltpu.VMEM((2, n_row, own.shape[1] - H, LANES), F32),
            pltpu.VMEM((F, 3 * F), F32),
        ],
        compiler_params=params(16),
        cost_estimate=LIGHT,
        name="assemble",
    )(row, own, other)


def shift(n_col, x, step):
    return lax.ppermute(x, "col", [(c, (c + step) % n_col) for c in range(n_col)])


def exchange(pieces):
    return lax.all_to_all(pieces, "row", split_axis=0, concat_axis=0, tiled=True)


def after(x, *others):
    return lax.optimization_barrier((x, *others))[0]


def opposite(field, below, above):
    col = lax.axis_index("col")
    sent = jnp.where(col == 1, above, jnp.where(col == 2, below, field))
    return lax.ppermute(sent, "col", [(1, 0), (2, 3), (3, 1), (0, 2)])


def gather(n_col, field, side):
    long = n_col // 2
    short = n_col - 1 - long
    ahead, behind = field, field
    steps = [[(0, field)]]
    for s in range(1, long + 1):
        if s == 2:
            ahead = after(ahead, behind)
        if s == 2 and n_col == 4:
            ahead = opposite(field, ahead, behind) if side > 0 else opposite(field, behind, ahead)
        else:
            ahead = shift(n_col, ahead, side)
        step = [((-side * s) % n_col, ahead)]
        if s <= short:
            behind = shift(n_col, behind, -side)
            step.append(((side * s) % n_col, behind))
        steps.append(step)
    return steps


def early(n_row, n_col, ids, operator, steps, total=None, done=0):
    pairs = [pair for step in steps[:-1] for pair in step][done:]
    for begin in range(0, len(pairs), 3):
        origins, fields = zip(*pairs[begin : begin + 3])
        total = product(n_row, n_col, ids, origins, operator, fields, total, False)
    return total


def final(n_row, n_col, ids, operator, steps, total, carrying=False):
    origins, fields = zip(*steps[-1])
    carriers = [x for _, x in sorted((p for step in steps for p in step), key=lambda p: p[0])] if carrying else ()
    return product(n_row, n_col, ids, origins, operator, fields, total, True, carriers)


def per_device(
    grad_out,
    relu_mask,
    basis_zero,
    basis_one,
    basis_two,
    cheb_weight,
    tile_values,
    tile_rows,
    tile_slots,
    send_blocks,
    live_tiles,
):
    n_row = lax.axis_size("row")
    n_col = lax.axis_size("col")
    ids = lax.axis_index("col").astype(jnp.int32).reshape(1)
    owners = send_blocks.reshape(n_row)
    left, right = term_two(grad_out, relu_mask, cheb_weight)
    one_left, one_right, diff, pieces = local_terms(
        n_row, left, grad_out, relu_mask, cheb_weight, basis_zero, basis_one, basis_two
    )
    steps = gather(n_col, left, 1)
    first = steps[0] + steps[1] if len(steps) > 2 else steps[0]
    operator, left_early = build_operator(
        n_row, n_col, ids, live_tiles, tile_rows, tile_slots, tile_values, first
    )
    pieces = exchange(pieces)
    common = (n_row, n_col, ids, operator)

    left_early = early(*common, steps, left_early, len(first))
    right_steps = gather(n_col, after(right, left_early, steps[-1][0][1]), -1)
    left_came = exchange(final(*common, steps, after(left_early, pieces)))
    right_early = early(*common, right_steps)

    left_carried = carry(n_row, owners, after(one_left, right_early, right_steps[-1][0][1]), left_came, pieces)
    steps = gather(n_col, left_carried, 1)
    right_came = exchange(final(*common, right_steps, right_early))
    left_early = early(*common, steps)

    right_carried = carry(n_row, owners, after(one_right, left_early, steps[-1][0][1]), right_came)
    right_steps = gather(n_col, right_carried, -1)
    left_came = exchange(final(*common, steps, left_early, carrying=True))
    right_early = early(*common, right_steps)

    right_last = final(*common, right_steps, right_early)
    right_came = exchange(right_last)
    other = lax.ppermute(after(left_came, right_last), "row", [(r, r ^ 1) for r in range(n_row)])
    row = lax.axis_index("row").astype(jnp.int32).reshape(1)
    weight_grad = assemble(n_row, row, left_came, other)
    return finish(n_row, owners, after(diff, weight_grad), left_came, right_came), weight_grad


def solution(mesh):
    placed = (
        P(("row", "col"), None),
        P(("row", "col"), None),
        P(("row", "col"), None),
        P(("row", "col"), None),
        P(("row", "col"), None),
        P(),
        P(("row", "col"), None, None, None),
        P(("row", "col"), None),
        P(("row", "col"), None),
        P(("row", "col"), None, None),
        P(("row", "col")),
    )
    return jax.shard_map(
        per_device,
        mesh=mesh,
        in_specs=placed,
        out_specs=(P(("row", "col"), None), P()),
        check_vma=False,
    )
```

```python
import functools

import jax
import jax.numpy as jnp
from jax import lax
from jax.experimental import pallas as pl
from jax.experimental.pallas import tpu as pltpu
from jax.sharding import PartitionSpec as P

F = 256
H = 128
TB = 128
CHB = 4
WIDE = 2 * TB
LANES = 128
NODES_DEV = CHB * TB
TILES_DEV = 128
GROUPS = 8
MIB = 1 << 20
WHOLE_BYTES = 12 * MIB
DEPTH = 4
HEAVY = pl.CostEstimate(flops=1 << 34, bytes_accessed=64 * MIB, transcendentals=0)
LIGHT = pl.CostEstimate(flops=1024, bytes_accessed=1024, transcendentals=0)
BF16 = jnp.bfloat16
F32 = jnp.float32

SMEM = pl.BlockSpec(memory_space=pltpu.SMEM)
VMEM = pl.BlockSpec(memory_space=pltpu.VMEM)
HBM = pl.BlockSpec(memory_space=pltpu.HBM)
ANY = pl.BlockSpec(memory_space=pl.ANY)


def params(mib):
    return pltpu.CompilerParams(vmem_limit_bytes=mib * MIB)


def in_hbm(*arrays):
    return [pltpu.with_memory_space_constraint(x, pltpu.HBM) for x in arrays]


def split(x):
    high = x.astype(BF16)
    low = (x - high.astype(F32)).astype(BF16)
    return high, low


def dot3(a, b, dims):
    ah, al = a
    bh, bl = b

    def one(x, y):
        return lax.dot_general(x, y, (dims, ((), ())), preferred_element_type=F32)

    return one(ah, bh) + (one(ah, bl) + one(al, bh))


def fetch(sources, targets, sems):
    copies = [pltpu.make_async_copy(a, b, sems.at[i]) for i, (a, b) in enumerate(zip(sources, targets))]
    for copy in copies:
        copy.start()
    return copies


def masked_of(grad, mask):
    return jnp.where(mask > 0, grad, jnp.zeros_like(grad))


def term_two_kernel(grad_hbm, mask_hbm, weight_hbm, left_ref, right_ref, grad, mask, weight, sems):
    for copy in fetch((grad_hbm, mask_hbm, weight_hbm.at[2]), (grad, mask, weight), sems):
        copy.wait()
    term = dot3(split(weight[...]), split(masked_of(grad[...], mask[...])), ((1,), (1,)))
    left_ref[...] = term[:H]
    right_ref[...] = term[H:]


def term_two(grad_out, relu_mask, cheb_weight):
    out = jax.ShapeDtypeStruct((H, NODES_DEV), F32)
    return pl.pallas_call(
        term_two_kernel,
        in_specs=[HBM] * 3,
        out_specs=[VMEM, VMEM],
        out_shape=[out, out],
        scratch_shapes=[
            pltpu.VMEM((NODES_DEV, F), F32),
            pltpu.VMEM((NODES_DEV, F), jnp.int32),
            pltpu.VMEM((F, F), F32),
            pltpu.SemaphoreType.DMA((3,)),
        ],
        compiler_params=params(16),
        cost_estimate=LIGHT,
        name="term_two",
    )(*in_hbm(grad_out, relu_mask, cheb_weight))


def local_kernel(
    n_row, first_ref, grad_hbm, mask_hbm, weight_hbm, h0, h1, h2, left_hbm, right_hbm, diff_ref, pieces_ref,
    grad, mask, weight, bases, one, sems, one_sems,
):
    sources = (grad_hbm, mask_hbm, weight_hbm, h0, h1, h2)
    copies = fetch(sources, (grad, mask, weight, bases.at[0], bases.at[1], bases.at[2]), sems)
    for copy in copies[:3]:
        copy.wait()
    values = masked_of(grad[...], mask[...])
    masked = split(values)
    term = dot3(split(weight[1]), masked, ((1,), (1,)))
    one[...] = term
    one_copies = fetch((one.at[pl.ds(0, H)], one.at[pl.ds(H, H)]), (left_hbm, right_hbm), one_sems)
    diff_ref[...] = dot3(split(weight[0] - weight[2]), masked, ((1,), (1,)))
    turned = split(values.T)
    rows = F // n_row
    for k in range(3):
        copies[3 + k].wait()
        part = dot3(turned, split(bases[k]), ((1,), (0,)))
        for j in range(F // LANES):
            here = (k * (F // LANES) + j) * rows
            for q in range(n_row):
                pieces_ref[q, here : here + rows, :] = part[q * rows : (q + 1) * rows, j * LANES : (j + 1) * LANES]
    for copy in one_copies:
        copy.wait()


def local_terms(n_row, first, grad_out, relu_mask, cheb_weight, b0, b1, b2):
    half = pltpu.HBM((H, NODES_DEV), F32)
    share = 3 * F * F // n_row // LANES
    return pl.pallas_call(
        functools.partial(local_kernel, n_row),
        in_specs=[ANY] + [HBM] * 6,
        out_specs=[HBM, HBM, VMEM, VMEM],
        out_shape=[
            half,
            half,
            jax.ShapeDtypeStruct((F, NODES_DEV), F32),
            jax.ShapeDtypeStruct((n_row, share, LANES), F32),
        ],
        scratch_shapes=[
            pltpu.VMEM((NODES_DEV, F), F32),
            pltpu.VMEM((NODES_DEV, F), jnp.int32),
            pltpu.VMEM((3, F, F), F32),
            pltpu.VMEM((3, NODES_DEV, F), F32),
            pltpu.VMEM((F, NODES_DEV), F32),
            pltpu.SemaphoreType.DMA((6,)),
            pltpu.SemaphoreType.DMA((2,)),
        ],
        compiler_params=params(32),
        cost_estimate=LIGHT,
        name="local_terms",
    )(first, *in_hbm(grad_out, relu_mask, cheb_weight, b0, b1, b2))


def stacked(field):
    return jnp.concatenate(split(field), axis=0)


def times(left, part):
    by_high = jnp.dot(left, part[:NODES_DEV, :], preferred_element_type=F32)
    by_low = jnp.dot(left[:H], part[NODES_DEV:, :], preferred_element_type=F32)
    return by_high[:H] + (by_high[H:] + by_low)


def operator_kernel(n_row, n_col, origins, ids_ref, live_ref, rows_hbm, slots_hbm, values_ref, *refs):
    fields, refs = refs[: len(origins)], refs[len(origins) :]
    out_hbm, total_ref, tiles, acc, buf, held, lists, counts, rows, slots, sems, small_sems, field_sems, out_sems = refs
    size = TILES_DEV // GROUPS
    pairs = n_row // 2
    whole = acc.shape[0] == n_col
    small = fetch((rows_hbm, slots_hbm), (rows, slots), small_sems)
    parts = [pl.ds(g * size, size) for g in range(GROUPS)]
    tile_copies = fetch([values_ref.at[0, part] for part in parts], [tiles.at[part] for part in parts], sems)
    field_copies = fetch(fields, [held.at[k] for k in range(len(fields))], field_sems)
    for item in small:
        item.wait()

    def place_of(t):
        row = rows[0, t]
        if n_col & (n_col - 1) == 0:
            s = (lax.shift_right_logical(row, CHB.bit_length() - 1) - ids_ref[0]) & (n_col - 1)
        else:
            s = lax.rem(row // CHB - ids_ref[0] + n_col, n_col)
        return s, slots[0, t] * CHB + (row & (CHB - 1))

    def add_block(into, position, tile):
        slot = lax.shift_right_logical(position, CHB.bit_length() - 1)
        at_row = pl.ds(pl.multiple_of((position & (CHB - 1)) * TB, TB), TB)
        at_lane = pl.ds(pl.multiple_of((slot & 1) * TB, TB), TB)
        acc[into, lax.shift_right_logical(slot, 1), at_row, at_lane] += tiles[tile]

    if whole:

        def add_now(t, carry):
            s, position = place_of(t)
            add_block(s, position, t)
            return carry

        acc[...] = jnp.zeros_like(acc)
        for g, item in enumerate(tile_copies):
            item.wait()
            end = (g + 1) * size

            @pl.when(live_ref[0] >= end)
            def _():
                lax.fori_loop(end - size, end, add_now, 0, unroll=4)

            @pl.when(live_ref[0] < end)
            def _():
                lax.fori_loop(end - size, live_ref[0], add_now, 0)

    else:

        def place(t, counted):
            s, position = place_of(t)
            n = counted[0]
            for k in range(1, n_col):
                n = jnp.where(s == k, counted[k], n)
            lists[s, n] = position * TILES_DEV + t
            return tuple(c + (s == k).astype(jnp.int32) for k, c in enumerate(counted))

        counted = lax.fori_loop(0, live_ref[0], place, (jnp.int32(0),) * n_col)
        for s in range(n_col):
            counts[s] = counted[s]
        for item in tile_copies:
            item.wait()

    def out_copy(origin, p):
        return pltpu.make_async_copy(buf.at[origin % 2, p], out_hbm.at[origin, p], out_sems.at[origin % 2, p])

    for origin in range(n_col):
        if not whole:

            def add(n, carry):
                entry = lists[origin, n]
                add_block(0, lax.shift_right_logical(entry, TILES_DEV.bit_length() - 1), entry & (TILES_DEV - 1))
                return carry

            acc[...] = jnp.zeros_like(acc)
            lax.fori_loop(0, counts[origin], add, 0)
        summed_blocks = acc.at[origin if whole else 0]
        for p in range(pairs):
            if origin >= 2:
                out_copy(origin - 2, p).wait()
            high, low = split(summed_blocks[p])
            buf[origin % 2, p, :NODES_DEV, :] = high
            buf[origin % 2, p, NODES_DEV:, :] = low
            out_copy(origin, p).start()
        if origin in origins:
            k = origins.index(origin)
            field_copies[k].wait()
            left = stacked(held[k])
            for p in range(pairs):
                summed = times(left, buf.at[origin % 2, p])
                here = slice(p * WIDE, (p + 1) * WIDE)
                total_ref[:, here] = summed if origin == 0 else total_ref[:, here] + summed
    for origin in range(n_col - 2, n_col):
        for p in range(pairs):
            out_copy(origin, p).wait()


def build_operator(n_row, n_col, ids, live, rows, slots, values, pairs):
    part = (n_row // 2, 2 * NODES_DEV, WIDE)
    sums = (n_row // 2, NODES_DEV, WIDE)
    held_origins = n_col if 4 * n_col * n_row * TB * NODES_DEV <= WHOLE_BYTES else 1
    origins, fields = zip(*pairs)
    return pl.pallas_call(
        functools.partial(operator_kernel, n_row, n_col, origins),
        in_specs=[SMEM] * 2 + [HBM] * 3 + [ANY] * len(fields),
        out_specs=[HBM, VMEM],
        out_shape=[pltpu.HBM((n_col,) + part, BF16), jax.ShapeDtypeStruct((H, n_row * TB), F32)],
        scratch_shapes=[
            pltpu.VMEM((TILES_DEV, TB, TB), F32),
            pltpu.VMEM((held_origins,) + sums, F32),
            pltpu.VMEM((2,) + part, BF16),
            pltpu.VMEM((len(fields), H, NODES_DEV), F32),
            pltpu.SMEM((n_col, TILES_DEV), jnp.int32),
            pltpu.SMEM((n_col,), jnp.int32),
            pltpu.SMEM((1, TILES_DEV), jnp.int32),
            pltpu.SMEM((1, TILES_DEV), jnp.int32),
            pltpu.SemaphoreType.DMA((GROUPS,)),
            pltpu.SemaphoreType.DMA((2,)),
            pltpu.SemaphoreType.DMA((len(fields),)),
            pltpu.SemaphoreType.DMA((2, n_row // 2)),
        ],
        compiler_params=params(48),
        cost_estimate=HEAVY,
        name="operator",
    )(ids, live, *in_hbm(rows, slots, values), *fields)


def product_kernel(n_row, n_col, origins, has_prev, last, n_carriers, has_base, *refs):
    n = len(origins)
    ids_ref, op_ref, refs = refs[0], refs[1], refs[2:]
    fields, refs = refs[:n], refs[n:]
    if has_prev:
        prev_hbm, refs = refs[0], refs[1:]
    carriers, refs = refs[:n_carriers], refs[n_carriers:]
    if has_base:
        base_hbm, out_ref, base_ref, refs = refs[0], refs[1], refs[2], refs[3:]
    else:
        out_ref, refs = refs[0], refs[1:]
    held, buf, field_sems, sems, out, out_sems, prev, other_sems = refs[:8]
    order = [(k, p) for p in range(n_row // 2) for k in range(n)]

    def copy(k, p):
        return pltpu.make_async_copy(op_ref.at[origins[k], p], buf.at[k, p], sems.at[k, p])

    field_copies = fetch([x.at[pl.ds(0, H)] for x in fields], [held.at[k] for k in range(n)], field_sems)
    for k, p in order[:DEPTH]:
        copy(k, p).start()
    if has_prev:
        (prev_copy,) = fetch([prev_hbm], [prev], other_sems.at[pl.ds(0, 1)])
    if has_base:
        (base_copy,) = fetch([base_hbm], [base_ref], other_sems.at[pl.ds(1, 1)])
    left = []
    for k in range(n):
        field_copies[k].wait()
        left.append(stacked(held[k]))
    if n_carriers:
        ordered = refs[8]
        for k in range(n_col):
            ordered[lax.rem(ids_ref[0] + k, n_col)] = carriers[k][H:, :]
        share = ordered[0]
        for k in range(1, n_col):
            share = share + ordered[k]
        rows = share.shape[0]
        groups = NODES_DEV // LANES // 2
        for j in range(groups):
            for q in range(n_row):
                from_lane = (q % 2 * groups + j) * LANES
                out[q, H + j * rows : H + (j + 1) * rows, :] = share[:, from_lane : from_lane + LANES]
    sent = []
    for p in range(n_row // 2):
        here = slice(p * WIDE, (p + 1) * WIDE)
        total = None
        for k in range(n):
            copy(k, p).wait()
            ahead = p * n + k + DEPTH
            if ahead < len(order):
                copy(*order[ahead]).start()
            part = times(left[k], buf.at[k, p])
            total = part if total is None else total + part
        if has_prev:
            if p == 0:
                prev_copy.wait()
            total = total + prev[:, here]
        if last:
            out[2 * p, :H, :] = total[:, :TB]
            out[2 * p + 1, :H, :] = total[:, TB:]
            place = pl.ds(2 * p, 2)
            sent.append(pltpu.make_async_copy(out.at[place], out_ref.at[place], out_sems.at[p]))
        else:
            out[:, here] = total
            place = (pl.ds(0, H), pl.ds(p * WIDE, WIDE))
            sent.append(pltpu.make_async_copy(out.at[place], out_ref.at[place], out_sems.at[p]))
        sent[-1].start()
    if has_base:
        base_copy.wait()
    for item in sent:
        item.wait()


def product(n_row, n_col, ids, origins, operator, fields, prev, last, carriers=(), base=None, prev_near=False):
    n = len(origins)
    has_prev = prev is not None
    has_base = base is not None
    rows = carriers[0].shape[0] - H if carriers else 0
    under = rows * NODES_DEV // LANES // 2
    shape = (n_row, H + under, TB) if last else (H, n_row * TB)
    scratch = [
        pltpu.VMEM((n, H, NODES_DEV), F32),
        pltpu.VMEM((n, n_row // 2, 2 * NODES_DEV, WIDE), BF16),
        pltpu.SemaphoreType.DMA((n,)),
        pltpu.SemaphoreType.DMA((n, n_row // 2)),
        pltpu.VMEM(shape, F32),
        pltpu.SemaphoreType.DMA((n_row // 2,)),
        pltpu.VMEM((H, n_row * TB) if has_prev else (8, LANES), F32),
        pltpu.SemaphoreType.DMA((2,)),
    ]
    if carriers:
        scratch.append(pltpu.VMEM((n_col, rows, NODES_DEV), F32))
    out = pltpu.HBM(shape, F32)
    return pl.pallas_call(
        functools.partial(product_kernel, n_row, n_col, origins, has_prev, last, len(carriers), has_base),
        in_specs=[SMEM, HBM] + [ANY] * (n + has_prev) + [VMEM] * len(carriers) + [HBM] * has_base,
        out_specs=[HBM, VMEM] if has_base else HBM,
        out_shape=[out, jax.ShapeDtypeStruct(base.shape, F32)] if has_base else out,
        scratch_shapes=scratch,
        compiler_params=params(48),
        cost_estimate=LIGHT if last else HEAVY,
        name="product",
    )(
        ids,
        *in_hbm(operator),
        *fields,
        *((prev,) if prev_near else in_hbm(prev) if has_prev else ()),
        *carriers,
        *(in_hbm(base) if has_base else ()),
    )


def carry_kernel(n_row, rows, owners_ref, base_ref, came_ref, *refs):
    out_ref = refs[-1]
    out_ref[:H, :] = base_ref[...]
    for q in range(n_row):
        here = pl.ds(pl.multiple_of(owners_ref[q] * TB, TB), TB)
        out_ref[:H, here] += 2.0 * came_ref[q]
    if rows:
        pieces_ref = refs[0]
        share = pieces_ref[0]
        for q in range(1, n_row):
            share = share + pieces_ref[q]
        for j in range(NODES_DEV // LANES):
            out_ref[H:, j * LANES : (j + 1) * LANES] = share[j * rows : (j + 1) * rows, :]


def carry(n_row, owners, base, came, *pieces):
    rows = pieces[0].shape[1] * LANES // NODES_DEV if pieces else 0
    return pl.pallas_call(
        functools.partial(carry_kernel, n_row, rows),
        in_specs=[SMEM] + [VMEM] * (2 + len(pieces)),
        out_specs=VMEM,
        out_shape=jax.ShapeDtypeStruct((H + rows, NODES_DEV), F32),
        compiler_params=params(24),
        cost_estimate=LIGHT,
        name="carry",
    )(owners, base, came, *pieces)


def finish_kernel(n_row, owners_ref, base_ref, left_ref, right_ref, out_ref, total):
    total[...] = base_ref[...]
    for h, came in enumerate((left_ref, right_ref)):
        for q in range(n_row):
            here = pl.ds(pl.multiple_of(owners_ref[q] * TB, TB), TB)
            total[h * H : (h + 1) * H, here] += came[q, :H, :]
    out_ref[...] = total[...].T


def finish(n_row, owners, base, left, right):
    return pl.pallas_call(
        functools.partial(finish_kernel, n_row),
        in_specs=[SMEM] + [VMEM] * 3,
        out_specs=VMEM,
        out_shape=jax.ShapeDtypeStruct((NODES_DEV, F), F32),
        scratch_shapes=[pltpu.VMEM((F, NODES_DEV), F32)],
        compiler_params=params(24),
        cost_estimate=LIGHT,
        name="finish",
    )(owners, base, left, right)


def assemble_kernel(n_row, row_ref, own_ref, other_ref, out_ref, halves, turned):
    rows = F // n_row
    half = lax.rem(row_ref[0], 2)
    halves[half] = own_ref[:, H:, :]
    halves[1 - half] = other_ref[:, H:, :]
    groups = 3 * F // LANES // 2
    for q in range(n_row):
        for j in range(2 * groups):
            here = slice(j % groups * rows, (j % groups + 1) * rows)
            turned[q * rows : (q + 1) * rows, j * LANES : (j + 1) * LANES] = halves[j // groups, q, here, :]
    for k in range(3):
        out_ref[k] = turned[:, k * F : (k + 1) * F].T


def assemble(n_row, row, own, other):
    return pl.pallas_call(
        functools.partial(assemble_kernel, n_row),
        in_specs=[SMEM, VMEM, VMEM],
        out_specs=VMEM,
        out_shape=jax.ShapeDtypeStruct((3, F, F), F32),
        scratch_shapes=[
            pltpu.VMEM((2, n_row, own.shape[1] - H, LANES), F32),
            pltpu.VMEM((F, 3 * F), F32),
        ],
        compiler_params=params(16),
        cost_estimate=LIGHT,
        name="assemble",
    )(row, own, other)


def shift(n_col, x, step):
    return lax.ppermute(x, "col", [(c, (c + step) % n_col) for c in range(n_col)])


def exchange(pieces):
    return lax.all_to_all(pieces, "row", split_axis=0, concat_axis=0, tiled=True)


def after(x, *others):
    return lax.optimization_barrier((x, *others))[0]


def opposite(field, below, above):
    col = lax.axis_index("col")
    sent = jnp.where(col == 1, above, jnp.where(col == 2, below, field))
    return lax.ppermute(sent, "col", [(1, 0), (2, 3), (3, 1), (0, 2)])


def gather(n_col, field, side):
    long = n_col // 2
    short = n_col - 1 - long
    ahead, behind = field, field
    steps = [[(0, field)]]
    for s in range(1, long + 1):
        if s == 2:
            ahead = after(ahead, behind)
        if s == 2 and n_col == 4:
            ahead = opposite(field, ahead, behind) if side > 0 else opposite(field, behind, ahead)
        else:
            ahead = shift(n_col, ahead, side)
        step = [((-side * s) % n_col, ahead)]
        if s <= short:
            behind = shift(n_col, behind, -side)
            step.append(((side * s) % n_col, behind))
        steps.append(step)
    return steps


def early(n_row, n_col, ids, operator, steps, total=None, done=0, base=None):
    pairs = [pair for step in steps[:-1] for pair in step][done:]
    for begin in range(0, len(pairs), 3):
        origins, fields = zip(*pairs[begin : begin + 3])
        brought = base if begin + 3 >= len(pairs) else None
        total = product(n_row, n_col, ids, origins, operator, fields, total, False, base=brought)
    return total


def final(n_row, n_col, ids, operator, steps, total, carrying=False, near=False):
    origins, fields = zip(*steps[-1])
    carriers = [x for _, x in sorted((p for step in steps for p in step), key=lambda p: p[0])] if carrying else ()
    return product(n_row, n_col, ids, origins, operator, fields, total, True, carriers, prev_near=near)


def per_device(
    grad_out,
    relu_mask,
    basis_zero,
    basis_one,
    basis_two,
    cheb_weight,
    tile_values,
    tile_rows,
    tile_slots,
    send_blocks,
    live_tiles,
):
    n_row = lax.axis_size("row")
    n_col = lax.axis_size("col")
    ids = lax.axis_index("col").astype(jnp.int32).reshape(1)
    owners = send_blocks.reshape(n_row)
    left, right = term_two(grad_out, relu_mask, cheb_weight)
    one_left, one_right, diff, pieces = local_terms(
        n_row, left, grad_out, relu_mask, cheb_weight, basis_zero, basis_one, basis_two
    )
    steps = gather(n_col, left, 1)
    first = steps[0] + steps[1] if len(steps) > 2 else steps[0]
    operator, left_early = build_operator(
        n_row, n_col, ids, live_tiles, tile_rows, tile_slots, tile_values, first
    )
    pieces = exchange(pieces)
    common = (n_row, n_col, ids, operator)

    left_early = early(*common, steps, left_early, len(first))
    right_steps = gather(n_col, after(right, left_early, steps[-1][0][1]), -1)
    left_came = exchange(final(*common, steps, after(left_early, pieces), near=len(steps) == 3))
    right_early, one_left = early(*common, right_steps, base=one_left)

    left_carried = carry(n_row, owners, after(one_left, right_early, right_steps[-1][0][1]), left_came, pieces)
    steps = gather(n_col, left_carried, 1)
    right_came = exchange(final(*common, right_steps, right_early))
    left_early, one_right = early(*common, steps, base=one_right)

    right_carried = carry(n_row, owners, after(one_right, left_early, steps[-1][0][1]), right_came)
    right_steps = gather(n_col, right_carried, -1)
    left_came = exchange(final(*common, steps, left_early, carrying=True))
    right_early = early(*common, right_steps)

    right_last = final(*common, right_steps, right_early)
    right_came = exchange(right_last)
    other = lax.ppermute(after(left_came, right_last), "row", [(r, r ^ 1) for r in range(n_row)])
    row = lax.axis_index("row").astype(jnp.int32).reshape(1)
    weight_grad = assemble(n_row, row, left_came, other)
    return finish(n_row, owners, after(diff, weight_grad), left_came, right_came), weight_grad


def solution(mesh):
    placed = (
        P(("row", "col"), None),
        P(("row", "col"), None),
        P(("row", "col"), None),
        P(("row", "col"), None),
        P(("row", "col"), None),
        P(),
        P(("row", "col"), None, None, None),
        P(("row", "col"), None),
        P(("row", "col"), None),
        P(("row", "col"), None, None),
        P(("row", "col")),
    )
    return jax.shard_map(
        per_device,
        mesh=mesh,
        in_specs=placed,
        out_specs=(P(("row", "col"), None), P()),
        check_vma=False,
    )
```

```python
import functools

import jax
import jax.numpy as jnp
from jax import lax
from jax.experimental import pallas as pl
from jax.experimental.pallas import tpu as pltpu
from jax.sharding import PartitionSpec as P

F = 256
H = 128
TB = 128
CHB = 4
WIDE = 2 * TB
LANES = 128
NODES_DEV = CHB * TB
TILES_DEV = 128
GROUPS = 8
MIB = 1 << 20
WHOLE_BYTES = 12 * MIB
DEPTH = 4
HEAVY = pl.CostEstimate(flops=1 << 34, bytes_accessed=64 * MIB, transcendentals=0)
LIGHT = pl.CostEstimate(flops=1024, bytes_accessed=1024, transcendentals=0)
BF16 = jnp.bfloat16
F32 = jnp.float32

SMEM = pl.BlockSpec(memory_space=pltpu.SMEM)
VMEM = pl.BlockSpec(memory_space=pltpu.VMEM)
HBM = pl.BlockSpec(memory_space=pltpu.HBM)
ANY = pl.BlockSpec(memory_space=pl.ANY)


def params(mib):
    return pltpu.CompilerParams(vmem_limit_bytes=mib * MIB)


def in_hbm(*arrays):
    return [pltpu.with_memory_space_constraint(x, pltpu.HBM) for x in arrays]


def split(x):
    high = x.astype(BF16)
    low = (x - high.astype(F32)).astype(BF16)
    return high, low


def dot3(a, b, dims):
    ah, al = a
    bh, bl = b

    def one(x, y):
        return lax.dot_general(x, y, (dims, ((), ())), preferred_element_type=F32)

    return one(ah, bh) + (one(ah, bl) + one(al, bh))


def fetch(sources, targets, sems):
    copies = [pltpu.make_async_copy(a, b, sems.at[i]) for i, (a, b) in enumerate(zip(sources, targets))]
    for copy in copies:
        copy.start()
    return copies


def masked_of(grad, mask):
    return jnp.where(mask > 0, grad, jnp.zeros_like(grad))


def term_two_kernel(grad_hbm, mask_hbm, weight_hbm, left_ref, right_ref, grad, mask, weight, sems):
    for copy in fetch((grad_hbm, mask_hbm, weight_hbm.at[2]), (grad, mask, weight), sems):
        copy.wait()
    term = dot3(split(weight[...]), split(masked_of(grad[...], mask[...])), ((1,), (1,)))
    left_ref[...] = term[:H]
    right_ref[...] = term[H:]


def term_two(grad_out, relu_mask, cheb_weight):
    out = jax.ShapeDtypeStruct((H, NODES_DEV), F32)
    return pl.pallas_call(
        term_two_kernel,
        in_specs=[HBM] * 3,
        out_specs=[VMEM, VMEM],
        out_shape=[out, out],
        scratch_shapes=[
            pltpu.VMEM((NODES_DEV, F), F32),
            pltpu.VMEM((NODES_DEV, F), jnp.int32),
            pltpu.VMEM((F, F), F32),
            pltpu.SemaphoreType.DMA((3,)),
        ],
        compiler_params=params(16),
        cost_estimate=LIGHT,
        name="term_two",
    )(*in_hbm(grad_out, relu_mask, cheb_weight))


def local_kernel(
    n_row, first_ref, grad_hbm, mask_hbm, weight_hbm, h0, h1, h2, left_hbm, right_hbm, diff_ref, pieces_ref,
    grad, mask, weight, bases, one, sems, one_sems,
):
    sources = (grad_hbm, mask_hbm, weight_hbm, h0, h1, h2)
    copies = fetch(sources, (grad, mask, weight, bases.at[0], bases.at[1], bases.at[2]), sems)
    for copy in copies[:3]:
        copy.wait()
    values = masked_of(grad[...], mask[...])
    masked = split(values)
    term = dot3(split(weight[1]), masked, ((1,), (1,)))
    one[...] = term
    one_copies = fetch((one.at[pl.ds(0, H)], one.at[pl.ds(H, H)]), (left_hbm, right_hbm), one_sems)
    diff_ref[...] = dot3(split(weight[0] - weight[2]), masked, ((1,), (1,)))
    turned = split(values.T)
    rows = F // n_row
    for k in range(3):
        copies[3 + k].wait()
        part = dot3(turned, split(bases[k]), ((1,), (0,)))
        for j in range(F // LANES):
            here = (k * (F // LANES) + j) * rows
            for q in range(n_row):
                pieces_ref[q, here : here + rows, :] = part[q * rows : (q + 1) * rows, j * LANES : (j + 1) * LANES]
    for copy in one_copies:
        copy.wait()


def local_terms(n_row, first, grad_out, relu_mask, cheb_weight, b0, b1, b2):
    half = pltpu.HBM((H, NODES_DEV), F32)
    share = 3 * F * F // n_row // LANES
    return pl.pallas_call(
        functools.partial(local_kernel, n_row),
        in_specs=[ANY] + [HBM] * 6,
        out_specs=[HBM, HBM, VMEM, VMEM],
        out_shape=[
            half,
            half,
            jax.ShapeDtypeStruct((F, NODES_DEV), F32),
            jax.ShapeDtypeStruct((n_row, share, LANES), F32),
        ],
        scratch_shapes=[
            pltpu.VMEM((NODES_DEV, F), F32),
            pltpu.VMEM((NODES_DEV, F), jnp.int32),
            pltpu.VMEM((3, F, F), F32),
            pltpu.VMEM((3, NODES_DEV, F), F32),
            pltpu.VMEM((F, NODES_DEV), F32),
            pltpu.SemaphoreType.DMA((6,)),
            pltpu.SemaphoreType.DMA((2,)),
        ],
        compiler_params=params(32),
        cost_estimate=LIGHT,
        name="local_terms",
    )(first, *in_hbm(grad_out, relu_mask, cheb_weight, b0, b1, b2))


def stacked(field):
    return jnp.concatenate(split(field), axis=0)


def times(left, part):
    by_high = jnp.dot(left, part[:NODES_DEV, :], preferred_element_type=F32)
    by_low = jnp.dot(left[:H], part[NODES_DEV:, :], preferred_element_type=F32)
    return by_high[:H] + (by_high[H:] + by_low)


def operator_kernel(n_row, n_col, origins, ids_ref, live_ref, rows_hbm, slots_hbm, values_ref, *refs):
    fields, refs = refs[: len(origins)], refs[len(origins) :]
    out_hbm, total_ref, tiles, acc, buf, held, lists, counts, rows, slots, sems, small_sems, field_sems, out_sems = refs
    size = TILES_DEV // GROUPS
    pairs = n_row // 2
    whole = acc.shape[0] == n_col
    small = fetch((rows_hbm, slots_hbm), (rows, slots), small_sems)
    parts = [pl.ds(g * size, size) for g in range(GROUPS)]
    tile_copies = fetch([values_ref.at[0, part] for part in parts], [tiles.at[part] for part in parts], sems)
    field_copies = fetch(fields, [held.at[k] for k in range(len(fields))], field_sems)
    for item in small:
        item.wait()

    def place_of(t):
        row = rows[0, t]
        if n_col & (n_col - 1) == 0:
            s = (lax.shift_right_logical(row, CHB.bit_length() - 1) - ids_ref[0]) & (n_col - 1)
        else:
            s = lax.rem(row // CHB - ids_ref[0] + n_col, n_col)
        return s, slots[0, t] * CHB + (row & (CHB - 1))

    def add_block(into, position, tile):
        slot = lax.shift_right_logical(position, CHB.bit_length() - 1)
        at_row = pl.ds(pl.multiple_of((position & (CHB - 1)) * TB, TB), TB)
        at_lane = pl.ds(pl.multiple_of((slot & 1) * TB, TB), TB)
        acc[into, lax.shift_right_logical(slot, 1), at_row, at_lane] += tiles[tile]

    if whole:

        def add_now(t, carry):
            s, position = place_of(t)
            add_block(s, position, t)
            return carry

        acc[...] = jnp.zeros_like(acc)
        for g, item in enumerate(tile_copies):
            item.wait()
            end = (g + 1) * size

            @pl.when(live_ref[0] >= end)
            def _():
                lax.fori_loop(end - size, end, add_now, 0, unroll=4)

            @pl.when(live_ref[0] < end)
            def _():
                lax.fori_loop(end - size, live_ref[0], add_now, 0)

    else:

        def place(t, counted):
            s, position = place_of(t)
            n = counted[0]
            for k in range(1, n_col):
                n = jnp.where(s == k, counted[k], n)
            lists[s, n] = position * TILES_DEV + t
            return tuple(c + (s == k).astype(jnp.int32) for k, c in enumerate(counted))

        counted = lax.fori_loop(0, live_ref[0], place, (jnp.int32(0),) * n_col)
        for s in range(n_col):
            counts[s] = counted[s]
        for item in tile_copies:
            item.wait()

    def out_copy(origin, p):
        return pltpu.make_async_copy(buf.at[origin % 2, p], out_hbm.at[origin, p], out_sems.at[origin % 2, p])

    for origin in range(n_col):
        if not whole:

            def add(n, carry):
                entry = lists[origin, n]
                add_block(0, lax.shift_right_logical(entry, TILES_DEV.bit_length() - 1), entry & (TILES_DEV - 1))
                return carry

            acc[...] = jnp.zeros_like(acc)
            lax.fori_loop(0, counts[origin], add, 0)
        summed_blocks = acc.at[origin if whole else 0]
        for p in range(pairs):
            if origin >= 2:
                out_copy(origin - 2, p).wait()
            high, low = split(summed_blocks[p])
            buf[origin % 2, p, :NODES_DEV, :] = high
            buf[origin % 2, p, NODES_DEV:, :] = low
            out_copy(origin, p).start()
        if origin in origins:
            k = origins.index(origin)
            field_copies[k].wait()
            left = stacked(held[k])
            for p in range(pairs):
                summed = times(left, buf.at[origin % 2, p])
                here = slice(p * WIDE, (p + 1) * WIDE)
                total_ref[:, here] = summed if origin == 0 else total_ref[:, here] + summed
    for origin in range(n_col - 2, n_col):
        for p in range(pairs):
            out_copy(origin, p).wait()


def build_operator(n_row, n_col, ids, live, rows, slots, values, pairs):
    part = (n_row // 2, 2 * NODES_DEV, WIDE)
    sums = (n_row // 2, NODES_DEV, WIDE)
    held_origins = n_col if 4 * n_col * n_row * TB * NODES_DEV <= WHOLE_BYTES else 1
    origins, fields = zip(*pairs)
    return pl.pallas_call(
        functools.partial(operator_kernel, n_row, n_col, origins),
        in_specs=[SMEM] * 2 + [HBM] * 3 + [ANY] * len(fields),
        out_specs=[HBM, VMEM],
        out_shape=[pltpu.HBM((n_col,) + part, BF16), jax.ShapeDtypeStruct((H, n_row * TB), F32)],
        scratch_shapes=[
            pltpu.VMEM((TILES_DEV, TB, TB), F32),
            pltpu.VMEM((held_origins,) + sums, F32),
            pltpu.VMEM((2,) + part, BF16),
            pltpu.VMEM((len(fields), H, NODES_DEV), F32),
            pltpu.SMEM((n_col, TILES_DEV), jnp.int32),
            pltpu.SMEM((n_col,), jnp.int32),
            pltpu.SMEM((1, TILES_DEV), jnp.int32),
            pltpu.SMEM((1, TILES_DEV), jnp.int32),
            pltpu.SemaphoreType.DMA((GROUPS,)),
            pltpu.SemaphoreType.DMA((2,)),
            pltpu.SemaphoreType.DMA((len(fields),)),
            pltpu.SemaphoreType.DMA((2, n_row // 2)),
        ],
        compiler_params=params(48),
        cost_estimate=HEAVY,
        name="operator",
    )(ids, live, *in_hbm(rows, slots, values), *fields)


def product_kernel(n_row, n_col, origins, has_prev, last, n_carriers, has_base, apart, *refs):
    n = len(origins)
    ids_ref, op_ref, refs = refs[0], refs[1], refs[2:]
    fields, refs = refs[:n], refs[n:]
    if has_prev:
        prev_hbm, refs = refs[0], refs[1:]
    carriers, refs = refs[:n_carriers], refs[n_carriers:]
    if has_base:
        base_hbm, out_ref, base_ref, refs = refs[0], refs[1], refs[2], refs[3:]
    elif apart:
        slot_refs, refs = refs[:n_row], refs[n_row:]
    else:
        out_ref, refs = refs[0], refs[1:]
    held, buf, field_sems, sems, out, out_sems, prev, other_sems = refs[:8]
    order = [(k, p) for p in range(n_row // 2) for k in range(n)]

    def copy(k, p):
        return pltpu.make_async_copy(op_ref.at[origins[k], p], buf.at[k, p], sems.at[k, p])

    field_copies = fetch([x.at[pl.ds(0, H)] for x in fields], [held.at[k] for k in range(n)], field_sems)
    for k, p in order[:DEPTH]:
        copy(k, p).start()
    if has_prev:
        (prev_copy,) = fetch([prev_hbm], [prev], other_sems.at[pl.ds(0, 1)])
    if has_base:
        (base_copy,) = fetch([base_hbm], [base_ref], other_sems.at[pl.ds(1, 1)])
    left = []
    for k in range(n):
        field_copies[k].wait()
        left.append(stacked(held[k]))
    if n_carriers:
        ordered = refs[8]
        for k in range(n_col):
            ordered[lax.rem(ids_ref[0] + k, n_col)] = carriers[k][H:, :]
        share = ordered[0]
        for k in range(1, n_col):
            share = share + ordered[k]
        rows = share.shape[0]
        groups = NODES_DEV // LANES // 2
        for j in range(groups):
            for q in range(n_row):
                from_lane = (q % 2 * groups + j) * LANES
                out[q, H + j * rows : H + (j + 1) * rows, :] = share[:, from_lane : from_lane + LANES]
    sent = []
    for p in range(n_row // 2):
        here = slice(p * WIDE, (p + 1) * WIDE)
        total = None
        for k in range(n):
            copy(k, p).wait()
            ahead = p * n + k + DEPTH
            if ahead < len(order):
                copy(*order[ahead]).start()
            part = times(left[k], buf.at[k, p])
            total = part if total is None else total + part
        if has_prev:
            if p == 0:
                prev_copy.wait()
            total = total + prev[:, here]
        if last:
            out[2 * p, :H, :] = total[:, :TB]
            out[2 * p + 1, :H, :] = total[:, TB:]
            place = pl.ds(2 * p, 2)
            if apart:
                continue
            sent.append(pltpu.make_async_copy(out.at[place], out_ref.at[place], out_sems.at[p]))
        else:
            out[:, here] = total
            place = (pl.ds(0, H), pl.ds(p * WIDE, WIDE))
            sent.append(pltpu.make_async_copy(out.at[place], out_ref.at[place], out_sems.at[p]))
        sent[-1].start()
    if has_base:
        base_copy.wait()
    if apart:
        for j, slot_ref in enumerate(slot_refs):
            slot_ref[...] = out[ids_ref[1] ^ j]
    for item in sent:
        item.wait()


def product(n_row, n_col, ids, origins, operator, fields, prev, last, carriers=(), base=None, prev_near=False, apart=False):
    n = len(origins)
    has_prev = prev is not None
    has_base = base is not None
    rows = carriers[0].shape[0] - H if carriers else 0
    under = rows * NODES_DEV // LANES // 2
    shape = (n_row, H + under, TB) if last else (H, n_row * TB)
    scratch = [
        pltpu.VMEM((n, H, NODES_DEV), F32),
        pltpu.VMEM((n, n_row // 2, 2 * NODES_DEV, WIDE), BF16),
        pltpu.SemaphoreType.DMA((n,)),
        pltpu.SemaphoreType.DMA((n, n_row // 2)),
        pltpu.VMEM(shape, F32),
        pltpu.SemaphoreType.DMA((n_row // 2,)),
        pltpu.VMEM((H, n_row * TB) if has_prev else (8, LANES), F32),
        pltpu.SemaphoreType.DMA((2,)),
    ]
    if carriers:
        scratch.append(pltpu.VMEM((n_col, rows, NODES_DEV), F32))
    out = pltpu.HBM(shape, F32)
    out_specs, out_shape = HBM, out
    if has_base:
        out_specs, out_shape = [HBM, VMEM], [out, jax.ShapeDtypeStruct(base.shape, F32)]
    elif apart:
        out_specs, out_shape = [VMEM] * n_row, [jax.ShapeDtypeStruct((H, TB), F32)] * n_row
    return pl.pallas_call(
        functools.partial(product_kernel, n_row, n_col, origins, has_prev, last, len(carriers), has_base, apart),
        in_specs=[SMEM, HBM] + [ANY] * (n + has_prev) + [VMEM] * len(carriers) + [HBM] * has_base,
        out_specs=out_specs,
        out_shape=out_shape,
        scratch_shapes=scratch,
        compiler_params=params(48),
        cost_estimate=LIGHT if last else HEAVY,
        name="product",
    )(
        ids,
        *in_hbm(operator),
        *fields,
        *((prev,) if prev_near else in_hbm(prev) if has_prev else ()),
        *carriers,
        *(in_hbm(base) if has_base else ()),
    )


def carry_kernel(n_row, rows, owners_ref, base_ref, came_ref, *refs):
    out_ref = refs[-1]
    out_ref[:H, :] = base_ref[...]
    for q in range(n_row):
        here = pl.ds(pl.multiple_of(owners_ref[q] * TB, TB), TB)
        out_ref[:H, here] += 2.0 * came_ref[q]
    if rows:
        pieces_ref = refs[0]
        share = pieces_ref[0]
        for q in range(1, n_row):
            share = share + pieces_ref[q]
        for j in range(NODES_DEV // LANES):
            out_ref[H:, j * LANES : (j + 1) * LANES] = share[j * rows : (j + 1) * rows, :]


def carry(n_row, owners, base, came, *pieces):
    rows = pieces[0].shape[1] * LANES // NODES_DEV if pieces else 0
    return pl.pallas_call(
        functools.partial(carry_kernel, n_row, rows),
        in_specs=[SMEM] + [VMEM] * (2 + len(pieces)),
        out_specs=VMEM,
        out_shape=jax.ShapeDtypeStruct((H + rows, NODES_DEV), F32),
        compiler_params=params(24),
        cost_estimate=LIGHT,
        name="carry",
    )(owners, base, came, *pieces)


def finish_kernel(n_row, ids_ref, owners_ref, base_ref, left_ref, *refs):
    right_refs, out_ref, total = refs[:n_row], refs[n_row], refs[n_row + 1]
    total[...] = base_ref[...]
    for q in range(n_row):
        here = pl.ds(pl.multiple_of(owners_ref[q] * TB, TB), TB)
        total[:H, here] += left_ref[q, :H, :]
    for j in range(n_row):
        here = pl.ds(pl.multiple_of(owners_ref[ids_ref[1] ^ j] * TB, TB), TB)
        total[H:, here] += right_refs[j][...]
    out_ref[...] = total[...].T


def finish(n_row, ids, owners, base, left, right):
    return pl.pallas_call(
        functools.partial(finish_kernel, n_row),
        in_specs=[SMEM] * 2 + [VMEM] * (2 + n_row),
        out_specs=VMEM,
        out_shape=jax.ShapeDtypeStruct((NODES_DEV, F), F32),
        scratch_shapes=[pltpu.VMEM((F, NODES_DEV), F32)],
        compiler_params=params(24),
        cost_estimate=LIGHT,
        name="finish",
    )(ids, owners, base, left, *right)


def assemble_kernel(n_row, row_ref, own_ref, other_ref, out_ref, halves, turned):
    rows = F // n_row
    half = lax.rem(row_ref[1], 2)
    halves[half] = own_ref[:, H:, :]
    halves[1 - half] = other_ref[:, H:, :]
    groups = 3 * F // LANES // 2
    for q in range(n_row):
        for j in range(2 * groups):
            here = slice(j % groups * rows, (j % groups + 1) * rows)
            turned[q * rows : (q + 1) * rows, j * LANES : (j + 1) * LANES] = halves[j // groups, q, here, :]
    for k in range(3):
        out_ref[k] = turned[:, k * F : (k + 1) * F].T


def assemble(n_row, row, own, other):
    return pl.pallas_call(
        functools.partial(assemble_kernel, n_row),
        in_specs=[SMEM, VMEM, VMEM],
        out_specs=VMEM,
        out_shape=jax.ShapeDtypeStruct((3, F, F), F32),
        scratch_shapes=[
            pltpu.VMEM((2, n_row, own.shape[1] - H, LANES), F32),
            pltpu.VMEM((F, 3 * F), F32),
        ],
        compiler_params=params(16),
        cost_estimate=LIGHT,
        name="assemble",
    )(row, own, other)


def shift(n_col, x, step):
    return lax.ppermute(x, "col", [(c, (c + step) % n_col) for c in range(n_col)])


def exchange(pieces):
    return lax.all_to_all(pieces, "row", split_axis=0, concat_axis=0, tiled=True)


def after(x, *others):
    return lax.optimization_barrier((x, *others))[0]


def opposite(field, below, above):
    col = lax.axis_index("col")
    sent = jnp.where(col == 1, above, jnp.where(col == 2, below, field))
    return lax.ppermute(sent, "col", [(1, 0), (2, 3), (3, 1), (0, 2)])


def gather(n_col, field, side):
    long = n_col // 2
    short = n_col - 1 - long
    ahead, behind = field, field
    steps = [[(0, field)]]
    for s in range(1, long + 1):
        if s == 2:
            ahead = after(ahead, behind)
        if s == 2 and n_col == 4:
            ahead = opposite(field, ahead, behind) if side > 0 else opposite(field, behind, ahead)
        else:
            ahead = shift(n_col, ahead, side)
        step = [((-side * s) % n_col, ahead)]
        if s <= short:
            behind = shift(n_col, behind, -side)
            step.append(((side * s) % n_col, behind))
        steps.append(step)
    return steps


def early(n_row, n_col, ids, operator, steps, total=None, done=0, base=None):
    pairs = [pair for step in steps[:-1] for pair in step][done:]
    for begin in range(0, len(pairs), 3):
        origins, fields = zip(*pairs[begin : begin + 3])
        brought = base if begin + 3 >= len(pairs) else None
        total = product(n_row, n_col, ids, origins, operator, fields, total, False, base=brought)
    return total


def final(n_row, n_col, ids, operator, steps, total, carrying=False, near=False, apart=False):
    origins, fields = zip(*steps[-1])
    carriers = [x for _, x in sorted((p for step in steps for p in step), key=lambda p: p[0])] if carrying else ()
    return product(n_row, n_col, ids, origins, operator, fields, total, True, carriers, prev_near=near, apart=apart)


def per_device(
    grad_out,
    relu_mask,
    basis_zero,
    basis_one,
    basis_two,
    cheb_weight,
    tile_values,
    tile_rows,
    tile_slots,
    send_blocks,
    live_tiles,
):
    n_row = lax.axis_size("row")
    n_col = lax.axis_size("col")
    ids = jnp.stack([lax.axis_index("col"), lax.axis_index("row")]).astype(jnp.int32)
    owners = send_blocks.reshape(n_row)
    left, right = term_two(grad_out, relu_mask, cheb_weight)
    one_left, one_right, diff, pieces = local_terms(
        n_row, left, grad_out, relu_mask, cheb_weight, basis_zero, basis_one, basis_two
    )
    steps = gather(n_col, left, 1)
    first = steps[0] + steps[1] if len(steps) > 2 else steps[0]
    operator, left_early = build_operator(
        n_row, n_col, ids, live_tiles, tile_rows, tile_slots, tile_values, first
    )
    pieces = exchange(pieces)
    common = (n_row, n_col, ids, operator)

    left_early = early(*common, steps, left_early, len(first))
    right_steps = gather(n_col, after(right, left_early, steps[-1][0][1]), -1)
    left_came = exchange(final(*common, steps, after(left_early, pieces), near=len(steps) == 3))
    right_early, one_left = early(*common, right_steps, base=one_left)

    left_carried = carry(n_row, owners, after(one_left, right_early, right_steps[-1][0][1]), left_came, pieces)
    steps = gather(n_col, left_carried, 1)
    right_came = exchange(final(*common, right_steps, right_early))
    left_early, one_right = early(*common, steps, base=one_right)

    right_carried = carry(n_row, owners, after(one_right, left_early, steps[-1][0][1]), right_came)
    right_steps = gather(n_col, right_carried, -1)
    left_came = exchange(final(*common, steps, left_early, carrying=True))
    right_early = early(*common, right_steps)

    right_last = final(*common, right_steps, right_early, apart=True)
    right_came = [right_last[0]] * n_row
    for j in range(n_row - 1, 0, -1):
        right_came[j] = lax.ppermute(right_last[j], "row", [(r, r ^ j) for r in range(n_row)])
    other = lax.ppermute(after(left_came, right_last[0]), "row", [(r, r ^ 1) for r in range(n_row)])
    weight_grad = assemble(n_row, ids, left_came, other)
    return finish(n_row, ids, owners, after(diff, weight_grad), left_came, right_came), weight_grad


def solution(mesh):
    placed = (
        P(("row", "col"), None),
        P(("row", "col"), None),
        P(("row", "col"), None),
        P(("row", "col"), None),
        P(("row", "col"), None),
        P(),
        P(("row", "col"), None, None, None),
        P(("row", "col"), None),
        P(("row", "col"), None),
        P(("row", "col"), None, None),
        P(("row", "col")),
    )
    return jax.shard_map(
        per_device,
        mesh=mesh,
        in_specs=placed,
        out_specs=(P(("row", "col"), None), P()),
        check_vma=False,
    )
```

```python
import functools

import jax
import jax.numpy as jnp
from jax import lax
from jax.experimental import pallas as pl
from jax.experimental.pallas import tpu as pltpu
from jax.sharding import PartitionSpec as P

F = 256
H = 128
TB = 128
CHB = 4
WIDE = 2 * TB
LANES = 128
NODES_DEV = CHB * TB
TILES_DEV = 128
GROUPS = 8
MIB = 1 << 20
WHOLE_BYTES = 12 * MIB
DEPTH = 4
HEAVY = pl.CostEstimate(flops=1 << 34, bytes_accessed=64 * MIB, transcendentals=0)
LIGHT = pl.CostEstimate(flops=1024, bytes_accessed=1024, transcendentals=0)
BF16 = jnp.bfloat16
F32 = jnp.float32

SMEM = pl.BlockSpec(memory_space=pltpu.SMEM)
VMEM = pl.BlockSpec(memory_space=pltpu.VMEM)
HBM = pl.BlockSpec(memory_space=pltpu.HBM)
ANY = pl.BlockSpec(memory_space=pl.ANY)


def params(mib):
    return pltpu.CompilerParams(vmem_limit_bytes=mib * MIB)


def in_hbm(*arrays):
    return [pltpu.with_memory_space_constraint(x, pltpu.HBM) for x in arrays]


def split(x):
    high = x.astype(BF16)
    low = (x - high.astype(F32)).astype(BF16)
    return high, low


def dot3(a, b, dims):
    ah, al = a
    bh, bl = b

    def one(x, y):
        return lax.dot_general(x, y, (dims, ((), ())), preferred_element_type=F32)

    return one(ah, bh) + (one(ah, bl) + one(al, bh))


def fetch(sources, targets, sems):
    copies = [pltpu.make_async_copy(a, b, sems.at[i]) for i, (a, b) in enumerate(zip(sources, targets))]
    for copy in copies:
        copy.start()
    return copies


def masked_of(grad, mask):
    return jnp.where(mask > 0, grad, jnp.zeros_like(grad))


def term_two_kernel(grad_hbm, mask_hbm, weight_hbm, left_ref, right_ref, grad, mask, weight, sems):
    for copy in fetch((grad_hbm, mask_hbm, weight_hbm.at[2]), (grad, mask, weight), sems):
        copy.wait()
    term = dot3(split(weight[...]), split(masked_of(grad[...], mask[...])), ((1,), (1,)))
    left_ref[...] = term[:H]
    right_ref[...] = term[H:]


def term_two(grad_out, relu_mask, cheb_weight):
    out = jax.ShapeDtypeStruct((H, NODES_DEV), F32)
    return pl.pallas_call(
        term_two_kernel,
        in_specs=[HBM] * 3,
        out_specs=[VMEM, VMEM],
        out_shape=[out, out],
        scratch_shapes=[
            pltpu.VMEM((NODES_DEV, F), F32),
            pltpu.VMEM((NODES_DEV, F), jnp.int32),
            pltpu.VMEM((F, F), F32),
            pltpu.SemaphoreType.DMA((3,)),
        ],
        compiler_params=params(16),
        cost_estimate=LIGHT,
        name="term_two",
    )(*in_hbm(grad_out, relu_mask, cheb_weight))


def local_kernel(
    n_row, first_ref, grad_hbm, mask_hbm, weight_hbm, h0, h1, h2, left_hbm, right_hbm, diff_ref, pieces_ref,
    grad, mask, weight, bases, one, sems, one_sems,
):
    sources = (grad_hbm, mask_hbm, weight_hbm, h0, h1, h2)
    copies = fetch(sources, (grad, mask, weight, bases.at[0], bases.at[1], bases.at[2]), sems)
    for copy in copies[:3]:
        copy.wait()
    values = masked_of(grad[...], mask[...])
    masked = split(values)
    term = dot3(split(weight[1]), masked, ((1,), (1,)))
    one[...] = term
    one_copies = fetch((one.at[pl.ds(0, H)], one.at[pl.ds(H, H)]), (left_hbm, right_hbm), one_sems)
    diff_ref[...] = dot3(split(weight[0] - weight[2]), masked, ((1,), (1,)))
    turned = split(values.T)
    rows = F // n_row
    for k in range(3):
        copies[3 + k].wait()
        part = dot3(turned, split(bases[k]), ((1,), (0,)))
        for j in range(F // LANES):
            here = (k * (F // LANES) + j) * rows
            for q in range(n_row):
                pieces_ref[q, here : here + rows, :] = part[q * rows : (q + 1) * rows, j * LANES : (j + 1) * LANES]
    for copy in one_copies:
        copy.wait()


def local_terms(n_row, first, grad_out, relu_mask, cheb_weight, b0, b1, b2):
    half = pltpu.HBM((H, NODES_DEV), F32)
    share = 3 * F * F // n_row // LANES
    return pl.pallas_call(
        functools.partial(local_kernel, n_row),
        in_specs=[ANY] + [HBM] * 6,
        out_specs=[HBM, HBM, VMEM, VMEM],
        out_shape=[
            half,
            half,
            jax.ShapeDtypeStruct((F, NODES_DEV), F32),
            jax.ShapeDtypeStruct((n_row, share, LANES), F32),
        ],
        scratch_shapes=[
            pltpu.VMEM((NODES_DEV, F), F32),
            pltpu.VMEM((NODES_DEV, F), jnp.int32),
            pltpu.VMEM((3, F, F), F32),
            pltpu.VMEM((3, NODES_DEV, F), F32),
            pltpu.VMEM((F, NODES_DEV), F32),
            pltpu.SemaphoreType.DMA((6,)),
            pltpu.SemaphoreType.DMA((2,)),
        ],
        compiler_params=params(32),
        cost_estimate=LIGHT,
        name="local_terms",
    )(first, *in_hbm(grad_out, relu_mask, cheb_weight, b0, b1, b2))


def stacked(field):
    return jnp.concatenate(split(field), axis=0)


def times(left, part):
    by_high = jnp.dot(left, part[:NODES_DEV, :], preferred_element_type=F32)
    by_low = jnp.dot(left[:H], part[NODES_DEV:, :], preferred_element_type=F32)
    return by_high[:H] + (by_high[H:] + by_low)


def operator_kernel(n_row, n_col, origins, ids_ref, live_ref, rows_hbm, slots_hbm, values_ref, *refs):
    fields, refs = refs[: len(origins)], refs[len(origins) :]
    out_hbm, total_ref, tiles, acc, buf, held, lists, counts, rows, slots, sems, small_sems, field_sems, out_sems = refs
    size = TILES_DEV // GROUPS
    pairs = n_row // 2
    whole = acc.shape[0] == n_col
    small = fetch((rows_hbm, slots_hbm), (rows, slots), small_sems)
    parts = [pl.ds(g * size, size) for g in range(GROUPS)]
    tile_copies = fetch([values_ref.at[0, part] for part in parts], [tiles.at[part] for part in parts], sems)
    field_copies = fetch(fields, [held.at[k] for k in range(len(fields))], field_sems)
    for item in small:
        item.wait()

    def place_of(t):
        row = rows[0, t]
        if n_col & (n_col - 1) == 0:
            s = (lax.shift_right_logical(row, CHB.bit_length() - 1) - ids_ref[0]) & (n_col - 1)
        else:
            s = lax.rem(row // CHB - ids_ref[0] + n_col, n_col)
        return s, slots[0, t] * CHB + (row & (CHB - 1))

    def add_block(into, position, tile):
        slot = lax.shift_right_logical(position, CHB.bit_length() - 1)
        at_row = pl.ds(pl.multiple_of((position & (CHB - 1)) * TB, TB), TB)
        at_lane = pl.ds(pl.multiple_of((slot & 1) * TB, TB), TB)
        acc[into, lax.shift_right_logical(slot, 1), at_row, at_lane] += tiles[tile]

    if whole:

        def add_now(t, carry):
            s, position = place_of(t)
            add_block(s, position, t)
            return carry

        acc[...] = jnp.zeros_like(acc)
        for g, item in enumerate(tile_copies):
            item.wait()
            end = (g + 1) * size

            @pl.when(live_ref[0] >= end)
            def _():
                lax.fori_loop(end - size, end, add_now, 0, unroll=4)

            @pl.when(live_ref[0] < end)
            def _():
                lax.fori_loop(end - size, live_ref[0], add_now, 0)

    else:

        def place(t, counted):
            s, position = place_of(t)
            n = counted[0]
            for k in range(1, n_col):
                n = jnp.where(s == k, counted[k], n)
            lists[s, n] = position * TILES_DEV + t
            return tuple(c + (s == k).astype(jnp.int32) for k, c in enumerate(counted))

        counted = lax.fori_loop(0, live_ref[0], place, (jnp.int32(0),) * n_col)
        for s in range(n_col):
            counts[s] = counted[s]
        for item in tile_copies:
            item.wait()

    def out_copy(origin, p):
        return pltpu.make_async_copy(buf.at[origin % 2, p], out_hbm.at[origin, p], out_sems.at[origin % 2, p])

    for origin in range(n_col):
        if not whole:

            def add(n, carry):
                entry = lists[origin, n]
                add_block(0, lax.shift_right_logical(entry, TILES_DEV.bit_length() - 1), entry & (TILES_DEV - 1))
                return carry

            acc[...] = jnp.zeros_like(acc)
            lax.fori_loop(0, counts[origin], add, 0)
        summed_blocks = acc.at[origin if whole else 0]
        for p in range(pairs):
            if origin >= 2:
                out_copy(origin - 2, p).wait()
            high, low = split(summed_blocks[p])
            buf[origin % 2, p, :NODES_DEV, :] = high
            buf[origin % 2, p, NODES_DEV:, :] = low
            out_copy(origin, p).start()
        if origin in origins:
            k = origins.index(origin)
            field_copies[k].wait()
            left = stacked(held[k])
            for p in range(pairs):
                summed = times(left, buf.at[origin % 2, p])
                here = slice(p * WIDE, (p + 1) * WIDE)
                total_ref[:, here] = summed if origin == 0 else total_ref[:, here] + summed
    for origin in range(n_col - 2, n_col):
        for p in range(pairs):
            out_copy(origin, p).wait()


def build_operator(n_row, n_col, ids, live, rows, slots, values, pairs):
    part = (n_row // 2, 2 * NODES_DEV, WIDE)
    sums = (n_row // 2, NODES_DEV, WIDE)
    held_origins = n_col if 4 * n_col * n_row * TB * NODES_DEV <= WHOLE_BYTES else 1
    origins, fields = zip(*pairs)
    return pl.pallas_call(
        functools.partial(operator_kernel, n_row, n_col, origins),
        in_specs=[SMEM] * 2 + [HBM] * 3 + [ANY] * len(fields),
        out_specs=[HBM, VMEM],
        out_shape=[pltpu.HBM((n_col,) + part, BF16), jax.ShapeDtypeStruct((H, n_row * TB), F32)],
        scratch_shapes=[
            pltpu.VMEM((TILES_DEV, TB, TB), F32),
            pltpu.VMEM((held_origins,) + sums, F32),
            pltpu.VMEM((2,) + part, BF16),
            pltpu.VMEM((len(fields), H, NODES_DEV), F32),
            pltpu.SMEM((n_col, TILES_DEV), jnp.int32),
            pltpu.SMEM((n_col,), jnp.int32),
            pltpu.SMEM((1, TILES_DEV), jnp.int32),
            pltpu.SMEM((1, TILES_DEV), jnp.int32),
            pltpu.SemaphoreType.DMA((GROUPS,)),
            pltpu.SemaphoreType.DMA((2,)),
            pltpu.SemaphoreType.DMA((len(fields),)),
            pltpu.SemaphoreType.DMA((2, n_row // 2)),
        ],
        compiler_params=params(48),
        cost_estimate=HEAVY,
        name="operator",
    )(ids, live, *in_hbm(rows, slots, values), *fields)


def product_kernel(n_row, n_col, origins, has_prev, last, n_carriers, has_base, apart, *refs):
    n = len(origins)
    if n_carriers or apart:
        index_ref, refs = refs[0], refs[1:]
    op_ref, refs = refs[0], refs[1:]
    fields, refs = refs[:n], refs[n:]
    if has_prev:
        prev_hbm, refs = refs[0], refs[1:]
    carriers, refs = refs[:n_carriers], refs[n_carriers:]
    if has_base:
        base_hbm, out_ref, base_ref, refs = refs[0], refs[1], refs[2], refs[3:]
    elif apart:
        slot_refs, refs = refs[:n_row], refs[n_row:]
    else:
        out_ref, refs = refs[0], refs[1:]
    held, buf, field_sems, sems, out, out_sems, prev, other_sems = refs[:8]
    order = [(k, p) for p in range(n_row // 2) for k in range(n)]

    def copy(k, p):
        return pltpu.make_async_copy(op_ref.at[origins[k], p], buf.at[k, p], sems.at[k, p])

    field_copies = fetch([x.at[pl.ds(0, H)] for x in fields], [held.at[k] for k in range(n)], field_sems)
    for k, p in order[:DEPTH]:
        copy(k, p).start()
    if has_prev:
        (prev_copy,) = fetch([prev_hbm], [prev], other_sems.at[pl.ds(0, 1)])
    if has_base:
        (base_copy,) = fetch([base_hbm], [base_ref], other_sems.at[pl.ds(1, 1)])
    left = []
    for k in range(n):
        field_copies[k].wait()
        left.append(stacked(held[k]))
    if n_carriers:
        ordered = refs[8]
        for k in range(n_col):
            ordered[lax.rem(index_ref[0] + k, n_col)] = carriers[k][H:, :]
        share = ordered[0]
        for k in range(1, n_col):
            share = share + ordered[k]
        rows = share.shape[0]
        groups = NODES_DEV // LANES // 2
        for j in range(groups):
            for q in range(n_row):
                from_lane = (q % 2 * groups + j) * LANES
                out[q, H + j * rows : H + (j + 1) * rows, :] = share[:, from_lane : from_lane + LANES]
    sent = []
    for p in range(n_row // 2):
        here = slice(p * WIDE, (p + 1) * WIDE)
        total = None
        for k in range(n):
            copy(k, p).wait()
            ahead = p * n + k + DEPTH
            if ahead < len(order):
                copy(*order[ahead]).start()
            part = times(left[k], buf.at[k, p])
            total = part if total is None else total + part
        if has_prev:
            if p == 0:
                prev_copy.wait()
            total = total + prev[:, here]
        if last:
            out[2 * p, :H, :] = total[:, :TB]
            out[2 * p + 1, :H, :] = total[:, TB:]
            place = pl.ds(2 * p, 2)
            if apart:
                continue
            sent.append(pltpu.make_async_copy(out.at[place], out_ref.at[place], out_sems.at[p]))
        else:
            out[:, here] = total
            place = (pl.ds(0, H), pl.ds(p * WIDE, WIDE))
            sent.append(pltpu.make_async_copy(out.at[place], out_ref.at[place], out_sems.at[p]))
        sent[-1].start()
    if has_base:
        base_copy.wait()
    if apart:
        for j, slot_ref in enumerate(slot_refs):
            slot_ref[...] = out[index_ref[0] ^ j]
    for item in sent:
        item.wait()


def product(n_row, n_col, ids, row, origins, operator, fields, prev, last, carriers=(), base=None, prev_near=False, apart=False):
    n = len(origins)
    has_prev = prev is not None
    has_base = base is not None
    rows = carriers[0].shape[0] - H if carriers else 0
    under = rows * NODES_DEV // LANES // 2
    shape = (n_row, H + under, TB) if last else (H, n_row * TB)
    scratch = [
        pltpu.VMEM((n, H, NODES_DEV), F32),
        pltpu.VMEM((n, n_row // 2, 2 * NODES_DEV, WIDE), BF16),
        pltpu.SemaphoreType.DMA((n,)),
        pltpu.SemaphoreType.DMA((n, n_row // 2)),
        pltpu.VMEM(shape, F32),
        pltpu.SemaphoreType.DMA((n_row // 2,)),
        pltpu.VMEM((H, n_row * TB) if has_prev else (8, LANES), F32),
        pltpu.SemaphoreType.DMA((2,)),
    ]
    if carriers:
        scratch.append(pltpu.VMEM((n_col, rows, NODES_DEV), F32))
    index = (ids,) if carriers else (row,) if apart else ()
    out = pltpu.HBM(shape, F32)
    out_specs, out_shape = HBM, out
    if has_base:
        out_specs, out_shape = [HBM, VMEM], [out, jax.ShapeDtypeStruct(base.shape, F32)]
    elif apart:
        out_specs, out_shape = [VMEM] * n_row, [jax.ShapeDtypeStruct((H, TB), F32)] * n_row
    return pl.pallas_call(
        functools.partial(product_kernel, n_row, n_col, origins, has_prev, last, len(carriers), has_base, apart),
        in_specs=[SMEM] * len(index) + [HBM] + [ANY] * (n + has_prev) + [VMEM] * len(carriers) + [HBM] * has_base,
        out_specs=out_specs,
        out_shape=out_shape,
        scratch_shapes=scratch,
        compiler_params=params(48),
        cost_estimate=LIGHT if last else HEAVY,
        name="product",
    )(
        *index,
        *in_hbm(operator),
        *fields,
        *((prev,) if prev_near else in_hbm(prev) if has_prev else ()),
        *carriers,
        *(in_hbm(base) if has_base else ()),
    )


def carry_kernel(n_row, rows, owners_ref, base_ref, came_ref, *refs):
    out_ref = refs[-1]
    out_ref[:H, :] = base_ref[...]
    for q in range(n_row):
        here = pl.ds(pl.multiple_of(owners_ref[q] * TB, TB), TB)
        out_ref[:H, here] += 2.0 * came_ref[q]
    if rows:
        pieces_ref = refs[0]
        share = pieces_ref[0]
        for q in range(1, n_row):
            share = share + pieces_ref[q]
        for j in range(NODES_DEV // LANES):
            out_ref[H:, j * LANES : (j + 1) * LANES] = share[j * rows : (j + 1) * rows, :]


def carry(n_row, owners, base, came, *pieces):
    rows = pieces[0].shape[1] * LANES // NODES_DEV if pieces else 0
    return pl.pallas_call(
        functools.partial(carry_kernel, n_row, rows),
        in_specs=[SMEM] + [VMEM] * (2 + len(pieces)),
        out_specs=VMEM,
        out_shape=jax.ShapeDtypeStruct((H + rows, NODES_DEV), F32),
        compiler_params=params(24),
        cost_estimate=LIGHT,
        name="carry",
    )(owners, base, came, *pieces)


def finish_kernel(n_row, row_ref, owners_ref, base_ref, left_ref, *refs):
    right_refs, out_ref, total = refs[:n_row], refs[n_row], refs[n_row + 1]
    total[...] = base_ref[...]
    for q in range(n_row):
        here = pl.ds(pl.multiple_of(owners_ref[q] * TB, TB), TB)
        total[:H, here] += left_ref[q, :H, :]
    for j in range(n_row):
        here = pl.ds(pl.multiple_of(owners_ref[row_ref[0] ^ j] * TB, TB), TB)
        total[H:, here] += right_refs[j][...]
    out_ref[...] = total[...].T


def finish(n_row, row, owners, base, left, right):
    return pl.pallas_call(
        functools.partial(finish_kernel, n_row),
        in_specs=[SMEM] * 2 + [VMEM] * (2 + n_row),
        out_specs=VMEM,
        out_shape=jax.ShapeDtypeStruct((NODES_DEV, F), F32),
        scratch_shapes=[pltpu.VMEM((F, NODES_DEV), F32)],
        compiler_params=params(24),
        cost_estimate=LIGHT,
        name="finish",
    )(row, owners, base, left, *right)


def assemble_kernel(n_row, row_ref, own_ref, other_ref, out_ref, halves, turned):
    rows = F // n_row
    half = lax.rem(row_ref[0], 2)
    halves[half] = own_ref[:, H:, :]
    halves[1 - half] = other_ref[:, H:, :]
    groups = 3 * F // LANES // 2
    for q in range(n_row):
        for j in range(2 * groups):
            here = slice(j % groups * rows, (j % groups + 1) * rows)
            turned[q * rows : (q + 1) * rows, j * LANES : (j + 1) * LANES] = halves[j // groups, q, here, :]
    for k in range(3):
        out_ref[k] = turned[:, k * F : (k + 1) * F].T


def assemble(n_row, row, own, other):
    return pl.pallas_call(
        functools.partial(assemble_kernel, n_row),
        in_specs=[SMEM, VMEM, VMEM],
        out_specs=VMEM,
        out_shape=jax.ShapeDtypeStruct((3, F, F), F32),
        scratch_shapes=[
            pltpu.VMEM((2, n_row, own.shape[1] - H, LANES), F32),
            pltpu.VMEM((F, 3 * F), F32),
        ],
        compiler_params=params(16),
        cost_estimate=LIGHT,
        name="assemble",
    )(row, own, other)


def shift(n_col, x, step):
    return lax.ppermute(x, "col", [(c, (c + step) % n_col) for c in range(n_col)])


def exchange(pieces):
    return lax.all_to_all(pieces, "row", split_axis=0, concat_axis=0, tiled=True)


def after(x, *others):
    return lax.optimization_barrier((x, *others))[0]


def opposite(field, below, above):
    col = lax.axis_index("col")
    sent = jnp.where(col == 1, above, jnp.where(col == 2, below, field))
    return lax.ppermute(sent, "col", [(1, 0), (2, 3), (3, 1), (0, 2)])


def gather(n_col, field, side):
    long = n_col // 2
    short = n_col - 1 - long
    ahead, behind = field, field
    steps = [[(0, field)]]
    for s in range(1, long + 1):
        if s == 2:
            ahead = after(ahead, behind)
        if s == 2 and n_col == 4:
            ahead = opposite(field, ahead, behind) if side > 0 else opposite(field, behind, ahead)
        else:
            ahead = shift(n_col, ahead, side)
        step = [((-side * s) % n_col, ahead)]
        if s <= short:
            behind = shift(n_col, behind, -side)
            step.append(((side * s) % n_col, behind))
        steps.append(step)
    return steps


def early(n_row, n_col, ids, row, operator, steps, total=None, done=0, base=None):
    pairs = [pair for step in steps[:-1] for pair in step][done:]
    for begin in range(0, len(pairs), 3):
        origins, fields = zip(*pairs[begin : begin + 3])
        brought = base if begin + 3 >= len(pairs) else None
        total = product(n_row, n_col, ids, row, origins, operator, fields, total, False, base=brought)
    return total


def final(n_row, n_col, ids, row, operator, steps, total, carrying=False, near=False, apart=False):
    origins, fields = zip(*steps[-1])
    carriers = [x for _, x in sorted((p for step in steps for p in step), key=lambda p: p[0])] if carrying else ()
    return product(n_row, n_col, ids, row, origins, operator, fields, total, True, carriers, prev_near=near, apart=apart)


def per_device(
    grad_out,
    relu_mask,
    basis_zero,
    basis_one,
    basis_two,
    cheb_weight,
    tile_values,
    tile_rows,
    tile_slots,
    send_blocks,
    live_tiles,
):
    n_row = lax.axis_size("row")
    n_col = lax.axis_size("col")
    ids = lax.axis_index("col").astype(jnp.int32).reshape(1)
    row = lax.axis_index("row").astype(jnp.int32).reshape(1)
    owners = send_blocks.reshape(n_row)
    left, right = term_two(grad_out, relu_mask, cheb_weight)
    one_left, one_right, diff, pieces = local_terms(
        n_row, left, grad_out, relu_mask, cheb_weight, basis_zero, basis_one, basis_two
    )
    steps = gather(n_col, left, 1)
    first = steps[0] + steps[1] if len(steps) > 2 else steps[0]
    operator, left_early = build_operator(
        n_row, n_col, ids, live_tiles, tile_rows, tile_slots, tile_values, first
    )
    pieces = exchange(pieces)
    common = (n_row, n_col, ids, row, operator)

    left_early = early(*common, steps, left_early, len(first))
    right_steps = gather(n_col, after(right, left_early, steps[-1][0][1]), -1)
    left_came = exchange(final(*common, steps, after(left_early, pieces), near=len(steps) == 3))
    right_early, one_left = early(*common, right_steps, base=one_left)

    left_carried = carry(n_row, owners, after(one_left, right_early, right_steps[-1][0][1]), left_came, pieces)
    steps = gather(n_col, left_carried, 1)
    right_came = exchange(final(*common, right_steps, right_early))
    left_early, one_right = early(*common, steps, base=one_right)

    right_carried = carry(n_row, owners, after(one_right, left_early, steps[-1][0][1]), right_came)
    right_steps = gather(n_col, right_carried, -1)
    left_came = exchange(final(*common, steps, left_early, carrying=True))
    right_early = early(*common, right_steps)

    right_last = final(*common, right_steps, right_early, apart=True)
    right_came = [right_last[0]] * n_row
    for j in range(n_row - 1, 0, -1):
        right_came[j] = lax.ppermute(right_last[j], "row", [(r, r ^ j) for r in range(n_row)])
    other = lax.ppermute(after(left_came, right_last[0]), "row", [(r, r ^ 1) for r in range(n_row)])
    weight_grad = assemble(n_row, row, left_came, other)
    return finish(n_row, row, owners, after(diff, weight_grad), left_came, right_came), weight_grad


def solution(mesh):
    placed = (
        P(("row", "col"), None),
        P(("row", "col"), None),
        P(("row", "col"), None),
        P(("row", "col"), None),
        P(("row", "col"), None),
        P(),
        P(("row", "col"), None, None, None),
        P(("row", "col"), None),
        P(("row", "col"), None),
        P(("row", "col"), None, None),
        P(("row", "col")),
    )
    return jax.shard_map(
        per_device,
        mesh=mesh,
        in_specs=placed,
        out_specs=(P(("row", "col"), None), P()),
        check_vma=False,
    )
```

```python
import functools

import jax
import jax.numpy as jnp
from jax import lax
from jax.experimental import pallas as pl
from jax.experimental.pallas import tpu as pltpu
from jax.sharding import PartitionSpec as P

F = 256
H = 128
TB = 128
CHB = 4
WIDE = 2 * TB
LANES = 128
NODES_DEV = CHB * TB
TILES_DEV = 128
GROUPS = 8
MIB = 1 << 20
WHOLE_BYTES = 12 * MIB
DEPTH = 4
HEAVY = pl.CostEstimate(flops=1 << 34, bytes_accessed=64 * MIB, transcendentals=0)
LIGHT = pl.CostEstimate(flops=1024, bytes_accessed=1024, transcendentals=0)
BF16 = jnp.bfloat16
F32 = jnp.float32

SMEM = pl.BlockSpec(memory_space=pltpu.SMEM)
VMEM = pl.BlockSpec(memory_space=pltpu.VMEM)
HBM = pl.BlockSpec(memory_space=pltpu.HBM)
ANY = pl.BlockSpec(memory_space=pl.ANY)


def params(mib):
    return pltpu.CompilerParams(vmem_limit_bytes=mib * MIB)


def in_hbm(*arrays):
    return [pltpu.with_memory_space_constraint(x, pltpu.HBM) for x in arrays]


def split(x):
    high = x.astype(BF16)
    low = (x - high.astype(F32)).astype(BF16)
    return high, low


def dot3(a, b, dims):
    ah, al = a
    bh, bl = b

    def one(x, y):
        return lax.dot_general(x, y, (dims, ((), ())), preferred_element_type=F32)

    return one(ah, bh) + (one(ah, bl) + one(al, bh))


def fetch(sources, targets, sems):
    copies = [pltpu.make_async_copy(a, b, sems.at[i]) for i, (a, b) in enumerate(zip(sources, targets))]
    for copy in copies:
        copy.start()
    return copies


def masked_of(grad, mask):
    return jnp.where(mask > 0, grad, jnp.zeros_like(grad))


def term_two_kernel(grad_hbm, mask_hbm, weight_hbm, left_ref, right_ref, grad, mask, weight, sems):
    for copy in fetch((grad_hbm, mask_hbm, weight_hbm.at[2]), (grad, mask, weight), sems):
        copy.wait()
    term = dot3(split(weight[...]), split(masked_of(grad[...], mask[...])), ((1,), (1,)))
    left_ref[...] = term[:H]
    right_ref[...] = term[H:]


def term_two(grad_out, relu_mask, cheb_weight):
    out = jax.ShapeDtypeStruct((H, NODES_DEV), F32)
    return pl.pallas_call(
        term_two_kernel,
        in_specs=[HBM] * 3,
        out_specs=[VMEM, VMEM],
        out_shape=[out, out],
        scratch_shapes=[
            pltpu.VMEM((NODES_DEV, F), F32),
            pltpu.VMEM((NODES_DEV, F), jnp.int32),
            pltpu.VMEM((F, F), F32),
            pltpu.SemaphoreType.DMA((3,)),
        ],
        compiler_params=params(16),
        cost_estimate=LIGHT,
        name="term_two",
    )(*in_hbm(grad_out, relu_mask, cheb_weight))


def local_kernel(
    n_row, first_ref, grad_hbm, mask_hbm, weight_hbm, h0, h1, h2, left_hbm, right_hbm, diff_ref, pieces_ref,
    grad, mask, weight, bases, one, sems, one_sems,
):
    sources = (grad_hbm, mask_hbm, weight_hbm, h0, h1, h2)
    copies = fetch(sources, (grad, mask, weight, bases.at[0], bases.at[1], bases.at[2]), sems)
    for copy in copies[:3]:
        copy.wait()
    values = masked_of(grad[...], mask[...])
    masked = split(values)
    term = dot3(split(weight[1]), masked, ((1,), (1,)))
    one[...] = term
    one_copies = fetch((one.at[pl.ds(0, H)], one.at[pl.ds(H, H)]), (left_hbm, right_hbm), one_sems)
    diff_ref[...] = dot3(split(weight[0] - weight[2]), masked, ((1,), (1,)))
    turned = split(values.T)
    rows = F // n_row
    for k in range(3):
        copies[3 + k].wait()
        part = dot3(turned, split(bases[k]), ((1,), (0,)))
        for j in range(F // LANES):
            here = (k * (F // LANES) + j) * rows
            for q in range(n_row):
                pieces_ref[q, here : here + rows, :] = part[q * rows : (q + 1) * rows, j * LANES : (j + 1) * LANES]
    for copy in one_copies:
        copy.wait()


def local_terms(n_row, first, grad_out, relu_mask, cheb_weight, b0, b1, b2):
    half = pltpu.HBM((H, NODES_DEV), F32)
    share = 3 * F * F // n_row // LANES
    return pl.pallas_call(
        functools.partial(local_kernel, n_row),
        in_specs=[ANY] + [HBM] * 6,
        out_specs=[HBM, HBM, VMEM, VMEM],
        out_shape=[
            half,
            half,
            jax.ShapeDtypeStruct((F, NODES_DEV), F32),
            jax.ShapeDtypeStruct((n_row, share, LANES), F32),
        ],
        scratch_shapes=[
            pltpu.VMEM((NODES_DEV, F), F32),
            pltpu.VMEM((NODES_DEV, F), jnp.int32),
            pltpu.VMEM((3, F, F), F32),
            pltpu.VMEM((3, NODES_DEV, F), F32),
            pltpu.VMEM((F, NODES_DEV), F32),
            pltpu.SemaphoreType.DMA((6,)),
            pltpu.SemaphoreType.DMA((2,)),
        ],
        compiler_params=params(32),
        cost_estimate=LIGHT,
        name="local_terms",
    )(first, *in_hbm(grad_out, relu_mask, cheb_weight, b0, b1, b2))


def stacked(field):
    return jnp.concatenate(split(field), axis=0)


def times(left, part):
    by_high = jnp.dot(left, part[:NODES_DEV, :], preferred_element_type=F32)
    by_low = jnp.dot(left[:H], part[NODES_DEV:, :], preferred_element_type=F32)
    return by_high[:H] + (by_high[H:] + by_low)


def operator_kernel(n_row, n_col, origins, ids_ref, live_ref, rows_hbm, slots_hbm, values_ref, *refs):
    fields, refs = refs[: len(origins)], refs[len(origins) :]
    out_hbm, total_ref, tiles, acc, buf, held, lists, counts, rows, slots, sems, small_sems, field_sems, out_sems = refs
    size = TILES_DEV // GROUPS
    pairs = n_row // 2
    whole = acc.shape[0] == n_col
    small = fetch((rows_hbm, slots_hbm), (rows, slots), small_sems)
    parts = [pl.ds(g * size, size) for g in range(GROUPS)]
    tile_copies = fetch([values_ref.at[0, part] for part in parts], [tiles.at[part] for part in parts], sems)
    field_copies = fetch(fields, [held.at[k] for k in range(len(fields))], field_sems)
    for item in small:
        item.wait()

    def place_of(t):
        row = rows[0, t]
        if n_col & (n_col - 1) == 0:
            s = (lax.shift_right_logical(row, CHB.bit_length() - 1) - ids_ref[0]) & (n_col - 1)
        else:
            s = lax.rem(row // CHB - ids_ref[0] + n_col, n_col)
        return s, slots[0, t] * CHB + (row & (CHB - 1))

    def add_block(into, position, tile):
        slot = lax.shift_right_logical(position, CHB.bit_length() - 1)
        at_row = pl.ds(pl.multiple_of((position & (CHB - 1)) * TB, TB), TB)
        at_lane = pl.ds(pl.multiple_of((slot & 1) * TB, TB), TB)
        acc[into, lax.shift_right_logical(slot, 1), at_row, at_lane] += tiles[tile]

    if whole:

        def add_now(t, carry):
            s, position = place_of(t)
            add_block(s, position, t)
            return carry

        acc[...] = jnp.zeros_like(acc)
        for g, item in enumerate(tile_copies):
            item.wait()
            end = (g + 1) * size

            @pl.when(live_ref[0] >= end)
            def _():
                lax.fori_loop(end - size, end, add_now, 0, unroll=4)

            @pl.when(live_ref[0] < end)
            def _():
                lax.fori_loop(end - size, live_ref[0], add_now, 0)

    else:

        def place(t, counted):
            s, position = place_of(t)
            n = counted[0]
            for k in range(1, n_col):
                n = jnp.where(s == k, counted[k], n)
            lists[s, n] = position * TILES_DEV + t
            return tuple(c + (s == k).astype(jnp.int32) for k, c in enumerate(counted))

        counted = lax.fori_loop(0, live_ref[0], place, (jnp.int32(0),) * n_col)
        for s in range(n_col):
            counts[s] = counted[s]
        for item in tile_copies:
            item.wait()

    def out_copy(origin, p):
        return pltpu.make_async_copy(buf.at[origin % 2, p], out_hbm.at[origin, p], out_sems.at[origin % 2, p])

    for origin in range(n_col):
        if not whole:

            def add(n, carry):
                entry = lists[origin, n]
                add_block(0, lax.shift_right_logical(entry, TILES_DEV.bit_length() - 1), entry & (TILES_DEV - 1))
                return carry

            acc[...] = jnp.zeros_like(acc)
            lax.fori_loop(0, counts[origin], add, 0)
        summed_blocks = acc.at[origin if whole else 0]
        for p in range(pairs):
            if origin >= 2:
                out_copy(origin - 2, p).wait()
            high, low = split(summed_blocks[p])
            buf[origin % 2, p, :NODES_DEV, :] = high
            buf[origin % 2, p, NODES_DEV:, :] = low
            out_copy(origin, p).start()
        if origin in origins:
            k = origins.index(origin)
            field_copies[k].wait()
            left = stacked(held[k])
            for p in range(pairs):
                summed = times(left, buf.at[origin % 2, p])
                here = slice(p * WIDE, (p + 1) * WIDE)
                total_ref[:, here] = summed if origin == 0 else total_ref[:, here] + summed
    for origin in range(n_col - 2, n_col):
        for p in range(pairs):
            out_copy(origin, p).wait()


def build_operator(n_row, n_col, ids, live, rows, slots, values, pairs):
    part = (n_row // 2, 2 * NODES_DEV, WIDE)
    sums = (n_row // 2, NODES_DEV, WIDE)
    held_origins = n_col if 4 * n_col * n_row * TB * NODES_DEV <= WHOLE_BYTES else 1
    origins, fields = zip(*pairs)
    return pl.pallas_call(
        functools.partial(operator_kernel, n_row, n_col, origins),
        in_specs=[SMEM] * 2 + [HBM] * 3 + [ANY] * len(fields),
        out_specs=[HBM, VMEM],
        out_shape=[pltpu.HBM((n_col,) + part, BF16), jax.ShapeDtypeStruct((H, n_row * TB), F32)],
        scratch_shapes=[
            pltpu.VMEM((TILES_DEV, TB, TB), F32),
            pltpu.VMEM((held_origins,) + sums, F32),
            pltpu.VMEM((2,) + part, BF16),
            pltpu.VMEM((len(fields), H, NODES_DEV), F32),
            pltpu.SMEM((n_col, TILES_DEV), jnp.int32),
            pltpu.SMEM((n_col,), jnp.int32),
            pltpu.SMEM((1, TILES_DEV), jnp.int32),
            pltpu.SMEM((1, TILES_DEV), jnp.int32),
            pltpu.SemaphoreType.DMA((GROUPS,)),
            pltpu.SemaphoreType.DMA((2,)),
            pltpu.SemaphoreType.DMA((len(fields),)),
            pltpu.SemaphoreType.DMA((2, n_row // 2)),
        ],
        compiler_params=params(48),
        cost_estimate=HEAVY,
        name="operator",
    )(ids, live, *in_hbm(rows, slots, values), *fields)


def product_kernel(n_row, n_col, origins, has_prev, last, n_carriers, has_base, apart, *refs):
    n = len(origins)
    if n_carriers or apart:
        index_ref, refs = refs[0], refs[1:]
    op_ref, refs = refs[0], refs[1:]
    fields, refs = refs[:n], refs[n:]
    if has_prev:
        prev_hbm, refs = refs[0], refs[1:]
    carriers, refs = refs[:n_carriers], refs[n_carriers:]
    if has_base:
        base_hbm, out_ref, base_ref, refs = refs[0], refs[1], refs[2], refs[3:]
    elif apart:
        slot_refs, refs = refs[:n_row], refs[n_row:]
    else:
        out_ref, refs = refs[0], refs[1:]
    held, buf, field_sems, sems, out, out_sems, prev, other_sems = refs[:8]
    order = [(k, p) for p in range(n_row // 2) for k in range(n)]

    def copy(k, p):
        return pltpu.make_async_copy(op_ref.at[origins[k], p], buf.at[k, p], sems.at[k, p])

    field_copies = fetch([x.at[pl.ds(0, H)] for x in fields], [held.at[k] for k in range(n)], field_sems)
    for k, p in order[:DEPTH]:
        copy(k, p).start()
    if has_prev:
        (prev_copy,) = fetch([prev_hbm], [prev], other_sems.at[pl.ds(0, 1)])
    if has_base:
        (base_copy,) = fetch([base_hbm], [base_ref], other_sems.at[pl.ds(1, 1)])
    left = []
    for k in range(n):
        field_copies[k].wait()
        left.append(stacked(held[k]))
    if n_carriers:
        ordered = refs[8]
        for k in range(n_col):
            ordered[lax.rem(index_ref[0] + k, n_col)] = carriers[k][H:, :]
        share = ordered[0]
        for k in range(1, n_col):
            share = share + ordered[k]
        rows = share.shape[0]
        groups = NODES_DEV // LANES // 2
        for j in range(groups):
            for q in range(n_row):
                from_lane = (q % 2 * groups + j) * LANES
                out[q, H + j * rows : H + (j + 1) * rows, :] = share[:, from_lane : from_lane + LANES]
    sent = []
    for p in range(n_row // 2):
        here = slice(p * WIDE, (p + 1) * WIDE)
        total = None
        for k in range(n):
            copy(k, p).wait()
            ahead = p * n + k + DEPTH
            if ahead < len(order):
                copy(*order[ahead]).start()
            part = times(left[k], buf.at[k, p])
            total = part if total is None else total + part
        if has_prev:
            if p == 0:
                prev_copy.wait()
            total = total + prev[:, here]
        if last:
            out[2 * p, :H, :] = total[:, :TB]
            out[2 * p + 1, :H, :] = total[:, TB:]
            place = pl.ds(2 * p, 2)
            if apart:
                continue
            sent.append(pltpu.make_async_copy(out.at[place], out_ref.at[place], out_sems.at[p]))
        else:
            out[:, here] = total
            place = (pl.ds(0, H), pl.ds(p * WIDE, WIDE))
            sent.append(pltpu.make_async_copy(out.at[place], out_ref.at[place], out_sems.at[p]))
        sent[-1].start()
    if has_base:
        base_copy.wait()
    if apart:
        for j, slot_ref in enumerate(slot_refs):
            slot_ref[...] = out[index_ref[0] ^ j]
    for item in sent:
        item.wait()


def product(n_row, n_col, ids, row, origins, operator, fields, prev, last, carriers=(), base=None, prev_near=False, apart=False):
    n = len(origins)
    has_prev = prev is not None
    has_base = base is not None
    rows = carriers[0].shape[0] - H if carriers else 0
    under = rows * NODES_DEV // LANES // 2
    shape = (n_row, H + under, TB) if last else (H, n_row * TB)
    scratch = [
        pltpu.VMEM((n, H, NODES_DEV), F32),
        pltpu.VMEM((n, n_row // 2, 2 * NODES_DEV, WIDE), BF16),
        pltpu.SemaphoreType.DMA((n,)),
        pltpu.SemaphoreType.DMA((n, n_row // 2)),
        pltpu.VMEM(shape, F32),
        pltpu.SemaphoreType.DMA((n_row // 2,)),
        pltpu.VMEM((H, n_row * TB) if has_prev else (8, LANES), F32),
        pltpu.SemaphoreType.DMA((2,)),
    ]
    if carriers:
        scratch.append(pltpu.VMEM((n_col, rows, NODES_DEV), F32))
    index = (ids,) if carriers else (row,) if apart else ()
    out = pltpu.HBM(shape, F32)
    out_specs, out_shape = HBM, out
    if has_base:
        out_specs, out_shape = [HBM, VMEM], [out, jax.ShapeDtypeStruct(base.shape, F32)]
    elif apart:
        out_specs, out_shape = [VMEM] * n_row, [jax.ShapeDtypeStruct((H, TB), F32)] * n_row
    return pl.pallas_call(
        functools.partial(product_kernel, n_row, n_col, origins, has_prev, last, len(carriers), has_base, apart),
        in_specs=[SMEM] * len(index) + [HBM] + [ANY] * (n + has_prev) + [VMEM] * len(carriers) + [HBM] * has_base,
        out_specs=out_specs,
        out_shape=out_shape,
        scratch_shapes=scratch,
        compiler_params=params(48),
        cost_estimate=LIGHT if last else HEAVY,
        name="product",
    )(
        *index,
        *in_hbm(operator),
        *fields,
        *((prev,) if prev_near else in_hbm(prev) if has_prev else ()),
        *carriers,
        *(in_hbm(base) if has_base else ()),
    )


def carry_kernel(n_row, rows, owners_ref, base_ref, came_ref, *refs):
    out_ref = refs[-1]
    out_ref[:H, :] = base_ref[...]
    for q in range(n_row):
        here = pl.ds(pl.multiple_of(owners_ref[q] * TB, TB), TB)
        out_ref[:H, here] += 2.0 * came_ref[q]
    if rows:
        pieces_ref = refs[0]
        share = pieces_ref[0]
        for q in range(1, n_row):
            share = share + pieces_ref[q]
        for j in range(NODES_DEV // LANES):
            out_ref[H:, j * LANES : (j + 1) * LANES] = share[j * rows : (j + 1) * rows, :]


def carry(n_row, owners, base, came, *pieces):
    rows = pieces[0].shape[1] * LANES // NODES_DEV if pieces else 0
    return pl.pallas_call(
        functools.partial(carry_kernel, n_row, rows),
        in_specs=[SMEM] + [VMEM] * (2 + len(pieces)),
        out_specs=VMEM,
        out_shape=jax.ShapeDtypeStruct((H + rows, NODES_DEV), F32),
        compiler_params=params(24),
        cost_estimate=LIGHT,
        name="carry",
    )(owners, base, came, *pieces)


def finish_kernel(n_row, row_ref, owners_ref, base_ref, left_ref, *refs):
    right_refs, out_ref, total = refs[:n_row], refs[n_row], refs[n_row + 1]
    total[...] = base_ref[...]
    for q in range(n_row):
        here = pl.ds(pl.multiple_of(owners_ref[q] * TB, TB), TB)
        total[:H, here] += left_ref[q, :H, :]
    for j in range(n_row):
        here = pl.ds(pl.multiple_of(owners_ref[row_ref[0] ^ j] * TB, TB), TB)
        total[H:, here] += right_refs[j][...]
    out_ref[...] = total[...].T


def finish(n_row, row, owners, base, left, right):
    return pl.pallas_call(
        functools.partial(finish_kernel, n_row),
        in_specs=[SMEM] * 2 + [VMEM] * (2 + n_row),
        out_specs=VMEM,
        out_shape=jax.ShapeDtypeStruct((NODES_DEV, F), F32),
        scratch_shapes=[pltpu.VMEM((F, NODES_DEV), F32)],
        compiler_params=params(24),
        cost_estimate=LIGHT,
        name="finish",
    )(row, owners, base, left, *right)


def assemble_kernel(n_row, row_ref, own_ref, other_ref, out_ref, halves, turned):
    rows = F // n_row
    half = lax.rem(row_ref[0], 2)
    halves[half] = own_ref[:, H:, :]
    halves[1 - half] = other_ref[:, H:, :]
    groups = 3 * F // LANES // 2
    for q in range(n_row):
        for j in range(2 * groups):
            here = slice(j % groups * rows, (j % groups + 1) * rows)
            turned[q * rows : (q + 1) * rows, j * LANES : (j + 1) * LANES] = halves[j // groups, q, here, :]
    for k in range(3):
        out_ref[k] = turned[:, k * F : (k + 1) * F].T


def assemble(n_row, row, own, other):
    return pl.pallas_call(
        functools.partial(assemble_kernel, n_row),
        in_specs=[SMEM, VMEM, VMEM],
        out_specs=VMEM,
        out_shape=jax.ShapeDtypeStruct((3, F, F), F32),
        scratch_shapes=[
            pltpu.VMEM((2, n_row, own.shape[1] - H, LANES), F32),
            pltpu.VMEM((F, 3 * F), F32),
        ],
        compiler_params=params(16),
        cost_estimate=LIGHT,
        name="assemble",
    )(row, own, other)


def shift(n_col, x, step):
    return lax.ppermute(x, "col", [(c, (c + step) % n_col) for c in range(n_col)])


def exchange(pieces):
    return lax.all_to_all(pieces, "row", split_axis=0, concat_axis=0, tiled=True)


def after(x, *others):
    return lax.optimization_barrier((x, *others))[0]


def opposite(field, below, above):
    col = lax.axis_index("col")
    sent = jnp.where(col == 1, above, jnp.where(col == 2, below, field))
    return lax.ppermute(sent, "col", [(1, 0), (2, 3), (3, 1), (0, 2)])


def gather(n_col, field, side):
    long = n_col // 2
    short = n_col - 1 - long
    ahead, behind = field, field
    steps = [[(0, field)]]
    for s in range(1, long + 1):
        if s == 2:
            ahead = after(ahead, behind)
        if s == 2 and n_col == 4:
            ahead = opposite(field, ahead, behind) if side > 0 else opposite(field, behind, ahead)
        else:
            ahead = shift(n_col, ahead, side)
        step = [((-side * s) % n_col, ahead)]
        if s <= short:
            behind = shift(n_col, behind, -side)
            step.append(((side * s) % n_col, behind))
        steps.append(step)
    return steps


def early(n_row, n_col, ids, row, operator, steps, total=None, done=0, base=None):
    pairs = [pair for step in steps[:-1] for pair in step][done:]
    for begin in range(0, len(pairs), 3):
        origins, fields = zip(*pairs[begin : begin + 3])
        brought = base if begin + 3 >= len(pairs) else None
        total = product(n_row, n_col, ids, row, origins, operator, fields, total, False, base=brought)
    return total


def final(n_row, n_col, ids, row, operator, steps, total, carrying=False, near=False, apart=False):
    origins, fields = zip(*steps[-1])
    carriers = [x for _, x in sorted((p for step in steps for p in step), key=lambda p: p[0])] if carrying else ()
    return product(n_row, n_col, ids, row, origins, operator, fields, total, True, carriers, prev_near=near, apart=apart)


def per_device(
    grad_out,
    relu_mask,
    basis_zero,
    basis_one,
    basis_two,
    cheb_weight,
    tile_values,
    tile_rows,
    tile_slots,
    send_blocks,
    live_tiles,
):
    n_row = lax.axis_size("row")
    n_col = lax.axis_size("col")
    ids = lax.axis_index("col").astype(jnp.int32).reshape(1)
    row = lax.axis_index("row").astype(jnp.int32).reshape(1)
    owners = send_blocks.reshape(n_row)
    left, right = term_two(grad_out, relu_mask, cheb_weight)
    one_left, one_right, diff, pieces = local_terms(
        n_row, left, grad_out, relu_mask, cheb_weight, basis_zero, basis_one, basis_two
    )
    steps = gather(n_col, left, 1)
    first = steps[0] + steps[1] if len(steps) > 2 else steps[0]
    operator, left_early = build_operator(
        n_row, n_col, ids, live_tiles, tile_rows, tile_slots, tile_values, first
    )
    pieces = exchange(pieces)
    common = (n_row, n_col, ids, row, operator)

    left_early = early(*common, steps, left_early, len(first))
    right_steps = gather(n_col, after(right, left_early, steps[-1][0][1]), -1)
    left_came = exchange(final(*common, steps, after(left_early, pieces), near=len(steps) == 3))
    right_early, one_left = early(*common, right_steps, base=one_left)

    left_carried = carry(n_row, owners, after(one_left, right_early, right_steps[-1][0][1]), left_came, pieces)
    steps = gather(n_col, left_carried, 1)
    right_came = exchange(final(*common, right_steps, right_early))
    left_early, one_right = early(*common, steps, base=one_right)

    right_carried = carry(n_row, owners, after(one_right, left_early, steps[-1][0][1]), right_came)
    right_steps = gather(n_col, right_carried, -1)
    left_came = exchange(final(*common, steps, left_early, carrying=True))
    right_early = early(*common, right_steps)

    right_last = final(*common, right_steps, right_early, apart=True)
    right_came = [right_last[0]] * n_row
    for j in range(n_row - 1, 0, -1):
        right_came[j] = lax.ppermute(right_last[j], "row", [(r, r ^ j) for r in range(n_row)])
    other = lax.ppermute(after(left_came, right_came[-1]), "row", [(r, r ^ 1) for r in range(n_row)])
    weight_grad = assemble(n_row, row, left_came, other)
    return finish(n_row, row, owners, after(diff, weight_grad), left_came, right_came), weight_grad


def solution(mesh):
    placed = (
        P(("row", "col"), None),
        P(("row", "col"), None),
        P(("row", "col"), None),
        P(("row", "col"), None),
        P(("row", "col"), None),
        P(),
        P(("row", "col"), None, None, None),
        P(("row", "col"), None),
        P(("row", "col"), None),
        P(("row", "col"), None, None),
        P(("row", "col")),
    )
    return jax.shard_map(
        per_device,
        mesh=mesh,
        in_specs=placed,
        out_specs=(P(("row", "col"), None), P()),
        check_vma=False,
    )
```

```python
import functools

import jax
import jax.numpy as jnp
from jax import lax
from jax.experimental import pallas as pl
from jax.experimental.pallas import tpu as pltpu
from jax.sharding import PartitionSpec as P

F = 256
H = 128
TB = 128
CHB = 4
WIDE = 2 * TB
LANES = 128
NODES_DEV = CHB * TB
TILES_DEV = 128
GROUPS = 8
MIB = 1 << 20
WHOLE_BYTES = 12 * MIB
DEPTH = 4
HEAVY = pl.CostEstimate(flops=1 << 34, bytes_accessed=64 * MIB, transcendentals=0)
LIGHT = pl.CostEstimate(flops=1024, bytes_accessed=1024, transcendentals=0)
BF16 = jnp.bfloat16
F32 = jnp.float32

SMEM = pl.BlockSpec(memory_space=pltpu.SMEM)
VMEM = pl.BlockSpec(memory_space=pltpu.VMEM)
HBM = pl.BlockSpec(memory_space=pltpu.HBM)
ANY = pl.BlockSpec(memory_space=pl.ANY)


def params(mib):
    return pltpu.CompilerParams(vmem_limit_bytes=mib * MIB)


def in_hbm(*arrays):
    return [pltpu.with_memory_space_constraint(x, pltpu.HBM) for x in arrays]


def split(x):
    high = x.astype(BF16)
    low = (x - high.astype(F32)).astype(BF16)
    return high, low


def dot3(a, b, dims):
    ah, al = a
    bh, bl = b

    def one(x, y):
        return lax.dot_general(x, y, (dims, ((), ())), preferred_element_type=F32)

    return one(ah, bh) + (one(ah, bl) + one(al, bh))


def fetch(sources, targets, sems):
    copies = [pltpu.make_async_copy(a, b, sems.at[i]) for i, (a, b) in enumerate(zip(sources, targets))]
    for copy in copies:
        copy.start()
    return copies


def masked_of(grad, mask):
    return jnp.where(mask > 0, grad, jnp.zeros_like(grad))


def term_two_kernel(grad_hbm, mask_hbm, weight_hbm, left_ref, right_ref, grad, mask, weight, sems):
    for copy in fetch((grad_hbm, mask_hbm, weight_hbm.at[2]), (grad, mask, weight), sems):
        copy.wait()
    term = dot3(split(weight[...]), split(masked_of(grad[...], mask[...])), ((1,), (1,)))
    left_ref[...] = term[:H]
    right_ref[...] = term[H:]


def term_two(grad_out, relu_mask, cheb_weight):
    out = jax.ShapeDtypeStruct((H, NODES_DEV), F32)
    return pl.pallas_call(
        term_two_kernel,
        in_specs=[HBM] * 3,
        out_specs=[VMEM, VMEM],
        out_shape=[out, out],
        scratch_shapes=[
            pltpu.VMEM((NODES_DEV, F), F32),
            pltpu.VMEM((NODES_DEV, F), jnp.int32),
            pltpu.VMEM((F, F), F32),
            pltpu.SemaphoreType.DMA((3,)),
        ],
        compiler_params=params(16),
        cost_estimate=LIGHT,
        name="term_two",
    )(*in_hbm(grad_out, relu_mask, cheb_weight))


def local_kernel(
    n_row, first_ref, grad_hbm, mask_hbm, weight_hbm, h0, h1, h2, left_hbm, right_hbm, diff_ref, pieces_ref,
    grad, mask, weight, bases, one, sems, one_sems,
):
    sources = (grad_hbm, mask_hbm, weight_hbm, h0, h1, h2)
    copies = fetch(sources, (grad, mask, weight, bases.at[0], bases.at[1], bases.at[2]), sems)
    for copy in copies[:3]:
        copy.wait()
    values = masked_of(grad[...], mask[...])
    masked = split(values)
    term = dot3(split(weight[1]), masked, ((1,), (1,)))
    one[...] = term
    one_copies = fetch((one.at[pl.ds(0, H)], one.at[pl.ds(H, H)]), (left_hbm, right_hbm), one_sems)
    diff_ref[...] = dot3(split(weight[0] - weight[2]), masked, ((1,), (1,)))
    turned = split(values.T)
    rows = F // n_row
    for k in range(3):
        copies[3 + k].wait()
        part = dot3(turned, split(bases[k]), ((1,), (0,)))
        for j in range(F // LANES):
            here = (k * (F // LANES) + j) * rows
            for q in range(n_row):
                pieces_ref[q, here : here + rows, :] = part[q * rows : (q + 1) * rows, j * LANES : (j + 1) * LANES]
    for copy in one_copies:
        copy.wait()


def local_terms(n_row, first, grad_out, relu_mask, cheb_weight, b0, b1, b2):
    half = pltpu.HBM((H, NODES_DEV), F32)
    share = 3 * F * F // n_row // LANES
    return pl.pallas_call(
        functools.partial(local_kernel, n_row),
        in_specs=[ANY] + [HBM] * 6,
        out_specs=[HBM, HBM, VMEM, VMEM],
        out_shape=[
            half,
            half,
            jax.ShapeDtypeStruct((F, NODES_DEV), F32),
            jax.ShapeDtypeStruct((n_row, share, LANES), F32),
        ],
        scratch_shapes=[
            pltpu.VMEM((NODES_DEV, F), F32),
            pltpu.VMEM((NODES_DEV, F), jnp.int32),
            pltpu.VMEM((3, F, F), F32),
            pltpu.VMEM((3, NODES_DEV, F), F32),
            pltpu.VMEM((F, NODES_DEV), F32),
            pltpu.SemaphoreType.DMA((6,)),
            pltpu.SemaphoreType.DMA((2,)),
        ],
        compiler_params=params(32),
        cost_estimate=LIGHT,
        name="local_terms",
    )(first, *in_hbm(grad_out, relu_mask, cheb_weight, b0, b1, b2))


def stacked(field):
    return jnp.concatenate(split(field), axis=0)


def times(left, part):
    by_high = jnp.dot(left, part[:NODES_DEV, :], preferred_element_type=F32)
    by_low = jnp.dot(left[:H], part[NODES_DEV:, :], preferred_element_type=F32)
    return by_high[:H] + (by_high[H:] + by_low)


def operator_kernel(n_row, n_col, origins, ids_ref, live_ref, rows_hbm, slots_hbm, values_ref, *refs):
    fields, refs = refs[: len(origins)], refs[len(origins) :]
    out_hbm, total_ref, tiles, acc, buf, held, lists, counts, rows, slots, sems, small_sems, field_sems, out_sems = refs
    size = TILES_DEV // GROUPS
    pairs = n_row // 2
    whole = acc.shape[0] == n_col
    small = fetch((rows_hbm, slots_hbm), (rows, slots), small_sems)
    parts = [pl.ds(g * size, size) for g in range(GROUPS)]
    tile_copies = fetch([values_ref.at[0, part] for part in parts], [tiles.at[part] for part in parts], sems)
    field_copies = fetch(fields, [held.at[k] for k in range(len(fields))], field_sems)
    for item in small:
        item.wait()

    def place_of(t):
        row = rows[0, t]
        if n_col & (n_col - 1) == 0:
            s = (lax.shift_right_logical(row, CHB.bit_length() - 1) - ids_ref[0]) & (n_col - 1)
        else:
            s = lax.rem(row // CHB - ids_ref[0] + n_col, n_col)
        return s, slots[0, t] * CHB + (row & (CHB - 1))

    def add_block(into, position, tile):
        slot = lax.shift_right_logical(position, CHB.bit_length() - 1)
        at_row = pl.ds(pl.multiple_of((position & (CHB - 1)) * TB, TB), TB)
        at_lane = pl.ds(pl.multiple_of((slot & 1) * TB, TB), TB)
        acc[into, lax.shift_right_logical(slot, 1), at_row, at_lane] += tiles[tile]

    if whole:

        def add_now(t, carry):
            s, position = place_of(t)
            add_block(s, position, t)
            return carry

        acc[...] = jnp.zeros_like(acc)
        for g, item in enumerate(tile_copies):
            item.wait()
            end = (g + 1) * size

            @pl.when(live_ref[0] >= end)
            def _():
                lax.fori_loop(end - size, end, add_now, 0, unroll=4)

            @pl.when(live_ref[0] < end)
            def _():
                lax.fori_loop(end - size, live_ref[0], add_now, 0)

    else:

        def place(t, counted):
            s, position = place_of(t)
            n = counted[0]
            for k in range(1, n_col):
                n = jnp.where(s == k, counted[k], n)
            lists[s, n] = position * TILES_DEV + t
            return tuple(c + (s == k).astype(jnp.int32) for k, c in enumerate(counted))

        counted = lax.fori_loop(0, live_ref[0], place, (jnp.int32(0),) * n_col)
        for s in range(n_col):
            counts[s] = counted[s]
        for item in tile_copies:
            item.wait()

    def out_copy(origin, p):
        return pltpu.make_async_copy(buf.at[origin % 2, p], out_hbm.at[origin, p], out_sems.at[origin % 2, p])

    for origin in range(n_col):
        if not whole:

            def add(n, carry):
                entry = lists[origin, n]
                add_block(0, lax.shift_right_logical(entry, TILES_DEV.bit_length() - 1), entry & (TILES_DEV - 1))
                return carry

            acc[...] = jnp.zeros_like(acc)
            lax.fori_loop(0, counts[origin], add, 0)
        summed_blocks = acc.at[origin if whole else 0]
        for p in range(pairs):
            if origin >= 2:
                out_copy(origin - 2, p).wait()
            high, low = split(summed_blocks[p])
            buf[origin % 2, p, :NODES_DEV, :] = high
            buf[origin % 2, p, NODES_DEV:, :] = low
            out_copy(origin, p).start()
        if origin in origins:
            k = origins.index(origin)
            field_copies[k].wait()
            left = stacked(held[k])
            for p in range(pairs):
                summed = times(left, buf.at[origin % 2, p])
                here = slice(p * WIDE, (p + 1) * WIDE)
                total_ref[:, here] = summed if origin == 0 else total_ref[:, here] + summed
    for origin in range(n_col - 2, n_col):
        for p in range(pairs):
            out_copy(origin, p).wait()


def build_operator(n_row, n_col, ids, live, rows, slots, values, pairs):
    part = (n_row // 2, 2 * NODES_DEV, WIDE)
    sums = (n_row // 2, NODES_DEV, WIDE)
    held_origins = n_col if 4 * n_col * n_row * TB * NODES_DEV <= WHOLE_BYTES else 1
    origins, fields = zip(*pairs)
    return pl.pallas_call(
        functools.partial(operator_kernel, n_row, n_col, origins),
        in_specs=[SMEM] * 2 + [HBM] * 3 + [ANY] * len(fields),
        out_specs=[HBM, VMEM],
        out_shape=[pltpu.HBM((n_col,) + part, BF16), jax.ShapeDtypeStruct((H, n_row * TB), F32)],
        scratch_shapes=[
            pltpu.VMEM((TILES_DEV, TB, TB), F32),
            pltpu.VMEM((held_origins,) + sums, F32),
            pltpu.VMEM((2,) + part, BF16),
            pltpu.VMEM((len(fields), H, NODES_DEV), F32),
            pltpu.SMEM((n_col, TILES_DEV), jnp.int32),
            pltpu.SMEM((n_col,), jnp.int32),
            pltpu.SMEM((1, TILES_DEV), jnp.int32),
            pltpu.SMEM((1, TILES_DEV), jnp.int32),
            pltpu.SemaphoreType.DMA((GROUPS,)),
            pltpu.SemaphoreType.DMA((2,)),
            pltpu.SemaphoreType.DMA((len(fields),)),
            pltpu.SemaphoreType.DMA((2, n_row // 2)),
        ],
        compiler_params=params(48),
        cost_estimate=HEAVY,
        name="operator",
    )(ids, live, *in_hbm(rows, slots, values), *fields)


def product_kernel(n_row, n_col, origins, has_prev, last, n_carriers, has_base, apart, *refs):
    n = len(origins)
    if n_carriers or apart:
        index_ref, refs = refs[0], refs[1:]
    op_ref, refs = refs[0], refs[1:]
    fields, refs = refs[:n], refs[n:]
    if has_prev:
        prev_hbm, refs = refs[0], refs[1:]
    carriers, refs = refs[:n_carriers], refs[n_carriers:]
    if has_base:
        base_hbm, out_ref, base_ref, refs = refs[0], refs[1], refs[2], refs[3:]
    elif apart:
        slot_refs, refs = refs[:n_row], refs[n_row:]
    else:
        out_ref, refs = refs[0], refs[1:]
    held, buf, field_sems, sems, out, out_sems, prev, other_sems = refs[:8]
    order = [(k, p) for p in range(n_row // 2) for k in range(n)]

    def copy(k, p):
        return pltpu.make_async_copy(op_ref.at[origins[k], p], buf.at[k, p], sems.at[k, p])

    field_copies = fetch([x.at[pl.ds(0, H)] for x in fields], [held.at[k] for k in range(n)], field_sems)
    for k, p in order[:DEPTH]:
        copy(k, p).start()
    if has_prev:
        (prev_copy,) = fetch([prev_hbm], [prev], other_sems.at[pl.ds(0, 1)])
    if has_base:
        (base_copy,) = fetch([base_hbm], [base_ref], other_sems.at[pl.ds(1, 1)])
    left = []
    for k in range(n):
        field_copies[k].wait()
        left.append(stacked(held[k]))
    if n_carriers:
        ordered = refs[8]
        for k in range(n_col):
            ordered[lax.rem(index_ref[0] + k, n_col)] = carriers[k][H:, :]
        share = ordered[0]
        for k in range(1, n_col):
            share = share + ordered[k]
        rows = share.shape[0]
        groups = NODES_DEV // LANES // 2
        for j in range(groups):
            for q in range(n_row):
                from_lane = (q % 2 * groups + j) * LANES
                out[q, H + j * rows : H + (j + 1) * rows, :] = share[:, from_lane : from_lane + LANES]
    sent = []
    for p in range(n_row // 2):
        here = slice(p * WIDE, (p + 1) * WIDE)
        total = None
        for k in range(n):
            copy(k, p).wait()
            ahead = p * n + k + DEPTH
            if ahead < len(order):
                copy(*order[ahead]).start()
            part = times(left[k], buf.at[k, p])
            total = part if total is None else total + part
        if has_prev:
            if p == 0:
                prev_copy.wait()
            total = total + prev[:, here]
        if last:
            out[2 * p, :H, :] = total[:, :TB]
            out[2 * p + 1, :H, :] = total[:, TB:]
            place = pl.ds(2 * p, 2)
            if apart:
                continue
            sent.append(pltpu.make_async_copy(out.at[place], out_ref.at[place], out_sems.at[p]))
        else:
            out[:, here] = total
            place = (pl.ds(0, H), pl.ds(p * WIDE, WIDE))
            sent.append(pltpu.make_async_copy(out.at[place], out_ref.at[place], out_sems.at[p]))
        sent[-1].start()
    if has_base:
        base_copy.wait()
    if apart:
        for j, slot_ref in enumerate(slot_refs):
            slot_ref[...] = out[index_ref[0] ^ j]
    for item in sent:
        item.wait()


def product(n_row, n_col, ids, row, origins, operator, fields, prev, last, carriers=(), base=None, prev_near=False, apart=False):
    n = len(origins)
    has_prev = prev is not None
    has_base = base is not None
    rows = carriers[0].shape[0] - H if carriers else 0
    under = rows * NODES_DEV // LANES // 2
    shape = (n_row, H + under, TB) if last else (H, n_row * TB)
    scratch = [
        pltpu.VMEM((n, H, NODES_DEV), F32),
        pltpu.VMEM((n, n_row // 2, 2 * NODES_DEV, WIDE), BF16),
        pltpu.SemaphoreType.DMA((n,)),
        pltpu.SemaphoreType.DMA((n, n_row // 2)),
        pltpu.VMEM(shape, F32),
        pltpu.SemaphoreType.DMA((n_row // 2,)),
        pltpu.VMEM((H, n_row * TB) if has_prev else (8, LANES), F32),
        pltpu.SemaphoreType.DMA((2,)),
    ]
    if carriers:
        scratch.append(pltpu.VMEM((n_col, rows, NODES_DEV), F32))
    index = (ids,) if carriers else (row,) if apart else ()
    out = pltpu.HBM(shape, F32)
    out_specs, out_shape = HBM, out
    if has_base:
        out_specs, out_shape = [HBM, VMEM], [out, jax.ShapeDtypeStruct(base.shape, F32)]
    elif apart:
        out_specs, out_shape = [VMEM] * n_row, [jax.ShapeDtypeStruct((H, TB), F32)] * n_row
    return pl.pallas_call(
        functools.partial(product_kernel, n_row, n_col, origins, has_prev, last, len(carriers), has_base, apart),
        in_specs=[SMEM] * len(index) + [HBM] + [ANY] * (n + has_prev) + [VMEM] * len(carriers) + [HBM] * has_base,
        out_specs=out_specs,
        out_shape=out_shape,
        scratch_shapes=scratch,
        compiler_params=params(48),
        cost_estimate=LIGHT if last else HEAVY,
        name="product",
    )(
        *index,
        *in_hbm(operator),
        *fields,
        *((prev,) if prev_near else in_hbm(prev) if has_prev else ()),
        *carriers,
        *(in_hbm(base) if has_base else ()),
    )


def carry_kernel(n_row, rows, owners_ref, base_ref, came_ref, *refs):
    out_ref = refs[-1]
    out_ref[:H, :] = base_ref[...]
    for q in range(n_row):
        here = pl.ds(pl.multiple_of(owners_ref[q] * TB, TB), TB)
        out_ref[:H, here] += 2.0 * came_ref[q]
    if rows:
        pieces_ref = refs[0]
        share = pieces_ref[0]
        for q in range(1, n_row):
            share = share + pieces_ref[q]
        for j in range(NODES_DEV // LANES):
            out_ref[H:, j * LANES : (j + 1) * LANES] = share[j * rows : (j + 1) * rows, :]


def carry(n_row, owners, base, came, *pieces):
    rows = pieces[0].shape[1] * LANES // NODES_DEV if pieces else 0
    return pl.pallas_call(
        functools.partial(carry_kernel, n_row, rows),
        in_specs=[SMEM] + [VMEM] * (2 + len(pieces)),
        out_specs=VMEM,
        out_shape=jax.ShapeDtypeStruct((H + rows, NODES_DEV), F32),
        compiler_params=params(24),
        cost_estimate=LIGHT,
        name="carry",
    )(owners, base, came, *pieces)


def finish_kernel(n_row, row_ref, owners_ref, base_ref, left_ref, *refs):
    right_refs, out_ref, total = refs[:n_row], refs[n_row], refs[n_row + 1]
    total[...] = base_ref[...]
    for q in range(n_row):
        here = pl.ds(pl.multiple_of(owners_ref[q] * TB, TB), TB)
        total[:H, here] += left_ref[q, :H, :]
    for j in range(n_row):
        here = pl.ds(pl.multiple_of(owners_ref[row_ref[0] ^ j] * TB, TB), TB)
        total[H:, here] += right_refs[j][...]
    out_ref[...] = total[...].T


def finish(n_row, row, owners, base, left, right):
    return pl.pallas_call(
        functools.partial(finish_kernel, n_row),
        in_specs=[SMEM] * 2 + [VMEM] * (2 + n_row),
        out_specs=VMEM,
        out_shape=jax.ShapeDtypeStruct((NODES_DEV, F), F32),
        scratch_shapes=[pltpu.VMEM((F, NODES_DEV), F32)],
        compiler_params=params(24),
        cost_estimate=LIGHT,
        name="finish",
    )(row, owners, base, left, *right)


def assemble_kernel(n_row, row_ref, own_ref, other_ref, out_ref, halves, turned):
    rows = F // n_row
    half = lax.rem(row_ref[0], 2)
    halves[half] = own_ref[:, H:, :]
    halves[1 - half] = other_ref[:, H:, :]
    groups = 3 * F // LANES // 2
    for q in range(n_row):
        for j in range(2 * groups):
            here = slice(j % groups * rows, (j % groups + 1) * rows)
            turned[q * rows : (q + 1) * rows, j * LANES : (j + 1) * LANES] = halves[j // groups, q, here, :]
    for k in range(3):
        out_ref[k] = turned[:, k * F : (k + 1) * F].T


def assemble(n_row, row, own, other):
    return pl.pallas_call(
        functools.partial(assemble_kernel, n_row),
        in_specs=[SMEM, VMEM, VMEM],
        out_specs=VMEM,
        out_shape=jax.ShapeDtypeStruct((3, F, F), F32),
        scratch_shapes=[
            pltpu.VMEM((2, n_row, own.shape[1] - H, LANES), F32),
            pltpu.VMEM((F, 3 * F), F32),
        ],
        compiler_params=params(16),
        cost_estimate=LIGHT,
        name="assemble",
    )(row, own, other)


def shift(n_col, x, step):
    return lax.ppermute(x, "col", [(c, (c + step) % n_col) for c in range(n_col)])


def exchange(pieces):
    return lax.all_to_all(pieces, "row", split_axis=0, concat_axis=0, tiled=True)


def after(x, *others):
    return lax.optimization_barrier((x, *others))[0]


def opposite(field, below, above):
    col = lax.axis_index("col")
    sent = jnp.where(col == 1, above, jnp.where(col == 2, below, field))
    return lax.ppermute(sent, "col", [(1, 0), (2, 3), (3, 1), (0, 2)])


def gather(n_col, field, side):
    long = n_col // 2
    short = n_col - 1 - long
    ahead, behind = field, field
    steps = [[(0, field)]]
    for s in range(1, long + 1):
        if s == 2:
            ahead = after(ahead, behind)
        if s == 2 and n_col == 4:
            ahead = opposite(field, ahead, behind) if side > 0 else opposite(field, behind, ahead)
        else:
            ahead = shift(n_col, ahead, side)
        step = [((-side * s) % n_col, ahead)]
        if s <= short:
            behind = shift(n_col, behind, -side)
            step.append(((side * s) % n_col, behind))
        steps.append(step)
    return steps


def early(n_row, n_col, ids, row, operator, steps, total=None, done=0, base=None):
    pairs = [pair for step in steps[:-1] for pair in step][done:]
    for begin in range(0, len(pairs), 3):
        origins, fields = zip(*pairs[begin : begin + 3])
        brought = base if begin + 3 >= len(pairs) else None
        total = product(n_row, n_col, ids, row, origins, operator, fields, total, False, base=brought)
    return total


def final(n_row, n_col, ids, row, operator, steps, total, carrying=False, near=False, apart=False):
    origins, fields = zip(*steps[-1])
    carriers = [x for _, x in sorted((p for step in steps for p in step), key=lambda p: p[0])] if carrying else ()
    return product(n_row, n_col, ids, row, origins, operator, fields, total, True, carriers, prev_near=near, apart=apart)


def per_device(
    grad_out,
    relu_mask,
    basis_zero,
    basis_one,
    basis_two,
    cheb_weight,
    tile_values,
    tile_rows,
    tile_slots,
    send_blocks,
    live_tiles,
):
    n_row = lax.axis_size("row")
    n_col = lax.axis_size("col")
    ids = lax.axis_index("col").astype(jnp.int32).reshape(1)
    row = lax.axis_index("row").astype(jnp.int32).reshape(1)
    owners = send_blocks.reshape(n_row)
    left, right = term_two(grad_out, relu_mask, cheb_weight)
    one_left, one_right, diff, pieces = local_terms(
        n_row, left, grad_out, relu_mask, cheb_weight, basis_zero, basis_one, basis_two
    )
    steps = gather(n_col, left, 1)
    first = steps[0] + steps[1] if len(steps) > 2 else steps[0]
    operator, left_early = build_operator(
        n_row, n_col, ids, live_tiles, tile_rows, tile_slots, tile_values, first
    )
    pieces = exchange(pieces)
    common = (n_row, n_col, ids, row, operator)

    left_early = early(*common, steps, left_early, len(first))
    right_steps = gather(n_col, after(right, left_early, steps[-1][0][1]), -1)
    left_came = exchange(final(*common, steps, after(left_early, pieces), near=len(steps) == 3))
    right_early, one_left = early(*common, right_steps, base=one_left)

    left_carried = carry(n_row, owners, after(one_left, right_early, right_steps[-1][0][1]), left_came, pieces)
    steps = gather(n_col, left_carried, 1)
    right_came = exchange(final(*common, right_steps, right_early))
    left_early, one_right = early(*common, steps, base=one_right)

    right_carried = carry(n_row, owners, after(one_right, left_early, steps[-1][0][1]), right_came)
    right_steps = gather(n_col, right_carried, -1)
    left_came = exchange(final(*common, steps, left_early, carrying=True))
    right_early = early(*common, right_steps)

    right_last = final(*common, right_steps, right_early, apart=True)
    right_came = [right_last[0]] * n_row
    for j in range(n_row - 1, 0, -1):
        right_came[j] = lax.ppermute(right_last[j], "row", [(r, r ^ j) for r in range(n_row)])
    other = lax.ppermute(after(left_came, *right_came[n_row // 2 :]), "row", [(r, r ^ 1) for r in range(n_row)])
    weight_grad = assemble(n_row, row, left_came, other)
    return finish(n_row, row, owners, after(diff, weight_grad), left_came, right_came), weight_grad


def solution(mesh):
    placed = (
        P(("row", "col"), None),
        P(("row", "col"), None),
        P(("row", "col"), None),
        P(("row", "col"), None),
        P(("row", "col"), None),
        P(),
        P(("row", "col"), None, None, None),
        P(("row", "col"), None),
        P(("row", "col"), None),
        P(("row", "col"), None, None),
        P(("row", "col")),
    )
    return jax.shard_map(
        per_device,
        mesh=mesh,
        in_specs=placed,
        out_specs=(P(("row", "col"), None), P()),
        check_vma=False,
    )
```

```python
import functools

import jax
import jax.numpy as jnp
from jax import lax
from jax.experimental import pallas as pl
from jax.experimental.pallas import tpu as pltpu
from jax.sharding import PartitionSpec as P

F = 256
H = 128
TB = 128
CHB = 4
WIDE = 2 * TB
LANES = 128
NODES_DEV = CHB * TB
TILES_DEV = 128
GROUPS = 8
MIB = 1 << 20
WHOLE_BYTES = 12 * MIB
DEPTH = 4
HEAVY = pl.CostEstimate(flops=1 << 34, bytes_accessed=64 * MIB, transcendentals=0)
LIGHT = pl.CostEstimate(flops=1024, bytes_accessed=1024, transcendentals=0)
BF16 = jnp.bfloat16
F32 = jnp.float32

SMEM = pl.BlockSpec(memory_space=pltpu.SMEM)
VMEM = pl.BlockSpec(memory_space=pltpu.VMEM)
HBM = pl.BlockSpec(memory_space=pltpu.HBM)
ANY = pl.BlockSpec(memory_space=pl.ANY)


def params(mib):
    return pltpu.CompilerParams(vmem_limit_bytes=mib * MIB)


def in_hbm(*arrays):
    return [pltpu.with_memory_space_constraint(x, pltpu.HBM) for x in arrays]


def split(x):
    high = x.astype(BF16)
    low = (x - high.astype(F32)).astype(BF16)
    return high, low


def dot3(a, b, dims):
    ah, al = a
    bh, bl = b

    def one(x, y):
        return lax.dot_general(x, y, (dims, ((), ())), preferred_element_type=F32)

    return one(ah, bh) + (one(ah, bl) + one(al, bh))


def fetch(sources, targets, sems):
    copies = [pltpu.make_async_copy(a, b, sems.at[i]) for i, (a, b) in enumerate(zip(sources, targets))]
    for copy in copies:
        copy.start()
    return copies


def masked_of(grad, mask):
    return jnp.where(mask > 0, grad, jnp.zeros_like(grad))


def term_two_kernel(grad_hbm, mask_hbm, weight_hbm, left_ref, right_ref, grad, mask, weight, sems):
    for copy in fetch((grad_hbm, mask_hbm, weight_hbm.at[2]), (grad, mask, weight), sems):
        copy.wait()
    term = dot3(split(weight[...]), split(masked_of(grad[...], mask[...])), ((1,), (1,)))
    left_ref[...] = term[:H]
    right_ref[...] = term[H:]


def term_two(grad_out, relu_mask, cheb_weight):
    out = jax.ShapeDtypeStruct((H, NODES_DEV), F32)
    return pl.pallas_call(
        term_two_kernel,
        in_specs=[HBM] * 3,
        out_specs=[VMEM, VMEM],
        out_shape=[out, out],
        scratch_shapes=[
            pltpu.VMEM((NODES_DEV, F), F32),
            pltpu.VMEM((NODES_DEV, F), jnp.int32),
            pltpu.VMEM((F, F), F32),
            pltpu.SemaphoreType.DMA((3,)),
        ],
        compiler_params=params(16),
        cost_estimate=LIGHT,
        name="term_two",
    )(*in_hbm(grad_out, relu_mask, cheb_weight))


def local_kernel(
    n_row, first_ref, grad_hbm, mask_hbm, weight_hbm, h0, h1, h2, left_hbm, right_hbm, diff_ref, pieces_ref,
    grad, mask, weight, bases, one, sems, one_sems,
):
    sources = (grad_hbm, mask_hbm, weight_hbm, h0, h1, h2)
    copies = fetch(sources, (grad, mask, weight, bases.at[0], bases.at[1], bases.at[2]), sems)
    for copy in copies[:3]:
        copy.wait()
    values = masked_of(grad[...], mask[...])
    masked = split(values)
    term = dot3(split(weight[1]), masked, ((1,), (1,)))
    one[...] = term
    one_copies = fetch((one.at[pl.ds(0, H)], one.at[pl.ds(H, H)]), (left_hbm, right_hbm), one_sems)
    diff_ref[...] = dot3(split(weight[0] - weight[2]), masked, ((1,), (1,)))
    turned = split(values.T)
    rows = F // n_row
    for k in range(3):
        copies[3 + k].wait()
        part = dot3(turned, split(bases[k]), ((1,), (0,)))
        for j in range(F // LANES):
            here = (k * (F // LANES) + j) * rows
            for q in range(n_row):
                pieces_ref[q, here : here + rows, :] = part[q * rows : (q + 1) * rows, j * LANES : (j + 1) * LANES]
    for copy in one_copies:
        copy.wait()


def local_terms(n_row, first, grad_out, relu_mask, cheb_weight, b0, b1, b2):
    half = pltpu.HBM((H, NODES_DEV), F32)
    share = 3 * F * F // n_row // LANES
    return pl.pallas_call(
        functools.partial(local_kernel, n_row),
        in_specs=[ANY] + [HBM] * 6,
        out_specs=[HBM, HBM, VMEM, VMEM],
        out_shape=[
            half,
            half,
            jax.ShapeDtypeStruct((F, NODES_DEV), F32),
            jax.ShapeDtypeStruct((n_row, share, LANES), F32),
        ],
        scratch_shapes=[
            pltpu.VMEM((NODES_DEV, F), F32),
            pltpu.VMEM((NODES_DEV, F), jnp.int32),
            pltpu.VMEM((3, F, F), F32),
            pltpu.VMEM((3, NODES_DEV, F), F32),
            pltpu.VMEM((F, NODES_DEV), F32),
            pltpu.SemaphoreType.DMA((6,)),
            pltpu.SemaphoreType.DMA((2,)),
        ],
        compiler_params=params(32),
        cost_estimate=LIGHT,
        name="local_terms",
    )(first, *in_hbm(grad_out, relu_mask, cheb_weight, b0, b1, b2))


def stacked(field):
    return jnp.concatenate(split(field), axis=0)


def times(left, part):
    by_high = jnp.dot(left, part[:NODES_DEV, :], preferred_element_type=F32)
    by_low = jnp.dot(left[:H], part[NODES_DEV:, :], preferred_element_type=F32)
    return by_high[:H] + (by_high[H:] + by_low)


def operator_kernel(n_row, n_col, origins, ids_ref, live_ref, rows_hbm, slots_hbm, values_ref, *refs):
    fields, refs = refs[: len(origins)], refs[len(origins) :]
    out_hbm, total_ref, tiles, acc, buf, held, lists, counts, rows, slots, sems, small_sems, field_sems, out_sems = refs
    size = TILES_DEV // GROUPS
    pairs = n_row // 2
    whole = acc.shape[0] == n_col
    small = fetch((rows_hbm, slots_hbm), (rows, slots), small_sems)
    parts = [pl.ds(g * size, size) for g in range(GROUPS)]
    tile_copies = fetch([values_ref.at[0, part] for part in parts], [tiles.at[part] for part in parts], sems)
    field_copies = fetch(fields, [held.at[k] for k in range(len(fields))], field_sems)
    for item in small:
        item.wait()

    def place_of(t):
        row = rows[0, t]
        if n_col & (n_col - 1) == 0:
            s = (lax.shift_right_logical(row, CHB.bit_length() - 1) - ids_ref[0]) & (n_col - 1)
        else:
            s = lax.rem(row // CHB - ids_ref[0] + n_col, n_col)
        return s, slots[0, t] * CHB + (row & (CHB - 1))

    def add_block(into, position, tile):
        slot = lax.shift_right_logical(position, CHB.bit_length() - 1)
        at_row = pl.ds(pl.multiple_of((position & (CHB - 1)) * TB, TB), TB)
        at_lane = pl.ds(pl.multiple_of((slot & 1) * TB, TB), TB)
        acc[into, lax.shift_right_logical(slot, 1), at_row, at_lane] += tiles[tile]

    if whole:

        def add_now(t, carry):
            s, position = place_of(t)
            add_block(s, position, t)
            return carry

        acc[...] = jnp.zeros_like(acc)
        for g, item in enumerate(tile_copies):
            item.wait()
            end = (g + 1) * size

            @pl.when(live_ref[0] >= end)
            def _():
                lax.fori_loop(end - size, end, add_now, 0, unroll=4)

            @pl.when(live_ref[0] < end)
            def _():
                lax.fori_loop(end - size, live_ref[0], add_now, 0)

    else:

        def place(t, counted):
            s, position = place_of(t)
            n = counted[0]
            for k in range(1, n_col):
                n = jnp.where(s == k, counted[k], n)
            lists[s, n] = position * TILES_DEV + t
            return tuple(c + (s == k).astype(jnp.int32) for k, c in enumerate(counted))

        counted = lax.fori_loop(0, live_ref[0], place, (jnp.int32(0),) * n_col)
        for s in range(n_col):
            counts[s] = counted[s]
        for item in tile_copies:
            item.wait()

    def out_copy(origin, p):
        return pltpu.make_async_copy(buf.at[origin % 2, p], out_hbm.at[origin, p], out_sems.at[origin % 2, p])

    for origin in range(n_col):
        if not whole:

            def add(n, carry):
                entry = lists[origin, n]
                add_block(0, lax.shift_right_logical(entry, TILES_DEV.bit_length() - 1), entry & (TILES_DEV - 1))
                return carry

            acc[...] = jnp.zeros_like(acc)
            lax.fori_loop(0, counts[origin], add, 0)
        summed_blocks = acc.at[origin if whole else 0]
        for p in range(pairs):
            if origin >= 2:
                out_copy(origin - 2, p).wait()
            high, low = split(summed_blocks[p])
            buf[origin % 2, p, :NODES_DEV, :] = high
            buf[origin % 2, p, NODES_DEV:, :] = low
            out_copy(origin, p).start()
        if origin in origins:
            k = origins.index(origin)
            field_copies[k].wait()
            left = stacked(held[k])
            for p in range(pairs):
                summed = times(left, buf.at[origin % 2, p])
                here = slice(p * WIDE, (p + 1) * WIDE)
                total_ref[:, here] = summed if origin == 0 else total_ref[:, here] + summed
    for origin in range(n_col - 2, n_col):
        for p in range(pairs):
            out_copy(origin, p).wait()


def build_operator(n_row, n_col, ids, live, rows, slots, values, pairs):
    part = (n_row // 2, 2 * NODES_DEV, WIDE)
    sums = (n_row // 2, NODES_DEV, WIDE)
    held_origins = n_col if 4 * n_col * n_row * TB * NODES_DEV <= WHOLE_BYTES else 1
    origins, fields = zip(*pairs)
    return pl.pallas_call(
        functools.partial(operator_kernel, n_row, n_col, origins),
        in_specs=[SMEM] * 2 + [HBM] * 3 + [ANY] * len(fields),
        out_specs=[HBM, VMEM],
        out_shape=[pltpu.HBM((n_col,) + part, BF16), jax.ShapeDtypeStruct((H, n_row * TB), F32)],
        scratch_shapes=[
            pltpu.VMEM((TILES_DEV, TB, TB), F32),
            pltpu.VMEM((held_origins,) + sums, F32),
            pltpu.VMEM((2,) + part, BF16),
            pltpu.VMEM((len(fields), H, NODES_DEV), F32),
            pltpu.SMEM((n_col, TILES_DEV), jnp.int32),
            pltpu.SMEM((n_col,), jnp.int32),
            pltpu.SMEM((1, TILES_DEV), jnp.int32),
            pltpu.SMEM((1, TILES_DEV), jnp.int32),
            pltpu.SemaphoreType.DMA((GROUPS,)),
            pltpu.SemaphoreType.DMA((2,)),
            pltpu.SemaphoreType.DMA((len(fields),)),
            pltpu.SemaphoreType.DMA((2, n_row // 2)),
        ],
        compiler_params=params(48),
        cost_estimate=HEAVY,
        name="operator",
    )(ids, live, *in_hbm(rows, slots, values), *fields)


def product_kernel(n_row, n_col, origins, has_prev, last, n_carriers, has_base, apart, *refs):
    n = len(origins)
    if n_carriers or apart:
        index_ref, refs = refs[0], refs[1:]
    op_ref, refs = refs[0], refs[1:]
    fields, refs = refs[:n], refs[n:]
    if has_prev:
        prev_hbm, refs = refs[0], refs[1:]
    carriers, refs = refs[:n_carriers], refs[n_carriers:]
    if has_base:
        base_hbm, out_ref, base_ref, refs = refs[0], refs[1], refs[2], refs[3:]
    elif apart:
        slot_refs, refs = refs[:n_row], refs[n_row:]
    else:
        out_ref, refs = refs[0], refs[1:]
    held, buf, field_sems, sems, out, out_sems, prev, other_sems = refs[:8]
    order = [(k, p) for p in range(n_row // 2) for k in range(n)]

    def copy(k, p):
        return pltpu.make_async_copy(op_ref.at[origins[k], p], buf.at[k, p], sems.at[k, p])

    field_copies = fetch([x.at[pl.ds(0, H)] for x in fields], [held.at[k] for k in range(n)], field_sems)
    for k, p in order[:DEPTH]:
        copy(k, p).start()
    if has_prev:
        (prev_copy,) = fetch([prev_hbm], [prev], other_sems.at[pl.ds(0, 1)])
    if has_base:
        (base_copy,) = fetch([base_hbm], [base_ref], other_sems.at[pl.ds(1, 1)])
    left = []
    for k in range(n):
        field_copies[k].wait()
        left.append(stacked(held[k]))
    if n_carriers:
        ordered = refs[8]
        for k in range(n_col):
            ordered[lax.rem(index_ref[0] + k, n_col)] = carriers[k][H:, :]
        share = ordered[0]
        for k in range(1, n_col):
            share = share + ordered[k]
        rows = share.shape[0]
        for j in range(NODES_DEV // LANES):
            for q in range(n_row):
                out[q, H + j * rows : H + (j + 1) * rows, :] = share[:, j * LANES : (j + 1) * LANES]
    sent = []
    for p in range(n_row // 2):
        here = slice(p * WIDE, (p + 1) * WIDE)
        total = None
        for k in range(n):
            copy(k, p).wait()
            ahead = p * n + k + DEPTH
            if ahead < len(order):
                copy(*order[ahead]).start()
            part = times(left[k], buf.at[k, p])
            total = part if total is None else total + part
        if has_prev:
            if p == 0:
                prev_copy.wait()
            total = total + prev[:, here]
        if last:
            out[2 * p, :H, :] = total[:, :TB]
            out[2 * p + 1, :H, :] = total[:, TB:]
            place = pl.ds(2 * p, 2)
            if apart:
                continue
            sent.append(pltpu.make_async_copy(out.at[place], out_ref.at[place], out_sems.at[p]))
        else:
            out[:, here] = total
            place = (pl.ds(0, H), pl.ds(p * WIDE, WIDE))
            sent.append(pltpu.make_async_copy(out.at[place], out_ref.at[place], out_sems.at[p]))
        sent[-1].start()
    if has_base:
        base_copy.wait()
    if apart:
        for j, slot_ref in enumerate(slot_refs):
            slot_ref[...] = out[index_ref[0] ^ j]
    for item in sent:
        item.wait()


def product(n_row, n_col, ids, row, origins, operator, fields, prev, last, carriers=(), base=None, prev_near=False, apart=False):
    n = len(origins)
    has_prev = prev is not None
    has_base = base is not None
    rows = carriers[0].shape[0] - H if carriers else 0
    under = rows * NODES_DEV // LANES
    shape = (n_row, H + under, TB) if last else (H, n_row * TB)
    scratch = [
        pltpu.VMEM((n, H, NODES_DEV), F32),
        pltpu.VMEM((n, n_row // 2, 2 * NODES_DEV, WIDE), BF16),
        pltpu.SemaphoreType.DMA((n,)),
        pltpu.SemaphoreType.DMA((n, n_row // 2)),
        pltpu.VMEM(shape, F32),
        pltpu.SemaphoreType.DMA((n_row // 2,)),
        pltpu.VMEM((H, n_row * TB) if has_prev else (8, LANES), F32),
        pltpu.SemaphoreType.DMA((2,)),
    ]
    if carriers:
        scratch.append(pltpu.VMEM((n_col, rows, NODES_DEV), F32))
    index = (ids,) if carriers else (row,) if apart else ()
    out = pltpu.HBM(shape, F32)
    out_specs, out_shape = HBM, out
    if has_base:
        out_specs, out_shape = [HBM, VMEM], [out, jax.ShapeDtypeStruct(base.shape, F32)]
    elif apart:
        out_specs, out_shape = [VMEM] * n_row, [jax.ShapeDtypeStruct((H, TB), F32)] * n_row
    return pl.pallas_call(
        functools.partial(product_kernel, n_row, n_col, origins, has_prev, last, len(carriers), has_base, apart),
        in_specs=[SMEM] * len(index) + [HBM] + [ANY] * (n + has_prev) + [VMEM] * len(carriers) + [HBM] * has_base,
        out_specs=out_specs,
        out_shape=out_shape,
        scratch_shapes=scratch,
        compiler_params=params(48),
        cost_estimate=LIGHT if last else HEAVY,
        name="product",
    )(
        *index,
        *in_hbm(operator),
        *fields,
        *((prev,) if prev_near else in_hbm(prev) if has_prev else ()),
        *carriers,
        *(in_hbm(base) if has_base else ()),
    )


def carry_kernel(n_row, rows, owners_ref, base_ref, came_ref, *refs):
    out_ref = refs[-1]
    out_ref[:H, :] = base_ref[...]
    for q in range(n_row):
        here = pl.ds(pl.multiple_of(owners_ref[q] * TB, TB), TB)
        out_ref[:H, here] += 2.0 * came_ref[q]
    if rows:
        pieces_ref = refs[0]
        share = pieces_ref[0]
        for q in range(1, n_row):
            share = share + pieces_ref[q]
        for j in range(NODES_DEV // LANES):
            out_ref[H:, j * LANES : (j + 1) * LANES] = share[j * rows : (j + 1) * rows, :]


def carry(n_row, owners, base, came, *pieces):
    rows = pieces[0].shape[1] * LANES // NODES_DEV if pieces else 0
    return pl.pallas_call(
        functools.partial(carry_kernel, n_row, rows),
        in_specs=[SMEM] + [VMEM] * (2 + len(pieces)),
        out_specs=VMEM,
        out_shape=jax.ShapeDtypeStruct((H + rows, NODES_DEV), F32),
        compiler_params=params(24),
        cost_estimate=LIGHT,
        name="carry",
    )(owners, base, came, *pieces)


def finish_kernel(n_row, row_ref, owners_ref, base_ref, left_ref, *refs):
    right_refs, out_ref, total = refs[:n_row], refs[n_row], refs[n_row + 1]
    total[...] = base_ref[...]
    for q in range(n_row):
        here = pl.ds(pl.multiple_of(owners_ref[q] * TB, TB), TB)
        total[:H, here] += left_ref[q, :H, :]
    for j in range(n_row):
        here = pl.ds(pl.multiple_of(owners_ref[row_ref[0] ^ j] * TB, TB), TB)
        total[H:, here] += right_refs[j][...]
    out_ref[...] = total[...].T


def finish(n_row, row, owners, base, left, right):
    return pl.pallas_call(
        functools.partial(finish_kernel, n_row),
        in_specs=[SMEM] * 2 + [VMEM] * (2 + n_row),
        out_specs=VMEM,
        out_shape=jax.ShapeDtypeStruct((NODES_DEV, F), F32),
        scratch_shapes=[pltpu.VMEM((F, NODES_DEV), F32)],
        compiler_params=params(24),
        cost_estimate=LIGHT,
        name="finish",
    )(row, owners, base, left, *right)


def assemble_kernel(n_row, came_ref, out_ref, turned):
    rows = F // n_row
    per = F // LANES
    for q in range(n_row):
        for j in range(3 * per):
            here = slice(H + j * rows, H + (j + 1) * rows)
            turned[q * rows : (q + 1) * rows, j * LANES : (j + 1) * LANES] = came_ref[q, here, :]
    for k in range(3):
        out_ref[k] = turned[:, k * F : (k + 1) * F].T


def assemble(n_row, came):
    return pl.pallas_call(
        functools.partial(assemble_kernel, n_row),
        in_specs=[VMEM],
        out_specs=VMEM,
        out_shape=jax.ShapeDtypeStruct((3, F, F), F32),
        scratch_shapes=[pltpu.VMEM((F, 3 * F), F32)],
        compiler_params=params(16),
        cost_estimate=LIGHT,
        name="assemble",
    )(came)


def shift(n_col, x, step):
    return lax.ppermute(x, "col", [(c, (c + step) % n_col) for c in range(n_col)])


def exchange(pieces):
    return lax.all_to_all(pieces, "row", split_axis=0, concat_axis=0, tiled=True)


def after(x, *others):
    return lax.optimization_barrier((x, *others))[0]


def opposite(field, below, above):
    col = lax.axis_index("col")
    sent = jnp.where(col == 1, above, jnp.where(col == 2, below, field))
    return lax.ppermute(sent, "col", [(1, 0), (2, 3), (3, 1), (0, 2)])


def gather(n_col, field, side):
    long = n_col // 2
    short = n_col - 1 - long
    ahead, behind = field, field
    steps = [[(0, field)]]
    for s in range(1, long + 1):
        if s == 2:
            ahead = after(ahead, behind)
        if s == 2 and n_col == 4:
            ahead = opposite(field, ahead, behind) if side > 0 else opposite(field, behind, ahead)
        else:
            ahead = shift(n_col, ahead, side)
        step = [((-side * s) % n_col, ahead)]
        if s <= short:
            behind = shift(n_col, behind, -side)
            step.append(((side * s) % n_col, behind))
        steps.append(step)
    return steps


def early(n_row, n_col, ids, row, operator, steps, total=None, done=0, base=None):
    pairs = [pair for step in steps[:-1] for pair in step][done:]
    for begin in range(0, len(pairs), 3):
        origins, fields = zip(*pairs[begin : begin + 3])
        brought = base if begin + 3 >= len(pairs) else None
        total = product(n_row, n_col, ids, row, origins, operator, fields, total, False, base=brought)
    return total


def final(n_row, n_col, ids, row, operator, steps, total, carrying=False, near=False, apart=False):
    origins, fields = zip(*steps[-1])
    carriers = [x for _, x in sorted((p for step in steps for p in step), key=lambda p: p[0])] if carrying else ()
    return product(n_row, n_col, ids, row, origins, operator, fields, total, True, carriers, prev_near=near, apart=apart)


def per_device(
    grad_out,
    relu_mask,
    basis_zero,
    basis_one,
    basis_two,
    cheb_weight,
    tile_values,
    tile_rows,
    tile_slots,
    send_blocks,
    live_tiles,
):
    n_row = lax.axis_size("row")
    n_col = lax.axis_size("col")
    ids = lax.axis_index("col").astype(jnp.int32).reshape(1)
    row = lax.axis_index("row").astype(jnp.int32).reshape(1)
    owners = send_blocks.reshape(n_row)
    left, right = term_two(grad_out, relu_mask, cheb_weight)
    one_left, one_right, diff, pieces = local_terms(
        n_row, left, grad_out, relu_mask, cheb_weight, basis_zero, basis_one, basis_two
    )
    steps = gather(n_col, left, 1)
    first = steps[0] + steps[1] if len(steps) > 2 else steps[0]
    operator, left_early = build_operator(
        n_row, n_col, ids, live_tiles, tile_rows, tile_slots, tile_values, first
    )
    pieces = exchange(pieces)
    common = (n_row, n_col, ids, row, operator)

    left_early = early(*common, steps, left_early, len(first))
    right_steps = gather(n_col, after(right, left_early, steps[-1][0][1]), -1)
    left_came = exchange(final(*common, steps, after(left_early, pieces), near=len(steps) == 3))
    right_early, one_left = early(*common, right_steps, base=one_left)

    left_carried = carry(n_row, owners, after(one_left, right_early, right_steps[-1][0][1]), left_came, pieces)
    steps = gather(n_col, left_carried, 1)
    right_came = exchange(final(*common, right_steps, right_early))
    left_early, one_right = early(*common, steps, base=one_right)

    right_carried = carry(n_row, owners, after(one_right, left_early, steps[-1][0][1]), right_came)
    right_steps = gather(n_col, right_carried, -1)
    left_last = final(*common, steps, left_early, carrying=True)
    left_came = exchange(left_last)
    right_steps[0] = [(0, after(right_carried, left_last))]
    right_early = early(*common, right_steps)

    right_last = final(*common, right_steps, right_early, apart=True)
    right_came = [right_last[0]] * n_row
    for j in range(n_row - 1, 0, -1):
        right_came[j] = lax.ppermute(right_last[j], "row", [(r, r ^ j) for r in range(n_row)])
    weight_grad = assemble(n_row, left_came)
    return finish(n_row, row, owners, after(diff, weight_grad), left_came, right_came), weight_grad


def solution(mesh):
    placed = (
        P(("row", "col"), None),
        P(("row", "col"), None),
        P(("row", "col"), None),
        P(("row", "col"), None),
        P(("row", "col"), None),
        P(),
        P(("row", "col"), None, None, None),
        P(("row", "col"), None),
        P(("row", "col"), None),
        P(("row", "col"), None, None),
        P(("row", "col")),
    )
    return jax.shard_map(
        per_device,
        mesh=mesh,
        in_specs=placed,
        out_specs=(P(("row", "col"), None), P()),
        check_vma=False,
    )
```

```python
import functools

import jax
import jax.numpy as jnp
from jax import lax
from jax.experimental import pallas as pl
from jax.experimental.pallas import tpu as pltpu
from jax.sharding import PartitionSpec as P

F = 256
H = 128
TB = 128
CHB = 4
WIDE = 2 * TB
LANES = 128
NODES_DEV = CHB * TB
TILES_DEV = 128
GROUPS = 8
MIB = 1 << 20
WHOLE_BYTES = 12 * MIB
DEPTH = 4
HEAVY = pl.CostEstimate(flops=1 << 34, bytes_accessed=64 * MIB, transcendentals=0)
LIGHT = pl.CostEstimate(flops=1024, bytes_accessed=1024, transcendentals=0)
BF16 = jnp.bfloat16
F32 = jnp.float32

SMEM = pl.BlockSpec(memory_space=pltpu.SMEM)
VMEM = pl.BlockSpec(memory_space=pltpu.VMEM)
HBM = pl.BlockSpec(memory_space=pltpu.HBM)
ANY = pl.BlockSpec(memory_space=pl.ANY)


def params(mib):
    return pltpu.CompilerParams(vmem_limit_bytes=mib * MIB)


def in_hbm(*arrays):
    return [pltpu.with_memory_space_constraint(x, pltpu.HBM) for x in arrays]


def split(x):
    high = x.astype(BF16)
    low = (x - high.astype(F32)).astype(BF16)
    return high, low


def dot3(a, b, dims):
    ah, al = a
    bh, bl = b

    def one(x, y):
        return lax.dot_general(x, y, (dims, ((), ())), preferred_element_type=F32)

    return one(ah, bh) + (one(ah, bl) + one(al, bh))


def fetch(sources, targets, sems):
    copies = [pltpu.make_async_copy(a, b, sems.at[i]) for i, (a, b) in enumerate(zip(sources, targets))]
    for copy in copies:
        copy.start()
    return copies


def masked_of(grad, mask):
    return jnp.where(mask > 0, grad, jnp.zeros_like(grad))


def term_two_kernel(grad_hbm, mask_hbm, weight_hbm, left_ref, right_ref, grad, mask, weight, sems):
    for copy in fetch((grad_hbm, mask_hbm, weight_hbm.at[2]), (grad, mask, weight), sems):
        copy.wait()
    term = dot3(split(weight[...]), split(masked_of(grad[...], mask[...])), ((1,), (1,)))
    left_ref[...] = term[:H]
    right_ref[...] = term[H:]


def term_two(grad_out, relu_mask, cheb_weight):
    out = jax.ShapeDtypeStruct((H, NODES_DEV), F32)
    return pl.pallas_call(
        term_two_kernel,
        in_specs=[HBM] * 3,
        out_specs=[VMEM, VMEM],
        out_shape=[out, out],
        scratch_shapes=[
            pltpu.VMEM((NODES_DEV, F), F32),
            pltpu.VMEM((NODES_DEV, F), jnp.int32),
            pltpu.VMEM((F, F), F32),
            pltpu.SemaphoreType.DMA((3,)),
        ],
        compiler_params=params(16),
        cost_estimate=LIGHT,
        name="term_two",
    )(*in_hbm(grad_out, relu_mask, cheb_weight))


def local_kernel(
    n_row, first_ref, grad_hbm, mask_hbm, weight_hbm, h0, h1, h2, left_hbm, right_hbm, diff_ref, pieces_ref,
    grad, mask, weight, bases, one, sems, one_sems,
):
    sources = (grad_hbm, mask_hbm, weight_hbm, h0, h1, h2)
    copies = fetch(sources, (grad, mask, weight, bases.at[0], bases.at[1], bases.at[2]), sems)
    for copy in copies[:3]:
        copy.wait()
    values = masked_of(grad[...], mask[...])
    masked = split(values)
    term = dot3(split(weight[1]), masked, ((1,), (1,)))
    one[...] = term
    one_copies = fetch((one.at[pl.ds(0, H)], one.at[pl.ds(H, H)]), (left_hbm, right_hbm), one_sems)
    diff_ref[...] = dot3(split(weight[0] - weight[2]), masked, ((1,), (1,)))
    turned = split(values.T)
    rows = F // n_row
    for k in range(3):
        copies[3 + k].wait()
        part = dot3(turned, split(bases[k]), ((1,), (0,)))
        for j in range(F // LANES):
            here = (k * (F // LANES) + j) * rows
            for q in range(n_row):
                pieces_ref[q, here : here + rows, :] = part[q * rows : (q + 1) * rows, j * LANES : (j + 1) * LANES]
    for copy in one_copies:
        copy.wait()


def local_terms(n_row, first, grad_out, relu_mask, cheb_weight, b0, b1, b2):
    half = pltpu.HBM((H, NODES_DEV), F32)
    share = 3 * F * F // n_row // LANES
    return pl.pallas_call(
        functools.partial(local_kernel, n_row),
        in_specs=[ANY] + [HBM] * 6,
        out_specs=[HBM, HBM, VMEM, VMEM],
        out_shape=[
            half,
            half,
            jax.ShapeDtypeStruct((F, NODES_DEV), F32),
            jax.ShapeDtypeStruct((n_row, share, LANES), F32),
        ],
        scratch_shapes=[
            pltpu.VMEM((NODES_DEV, F), F32),
            pltpu.VMEM((NODES_DEV, F), jnp.int32),
            pltpu.VMEM((3, F, F), F32),
            pltpu.VMEM((3, NODES_DEV, F), F32),
            pltpu.VMEM((F, NODES_DEV), F32),
            pltpu.SemaphoreType.DMA((6,)),
            pltpu.SemaphoreType.DMA((2,)),
        ],
        compiler_params=params(32),
        cost_estimate=LIGHT,
        name="local_terms",
    )(first, *in_hbm(grad_out, relu_mask, cheb_weight, b0, b1, b2))


def stacked(field):
    return jnp.concatenate(split(field), axis=0)


def times(left, part):
    by_high = jnp.dot(left, part[:NODES_DEV, :], preferred_element_type=F32)
    by_low = jnp.dot(left[:H], part[NODES_DEV:, :], preferred_element_type=F32)
    return by_high[:H] + (by_high[H:] + by_low)


def operator_kernel(n_row, n_col, origins, ids_ref, live_ref, rows_hbm, slots_hbm, values_ref, *refs):
    fields, refs = refs[: len(origins)], refs[len(origins) :]
    out_hbm, total_ref, tiles, acc, buf, held, lists, counts, rows, slots, sems, small_sems, field_sems, out_sems = refs
    size = TILES_DEV // GROUPS
    pairs = n_row // 2
    whole = acc.shape[0] == n_col
    small = fetch((rows_hbm, slots_hbm), (rows, slots), small_sems)
    parts = [pl.ds(g * size, size) for g in range(GROUPS)]
    tile_copies = fetch([values_ref.at[0, part] for part in parts], [tiles.at[part] for part in parts], sems)
    field_copies = fetch(fields, [held.at[k] for k in range(len(fields))], field_sems)
    for item in small:
        item.wait()

    def place_of(t):
        row = rows[0, t]
        if n_col & (n_col - 1) == 0:
            s = (lax.shift_right_logical(row, CHB.bit_length() - 1) - ids_ref[0]) & (n_col - 1)
        else:
            s = lax.rem(row // CHB - ids_ref[0] + n_col, n_col)
        return s, slots[0, t] * CHB + (row & (CHB - 1))

    def add_block(into, position, tile):
        slot = lax.shift_right_logical(position, CHB.bit_length() - 1)
        at_row = pl.ds(pl.multiple_of((position & (CHB - 1)) * TB, TB), TB)
        at_lane = pl.ds(pl.multiple_of((slot & 1) * TB, TB), TB)
        acc[into, lax.shift_right_logical(slot, 1), at_row, at_lane] += tiles[tile]

    if whole:

        def add_now(t, carry):
            s, position = place_of(t)
            add_block(s, position, t)
            return carry

        acc[...] = jnp.zeros_like(acc)
        for g, item in enumerate(tile_copies):
            item.wait()
            end = (g + 1) * size

            @pl.when(live_ref[0] >= end)
            def _():
                lax.fori_loop(end - size, end, add_now, 0, unroll=4)

            @pl.when(live_ref[0] < end)
            def _():
                lax.fori_loop(end - size, live_ref[0], add_now, 0)

    else:

        def place(t, counted):
            s, position = place_of(t)
            n = counted[0]
            for k in range(1, n_col):
                n = jnp.where(s == k, counted[k], n)
            lists[s, n] = position * TILES_DEV + t
            return tuple(c + (s == k).astype(jnp.int32) for k, c in enumerate(counted))

        counted = lax.fori_loop(0, live_ref[0], place, (jnp.int32(0),) * n_col)
        for s in range(n_col):
            counts[s] = counted[s]
        for item in tile_copies:
            item.wait()

    def out_copy(origin, p):
        return pltpu.make_async_copy(buf.at[origin % 2, p], out_hbm.at[origin, p], out_sems.at[origin % 2, p])

    for origin in range(n_col):
        if not whole:

            def add(n, carry):
                entry = lists[origin, n]
                add_block(0, lax.shift_right_logical(entry, TILES_DEV.bit_length() - 1), entry & (TILES_DEV - 1))
                return carry

            acc[...] = jnp.zeros_like(acc)
            lax.fori_loop(0, counts[origin], add, 0)
        summed_blocks = acc.at[origin if whole else 0]
        for p in range(pairs):
            if origin >= 2:
                out_copy(origin - 2, p).wait()
            high, low = split(summed_blocks[p])
            buf[origin % 2, p, :NODES_DEV, :] = high
            buf[origin % 2, p, NODES_DEV:, :] = low
            out_copy(origin, p).start()
        if origin in origins:
            k = origins.index(origin)
            field_copies[k].wait()
            left = stacked(held[k])
            for p in range(pairs):
                summed = times(left, buf.at[origin % 2, p])
                here = slice(p * WIDE, (p + 1) * WIDE)
                total_ref[:, here] = summed if origin == 0 else total_ref[:, here] + summed
    for origin in range(n_col - 2, n_col):
        for p in range(pairs):
            out_copy(origin, p).wait()


def build_operator(n_row, n_col, ids, live, rows, slots, values, pairs):
    part = (n_row // 2, 2 * NODES_DEV, WIDE)
    sums = (n_row // 2, NODES_DEV, WIDE)
    held_origins = n_col if 4 * n_col * n_row * TB * NODES_DEV <= WHOLE_BYTES else 1
    origins, fields = zip(*pairs)
    return pl.pallas_call(
        functools.partial(operator_kernel, n_row, n_col, origins),
        in_specs=[SMEM] * 2 + [HBM] * 3 + [ANY] * len(fields),
        out_specs=[HBM, VMEM],
        out_shape=[pltpu.HBM((n_col,) + part, BF16), jax.ShapeDtypeStruct((H, n_row * TB), F32)],
        scratch_shapes=[
            pltpu.VMEM((TILES_DEV, TB, TB), F32),
            pltpu.VMEM((held_origins,) + sums, F32),
            pltpu.VMEM((2,) + part, BF16),
            pltpu.VMEM((len(fields), H, NODES_DEV), F32),
            pltpu.SMEM((n_col, TILES_DEV), jnp.int32),
            pltpu.SMEM((n_col,), jnp.int32),
            pltpu.SMEM((1, TILES_DEV), jnp.int32),
            pltpu.SMEM((1, TILES_DEV), jnp.int32),
            pltpu.SemaphoreType.DMA((GROUPS,)),
            pltpu.SemaphoreType.DMA((2,)),
            pltpu.SemaphoreType.DMA((len(fields),)),
            pltpu.SemaphoreType.DMA((2, n_row // 2)),
        ],
        compiler_params=params(48),
        cost_estimate=HEAVY,
        name="operator",
    )(ids, live, *in_hbm(rows, slots, values), *fields)


def product_kernel(n_row, n_col, origins, has_prev, last, n_carriers, has_base, apart, *refs):
    n = len(origins)
    if n_carriers or apart:
        index_ref, refs = refs[0], refs[1:]
    op_ref, refs = refs[0], refs[1:]
    fields, refs = refs[:n], refs[n:]
    if has_prev:
        prev_hbm, refs = refs[0], refs[1:]
    carriers, refs = refs[:n_carriers], refs[n_carriers:]
    if has_base:
        base_hbm, out_ref, base_ref, refs = refs[0], refs[1], refs[2], refs[3:]
    elif apart:
        slot_refs, refs = refs[:n_row], refs[n_row:]
    else:
        out_ref, refs = refs[0], refs[1:]
    held, buf, field_sems, sems, out, out_sems, prev, other_sems = refs[:8]
    order = [(k, p) for p in range(n_row // 2) for k in range(n)]

    def copy(k, p):
        return pltpu.make_async_copy(op_ref.at[origins[k], p], buf.at[k, p], sems.at[k, p])

    field_copies = fetch([x.at[pl.ds(0, H)] for x in fields], [held.at[k] for k in range(n)], field_sems)
    for k, p in order[:DEPTH]:
        copy(k, p).start()
    if has_prev:
        (prev_copy,) = fetch([prev_hbm], [prev], other_sems.at[pl.ds(0, 1)])
    if has_base:
        (base_copy,) = fetch([base_hbm], [base_ref], other_sems.at[pl.ds(1, 1)])
    left = []
    for k in range(n):
        field_copies[k].wait()
        left.append(stacked(held[k]))
    if n_carriers:
        ordered = refs[8]
        for k in range(n_col):
            ordered[lax.rem(index_ref[0] + k, n_col)] = carriers[k][H:, :]
        share = ordered[0]
        for k in range(1, n_col):
            share = share + ordered[k]
        rows = share.shape[0]
        for j in range(NODES_DEV // LANES):
            for q in range(n_row):
                out[q, H + j * rows : H + (j + 1) * rows, :] = share[:, j * LANES : (j + 1) * LANES]
    sent = []
    for p in range(n_row // 2):
        here = slice(p * WIDE, (p + 1) * WIDE)
        total = None
        for k in range(n):
            copy(k, p).wait()
            ahead = p * n + k + DEPTH
            if ahead < len(order):
                copy(*order[ahead]).start()
            part = times(left[k], buf.at[k, p])
            total = part if total is None else total + part
        if has_prev:
            if p == 0:
                prev_copy.wait()
            total = total + prev[:, here]
        if last:
            out[2 * p, :H, :] = total[:, :TB]
            out[2 * p + 1, :H, :] = total[:, TB:]
            place = pl.ds(2 * p, 2)
            if apart:
                continue
            sent.append(pltpu.make_async_copy(out.at[place], out_ref.at[place], out_sems.at[p]))
        else:
            out[:, here] = total
            place = (pl.ds(0, H), pl.ds(p * WIDE, WIDE))
            sent.append(pltpu.make_async_copy(out.at[place], out_ref.at[place], out_sems.at[p]))
        sent[-1].start()
    if has_base:
        base_copy.wait()
    if apart:
        for j, slot_ref in enumerate(slot_refs):
            slot_ref[...] = out[index_ref[0] ^ j]
    for item in sent:
        item.wait()


def product(n_row, n_col, ids, row, origins, operator, fields, prev, last, carriers=(), base=None, prev_near=False, apart=False):
    n = len(origins)
    has_prev = prev is not None
    has_base = base is not None
    rows = carriers[0].shape[0] - H if carriers else 0
    under = rows * NODES_DEV // LANES
    shape = (n_row, H + under, TB) if last else (H, n_row * TB)
    scratch = [
        pltpu.VMEM((n, H, NODES_DEV), F32),
        pltpu.VMEM((n, n_row // 2, 2 * NODES_DEV, WIDE), BF16),
        pltpu.SemaphoreType.DMA((n,)),
        pltpu.SemaphoreType.DMA((n, n_row // 2)),
        pltpu.VMEM(shape, F32),
        pltpu.SemaphoreType.DMA((n_row // 2,)),
        pltpu.VMEM((H, n_row * TB) if has_prev else (8, LANES), F32),
        pltpu.SemaphoreType.DMA((2,)),
    ]
    if carriers:
        scratch.append(pltpu.VMEM((n_col, rows, NODES_DEV), F32))
    index = (ids,) if carriers else (row,) if apart else ()
    out = pltpu.HBM(shape, F32)
    out_specs, out_shape = HBM, out
    if has_base:
        out_specs, out_shape = [HBM, VMEM], [out, jax.ShapeDtypeStruct(base.shape, F32)]
    elif apart:
        out_specs, out_shape = [VMEM] * n_row, [jax.ShapeDtypeStruct((H, TB), F32)] * n_row
    return pl.pallas_call(
        functools.partial(product_kernel, n_row, n_col, origins, has_prev, last, len(carriers), has_base, apart),
        in_specs=[SMEM] * len(index) + [HBM] + [ANY] * (n + has_prev) + [VMEM] * len(carriers) + [HBM] * has_base,
        out_specs=out_specs,
        out_shape=out_shape,
        scratch_shapes=scratch,
        compiler_params=params(48),
        cost_estimate=LIGHT if last else HEAVY,
        name="product",
    )(
        *index,
        *in_hbm(operator),
        *fields,
        *((prev,) if prev_near else in_hbm(prev) if has_prev else ()),
        *carriers,
        *(in_hbm(base) if has_base else ()),
    )


def carry_kernel(n_row, rows, owners_ref, base_ref, came_ref, *refs):
    out_ref = refs[-1]
    out_ref[:H, :] = base_ref[...]
    for q in range(n_row):
        here = pl.ds(pl.multiple_of(owners_ref[q] * TB, TB), TB)
        out_ref[:H, here] += 2.0 * came_ref[q]
    if rows:
        pieces_ref = refs[0]
        share = pieces_ref[0]
        for q in range(1, n_row):
            share = share + pieces_ref[q]
        for j in range(NODES_DEV // LANES):
            out_ref[H:, j * LANES : (j + 1) * LANES] = share[j * rows : (j + 1) * rows, :]


def carry(n_row, owners, base, came, *pieces):
    rows = pieces[0].shape[1] * LANES // NODES_DEV if pieces else 0
    return pl.pallas_call(
        functools.partial(carry_kernel, n_row, rows),
        in_specs=[SMEM] + [VMEM] * (2 + len(pieces)),
        out_specs=VMEM,
        out_shape=jax.ShapeDtypeStruct((H + rows, NODES_DEV), F32),
        compiler_params=params(24),
        cost_estimate=LIGHT,
        name="carry",
    )(owners, base, came, *pieces)


def finish_kernel(n_row, row_ref, owners_ref, base_ref, left_ref, *refs):
    right_refs, out_ref, total = refs[:n_row], refs[n_row], refs[n_row + 1]
    total[...] = base_ref[...]
    for q in range(n_row):
        here = pl.ds(pl.multiple_of(owners_ref[q] * TB, TB), TB)
        total[:H, here] += left_ref[q, :H, :]
    for j in range(n_row):
        here = pl.ds(pl.multiple_of(owners_ref[row_ref[0] ^ j] * TB, TB), TB)
        total[H:, here] += right_refs[j][...]
    out_ref[...] = total[...].T


def finish(n_row, row, owners, base, left, right):
    return pl.pallas_call(
        functools.partial(finish_kernel, n_row),
        in_specs=[SMEM] * 2 + [VMEM] * (2 + n_row),
        out_specs=VMEM,
        out_shape=jax.ShapeDtypeStruct((NODES_DEV, F), F32),
        scratch_shapes=[pltpu.VMEM((F, NODES_DEV), F32)],
        compiler_params=params(24),
        cost_estimate=LIGHT,
        name="finish",
    )(row, owners, base, left, *right)


def assemble_kernel(n_row, came_ref, out_ref, turned):
    rows = F // n_row
    per = F // LANES
    for q in range(n_row):
        for j in range(3 * per):
            here = slice(H + j * rows, H + (j + 1) * rows)
            turned[q * rows : (q + 1) * rows, j * LANES : (j + 1) * LANES] = came_ref[q, here, :]
    for k in range(3):
        out_ref[k] = turned[:, k * F : (k + 1) * F].T


def assemble(n_row, came):
    return pl.pallas_call(
        functools.partial(assemble_kernel, n_row),
        in_specs=[VMEM],
        out_specs=VMEM,
        out_shape=jax.ShapeDtypeStruct((3, F, F), F32),
        scratch_shapes=[pltpu.VMEM((F, 3 * F), F32)],
        compiler_params=params(16),
        cost_estimate=LIGHT,
        name="assemble",
    )(came)


def shift(n_col, x, step):
    return lax.ppermute(x, "col", [(c, (c + step) % n_col) for c in range(n_col)])


def exchange(pieces):
    return lax.all_to_all(pieces, "row", split_axis=0, concat_axis=0, tiled=True)


def after(x, *others):
    return lax.optimization_barrier((x, *others))[0]


def opposite(field, below, above):
    col = lax.axis_index("col")
    sent = jnp.where(col == 1, above, jnp.where(col == 2, below, field))
    return lax.ppermute(sent, "col", [(1, 0), (2, 3), (3, 1), (0, 2)])


def gather(n_col, field, side):
    long = n_col // 2
    short = n_col - 1 - long
    ahead, behind = field, field
    steps = [[(0, field)]]
    for s in range(1, long + 1):
        if s == 2:
            ahead = after(ahead, behind)
        if s == 2 and n_col == 4:
            ahead = opposite(field, ahead, behind) if side > 0 else opposite(field, behind, ahead)
        else:
            ahead = shift(n_col, ahead, side)
        step = [((-side * s) % n_col, ahead)]
        if s <= short:
            behind = shift(n_col, behind, -side)
            step.append(((side * s) % n_col, behind))
        steps.append(step)
    return steps


def early(n_row, n_col, ids, row, operator, steps, total=None, done=0, base=None):
    pairs = [pair for step in steps[:-1] for pair in step][done:]
    for begin in range(0, len(pairs), 3):
        origins, fields = zip(*pairs[begin : begin + 3])
        brought = base if begin + 3 >= len(pairs) else None
        total = product(n_row, n_col, ids, row, origins, operator, fields, total, False, base=brought)
    return total


def final(n_row, n_col, ids, row, operator, steps, total, carrying=False, near=False, apart=False):
    origins, fields = zip(*steps[-1])
    carriers = [x for _, x in sorted((p for step in steps for p in step), key=lambda p: p[0])] if carrying else ()
    return product(n_row, n_col, ids, row, origins, operator, fields, total, True, carriers, prev_near=near, apart=apart)


def per_device(
    grad_out,
    relu_mask,
    basis_zero,
    basis_one,
    basis_two,
    cheb_weight,
    tile_values,
    tile_rows,
    tile_slots,
    send_blocks,
    live_tiles,
):
    n_row = lax.axis_size("row")
    n_col = lax.axis_size("col")
    ids = lax.axis_index("col").astype(jnp.int32).reshape(1)
    row = lax.axis_index("row").astype(jnp.int32).reshape(1)
    owners = send_blocks.reshape(n_row)
    left, right = term_two(grad_out, relu_mask, cheb_weight)
    one_left, one_right, diff, pieces = local_terms(
        n_row, left, grad_out, relu_mask, cheb_weight, basis_zero, basis_one, basis_two
    )
    steps = gather(n_col, left, 1)
    first = steps[0] + steps[1] if len(steps) > 2 else steps[0]
    operator, left_early = build_operator(
        n_row, n_col, ids, live_tiles, tile_rows, tile_slots, tile_values, first
    )
    pieces = exchange(pieces)
    common = (n_row, n_col, ids, row, operator)

    left_early = early(*common, steps, left_early, len(first))
    right_steps = gather(n_col, after(right, left_early, steps[-1][0][1]), -1)
    left_came = exchange(final(*common, steps, after(left_early, pieces), near=len(steps) == 3))
    right_early, one_left = early(*common, right_steps, base=one_left)

    left_carried = carry(n_row, owners, after(one_left, right_early, right_steps[-1][0][1]), left_came, pieces)
    steps = gather(n_col, left_carried, 1)
    right_came = exchange(final(*common, right_steps, right_early))
    left_early, one_right = early(*common, steps, base=one_right)

    right_carried = carry(n_row, owners, after(one_right, left_early, steps[-1][0][1]), right_came)
    right_steps = gather(n_col, right_carried, -1)
    left_last = final(*common, steps, left_early, carrying=True)
    left_came = exchange(left_last)
    right_steps[0] = [(0, after(right_carried, left_last))]
    right_early = early(*common, right_steps)

    right_last = final(*common, right_steps, right_early, apart=True)
    right_came = [right_last[0]] * n_row
    for j in range(n_row - 1, 0, -1):
        sent = right_last[j] if j > 1 else after(right_last[j], right_came[-1])
        right_came[j] = lax.ppermute(sent, "row", [(r, r ^ j) for r in range(n_row)])
    weight_grad = assemble(n_row, left_came)
    return finish(n_row, row, owners, after(diff, weight_grad), left_came, right_came), weight_grad


def solution(mesh):
    placed = (
        P(("row", "col"), None),
        P(("row", "col"), None),
        P(("row", "col"), None),
        P(("row", "col"), None),
        P(("row", "col"), None),
        P(),
        P(("row", "col"), None, None, None),
        P(("row", "col"), None),
        P(("row", "col"), None),
        P(("row", "col"), None, None),
        P(("row", "col")),
    )
    return jax.shard_map(
        per_device,
        mesh=mesh,
        in_specs=placed,
        out_specs=(P(("row", "col"), None), P()),
        check_vma=False,
    )
```
